32 devices in a mesh: groups: 2 (over y), batch: 4 (over z), ctx: 2 (over x), head: 2 (over core).
Axes of the slice: x: 2, y: 2, z: 4, core: 2. Of those that a mesh axis runs over, the one named last changes fastest.
Arguments:
- tokens: bfloat16 [2048, 16384], P(('groups', 'batch'), ('ctx', 'head')), parts along dimension 0, may hold values from -6 to 6
- key_weight: bfloat16 [2, 2, 4096, 4, 2, 128], P('ctx', 'head', 'batch'), may hold values from -0.046875 to 0.046875
- value_weight: bfloat16 [2, 2, 4096, 4, 2, 128], P('ctx', 'head', 'batch'), may hold values from -0.09375 to 0.09375
- queries: bfloat16 [2048, 4, 2, 2048], P(('groups', 'batch'), 'ctx', 'head'), parts along dimension 0, may hold values from -8 to 8
- prefix_pool: bfloat16 [32, 128, 4, 2, 256], P(('groups', 'ctx'), None, None, 'head'), parts along dimension 0, may hold values from -8 to 8
- block_table: int32 [8, 8], P(('groups', 'batch')), parts along dimension 0, may hold values from 0 to 15, as said below
- lengths: int32 [8], P(('groups', 'batch')), parts along dimension 0, may hold values from 128 to 256, as said below
Outputs:
- attended: bfloat16 [2048, 4, 2, 2048], P(('groups', 'batch'), 'ctx', 'head'), parts along dimension 0
The draws below stay inside these ranges and needn't reach their ends.
There are 2 independent parts, one for each index of `groups`. The reference program is written for one: setup_inputs(seed, part) draws one part's arguments, and reference() takes and returns one part's arrays. A program takes and returns all parts, laid end to end along the dimension named above; an argument that names none is the same for every part. Nothing has to cross between parts.
Inputs may be any that keep to these rules, and one draw needn't show every extreme that they name: `block_table`: each row names 8 different pool blocks. `lengths`: each a multiple of 128; some prompt has 256 and some has 128.
All inputs are finite; a program needn't handle non-finite values.
Results may differ from the reference program's by a relative error of at most 0.0073.
Values may be sent and summed in bfloat16 or wider, within the bound.
No kernel may reach another device: no remote copies, remote signals or barrier semaphores. Data moves between devices by JAX's collectives and lax.ppermute only.
A program may use at most 128 MiB of HBM per device.

```python
import jax
import jax.numpy as jnp
from jax import lax

D = 16384
KVH = 8
HD = 128
GRP = 16
NEW = 256
UNIT = 128
BLK = 128
POOL = 16
PB = 8
PROMPTS = 4
TOKENS = 1024
DC = 4096
N_CTX = 2
N_HEAD = 2


def draw_queries(key, part):
    key = jax.random.fold_in(key, 1)
    shape = (TOKENS, KVH // N_HEAD, N_HEAD, GRP * HD)
    return (2.0 * jax.random.truncated_normal(key, -4.0, 4.0, shape, jnp.float32)).astype(jnp.bfloat16)


def draw_prefix_pool(key, part):
    key = jax.random.fold_in(key, 2)
    shape = (POOL, BLK, KVH // N_HEAD, N_HEAD, HD)
    key_draw = jax.random.fold_in(key, 1)
    value_draw = jax.random.fold_in(key, 2)
    key_rows = jax.random.truncated_normal(key_draw, -4.0, 4.0, shape, jnp.float32)
    value_rows = 2.0 * jax.random.truncated_normal(value_draw, -4.0, 4.0, shape, jnp.float32)
    return jnp.concatenate([key_rows, value_rows], 4).astype(jnp.bfloat16)


def pick_row(row_key):
    return jax.random.permutation(row_key, POOL)[:PB]


def draw_block_table(key, part):
    key = jax.random.fold_in(key, 3)
    row_keys = jax.random.split(key, PROMPTS)
    return jax.vmap(pick_row)(row_keys).astype(jnp.int32)


def draw_lengths(key, part):
    key = jax.random.fold_in(key, 4)
    units = jax.random.randint(jax.random.fold_in(key, 1), (PROMPTS,), 1, NEW // UNIT + 1)
    longest = jax.random.randint(jax.random.fold_in(key, 2), (), 0, PROMPTS)
    shortest = (longest + jax.random.randint(jax.random.fold_in(key, 3), (), 1, PROMPTS)) % PROMPTS
    units = units.at[longest].set(NEW // UNIT).at[shortest].set(1)
    return (units * UNIT).astype(jnp.int32)


def levels(stream_key, shape, cuts, low, largest):
    loudness = 1.0
    for axis_at, shards_of in cuts:
        draws = jax.random.uniform(jax.random.fold_in(jax.random.fold_in(stream_key, 6), axis_at), (shards_of,), jnp.float32, low / len(cuts), largest / len(cuts))
        loudness = loudness * jnp.repeat(jnp.exp(draws), shape[axis_at] // shards_of).reshape((-1,) + (1,) * (len(shape) - 1 - axis_at))
    return loudness


def centred(stream_key, extent, deviation, most, cuts=(), held_as=jnp.bfloat16):
    entries = deviation * jax.random.normal(stream_key, extent, jnp.float32)
    if cuts:
        entries = entries * levels(stream_key, extent, cuts, -0.22, 0.18)
    return jnp.clip(entries, -most, most).astype(held_as)


def setup_inputs(seed: int = 0, part: int = 0) -> dict:
    seeds = jax.random.split(jax.random.key(seed), 8)
    part_splits = jax.random.split(jax.random.fold_in(seeds[7], part), 8)
    return {
        "tokens": centred(part_splits[0], (TOKENS, D), 1.0, 6.0, ((0, 4), (1, 4))),
        "key_weight": centred(seeds[1], (N_CTX, N_HEAD, DC, KVH // N_HEAD, N_HEAD, HD), D ** -0.5, 0.046875, ((0, 2), (1, 2), (2, 4))),
        "value_weight": centred(seeds[2], (N_CTX, N_HEAD, DC, KVH // N_HEAD, N_HEAD, HD), (D // 4) ** -0.5, 0.09375, ((0, 2), (1, 2), (2, 4))),
        "queries": draw_queries(jax.random.fold_in(jax.random.fold_in(seeds[7], part), 71), part),
        "prefix_pool": draw_prefix_pool(jax.random.fold_in(jax.random.fold_in(seeds[7], part), 71), part),
        "block_table": draw_block_table(jax.random.fold_in(jax.random.fold_in(seeds[7], part), 71), part),
        "lengths": draw_lengths(jax.random.fold_in(jax.random.fold_in(seeds[7], part), 71), part),
    }


def attend_head(query_rows, prefix, fresh_rows, length):
    token_count = query_rows.shape[0]
    head_width = prefix.shape[1] // 2
    group_size = query_rows.shape[1] // head_width
    prefix_len = prefix.shape[0]
    key_rows = jnp.concatenate([prefix[:, :head_width], fresh_rows[:, :head_width]], 0)
    value_rows = jnp.concatenate([prefix[:, head_width:], fresh_rows[:, head_width:]], 0)
    block_len = min(token_count, 64)
    pieces = []
    for first_row in range(0, token_count, block_len):
        block_rows = query_rows[first_row:first_row + block_len].reshape(block_len * group_size, head_width)
        scores = jnp.dot(block_rows, key_rows.T, preferred_element_type=jnp.float32) * (head_width ** -0.5)
        position = first_row + jnp.arange(block_len * group_size) // group_size
        column = jnp.arange(prefix_len + token_count) - prefix_len
        allowed = column[None, :] <= position[:, None]
        scores = jnp.where(allowed, scores, -jnp.inf)
        row_max = jnp.max(scores, axis=1, keepdims=True)
        weights = jnp.exp(scores - row_max)
        row_total = jnp.sum(weights, axis=1, keepdims=True)
        probs_bf = (weights / row_total).astype(jnp.bfloat16)
        mixed_rows = jnp.dot(probs_bf, value_rows, preferred_element_type=jnp.float32)
        is_live = position < length
        mixed_rows = jnp.where(is_live[:, None], mixed_rows, 0.0)
        pieces.append(mixed_rows.astype(jnp.bfloat16).reshape(block_len, group_size * head_width))
    return jnp.concatenate(pieces, 0)


def reference(tokens, key_weight, value_weight, queries, prefix_pool, block_table, lengths):
    flat_keys = key_weight.reshape(D, KVH * HD)
    flat_values = value_weight.reshape(D, KVH * HD)
    new_keys = jnp.dot(tokens, flat_keys, preferred_element_type=jnp.float32).astype(jnp.bfloat16)
    new_values = jnp.dot(tokens, flat_values, preferred_element_type=jnp.float32).astype(jnp.bfloat16)
    fresh_all = jnp.concatenate([new_keys.reshape(PROMPTS, NEW, KVH, HD), new_values.reshape(PROMPTS, NEW, KVH, HD)], 3)
    pool_rows = prefix_pool.reshape(POOL, BLK, KVH, 2 * HD)
    query_all = queries.reshape(PROMPTS, NEW, KVH, GRP * HD)

    def one_prompt(packed):
        query_rows, fresh_rows, table_row, length = packed
        prefix = jnp.take(pool_rows, table_row.astype(jnp.int32), axis=0).reshape(PB * BLK, KVH, 2 * HD)
        outputs = [attend_head(query_rows[:, head_idx], prefix[:, head_idx], fresh_rows[:, head_idx], length) for head_idx in range(KVH)]
        return jnp.stack(outputs, 1)

    result = lax.map(one_prompt, (query_all, fresh_all, block_table, lengths))
    return result.reshape(TOKENS, KVH // N_HEAD, N_HEAD, GRP * HD)
```

```python
import functools
import math

import jax
import jax.numpy as jnp
from jax import lax
from jax.experimental import pallas as pl
from jax.experimental.pallas import tpu as pltpu
from jax.sharding import PartitionSpec as P

CHUNKS = 2
VMEM_BYTES = 48 * 1024 * 1024


def attend_head(query_rows, prefix, fresh_rows, length):
    token_count = query_rows.shape[0]
    head_width = prefix.shape[1] // 2
    group_size = query_rows.shape[1] // head_width
    prefix_len = prefix.shape[0]
    key_rows = jnp.concatenate([prefix[:, :head_width], fresh_rows[:, :head_width]], 0)
    value_rows = jnp.concatenate([prefix[:, head_width:], fresh_rows[:, head_width:]], 0)
    block_len = min(token_count, 64)
    pieces = []
    for first_row in range(0, token_count, block_len):
        block_rows = query_rows[first_row : first_row + block_len].reshape(
            block_len * group_size, head_width
        )
        scores = jnp.dot(
            block_rows, key_rows.T, preferred_element_type=jnp.float32
        ) * head_width ** (-0.5)
        position = first_row + jnp.arange(block_len * group_size) // group_size
        column = jnp.arange(prefix_len + token_count) - prefix_len
        allowed = column[None, :] <= position[:, None]
        scores = jnp.where(allowed, scores, -jnp.inf)
        row_max = jnp.max(scores, axis=1, keepdims=True)
        weights = jnp.exp(scores - row_max)
        row_total = jnp.sum(weights, axis=1, keepdims=True)
        probs_bf = (weights / row_total).astype(jnp.bfloat16)
        mixed_rows = jnp.dot(probs_bf, value_rows, preferred_element_type=jnp.float32)
        is_live = position < length
        mixed_rows = jnp.where(is_live[:, None], mixed_rows, 0.0)
        pieces.append(mixed_rows.astype(jnp.bfloat16).reshape(block_len, group_size * head_width))
    return jnp.concatenate(pieces, 0)


def gathered_shards(tokens, key_weight, value_weight, queries, prefix_pool, block_table, lengths):
    token_count = tokens.shape[0]
    local_heads = queries.shape[1]
    head_width = prefix_pool.shape[4] // 2
    ctx_count = lax.axis_size("ctx")
    head_count = lax.axis_size("head")
    features = lax.all_gather(tokens, ("ctx", "head"), axis=1, tiled=True)
    key_cols, value_cols = (
        lax.all_to_all(
            lax.all_to_all(weight, "ctx", split_axis=3, concat_axis=0, tiled=True),
            "head",
            split_axis=4,
            concat_axis=1,
            tiled=True,
        )
        for weight in (key_weight, value_weight)
    )
    span_len = features.shape[1] // (ctx_count * head_count)
    feature_view = features.reshape(token_count, ctx_count, head_count, span_len)
    pieces = (
        lax.all_gather(key_cols, "batch", axis=2, tiled=True),
        lax.all_gather(value_cols, "batch", axis=2, tiled=True),
    )
    row_count = pieces[0].shape[2]

    def one_term(weight_piece):
        shaped = weight_piece.reshape(ctx_count, head_count, row_count, local_heads * head_width)
        return jnp.einsum("tchr,chrk->tk", feature_view, shaped, preferred_element_type=jnp.float32)

    new_keys = one_term(pieces[0]).astype(jnp.bfloat16).reshape(token_count, local_heads, head_width)
    new_values = one_term(pieces[1]).astype(jnp.bfloat16).reshape(token_count, local_heads, head_width)
    fresh_all = jnp.concatenate([new_keys, new_values], 2)
    pool_heads = lax.all_to_all(prefix_pool, "ctx", split_axis=2, concat_axis=0, tiled=True)
    chosen = jnp.take(pool_heads, block_table[0], axis=0)
    chosen = chosen.reshape(-1, local_heads, 2 * head_width)
    outputs = [
        attend_head(
            queries[:, head_idx, 0], chosen[:, head_idx], fresh_all[:, head_idx], lengths[0]
        )
        for head_idx in range(local_heads)
    ]
    return jnp.stack(outputs, 1)[:, :, None, :]


def shift(array, axis, step):
    count = lax.axis_size(axis)
    return lax.ppermute(array, axis, [(i, (i + step) % count) for i in range(count)])


def project_kernel(place_ref, *refs):
    weight_ref, out_ref = refs[-2], refs[-1]
    rows = refs[0].shape[0]
    for index, token_ref in enumerate(refs[:-2]):
        out_ref[pl.ds(index * rows, rows), :] = jnp.dot(
            token_ref[...], weight_ref[0, 0], preferred_element_type=jnp.float32
        ).astype(out_ref.dtype)


def project(place, tokens, received, weights, chunk, head_step, out_dtype):
    head_count, ctx_count, depth, width = weights.shape
    rows = tokens.shape[0] // CHUNKS
    row_total = rows * (1 + len(received))

    return pl.pallas_call(
        project_kernel,
        grid_spec=pltpu.PrefetchScalarGridSpec(
            num_scalar_prefetch=1,
            grid=(ctx_count,),
            in_specs=[pl.BlockSpec((rows, depth), lambda j, place: (chunk, place[0]))]
            + [pl.BlockSpec((rows, depth), lambda j, place: (0, 0)) for _ in received]
            + [
                pl.BlockSpec(
                    (1, 1, depth, width),
                    lambda j, place: (
                        lax.rem(place[2] + head_step, head_count),
                        lax.rem(place[1] + j, ctx_count),
                        0,
                        0,
                    ),
                )
            ],
            out_specs=pl.BlockSpec((row_total, width), lambda j, place: (0, j)),
        ),
        out_shape=jax.ShapeDtypeStruct((row_total, ctx_count * width), out_dtype),
        compiler_params=pltpu.CompilerParams(vmem_limit_bytes=VMEM_BYTES),
        cost_estimate=pl.CostEstimate(
            flops=2 * row_total * depth * ctx_count * width,
            bytes_accessed=2 * depth * (ctx_count * width + row_total),
            transcendentals=0,
        ),
        name="project",
    )(place, tokens, *received, weights)


def split_heads(block, heads):
    if heads == 1:
        return block
    head_of = lax.broadcasted_iota(jnp.int32, block.shape, 0) % heads
    zero = jnp.zeros_like(block)
    return jnp.concatenate([jnp.where(head_of == i, block, zero) for i in range(heads)], 1)


def own_head(block, heads):
    width = block.shape[1] // heads
    result = block[:, :width]
    head_of = lax.broadcasted_iota(jnp.int32, result.shape, 0) % heads
    for i in range(1, heads):
        result = jnp.where(head_of == i, block[:, i * width : (i + 1) * width], result)
    return result


def dot_keys(query_block, keys):
    return lax.dot_general(
        query_block, keys, (((1,), (1,)), ((), ())), preferred_element_type=jnp.float32
    )


def prefix_kernel(scale, heads, query_ref, key_ref, value_ref, acc_ref, stat_ref):
    scores = dot_keys(split_heads(query_ref[...], heads), key_ref[...]) * scale
    row_max = jnp.max(scores, axis=1, keepdims=True)
    weights = jnp.exp2(scores - row_max)
    row_total = jnp.sum(weights, axis=1, keepdims=True)
    mixed = jnp.dot(
        weights.astype(jnp.bfloat16), value_ref[...], preferred_element_type=jnp.float32
    )
    acc_ref[...] = own_head(mixed, heads)
    lane = lax.broadcasted_iota(jnp.int32, stat_ref.shape, 1)
    stat_ref[...] = jnp.where(lane < stat_ref.shape[1] // 2, row_max, row_total)


def fresh_kernel(
    scale, heads, per_token, first_row, length_ref, query_ref, acc_ref, stat_ref, fresh_ref, *rest
):
    out_ref = rest[-1]
    rows, width = query_ref.shape
    wide = heads * width
    step = pl.program_id(0)
    keys, values = fresh_ref[:, :wide], fresh_ref[:, wide:]
    scores = dot_keys(split_heads(query_ref[...], heads), keys) * scale
    row_at = lax.broadcasted_iota(jnp.int32, scores.shape, 0)
    position = first_row + step * (rows // per_token) + row_at // per_token
    column = lax.broadcasted_iota(jnp.int32, scores.shape, 1)
    scores = jnp.where(column <= position, scores, -jnp.inf)
    old_max, old_total = stat_ref[:, :1], stat_ref[:, width // 2 : width // 2 + 1]
    row_max = jnp.maximum(jnp.max(scores, axis=1, keepdims=True), old_max)
    weights = jnp.exp2(scores - row_max)
    fade = jnp.exp2(old_max - row_max)
    row_total = old_total * fade + jnp.sum(weights, axis=1, keepdims=True)
    mixed = own_head(
        jnp.dot(weights.astype(jnp.bfloat16), values, preferred_element_type=jnp.float32), heads
    )
    result = (acc_ref[...] * fade + mixed) / row_total
    token = first_row + step * (rows // per_token)
    token = token + lax.broadcasted_iota(jnp.int32, result.shape, 0) // per_token
    out_ref[...] = jnp.where(token < length_ref[0], result, 0.0).astype(out_ref.dtype)


def prefix_attend(query_rows, keys, values, scale, heads):
    row_total, width = query_rows.shape
    rows = min(512, row_total)
    key_count = keys.shape[0]
    whole = pl.BlockSpec(keys.shape, lambda i: (0, 0))
    block = pl.BlockSpec((rows, width), lambda i: (i, 0))
    return pl.pallas_call(
        functools.partial(prefix_kernel, scale, heads),
        grid=(row_total // rows,),
        in_specs=[block, whole, whole],
        out_specs=[block, block],
        out_shape=[jax.ShapeDtypeStruct((row_total, width), jnp.float32)] * 2,
        compiler_params=pltpu.CompilerParams(vmem_limit_bytes=VMEM_BYTES),
        cost_estimate=pl.CostEstimate(
            flops=4 * row_total * key_count * keys.shape[1],
            bytes_accessed=row_total * width * 10,
            transcendentals=row_total * key_count,
        ),
        name="prefix_attend",
    )(query_rows, keys, values)


def fresh_attend(length, query_rows, acc, stat, fresh, earlier, chunk, scale, heads, per_token):
    row_total, width = query_rows.shape
    chunk_rows = row_total // CHUNKS
    rows = min(512, chunk_rows)
    steps = chunk_rows // rows
    block = pl.BlockSpec((rows, width), lambda i, length: (chunk * steps + i, 0))
    in_specs = [block, block, block, pl.BlockSpec(fresh.shape, lambda i, length: (0, 0))]
    operands = [length, query_rows, acc, stat, fresh]
    aliases = {}
    if earlier is not None:
        in_specs.append(pl.BlockSpec(memory_space=pl.ANY))
        operands.append(earlier)
        aliases = {5: 0}
    return pl.pallas_call(
        functools.partial(
            fresh_kernel, scale, heads, per_token, chunk * (chunk_rows // per_token)
        ),
        grid_spec=pltpu.PrefetchScalarGridSpec(
            num_scalar_prefetch=1, grid=(steps,), in_specs=in_specs, out_specs=block
        ),
        out_shape=jax.ShapeDtypeStruct((row_total, width), jnp.bfloat16),
        input_output_aliases=aliases,
        compiler_params=pltpu.CompilerParams(vmem_limit_bytes=VMEM_BYTES),
        cost_estimate=pl.CostEstimate(
            flops=2 * chunk_rows * fresh.shape[0] * fresh.shape[1],
            bytes_accessed=chunk_rows * width * 12,
            transcendentals=chunk_rows * fresh.shape[0],
        ),
        name="fresh_attend",
    )(*operands)


def reduced_shards(tokens, key_weight, value_weight, queries, prefix_pool, block_table, lengths):
    batch_count = lax.axis_size("batch")
    ctx_count = lax.axis_size("ctx")
    head_count = lax.axis_size("head")
    batch_at, ctx_at, head_at = (lax.axis_index(a) for a in ("batch", "ctx", "head"))
    place = jnp.stack([batch_at, ctx_at, head_at]).astype(jnp.int32)
    token_count = tokens.shape[0]
    heads = queries.shape[1]
    width = prefix_pool.shape[4] // 2
    group = queries.shape[3] // width
    per_token = heads * group
    depth = key_weight.shape[2]
    rows = token_count // CHUNKS
    scale = math.log2(math.e) / math.sqrt(width)

    received = []
    for chunk in range(CHUNKS):
        arrived = []
        for step in range(1, batch_count):
            target = lax.rem(batch_at + step, batch_count)
            piece = lax.dynamic_slice(tokens, (chunk * rows, target * depth), (rows, depth))
            arrived.append(shift(piece, "batch", step))
        received.append(arrived)

    pool = prefix_pool[:, :, :, 0, :]
    blocks, block_len = pool.shape[0], pool.shape[1]
    parts = []
    for step in range(ctx_count):
        target = lax.rem(ctx_at + step, ctx_count)
        part = lax.dynamic_slice_in_dim(pool, target * heads, heads, 2)
        parts.append(shift(part, "ctx", step) if step else part)
    pool_rows = jnp.stack(parts)
    table = block_table[0]
    source = lax.rem(ctx_at - table // blocks + ctx_count, ctx_count)
    pool_rows = pool_rows.reshape(ctx_count * blocks, block_len, heads, 2 * width)
    chosen = jnp.take(pool_rows, source * blocks + table % blocks, axis=0, mode="clip")
    chosen = chosen.reshape(-1, heads, 2, width)
    prefix_keys = chosen[:, :, 0].reshape(-1, heads * width)
    prefix_values = chosen[:, :, 1].reshape(-1, heads * width)

    def arranged(weight):
        view = weight.reshape(depth, ctx_count, heads, head_count, width)
        return view.transpose(3, 1, 0, 2, 4).reshape(head_count, ctx_count, depth, heads * width)

    weights = jnp.concatenate([arranged(key_weight), arranged(value_weight)], 3)

    query_rows = queries.reshape(token_count, heads, group, width)
    query_rows = query_rows.transpose(0, 2, 1, 3).reshape(-1, width)
    acc, stat = prefix_attend(query_rows, prefix_keys, prefix_values, scale, heads)

    fresh_parts = []
    result = None
    cols = weights.shape[3]
    for chunk in range(CHUNKS):
        sent = [
            project(place, tokens, received[chunk], weights, chunk, step, jnp.bfloat16)
            for step in range(1, head_count)
        ]
        sent = [shift(part, "head", step + 1) for step, part in enumerate(sent)]
        total = project(place, tokens, received[chunk], weights, chunk, 0, jnp.float32)
        for part in sent:
            total = total + part.astype(jnp.float32)
        mine = total[:, :cols]
        for step in range(1, ctx_count):
            part = total[:, step * cols : (step + 1) * cols].astype(jnp.bfloat16)
            mine = mine + shift(part, "ctx", step).astype(jnp.float32)
        fresh = mine[:rows]
        for step in range(1, batch_count):
            part = mine[step * rows : (step + 1) * rows].astype(jnp.bfloat16)
            fresh = fresh + shift(part, "batch", -step).astype(jnp.float32)
        fresh_parts.append(fresh.astype(jnp.bfloat16))
        result = fresh_attend(
            lengths,
            query_rows,
            acc,
            stat,
            jnp.concatenate(fresh_parts, 0),
            result,
            chunk,
            scale,
            heads,
            per_token,
        )
    result = result.reshape(token_count, group, heads, width).transpose(0, 2, 1, 3)
    return result.reshape(token_count, heads, 1, group * width)


def solution(mesh):
    def shards(tokens, key_weight, value_weight, *rest):
        prompts = mesh.shape["batch"]
        columns = 2 * math.prod(key_weight.shape[3:])
        few_tokens = prompts * tokens.shape[0] <= columns
        form = reduced_shards if few_tokens else gathered_shards
        return form(tokens, key_weight, value_weight, *rest)

    return jax.shard_map(
        shards,
        mesh=mesh,
        in_specs=(
            P(("groups", "batch"), ("ctx", "head")),
            P("ctx", "head", "batch", None, None, None),
            P("ctx", "head", "batch", None, None, None),
            P(("groups", "batch"), "ctx", "head", None),
            P(("groups", "ctx"), None, None, "head", None),
            P(("groups", "batch"), None),
            P(("groups", "batch")),
        ),
        out_specs=P(("groups", "batch"), "ctx", "head", None),
        check_vma=False,
    )
```

```python
import functools
import math

import jax
import jax.numpy as jnp
from jax import lax
from jax.experimental import pallas as pl
from jax.experimental.pallas import tpu as pltpu
from jax.sharding import PartitionSpec as P

CHUNKS = 2
VMEM_BYTES = 48 * 1024 * 1024


def attend_head(query_rows, prefix, fresh_rows, length):
    token_count = query_rows.shape[0]
    head_width = prefix.shape[1] // 2
    group_size = query_rows.shape[1] // head_width
    prefix_len = prefix.shape[0]
    key_rows = jnp.concatenate([prefix[:, :head_width], fresh_rows[:, :head_width]], 0)
    value_rows = jnp.concatenate([prefix[:, head_width:], fresh_rows[:, head_width:]], 0)
    block_len = min(token_count, 64)
    pieces = []
    for first_row in range(0, token_count, block_len):
        block_rows = query_rows[first_row : first_row + block_len].reshape(
            block_len * group_size, head_width
        )
        scores = jnp.dot(
            block_rows, key_rows.T, preferred_element_type=jnp.float32
        ) * head_width ** (-0.5)
        position = first_row + jnp.arange(block_len * group_size) // group_size
        column = jnp.arange(prefix_len + token_count) - prefix_len
        allowed = column[None, :] <= position[:, None]
        scores = jnp.where(allowed, scores, -jnp.inf)
        row_max = jnp.max(scores, axis=1, keepdims=True)
        weights = jnp.exp(scores - row_max)
        row_total = jnp.sum(weights, axis=1, keepdims=True)
        probs_bf = (weights / row_total).astype(jnp.bfloat16)
        mixed_rows = jnp.dot(probs_bf, value_rows, preferred_element_type=jnp.float32)
        is_live = position < length
        mixed_rows = jnp.where(is_live[:, None], mixed_rows, 0.0)
        pieces.append(mixed_rows.astype(jnp.bfloat16).reshape(block_len, group_size * head_width))
    return jnp.concatenate(pieces, 0)


def gathered_shards(tokens, key_weight, value_weight, queries, prefix_pool, block_table, lengths):
    token_count = tokens.shape[0]
    local_heads = queries.shape[1]
    head_width = prefix_pool.shape[4] // 2
    ctx_count = lax.axis_size("ctx")
    head_count = lax.axis_size("head")
    features = lax.all_gather(tokens, ("ctx", "head"), axis=1, tiled=True)
    key_cols, value_cols = (
        lax.all_to_all(
            lax.all_to_all(weight, "ctx", split_axis=3, concat_axis=0, tiled=True),
            "head",
            split_axis=4,
            concat_axis=1,
            tiled=True,
        )
        for weight in (key_weight, value_weight)
    )
    span_len = features.shape[1] // (ctx_count * head_count)
    feature_view = features.reshape(token_count, ctx_count, head_count, span_len)
    pieces = (
        lax.all_gather(key_cols, "batch", axis=2, tiled=True),
        lax.all_gather(value_cols, "batch", axis=2, tiled=True),
    )
    row_count = pieces[0].shape[2]

    def one_term(weight_piece):
        shaped = weight_piece.reshape(ctx_count, head_count, row_count, local_heads * head_width)
        return jnp.einsum("tchr,chrk->tk", feature_view, shaped, preferred_element_type=jnp.float32)

    new_keys = one_term(pieces[0]).astype(jnp.bfloat16).reshape(token_count, local_heads, head_width)
    new_values = one_term(pieces[1]).astype(jnp.bfloat16).reshape(token_count, local_heads, head_width)
    fresh_all = jnp.concatenate([new_keys, new_values], 2)
    pool_heads = lax.all_to_all(prefix_pool, "ctx", split_axis=2, concat_axis=0, tiled=True)
    chosen = jnp.take(pool_heads, block_table[0], axis=0)
    chosen = chosen.reshape(-1, local_heads, 2 * head_width)
    outputs = [
        attend_head(
            queries[:, head_idx, 0], chosen[:, head_idx], fresh_all[:, head_idx], lengths[0]
        )
        for head_idx in range(local_heads)
    ]
    return jnp.stack(outputs, 1)[:, :, None, :]


def shift(array, axis, step):
    count = lax.axis_size(axis)
    return lax.ppermute(array, axis, [(i, (i + step) % count) for i in range(count)])


def unit_index(shape, unit):
    row = lax.broadcasted_iota(jnp.int32, shape, 0)
    if unit & (unit - 1):
        return row // unit, row % unit
    return row >> (unit.bit_length() - 1), row & (unit - 1)


def head_mask(shape, heads):
    column = lax.broadcasted_iota(jnp.int32, shape, 1)
    low = unit_index(shape, heads)[1] * (shape[1] // heads)
    inside = (column >= low) & (column < low + shape[1] // heads)
    return jnp.where(inside, 1.0, 0.0).astype(jnp.bfloat16)


def own_head(block, heads):
    width = block.shape[1] // heads
    result = block[:, :width]
    head_of = unit_index(result.shape, heads)[1]
    for i in range(1, heads):
        result = jnp.where(head_of == i, block[:, i * width : (i + 1) * width], result)
    return result


def dot_keys(query_block, keys):
    return lax.dot_general(
        query_block, keys, (((1,), (1,)), ((), ())), preferred_element_type=jnp.float32
    )


def params():
    return pltpu.CompilerParams(vmem_limit_bytes=VMEM_BYTES)


def weight_kernel(ctx_count, heads, head_count, key_ref, value_ref, out_ref, flat):
    depth, slots, width = key_ref.shape
    for kind, ref in enumerate((key_ref, value_ref)):
        flat[...] = ref[...].astype(jnp.float32).reshape(depth * slots, width)
        for ctx in range(ctx_count):
            for head in range(heads):
                for core in range(head_count):
                    slot = (ctx * heads + head) * head_count + core
                    at = (kind * heads + head) * width
                    out_ref[core, ctx, :, at : at + width] = flat[
                        pl.ds(slot, depth, stride=slots), :
                    ].astype(out_ref.dtype)


def arrange_weights(key_weight, value_weight, ctx_count, heads, head_count):
    depth, width = key_weight.shape[2], key_weight.shape[5]
    slots = ctx_count * heads * head_count
    rows = min(128, depth)
    views = [w.reshape(depth, slots, width) for w in (key_weight, value_weight)]
    block = pl.BlockSpec((rows, slots, width), lambda i: (i, 0, 0))
    columns = 2 * heads * width
    return pl.pallas_call(
        functools.partial(weight_kernel, ctx_count, heads, head_count),
        grid=(depth // rows,),
        in_specs=[block, block],
        out_specs=pl.BlockSpec((head_count, ctx_count, rows, columns), lambda i: (0, 0, i, 0)),
        out_shape=jax.ShapeDtypeStruct((head_count, ctx_count, depth, columns), jnp.bfloat16),
        scratch_shapes=[pltpu.VMEM((rows * slots, width), jnp.float32)],
        compiler_params=params(),
        cost_estimate=pl.CostEstimate(
            flops=0, bytes_accessed=8 * depth * slots * width, transcendentals=0
        ),
        name="arrange_weights",
    )(*views)


def pool_kernel(ctx_count, heads, place_ref, pool_ref, *refs):
    flat, outs = refs[-1], refs[:-1]
    length, slots, width = pool_ref.shape[1:]
    flat[...] = pool_ref[0].astype(jnp.float32).reshape(length * slots, width)
    for kind in range(2):
        for head in range(heads):
            at = (kind * heads + head) * width
            held = []
            for ctx in range(ctx_count):
                slot = (kind * ctx_count + ctx) * heads + head
                held.append(flat[pl.ds(slot, length, stride=slots), :])
            for step, out_ref in enumerate(outs):
                target = lax.rem(place_ref[1] + step, ctx_count)
                value = held[0]
                for ctx in range(1, ctx_count):
                    value = jnp.where(target == ctx, held[ctx], value)
                out_ref[0, :, at : at + width] = value.astype(out_ref.dtype)


def arrange_pool(place, prefix_pool, ctx_count, heads):
    blocks, length, all_heads, _, double = prefix_pool.shape
    width = double // 2
    slots = 2 * all_heads
    view = prefix_pool.reshape(blocks, length, all_heads, 2, width)
    view = view.transpose(0, 1, 3, 2, 4).reshape(blocks, length, slots, width)
    columns = 2 * heads * width
    out = pl.BlockSpec((1, length, columns), lambda i, place: (i, 0, 0))
    return pl.pallas_call(
        functools.partial(pool_kernel, ctx_count, heads),
        grid_spec=pltpu.PrefetchScalarGridSpec(
            num_scalar_prefetch=1,
            grid=(blocks,),
            in_specs=[pl.BlockSpec((1, length, slots, width), lambda i, place: (i, 0, 0, 0))],
            out_specs=[out] * ctx_count,
            scratch_shapes=[pltpu.VMEM((length * slots, width), jnp.float32)],
        ),
        out_shape=[jax.ShapeDtypeStruct((blocks, length, columns), jnp.bfloat16)] * ctx_count,
        compiler_params=params(),
        cost_estimate=pl.CostEstimate(
            flops=0, bytes_accessed=4 * blocks * length * slots * width, transcendentals=0
        ),
        name="arrange_pool",
    )(place, view)


def project_kernel(parts, has_term, place_ref, *refs):
    token_refs, weight_ref = refs[:parts], refs[parts]
    out_ref, stacked = refs[-2], refs[-1]
    rows = token_refs[0].shape[0]

    @pl.when(pl.program_id(0) == 0)
    def _():
        for index, token_ref in enumerate(token_refs):
            stacked[index * rows : (index + 1) * rows, :] = token_ref[...]

    total = jnp.dot(stacked[...], weight_ref[0, 0], preferred_element_type=jnp.float32)
    if has_term:
        total = total + refs[parts + 1][...].astype(jnp.float32)
    out_ref[...] = total.astype(out_ref.dtype)


def project(place, tokens, received, weights, chunk, head_step, ctx_steps, term, out_dtype):
    head_count, ctx_count, depth, width = weights.shape
    rows = tokens.shape[0] // CHUNKS
    row_total = rows * (1 + len(received))
    tile = min(256, width)
    tiles = width // tile
    first, last = ctx_steps
    in_specs = [pl.BlockSpec((rows, depth), lambda j, place: (chunk, place[0]))]
    in_specs += [pl.BlockSpec((rows, depth), lambda j, place: (0, 0)) for _ in received]
    in_specs += [
        pl.BlockSpec(
            (1, 1, depth, tile),
            lambda j, place: (
                lax.rem(place[2] + head_step, head_count),
                lax.rem(place[1] + first + j // tiles, ctx_count),
                0,
                j % tiles,
            ),
        )
    ]
    operands = [place, tokens, *received, weights]
    if term is not None:
        in_specs.append(
            pl.BlockSpec((row_total, tile), lambda j, place: (0, first * tiles + j))
        )
        operands.append(term)
    columns = (last - first) * width
    return pl.pallas_call(
        functools.partial(project_kernel, 1 + len(received), term is not None),
        grid_spec=pltpu.PrefetchScalarGridSpec(
            num_scalar_prefetch=1,
            grid=(columns // tile,),
            in_specs=in_specs,
            out_specs=pl.BlockSpec((row_total, tile), lambda j, place: (0, j)),
            scratch_shapes=[pltpu.VMEM((row_total, depth), tokens.dtype)],
        ),
        out_shape=jax.ShapeDtypeStruct((row_total, columns), out_dtype),
        compiler_params=params(),
        cost_estimate=pl.CostEstimate(
            flops=2 * row_total * depth * columns,
            bytes_accessed=2 * (depth * (columns + row_total) + 2 * row_total * columns),
            transcendentals=0,
        ),
        name="project",
    )(*operands)


def prefix_kernel(scale, heads, ctx_count, place_ref, table_ref, query_ref, *refs):
    pool_refs = refs[:ctx_count]
    acc_ref, stat_ref, keys, values, mask = refs[ctx_count:]
    blocks, length, columns = pool_refs[0].shape
    rows, width = query_ref.shape
    half = rows // 2

    @pl.when(pl.program_id(0) == 0)
    def _():
        mask[...] = head_mask(mask.shape, heads)
        for at in range(table_ref.shape[0]):
            entry = table_ref[at]
            step = lax.rem(place_ref[1] - entry // blocks + ctx_count, ctx_count)
            for ctx_step, pool_ref in enumerate(pool_refs):

                @pl.when(step == ctx_step)
                def _():
                    block = pool_ref[entry % blocks]
                    keys[at * length : (at + 1) * length, :] = block[:, : columns // 2]
                    values[at * length : (at + 1) * length, :] = block[:, columns // 2 :]

    lane = lax.broadcasted_iota(jnp.int32, (half, width), 1)
    for part in range(2):
        here = slice(part * half, (part + 1) * half)
        query_block = jnp.concatenate([query_ref[here, :]] * heads, 1) * mask[...]
        scores = dot_keys(query_block, keys[...]) * scale
        row_max = jnp.max(scores, axis=1, keepdims=True)
        weights = jnp.exp2(scores - row_max)
        row_total = jnp.sum(weights, axis=1, keepdims=True)
        mixed = jnp.dot(
            weights.astype(jnp.bfloat16), values[...], preferred_element_type=jnp.float32
        )
        acc_ref[here, :] = own_head(mixed, heads)
        stat_ref[here, :] = jnp.where(lane < width // 2, row_max, row_total)


def prefix_attend(place, table, query_rows, pools, scale, heads):
    row_total, width = query_rows.shape
    rows = min(1024, row_total)
    length, columns = pools[0].shape[1:]
    key_count = table.shape[0] * length
    block = pl.BlockSpec((rows, width), lambda i, *_: (i, 0))
    return pl.pallas_call(
        functools.partial(prefix_kernel, scale, heads, len(pools)),
        grid_spec=pltpu.PrefetchScalarGridSpec(
            num_scalar_prefetch=2,
            grid=(row_total // rows,),
            in_specs=[block] + [pl.BlockSpec(p.shape, lambda i, *_: (0, 0, 0)) for p in pools],
            out_specs=[block, block],
            scratch_shapes=[
                pltpu.VMEM((key_count, columns // 2), jnp.bfloat16),
                pltpu.VMEM((key_count, columns // 2), jnp.bfloat16),
                pltpu.VMEM((rows // 2, columns // 2), jnp.bfloat16),
            ],
        ),
        out_shape=[jax.ShapeDtypeStruct((row_total, width), jnp.float32)] * 2,
        compiler_params=params(),
        cost_estimate=pl.CostEstimate(
            flops=2 * row_total * key_count * columns,
            bytes_accessed=row_total * width * 10,
            transcendentals=row_total * key_count,
        ),
        name="prefix_attend",
    )(place, table, query_rows, *pools)


def fresh_kernel(
    scale, heads, per_token, first_row, length_ref, query_ref, acc_ref, stat_ref, fresh_ref, *rest
):
    out_ref, mask = rest[-2:]
    rows, width = query_ref.shape
    wide = heads * width
    step = pl.program_id(0)

    @pl.when(step == 0)
    def _():
        mask[...] = head_mask(mask.shape, heads)

    keys, values = fresh_ref[:, :wide], fresh_ref[:, wide:]
    query_block = jnp.concatenate([query_ref[...]] * heads, 1) * mask[...]
    scores = dot_keys(query_block, keys) * scale
    token = first_row + step * (rows // per_token)
    position = token + unit_index(scores.shape, per_token)[0]
    column = lax.broadcasted_iota(jnp.int32, scores.shape, 1)
    scores = jnp.where(column <= position, scores, -jnp.inf)
    old_max, old_total = stat_ref[:, :1], stat_ref[:, width // 2 : width // 2 + 1]
    row_max = jnp.maximum(jnp.max(scores, axis=1, keepdims=True), old_max)
    weights = jnp.exp2(scores - row_max)
    fade = jnp.exp2(old_max - row_max)
    row_total = old_total * fade + jnp.sum(weights, axis=1, keepdims=True)
    mixed = own_head(
        jnp.dot(weights.astype(jnp.bfloat16), values, preferred_element_type=jnp.float32), heads
    )
    live = token + unit_index((rows, 1), per_token)[0] < length_ref[0]
    share = jnp.where(live, 1.0 / row_total, 0.0)
    out_ref[...] = ((acc_ref[...] * fade + mixed) * share).astype(out_ref.dtype)


def fresh_attend(length, query_rows, acc, stat, fresh, earlier, chunk, scale, heads, per_token):
    row_total, width = query_rows.shape
    chunk_rows = row_total // CHUNKS
    rows = min(512, chunk_rows)
    steps = chunk_rows // rows
    block = pl.BlockSpec((rows, width), lambda i, length: (chunk * steps + i, 0))
    in_specs = [block, block, block, pl.BlockSpec(fresh.shape, lambda i, length: (0, 0))]
    operands = [length, query_rows, acc, stat, fresh]
    aliases = {}
    if earlier is not None:
        in_specs.append(pl.BlockSpec(memory_space=pl.ANY))
        operands.append(earlier)
        aliases = {5: 0}
    return pl.pallas_call(
        functools.partial(
            fresh_kernel, scale, heads, per_token, chunk * (chunk_rows // per_token)
        ),
        grid_spec=pltpu.PrefetchScalarGridSpec(
            num_scalar_prefetch=1,
            grid=(steps,),
            in_specs=in_specs,
            out_specs=block,
            scratch_shapes=[pltpu.VMEM((rows, heads * width), jnp.bfloat16)],
        ),
        out_shape=jax.ShapeDtypeStruct((row_total, width), jnp.bfloat16),
        input_output_aliases=aliases,
        compiler_params=params(),
        cost_estimate=pl.CostEstimate(
            flops=2 * chunk_rows * fresh.shape[0] * fresh.shape[1],
            bytes_accessed=chunk_rows * width * 12,
            transcendentals=chunk_rows * fresh.shape[0],
        ),
        name="fresh_attend",
    )(*operands)


def reduced_shards(tokens, key_weight, value_weight, queries, prefix_pool, block_table, lengths):
    batch_count = lax.axis_size("batch")
    ctx_count = lax.axis_size("ctx")
    head_count = lax.axis_size("head")
    batch_at, ctx_at, head_at = (lax.axis_index(a) for a in ("batch", "ctx", "head"))
    place = jnp.stack([batch_at, ctx_at, head_at]).astype(jnp.int32)
    token_count = tokens.shape[0]
    heads = queries.shape[1]
    width = prefix_pool.shape[4] // 2
    group = queries.shape[3] // width
    per_token = heads * group
    depth = key_weight.shape[2]
    rows = token_count // CHUNKS
    scale = math.log2(math.e) / math.sqrt(width)

    received = []
    for chunk in range(CHUNKS):
        arrived = []
        for step in range(1, batch_count):
            target = lax.rem(batch_at + step, batch_count)
            piece = lax.dynamic_slice(tokens, (chunk * rows, target * depth), (rows, depth))
            arrived.append(shift(piece, "batch", step))
        received.append(arrived)

    pools = arrange_pool(place, prefix_pool, ctx_count, heads)
    pools, key_weight, value_weight = lax.optimization_barrier((pools, key_weight, value_weight))
    pools = [shift(part, "ctx", step) if step else part for step, part in enumerate(pools)]

    weights = arrange_weights(key_weight, value_weight, ctx_count, heads, head_count)

    query_rows = queries.reshape(token_count, heads, group, width)
    query_rows = query_rows.transpose(0, 2, 1, 3).reshape(-1, width)
    acc, stat = prefix_attend(place, block_table[0], query_rows, pools, scale, heads)

    fresh_parts = []
    result = None
    cols = weights.shape[3]
    for chunk in range(CHUNKS):
        call = functools.partial(project, place, tokens, received[chunk], weights, chunk)
        term = None
        for step in range(1, head_count):
            part = shift(call(step, (0, ctx_count), None, jnp.bfloat16), "head", step)
            term = part if term is None else term.astype(jnp.float32) + part.astype(jnp.float32)
        sent = call(0, (1, ctx_count), term, jnp.bfloat16)
        mine = call(0, (0, 1), term, jnp.float32)
        for step in range(1, ctx_count):
            part = sent[:, (step - 1) * cols : step * cols]
            mine = mine + shift(part, "ctx", step).astype(jnp.float32)
        fresh = mine[:rows]
        for step in range(1, batch_count):
            part = mine[step * rows : (step + 1) * rows].astype(jnp.bfloat16)
            fresh = fresh + shift(part, "batch", -step).astype(jnp.float32)
        fresh_parts.append(fresh.astype(jnp.bfloat16))
        result = fresh_attend(
            lengths,
            query_rows,
            acc,
            stat,
            jnp.concatenate(fresh_parts, 0),
            result,
            chunk,
            scale,
            heads,
            per_token,
        )
    result = result.reshape(token_count, group, heads, width).transpose(0, 2, 1, 3)
    return result.reshape(token_count, heads, 1, group * width)


def solution(mesh):
    def shards(tokens, key_weight, value_weight, *rest):
        prompts = mesh.shape["batch"]
        columns = 2 * math.prod(key_weight.shape[3:])
        few_tokens = prompts * tokens.shape[0] <= columns
        form = reduced_shards if few_tokens else gathered_shards
        return form(tokens, key_weight, value_weight, *rest)

    return jax.shard_map(
        shards,
        mesh=mesh,
        in_specs=(
            P(("groups", "batch"), ("ctx", "head")),
            P("ctx", "head", "batch", None, None, None),
            P("ctx", "head", "batch", None, None, None),
            P(("groups", "batch"), "ctx", "head", None),
            P(("groups", "ctx"), None, None, "head", None),
            P(("groups", "batch"), None),
            P(("groups", "batch")),
        ),
        out_specs=P(("groups", "batch"), "ctx", "head", None),
        check_vma=False,
    )
```

```python
import functools
import math

import jax
import jax.numpy as jnp
from jax import lax
from jax.experimental import pallas as pl
from jax.experimental.pallas import tpu as pltpu
from jax.sharding import PartitionSpec as P

CHUNKS = 2
VMEM_BYTES = 48 * 1024 * 1024


def attend_head(query_rows, prefix, fresh_rows, length):
    token_count = query_rows.shape[0]
    head_width = prefix.shape[1] // 2
    group_size = query_rows.shape[1] // head_width
    prefix_len = prefix.shape[0]
    key_rows = jnp.concatenate([prefix[:, :head_width], fresh_rows[:, :head_width]], 0)
    value_rows = jnp.concatenate([prefix[:, head_width:], fresh_rows[:, head_width:]], 0)
    block_len = min(token_count, 64)
    pieces = []
    for first_row in range(0, token_count, block_len):
        block_rows = query_rows[first_row : first_row + block_len].reshape(
            block_len * group_size, head_width
        )
        scores = jnp.dot(
            block_rows, key_rows.T, preferred_element_type=jnp.float32
        ) * head_width ** (-0.5)
        position = first_row + jnp.arange(block_len * group_size) // group_size
        column = jnp.arange(prefix_len + token_count) - prefix_len
        allowed = column[None, :] <= position[:, None]
        scores = jnp.where(allowed, scores, -jnp.inf)
        row_max = jnp.max(scores, axis=1, keepdims=True)
        weights = jnp.exp(scores - row_max)
        row_total = jnp.sum(weights, axis=1, keepdims=True)
        probs_bf = (weights / row_total).astype(jnp.bfloat16)
        mixed_rows = jnp.dot(probs_bf, value_rows, preferred_element_type=jnp.float32)
        is_live = position < length
        mixed_rows = jnp.where(is_live[:, None], mixed_rows, 0.0)
        pieces.append(mixed_rows.astype(jnp.bfloat16).reshape(block_len, group_size * head_width))
    return jnp.concatenate(pieces, 0)


def gathered_shards(tokens, key_weight, value_weight, queries, prefix_pool, block_table, lengths):
    token_count = tokens.shape[0]
    local_heads = queries.shape[1]
    head_width = prefix_pool.shape[4] // 2
    ctx_count = lax.axis_size("ctx")
    head_count = lax.axis_size("head")
    features = lax.all_gather(tokens, ("ctx", "head"), axis=1, tiled=True)
    key_cols, value_cols = (
        lax.all_to_all(
            lax.all_to_all(weight, "ctx", split_axis=3, concat_axis=0, tiled=True),
            "head",
            split_axis=4,
            concat_axis=1,
            tiled=True,
        )
        for weight in (key_weight, value_weight)
    )
    span_len = features.shape[1] // (ctx_count * head_count)
    feature_view = features.reshape(token_count, ctx_count, head_count, span_len)
    pieces = (
        lax.all_gather(key_cols, "batch", axis=2, tiled=True),
        lax.all_gather(value_cols, "batch", axis=2, tiled=True),
    )
    row_count = pieces[0].shape[2]

    def one_term(weight_piece):
        shaped = weight_piece.reshape(ctx_count, head_count, row_count, local_heads * head_width)
        return jnp.einsum("tchr,chrk->tk", feature_view, shaped, preferred_element_type=jnp.float32)

    new_keys = one_term(pieces[0]).astype(jnp.bfloat16).reshape(token_count, local_heads, head_width)
    new_values = one_term(pieces[1]).astype(jnp.bfloat16).reshape(token_count, local_heads, head_width)
    fresh_all = jnp.concatenate([new_keys, new_values], 2)
    pool_heads = lax.all_to_all(prefix_pool, "ctx", split_axis=2, concat_axis=0, tiled=True)
    chosen = jnp.take(pool_heads, block_table[0], axis=0)
    chosen = chosen.reshape(-1, local_heads, 2 * head_width)
    outputs = [
        attend_head(
            queries[:, head_idx, 0], chosen[:, head_idx], fresh_all[:, head_idx], lengths[0]
        )
        for head_idx in range(local_heads)
    ]
    return jnp.stack(outputs, 1)[:, :, None, :]


def shift(array, axis, step):
    count = lax.axis_size(axis)
    return lax.ppermute(array, axis, [(i, (i + step) % count) for i in range(count)])


def trade(array, axis, bits):
    return lax.ppermute(array, axis, [(i, i ^ bits) for i in range(lax.axis_size(axis))])


def halving_order(count):
    order, bit = [0], count // 2
    while bit:
        order, bit = order + [i ^ bit for i in order], bit // 2
    return order


def unit_index(shape, unit):
    row = lax.broadcasted_iota(jnp.int32, shape, 0)
    if unit & (unit - 1):
        return row // unit, row % unit
    return row >> (unit.bit_length() - 1), row & (unit - 1)


def head_mask(shape, heads):
    column = lax.broadcasted_iota(jnp.int32, shape, 1)
    low = unit_index(shape, heads)[1] * (shape[1] // heads)
    inside = (column >= low) & (column < low + shape[1] // heads)
    return jnp.where(inside, 1.0, 0.0).astype(jnp.bfloat16)


def own_head(block, heads, width):
    result = block[:width]
    row = lax.broadcasted_iota(jnp.int32, result.shape, 1)
    head_of = row % heads if heads & (heads - 1) else row & (heads - 1)
    for i in range(1, heads):
        result = jnp.where(head_of == i, block[i * width : (i + 1) * width], result)
    return result


def softmax_parts(scores, old_max=None):
    row_max = jnp.max(scores, axis=0, keepdims=True)
    if old_max is not None:
        row_max = jnp.maximum(row_max, old_max)
    return row_max, jnp.exp2(scores - row_max).astype(jnp.bfloat16)


def dot_queries(keys, query_block):
    return lax.dot_general(
        keys, query_block, (((1,), (1,)), ((), ())), preferred_element_type=jnp.float32
    )


def params():
    return pltpu.CompilerParams(vmem_limit_bytes=VMEM_BYTES)


def weight_kernel(ctx_count, heads, head_count, key_ref, value_ref, out_ref, flat):
    depth, slots, width = key_ref.shape
    for kind, ref in enumerate((key_ref, value_ref)):
        flat[...] = ref[...].astype(jnp.float32).reshape(depth * slots, width)
        for ctx in range(ctx_count):
            for head in range(heads):
                for core in range(head_count):
                    slot = (ctx * heads + head) * head_count + core
                    at = (kind * heads + head) * width
                    out_ref[core, ctx, :, at : at + width] = flat[
                        pl.ds(slot, depth, stride=slots), :
                    ].astype(out_ref.dtype)


def arrange_weights(key_weight, value_weight, ctx_count, heads, head_count):
    depth, width = key_weight.shape[2], key_weight.shape[5]
    slots = ctx_count * heads * head_count
    rows = min(128, depth)
    views = [w.reshape(depth, slots, width) for w in (key_weight, value_weight)]
    block = pl.BlockSpec((rows, slots, width), lambda i: (i, 0, 0))
    columns = 2 * heads * width
    return pl.pallas_call(
        functools.partial(weight_kernel, ctx_count, heads, head_count),
        grid=(depth // rows,),
        in_specs=[block, block],
        out_specs=pl.BlockSpec((head_count, ctx_count, rows, columns), lambda i: (0, 0, i, 0)),
        out_shape=jax.ShapeDtypeStruct((head_count, ctx_count, depth, columns), jnp.bfloat16),
        scratch_shapes=[pltpu.VMEM((rows * slots, width), jnp.float32)],
        compiler_params=params(),
        cost_estimate=pl.CostEstimate(
            flops=0, bytes_accessed=8 * depth * slots * width, transcendentals=0
        ),
        name="arrange_weights",
    )(*views)


def pool_kernel(ctx_count, heads, place_ref, pool_ref, *refs):
    flat, outs = refs[-1], refs[:-1]
    length, slots, width = pool_ref.shape[1:]
    flat[...] = pool_ref[0].astype(jnp.float32).reshape(length * slots, width)
    for kind in range(2):
        for head in range(heads):
            at = (kind * heads + head) * width
            held = []
            for ctx in range(ctx_count):
                slot = (kind * ctx_count + ctx) * heads + head
                held.append(flat[pl.ds(slot, length, stride=slots), :])
            for step, out_ref in enumerate(outs):
                target = lax.rem(place_ref[1] + step, ctx_count)
                value = held[0]
                for ctx in range(1, ctx_count):
                    value = jnp.where(target == ctx, held[ctx], value)
                value = value.T if kind else value
                out_ref[0, :, at : at + width] = value.astype(out_ref.dtype)


def arrange_pool(place, prefix_pool, ctx_count, heads):
    blocks, length, all_heads, _, double = prefix_pool.shape
    width = double // 2
    slots = 2 * all_heads
    view = prefix_pool.reshape(blocks, length, all_heads, 2, width)
    view = view.transpose(0, 1, 3, 2, 4).reshape(blocks, length, slots, width)
    columns = 2 * heads * width
    out = pl.BlockSpec((1, length, columns), lambda i, place: (i, 0, 0))
    return pl.pallas_call(
        functools.partial(pool_kernel, ctx_count, heads),
        grid_spec=pltpu.PrefetchScalarGridSpec(
            num_scalar_prefetch=1,
            grid=(blocks,),
            in_specs=[pl.BlockSpec((1, length, slots, width), lambda i, place: (i, 0, 0, 0))],
            out_specs=[out] * ctx_count,
            scratch_shapes=[pltpu.VMEM((length * slots, width), jnp.float32)],
        ),
        out_shape=[jax.ShapeDtypeStruct((blocks, length, columns), jnp.bfloat16)] * ctx_count,
        compiler_params=params(),
        cost_estimate=pl.CostEstimate(
            flops=0, bytes_accessed=4 * blocks * length * slots * width, transcendentals=0
        ),
        name="arrange_pool",
    )(place, view)


def project_kernel(parts, has_term, place_ref, *refs):
    token_refs, weight_ref = refs[:parts], refs[parts]
    out_ref, stacked = refs[-2], refs[-1]
    rows = token_refs[0].shape[0]

    @pl.when(pl.program_id(0) == 0)
    def _():
        for index, token_ref in enumerate(token_refs):
            stacked[index * rows : (index + 1) * rows, :] = token_ref[...]

    total = jnp.dot(stacked[...], weight_ref[0, 0], preferred_element_type=jnp.float32)
    if has_term:
        total = total + refs[parts + 1][...].astype(jnp.float32)
    out_ref[...] = total.astype(out_ref.dtype)


def project(place, tokens, received, weights, chunk, head_step, ctx_steps, term, out_dtype):
    head_count, ctx_count, depth, width = weights.shape
    rows = tokens.shape[0] // CHUNKS
    row_total = rows * (1 + len(received))
    tile = min(256, width)
    tiles = width // tile
    first, last = ctx_steps
    in_specs = [pl.BlockSpec((rows, depth), lambda j, place: (chunk, place[0]))]
    in_specs += [pl.BlockSpec((rows, depth), lambda j, place: (0, 0)) for _ in received]
    in_specs += [
        pl.BlockSpec(
            (1, 1, depth, tile),
            lambda j, place: (
                lax.rem(place[2] + head_step, head_count),
                lax.rem(place[1] + first + j // tiles, ctx_count),
                0,
                j % tiles,
            ),
        )
    ]
    operands = [place, tokens, *received, weights]
    if term is not None:
        in_specs.append(
            pl.BlockSpec((row_total, tile), lambda j, place: (0, first * tiles + j))
        )
        operands.append(term)
    columns = (last - first) * width
    return pl.pallas_call(
        functools.partial(project_kernel, 1 + len(received), term is not None),
        grid_spec=pltpu.PrefetchScalarGridSpec(
            num_scalar_prefetch=1,
            grid=(columns // tile,),
            in_specs=in_specs,
            out_specs=pl.BlockSpec((row_total, tile), lambda j, place: (0, j)),
            scratch_shapes=[pltpu.VMEM((row_total, depth), tokens.dtype)],
        ),
        out_shape=jax.ShapeDtypeStruct((row_total, columns), out_dtype),
        compiler_params=params(),
        cost_estimate=pl.CostEstimate(
            flops=2 * row_total * depth * columns,
            bytes_accessed=2 * (depth * (columns + row_total) + 2 * row_total * columns),
            transcendentals=0,
        ),
        name="project",
    )(*operands)


def prefix_kernel(scale, heads, ctx_count, place_ref, table_ref, query_ref, *refs):
    pool_refs = refs[:ctx_count]
    acc_ref, stat_ref, keys, values, mask = refs[ctx_count:]
    blocks, length, columns = pool_refs[0].shape
    rows, width = query_ref.shape
    part_rows = mask.shape[0]
    wide = heads * width

    @pl.when(pl.program_id(0) == 0)
    def _():
        mask[...] = head_mask(mask.shape, heads)
        values[wide:, :] = jnp.ones_like(values[wide:, :])
        for at in range(table_ref.shape[0]):
            entry = table_ref[at]
            here = slice(at * length, (at + 1) * length)
            step = lax.rem(place_ref[1] - entry // blocks + ctx_count, ctx_count)
            for ctx_step, pool_ref in enumerate(pool_refs):

                @pl.when(step == ctx_step)
                def _():
                    block = pool_ref[entry % blocks]
                    keys[here, :] = block[:, :wide]
                    for head in range(heads):
                        low = wide + head * length
                        values[head * width : (head + 1) * width, here] = block[
                            :, low : low + length
                        ]

    for part in range(rows // part_rows):
        here = slice(part * part_rows, (part + 1) * part_rows)
        query_block = jnp.concatenate([query_ref[here, :]] * heads, 1) * mask[...]
        row_max, weights = softmax_parts(dot_queries(keys[...], query_block) * scale)
        mixed = jnp.dot(values[...], weights, preferred_element_type=jnp.float32)
        acc_ref[:, here] = own_head(mixed, heads, width)
        half = stat_ref.shape[0] // 2
        stat_ref[:half, here] = jnp.broadcast_to(row_max, (half, part_rows))
        stat_ref[half:, here] = jnp.broadcast_to(mixed[wide : wide + 1], (half, part_rows))


def prefix_attend(place, table, query_rows, pools, scale, heads):
    row_total, width = query_rows.shape
    rows = min(1024, row_total)
    length, columns = pools[0].shape[1:]
    key_count = table.shape[0] * length
    wide = columns // 2
    return pl.pallas_call(
        functools.partial(prefix_kernel, scale, heads, len(pools)),
        grid_spec=pltpu.PrefetchScalarGridSpec(
            num_scalar_prefetch=2,
            grid=(row_total // rows,),
            in_specs=[pl.BlockSpec((rows, width), lambda i, *_: (i, 0))]
            + [pl.BlockSpec(p.shape, lambda i, *_: (0, 0, 0)) for p in pools],
            out_specs=[
                pl.BlockSpec((width, rows), lambda i, *_: (0, i)),
                pl.BlockSpec((8, rows), lambda i, *_: (0, i)),
            ],
            scratch_shapes=[
                pltpu.VMEM((key_count, wide), jnp.bfloat16),
                pltpu.VMEM((wide + 16, key_count), jnp.bfloat16),
                pltpu.VMEM((min(256, rows), wide), jnp.bfloat16),
            ],
        ),
        out_shape=[
            jax.ShapeDtypeStruct((width, row_total), jnp.float32),
            jax.ShapeDtypeStruct((8, row_total), jnp.float32),
        ],
        compiler_params=params(),
        cost_estimate=pl.CostEstimate(
            flops=2 * row_total * key_count * columns,
            bytes_accessed=row_total * width * 6,
            transcendentals=row_total * key_count,
        ),
        name="prefix_attend",
    )(place, table, query_rows, *pools)


def fresh_kernel(
    scale, heads, per_token, first_row, length_ref, query_ref, acc_ref, stat_ref, fresh_ref, *rest
):
    out_ref, values, mask = rest[-3:]
    rows, width = query_ref.shape
    wide = heads * width
    step = pl.program_id(0)

    @pl.when(step == 0)
    def _():
        mask[...] = head_mask(mask.shape, heads)
        values[wide:, :] = jnp.ones_like(values[wide:, :])
        values[:wide, :] = fresh_ref[:, wide:].astype(jnp.float32).T.astype(jnp.bfloat16)

    query_block = jnp.concatenate([query_ref[...]] * heads, 1) * mask[...]
    scores = dot_queries(fresh_ref[:, :wide], query_block) * scale
    token = first_row + step * (rows // per_token)
    row = lax.broadcasted_iota(jnp.int32, (1, rows), 1)
    token = token + (
        row // per_token if per_token & (per_token - 1) else row >> (per_token.bit_length() - 1)
    )
    key_at = lax.broadcasted_iota(jnp.int32, scores.shape, 0)
    scores = jnp.where(key_at <= token, scores, -jnp.inf)
    half = stat_ref.shape[0] // 2
    old_max, old_total = stat_ref[:1, :], stat_ref[half : half + 1, :]
    row_max, weights = softmax_parts(scores, old_max)
    fade = jnp.exp2(old_max - row_max)
    mixed = jnp.dot(values[...], weights, preferred_element_type=jnp.float32)
    row_total = old_total * fade + mixed[wide : wide + 1]
    share = jnp.where(token < length_ref[0], 1.0 / row_total, 0.0)
    result = acc_ref[...] * (fade * share) + own_head(mixed, heads, width) * share
    out_ref[...] = result.T.astype(out_ref.dtype)


def fresh_attend(length, query_rows, acc, stat, fresh, earlier, chunk, scale, heads, per_token):
    row_total, width = query_rows.shape
    chunk_rows = row_total // CHUNKS
    rows = min(512, chunk_rows)
    steps = chunk_rows // rows
    block = pl.BlockSpec((rows, width), lambda i, length: (chunk * steps + i, 0))
    in_specs = [
        block,
        pl.BlockSpec((width, rows), lambda i, length: (0, chunk * steps + i)),
        pl.BlockSpec((stat.shape[0], rows), lambda i, length: (0, chunk * steps + i)),
        pl.BlockSpec(fresh.shape, lambda i, length: (0, 0)),
    ]
    operands = [length, query_rows, acc, stat, fresh]
    aliases = {}
    if earlier is not None:
        in_specs.append(pl.BlockSpec(memory_space=pl.ANY))
        operands.append(earlier)
        aliases = {5: 0}
    return pl.pallas_call(
        functools.partial(
            fresh_kernel, scale, heads, per_token, chunk * (chunk_rows // per_token)
        ),
        grid_spec=pltpu.PrefetchScalarGridSpec(
            num_scalar_prefetch=1,
            grid=(steps,),
            in_specs=in_specs,
            out_specs=block,
            scratch_shapes=[
                pltpu.VMEM((heads * width + 16, fresh.shape[0]), jnp.bfloat16),
                pltpu.VMEM((rows, heads * width), jnp.bfloat16),
            ],
        ),
        out_shape=jax.ShapeDtypeStruct((row_total, width), jnp.bfloat16),
        input_output_aliases=aliases,
        compiler_params=params(),
        cost_estimate=pl.CostEstimate(
            flops=2 * chunk_rows * fresh.shape[0] * fresh.shape[1],
            bytes_accessed=chunk_rows * width * 8,
            transcendentals=chunk_rows * fresh.shape[0],
        ),
        name="fresh_attend",
    )(*operands)


def reduced_shards(tokens, key_weight, value_weight, queries, prefix_pool, block_table, lengths):
    batch_count = lax.axis_size("batch")
    ctx_count = lax.axis_size("ctx")
    head_count = lax.axis_size("head")
    batch_at, ctx_at, head_at = (lax.axis_index(a) for a in ("batch", "ctx", "head"))
    place = jnp.stack([batch_at, ctx_at, head_at]).astype(jnp.int32)
    token_count = tokens.shape[0]
    heads = queries.shape[1]
    width = prefix_pool.shape[4] // 2
    group = queries.shape[3] // width
    per_token = heads * group
    depth = key_weight.shape[2]
    rows = token_count // CHUNKS
    scale = math.log2(math.e) / math.sqrt(width)

    order = halving_order(batch_count)
    received = []
    for chunk in range(CHUNKS):
        arrived = []
        for bits in order[1:]:
            start = (batch_at ^ bits) * depth
            piece = lax.dynamic_slice(tokens, (chunk * rows, start), (rows, depth))
            arrived.append(trade(piece, "batch", bits))
        received.append(arrived)

    pools = arrange_pool(place, prefix_pool, ctx_count, heads)
    pools, key_weight, value_weight = lax.optimization_barrier((pools, key_weight, value_weight))
    pools = [shift(part, "ctx", step) if step else part for step, part in enumerate(pools)]

    weights = arrange_weights(key_weight, value_weight, ctx_count, heads, head_count)

    query_rows = queries.reshape(token_count, heads, group, width)
    query_rows = query_rows.transpose(0, 2, 1, 3).reshape(-1, width)
    acc, stat = prefix_attend(place, block_table[0], query_rows, pools, scale, heads)

    fresh_parts = []
    result = None
    cols = weights.shape[3]
    for chunk in range(CHUNKS):
        call = functools.partial(project, place, tokens, received[chunk], weights, chunk)
        term = None
        for step in range(1, head_count):
            part = shift(call(step, (0, ctx_count), None, jnp.bfloat16), "head", step)
            term = part if term is None else term.astype(jnp.float32) + part.astype(jnp.float32)
        sent = call(0, (1, ctx_count), term, jnp.bfloat16)
        mine = call(0, (0, 1), term, jnp.float32)
        for step in range(1, ctx_count):
            part = sent[:, (step - 1) * cols : step * cols]
            mine = mine + shift(part, "ctx", step).astype(jnp.float32)
        bit = 1
        while bit < batch_count:
            half = mine.shape[0] // 2
            part = trade(mine[half:].astype(jnp.bfloat16), "batch", bit)
            mine = mine[:half] + part.astype(jnp.float32)
            bit *= 2
        fresh_parts.append(mine.astype(jnp.bfloat16))
        result = fresh_attend(
            lengths,
            query_rows,
            acc,
            stat,
            jnp.concatenate(fresh_parts, 0),
            result,
            chunk,
            scale,
            heads,
            per_token,
        )
    result = result.reshape(token_count, group, heads, width).transpose(0, 2, 1, 3)
    return result.reshape(token_count, heads, 1, group * width)


def solution(mesh):
    def shards(tokens, key_weight, value_weight, *rest):
        prompts = mesh.shape["batch"]
        columns = 2 * math.prod(key_weight.shape[3:])
        few_tokens = prompts * tokens.shape[0] <= columns and not prompts & (prompts - 1)
        form = reduced_shards if few_tokens else gathered_shards
        return form(tokens, key_weight, value_weight, *rest)

    return jax.shard_map(
        shards,
        mesh=mesh,
        in_specs=(
            P(("groups", "batch"), ("ctx", "head")),
            P("ctx", "head", "batch", None, None, None),
            P("ctx", "head", "batch", None, None, None),
            P(("groups", "batch"), "ctx", "head", None),
            P(("groups", "ctx"), None, None, "head", None),
            P(("groups", "batch"), None),
            P(("groups", "batch")),
        ),
        out_specs=P(("groups", "batch"), "ctx", "head", None),
        check_vma=False,
    )
```

```python
import functools
import math

import jax
import jax.numpy as jnp
from jax import lax
from jax.experimental import pallas as pl
from jax.experimental.pallas import tpu as pltpu
from jax.sharding import PartitionSpec as P

CHUNKS = 2
VMEM_BYTES = 48 * 1024 * 1024
LONG = pl.CostEstimate(flops=10**11, bytes_accessed=1, transcendentals=0)


def attend_head(query_rows, prefix, fresh_rows, length):
    token_count = query_rows.shape[0]
    head_width = prefix.shape[1] // 2
    group_size = query_rows.shape[1] // head_width
    prefix_len = prefix.shape[0]
    key_rows = jnp.concatenate([prefix[:, :head_width], fresh_rows[:, :head_width]], 0)
    value_rows = jnp.concatenate([prefix[:, head_width:], fresh_rows[:, head_width:]], 0)
    block_len = min(token_count, 64)
    pieces = []
    for first_row in range(0, token_count, block_len):
        block_rows = query_rows[first_row : first_row + block_len].reshape(
            block_len * group_size, head_width
        )
        scores = jnp.dot(
            block_rows, key_rows.T, preferred_element_type=jnp.float32
        ) * head_width ** (-0.5)
        position = first_row + jnp.arange(block_len * group_size) // group_size
        column = jnp.arange(prefix_len + token_count) - prefix_len
        allowed = column[None, :] <= position[:, None]
        scores = jnp.where(allowed, scores, -jnp.inf)
        row_max = jnp.max(scores, axis=1, keepdims=True)
        weights = jnp.exp(scores - row_max)
        row_total = jnp.sum(weights, axis=1, keepdims=True)
        probs_bf = (weights / row_total).astype(jnp.bfloat16)
        mixed_rows = jnp.dot(probs_bf, value_rows, preferred_element_type=jnp.float32)
        is_live = position < length
        mixed_rows = jnp.where(is_live[:, None], mixed_rows, 0.0)
        pieces.append(mixed_rows.astype(jnp.bfloat16).reshape(block_len, group_size * head_width))
    return jnp.concatenate(pieces, 0)


def gathered_shards(tokens, key_weight, value_weight, queries, prefix_pool, block_table, lengths):
    token_count = tokens.shape[0]
    local_heads = queries.shape[1]
    head_width = prefix_pool.shape[4] // 2
    ctx_count = lax.axis_size("ctx")
    head_count = lax.axis_size("head")
    features = lax.all_gather(tokens, ("ctx", "head"), axis=1, tiled=True)
    key_cols, value_cols = (
        lax.all_to_all(
            lax.all_to_all(weight, "ctx", split_axis=3, concat_axis=0, tiled=True),
            "head",
            split_axis=4,
            concat_axis=1,
            tiled=True,
        )
        for weight in (key_weight, value_weight)
    )
    span_len = features.shape[1] // (ctx_count * head_count)
    feature_view = features.reshape(token_count, ctx_count, head_count, span_len)
    pieces = (
        lax.all_gather(key_cols, "batch", axis=2, tiled=True),
        lax.all_gather(value_cols, "batch", axis=2, tiled=True),
    )
    row_count = pieces[0].shape[2]

    def one_term(weight_piece):
        shaped = weight_piece.reshape(ctx_count, head_count, row_count, local_heads * head_width)
        return jnp.einsum("tchr,chrk->tk", feature_view, shaped, preferred_element_type=jnp.float32)

    new_keys = one_term(pieces[0]).astype(jnp.bfloat16).reshape(token_count, local_heads, head_width)
    new_values = one_term(pieces[1]).astype(jnp.bfloat16).reshape(token_count, local_heads, head_width)
    fresh_all = jnp.concatenate([new_keys, new_values], 2)
    pool_heads = lax.all_to_all(prefix_pool, "ctx", split_axis=2, concat_axis=0, tiled=True)
    chosen = jnp.take(pool_heads, block_table[0], axis=0)
    chosen = chosen.reshape(-1, local_heads, 2 * head_width)
    outputs = [
        attend_head(
            queries[:, head_idx, 0], chosen[:, head_idx], fresh_all[:, head_idx], lengths[0]
        )
        for head_idx in range(local_heads)
    ]
    return jnp.stack(outputs, 1)[:, :, None, :]


def shift(array, axis, step):
    count = lax.axis_size(axis)
    return lax.ppermute(array, axis, [(i, (i + step) % count) for i in range(count)])


def trade(array, axis, bits):
    return lax.ppermute(array, axis, [(i, i ^ bits) for i in range(lax.axis_size(axis))])


def halving_order(count):
    order, bit = [0], count // 2
    while bit:
        order, bit = order + [i ^ bit for i in order], bit // 2
    return order


def unit_index(shape, unit):
    row = lax.broadcasted_iota(jnp.int32, shape, 0)
    if unit & (unit - 1):
        return row // unit, row % unit
    return row >> (unit.bit_length() - 1), row & (unit - 1)


def head_mask(shape, heads):
    column = lax.broadcasted_iota(jnp.int32, shape, 1)
    low = unit_index(shape, heads)[1] * (shape[1] // heads)
    inside = (column >= low) & (column < low + shape[1] // heads)
    return jnp.where(inside, 1.0, 0.0).astype(jnp.bfloat16)


def own_head(block, heads, width):
    result = block[:width]
    row = lax.broadcasted_iota(jnp.int32, result.shape, 1)
    head_of = row % heads if heads & (heads - 1) else row & (heads - 1)
    for i in range(1, heads):
        result = jnp.where(head_of == i, block[i * width : (i + 1) * width], result)
    return result


def softmax_parts(scores, old_max=None):
    row_max = jnp.max(scores, axis=0, keepdims=True)
    if old_max is not None:
        row_max = jnp.maximum(row_max, old_max)
    return row_max, jnp.exp2(scores - row_max).astype(jnp.bfloat16)


def dot_queries(keys, query_block):
    return lax.dot_general(
        keys, query_block, (((1,), (1,)), ((), ())), preferred_element_type=jnp.float32
    )


def params():
    return pltpu.CompilerParams(vmem_limit_bytes=VMEM_BYTES)


def weight_kernel(ctx_count, heads, head_count, key_ref, value_ref, out_ref, flat):
    depth, slots, width = key_ref.shape
    for kind, ref in enumerate((key_ref, value_ref)):
        flat[...] = ref[...].astype(jnp.float32).reshape(depth * slots, width)
        for ctx in range(ctx_count):
            for head in range(heads):
                for core in range(head_count):
                    slot = (ctx * heads + head) * head_count + core
                    at = (kind * heads + head) * width
                    out_ref[core, ctx, :, at : at + width] = flat[
                        pl.ds(slot, depth, stride=slots), :
                    ].astype(out_ref.dtype)


def arrange_weights(key_weight, value_weight, ctx_count, heads, head_count):
    depth, width = key_weight.shape[2], key_weight.shape[5]
    slots = ctx_count * heads * head_count
    rows = min(128, depth)
    views = [w.reshape(depth, slots, width) for w in (key_weight, value_weight)]
    block = pl.BlockSpec((rows, slots, width), lambda i: (i, 0, 0))
    columns = 2 * heads * width
    return pl.pallas_call(
        functools.partial(weight_kernel, ctx_count, heads, head_count),
        grid=(depth // rows,),
        in_specs=[block, block],
        out_specs=pl.BlockSpec((head_count, ctx_count, rows, columns), lambda i: (0, 0, i, 0)),
        out_shape=jax.ShapeDtypeStruct((head_count, ctx_count, depth, columns), jnp.bfloat16),
        scratch_shapes=[pltpu.VMEM((rows * slots, width), jnp.float32)],
        compiler_params=params(),
        cost_estimate=LONG,
        name="arrange_weights",
    )(*views)


def pool_kernel(ctx_count, heads, place_ref, pool_ref, *refs):
    flat, outs = refs[-1], refs[:-1]
    length, slots, width = pool_ref.shape[1:]
    flat[...] = pool_ref[0].astype(jnp.float32).reshape(length * slots, width)
    for kind in range(2):
        for head in range(heads):
            at = (kind * heads + head) * width
            held = []
            for ctx in range(ctx_count):
                slot = (kind * ctx_count + ctx) * heads + head
                held.append(flat[pl.ds(slot, length, stride=slots), :])
            for step, out_ref in enumerate(outs):
                target = lax.rem(place_ref[1] + step, ctx_count)
                value = held[0]
                for ctx in range(1, ctx_count):
                    value = jnp.where(target == ctx, held[ctx], value)
                value = value.T if kind else value
                out_ref[0, :, at : at + width] = value.astype(out_ref.dtype)


def arrange_pool(place, prefix_pool, ctx_count, heads):
    blocks, length, all_heads, _, double = prefix_pool.shape
    width = double // 2
    slots = 2 * all_heads
    view = prefix_pool.reshape(blocks, length, all_heads, 2, width)
    view = view.transpose(0, 1, 3, 2, 4).reshape(blocks, length, slots, width)
    columns = 2 * heads * width
    out = pl.BlockSpec((1, length, columns), lambda i, place: (i, 0, 0))
    return pl.pallas_call(
        functools.partial(pool_kernel, ctx_count, heads),
        grid_spec=pltpu.PrefetchScalarGridSpec(
            num_scalar_prefetch=1,
            grid=(blocks,),
            in_specs=[pl.BlockSpec((1, length, slots, width), lambda i, place: (i, 0, 0, 0))],
            out_specs=[out] * ctx_count,
            scratch_shapes=[pltpu.VMEM((length * slots, width), jnp.float32)],
        ),
        out_shape=[jax.ShapeDtypeStruct((blocks, length, columns), jnp.bfloat16)] * ctx_count,
        compiler_params=params(),
        cost_estimate=LONG,
        name="arrange_pool",
    )(place, view)


def project_kernel(place_ref, *refs):
    token_refs, (weight_ref, out_ref, stacked) = refs[:-3], refs[-3:]
    rows = token_refs[0].shape[0]

    @pl.when(pl.program_id(0) == 0)
    def _():
        for index, token_ref in enumerate(token_refs):
            stacked[index * rows : (index + 1) * rows, :] = token_ref[...]

    out_ref[...] = jnp.dot(
        stacked[...], weight_ref[0, 0], preferred_element_type=jnp.float32
    ).astype(out_ref.dtype)


def project(place, tokens, received, weights, chunk, head_step, out_dtype):
    head_count, ctx_count, depth, width = weights.shape
    rows = tokens.shape[0] // CHUNKS
    row_total = rows * (1 + len(received))
    columns = ctx_count * width
    return pl.pallas_call(
        project_kernel,
        grid_spec=pltpu.PrefetchScalarGridSpec(
            num_scalar_prefetch=1,
            grid=(ctx_count,),
            in_specs=[pl.BlockSpec((rows, depth), lambda j, place: (chunk, place[0]))]
            + [pl.BlockSpec((rows, depth), lambda j, place: (0, 0)) for _ in received]
            + [
                pl.BlockSpec(
                    (1, 1, depth, width),
                    lambda j, place: (
                        lax.rem(place[2] + head_step, head_count),
                        lax.rem(place[1] + j, ctx_count),
                        0,
                        0,
                    ),
                )
            ],
            out_specs=pl.BlockSpec((row_total, width), lambda j, place: (0, j)),
            scratch_shapes=[pltpu.VMEM((row_total, depth), tokens.dtype)],
        ),
        out_shape=jax.ShapeDtypeStruct((row_total, columns), out_dtype),
        compiler_params=params(),
        cost_estimate=LONG,
        name="project",
    )(place, tokens, *received, weights)


def pick_kernel(heads, ctx_count, place_ref, table_ref, *refs):
    pool_refs, (keys, values) = refs[:ctx_count], refs[ctx_count:]
    blocks, length, columns = pool_refs[0].shape
    wide = columns // 2
    width = wide // heads
    values[wide:, :] = jnp.ones_like(values[wide:, :])
    for at in range(table_ref.shape[0]):
        entry = table_ref[at]
        here = slice(at * length, (at + 1) * length)
        step = lax.rem(place_ref[1] - entry // blocks + ctx_count, ctx_count)
        for ctx_step, pool_ref in enumerate(pool_refs):

            @pl.when(step == ctx_step)
            def _():
                block = pool_ref[entry % blocks]
                keys[here, :] = block[:, :wide]
                for head in range(heads):
                    low = wide + head * length
                    values[head * width : (head + 1) * width, here] = block[:, low : low + length]


def pick_blocks(place, table, pools, heads):
    length, columns = pools[0].shape[1:]
    count = table.shape[0] * length
    wide = columns // 2
    return pl.pallas_call(
        functools.partial(pick_kernel, heads, len(pools)),
        grid_spec=pltpu.PrefetchScalarGridSpec(
            num_scalar_prefetch=2,
            grid=(1,),
            in_specs=[pl.BlockSpec(p.shape, lambda i, *_: (0, 0, 0)) for p in pools],
            out_specs=[
                pl.BlockSpec((count, wide), lambda i, *_: (0, 0)),
                pl.BlockSpec((wide + 16, count), lambda i, *_: (0, 0)),
            ],
        ),
        out_shape=[
            jax.ShapeDtypeStruct((count, wide), jnp.bfloat16),
            jax.ShapeDtypeStruct((wide + 16, count), jnp.bfloat16),
        ],
        compiler_params=params(),
        cost_estimate=LONG,
        name="pick_blocks",
    )(place, table, *pools)


def prefix_kernel(scale, heads, query_ref, keys, values, acc_ref, stat_ref, mask):
    rows, width = query_ref.shape
    part_rows = mask.shape[0]
    wide = heads * width

    @pl.when(pl.program_id(0) == 0)
    def _():
        mask[...] = head_mask(mask.shape, heads)

    for part in range(rows // part_rows):
        here = slice(part * part_rows, (part + 1) * part_rows)
        query_block = jnp.concatenate([query_ref[here, :]] * heads, 1) * mask[...]
        row_max, weights = softmax_parts(dot_queries(keys[...], query_block) * scale)
        mixed = jnp.dot(values[...], weights, preferred_element_type=jnp.float32)
        acc_ref[:, here] = own_head(mixed, heads, width)
        half = stat_ref.shape[0] // 2
        stat_ref[:half, here] = jnp.broadcast_to(row_max, (half, part_rows))
        stat_ref[half:, here] = jnp.broadcast_to(mixed[wide : wide + 1], (half, part_rows))


def prefix_attend(query_rows, keys, values, chunk, scale, heads):
    all_rows, width = query_rows.shape
    row_total = all_rows // CHUNKS
    rows = min(1024, row_total)
    steps = row_total // rows
    key_count, wide = keys.shape
    return pl.pallas_call(
        functools.partial(prefix_kernel, scale, heads),
        grid=(steps,),
        in_specs=[
            pl.BlockSpec((rows, width), lambda i: (chunk * steps + i, 0)),
            pl.BlockSpec(keys.shape, lambda i: (0, 0)),
            pl.BlockSpec(values.shape, lambda i: (0, 0)),
        ],
        out_specs=[
            pl.BlockSpec((width, rows), lambda i: (0, i)),
            pl.BlockSpec((8, rows), lambda i: (0, i)),
        ],
        out_shape=[
            jax.ShapeDtypeStruct((width, row_total), jnp.float32),
            jax.ShapeDtypeStruct((8, row_total), jnp.float32),
        ],
        scratch_shapes=[pltpu.VMEM((min(512, rows), wide), jnp.bfloat16)],
        compiler_params=params(),
        cost_estimate=LONG,
        name="prefix_attend",
    )(query_rows, keys, values)


def fresh_kernel(
    scale, heads, per_token, first_row, length_ref, query_ref, acc_ref, stat_ref, fresh_ref, *rest
):
    out_ref, values, mask = rest[-3:]
    rows, width = query_ref.shape
    wide = heads * width
    step = pl.program_id(0)

    @pl.when(step == 0)
    def _():
        mask[...] = head_mask(mask.shape, heads)
        values[wide:, :] = jnp.ones_like(values[wide:, :])
        values[:wide, :] = fresh_ref[:, wide:].astype(jnp.float32).T.astype(jnp.bfloat16)

    part_rows = mask.shape[0]
    half = stat_ref.shape[0] // 2
    for part in range(rows // part_rows):
        here = slice(part * part_rows, (part + 1) * part_rows)
        query_block = jnp.concatenate([query_ref[here, :]] * heads, 1) * mask[...]
        scores = dot_queries(fresh_ref[:, :wide], query_block) * scale
        row = part * part_rows + lax.broadcasted_iota(jnp.int32, (1, part_rows), 1)
        token = first_row + step * (rows // per_token) + (
            row // per_token if per_token & (per_token - 1) else row >> (per_token.bit_length() - 1)
        )
        key_at = lax.broadcasted_iota(jnp.int32, scores.shape, 0)
        scores = jnp.where(key_at <= token, scores, -jnp.inf)
        old_max, old_total = stat_ref[:1, here], stat_ref[half : half + 1, here]
        row_max, weights = softmax_parts(scores, old_max)
        fade = jnp.exp2(old_max - row_max)
        mixed = jnp.dot(values[...], weights, preferred_element_type=jnp.float32)
        row_total = old_total * fade + mixed[wide : wide + 1]
        share = jnp.where(token < length_ref[0], 1.0 / row_total, 0.0)
        result = acc_ref[:, here] * (fade * share) + own_head(mixed, heads, width) * share
        out_ref[here, :] = result.T.astype(out_ref.dtype)


def fresh_attend(length, query_rows, acc, stat, fresh, earlier, chunk, scale, heads, per_token):
    row_total, width = query_rows.shape
    chunk_rows = row_total // CHUNKS
    rows = min(1024, chunk_rows)
    steps = chunk_rows // rows
    block = pl.BlockSpec((rows, width), lambda i, length: (chunk * steps + i, 0))
    in_specs = [
        block,
        pl.BlockSpec((width, rows), lambda i, length: (0, i)),
        pl.BlockSpec((stat.shape[0], rows), lambda i, length: (0, i)),
        pl.BlockSpec(fresh.shape, lambda i, length: (0, 0)),
    ]
    operands = [length, query_rows, acc, stat, fresh]
    aliases = {}
    if earlier is not None:
        in_specs.append(pl.BlockSpec(memory_space=pl.ANY))
        operands.append(earlier)
        aliases = {5: 0}
    return pl.pallas_call(
        functools.partial(
            fresh_kernel, scale, heads, per_token, chunk * (chunk_rows // per_token)
        ),
        grid_spec=pltpu.PrefetchScalarGridSpec(
            num_scalar_prefetch=1,
            grid=(steps,),
            in_specs=in_specs,
            out_specs=block,
            scratch_shapes=[
                pltpu.VMEM((heads * width + 16, fresh.shape[0]), jnp.bfloat16),
                pltpu.VMEM((min(512, rows), heads * width), jnp.bfloat16),
            ],
        ),
        out_shape=jax.ShapeDtypeStruct((row_total, width), jnp.bfloat16),
        input_output_aliases=aliases,
        compiler_params=params(),
        cost_estimate=LONG,
        name="fresh_attend",
    )(*operands)


def reduced_shards(tokens, key_weight, value_weight, queries, prefix_pool, block_table, lengths):
    batch_count = lax.axis_size("batch")
    ctx_count = lax.axis_size("ctx")
    head_count = lax.axis_size("head")
    batch_at, ctx_at, head_at = (lax.axis_index(a) for a in ("batch", "ctx", "head"))
    place = jnp.stack([batch_at, ctx_at, head_at]).astype(jnp.int32)
    token_count = tokens.shape[0]
    heads = queries.shape[1]
    width = prefix_pool.shape[4] // 2
    group = queries.shape[3] // width
    per_token = heads * group
    depth = key_weight.shape[2]
    rows = token_count // CHUNKS
    scale = math.log2(math.e) / math.sqrt(width)

    order = halving_order(batch_count)
    received = []
    for chunk in range(CHUNKS):
        arrived = []
        for bits in order[1:]:
            start = (batch_at ^ bits) * depth
            piece = lax.dynamic_slice(tokens, (chunk * rows, start), (rows, depth))
            arrived.append(trade(piece, "batch", bits))
        received.append(arrived)

    pools = arrange_pool(place, prefix_pool, ctx_count, heads)
    pools, key_weight, value_weight = lax.optimization_barrier((pools, key_weight, value_weight))
    pools = [shift(part, "ctx", step) if step else part for step, part in enumerate(pools)]

    weights = arrange_weights(key_weight, value_weight, ctx_count, heads, head_count)

    query_rows = queries.reshape(token_count, heads, group, width)
    query_rows = query_rows.transpose(0, 2, 1, 3).reshape(-1, width)
    keys = values = None
    fresh_parts = []
    result = None
    cols = weights.shape[3]
    for chunk in range(CHUNKS):
        call = functools.partial(project, place, tokens, received[chunk], weights, chunk)
        terms = [
            shift(call(step, jnp.bfloat16), "head", step).astype(jnp.float32)
            for step in range(1, head_count)
        ]
        own = call(0, jnp.float32)
        mine = sum(terms, own[:, :])
        parts = [
            mine[:, step * cols : (step + 1) * cols].astype(jnp.bfloat16)
            for step in range(1, ctx_count)
        ]
        parts, pools, query_rows = lax.optimization_barrier((parts, pools, query_rows))
        parts = [shift(part, "ctx", step + 1) for step, part in enumerate(parts)]
        if keys is None:
            keys, values = pick_blocks(place, block_table[0], pools, heads)
        acc, stat = prefix_attend(query_rows, keys, values, chunk, scale, heads)
        if chunk + 1 < CHUNKS:
            acc, received[chunk + 1] = lax.optimization_barrier((acc, received[chunk + 1]))
        parts, acc, stat = lax.optimization_barrier((parts, acc, stat))
        mine = sum((part.astype(jnp.float32) for part in parts), mine[:, :cols])
        bit = 1
        while bit < batch_count:
            half = mine.shape[0] // 2
            part = trade(mine[half:].astype(jnp.bfloat16), "batch", bit)
            if result is not None and bit == 1:
                part, result = lax.optimization_barrier((part, result))
            mine = mine[:half] + part.astype(jnp.float32)
            bit *= 2
        fresh_parts.append(mine.astype(jnp.bfloat16))
        result = fresh_attend(
            lengths,
            query_rows,
            acc,
            stat,
            jnp.concatenate(fresh_parts, 0),
            result,
            chunk,
            scale,
            heads,
            per_token,
        )
    result = result.reshape(token_count, group, heads, width).transpose(0, 2, 1, 3)
    return result.reshape(token_count, heads, 1, group * width)


def solution(mesh):
    def shards(tokens, key_weight, value_weight, *rest):
        prompts = mesh.shape["batch"]
        columns = 2 * math.prod(key_weight.shape[3:])
        few_tokens = prompts * tokens.shape[0] <= columns and not prompts & (prompts - 1)
        form = reduced_shards if few_tokens else gathered_shards
        return form(tokens, key_weight, value_weight, *rest)

    return jax.shard_map(
        shards,
        mesh=mesh,
        in_specs=(
            P(("groups", "batch"), ("ctx", "head")),
            P("ctx", "head", "batch", None, None, None),
            P("ctx", "head", "batch", None, None, None),
            P(("groups", "batch"), "ctx", "head", None),
            P(("groups", "ctx"), None, None, "head", None),
            P(("groups", "batch"), None),
            P(("groups", "batch")),
        ),
        out_specs=P(("groups", "batch"), "ctx", "head", None),
        check_vma=False,
    )
```

```python
import functools
import math

import jax
import jax.numpy as jnp
from jax import lax
from jax.experimental import pallas as pl
from jax.experimental.pallas import tpu as pltpu
from jax.sharding import PartitionSpec as P

CHUNKS = 2
VMEM_BYTES = 32 * 1024 * 1024
LONG = pl.CostEstimate(flops=10**11, bytes_accessed=1, transcendentals=0)


def attend_head(query_rows, prefix, fresh_rows, length):
    token_count = query_rows.shape[0]
    head_width = prefix.shape[1] // 2
    group_size = query_rows.shape[1] // head_width
    prefix_len = prefix.shape[0]
    key_rows = jnp.concatenate([prefix[:, :head_width], fresh_rows[:, :head_width]], 0)
    value_rows = jnp.concatenate([prefix[:, head_width:], fresh_rows[:, head_width:]], 0)
    block_len = min(token_count, 64)
    pieces = []
    for first_row in range(0, token_count, block_len):
        block_rows = query_rows[first_row : first_row + block_len].reshape(
            block_len * group_size, head_width
        )
        scores = jnp.dot(
            block_rows, key_rows.T, preferred_element_type=jnp.float32
        ) * head_width ** (-0.5)
        position = first_row + jnp.arange(block_len * group_size) // group_size
        column = jnp.arange(prefix_len + token_count) - prefix_len
        allowed = column[None, :] <= position[:, None]
        scores = jnp.where(allowed, scores, -jnp.inf)
        row_max = jnp.max(scores, axis=1, keepdims=True)
        weights = jnp.exp(scores - row_max)
        row_total = jnp.sum(weights, axis=1, keepdims=True)
        probs_bf = (weights / row_total).astype(jnp.bfloat16)
        mixed_rows = jnp.dot(probs_bf, value_rows, preferred_element_type=jnp.float32)
        is_live = position < length
        mixed_rows = jnp.where(is_live[:, None], mixed_rows, 0.0)
        pieces.append(mixed_rows.astype(jnp.bfloat16).reshape(block_len, group_size * head_width))
    return jnp.concatenate(pieces, 0)


def gathered_shards(tokens, key_weight, value_weight, queries, prefix_pool, block_table, lengths):
    token_count = tokens.shape[0]
    local_heads = queries.shape[1]
    head_width = prefix_pool.shape[4] // 2
    ctx_count = lax.axis_size("ctx")
    head_count = lax.axis_size("head")
    features = lax.all_gather(tokens, ("ctx", "head"), axis=1, tiled=True)
    key_cols, value_cols = (
        lax.all_to_all(
            lax.all_to_all(weight, "ctx", split_axis=3, concat_axis=0, tiled=True),
            "head",
            split_axis=4,
            concat_axis=1,
            tiled=True,
        )
        for weight in (key_weight, value_weight)
    )
    span_len = features.shape[1] // (ctx_count * head_count)
    feature_view = features.reshape(token_count, ctx_count, head_count, span_len)
    pieces = (
        lax.all_gather(key_cols, "batch", axis=2, tiled=True),
        lax.all_gather(value_cols, "batch", axis=2, tiled=True),
    )
    row_count = pieces[0].shape[2]

    def one_term(weight_piece):
        shaped = weight_piece.reshape(ctx_count, head_count, row_count, local_heads * head_width)
        return jnp.einsum("tchr,chrk->tk", feature_view, shaped, preferred_element_type=jnp.float32)

    new_keys = one_term(pieces[0]).astype(jnp.bfloat16).reshape(token_count, local_heads, head_width)
    new_values = one_term(pieces[1]).astype(jnp.bfloat16).reshape(token_count, local_heads, head_width)
    fresh_all = jnp.concatenate([new_keys, new_values], 2)
    pool_heads = lax.all_to_all(prefix_pool, "ctx", split_axis=2, concat_axis=0, tiled=True)
    chosen = jnp.take(pool_heads, block_table[0], axis=0)
    chosen = chosen.reshape(-1, local_heads, 2 * head_width)
    outputs = [
        attend_head(
            queries[:, head_idx, 0], chosen[:, head_idx], fresh_all[:, head_idx], lengths[0]
        )
        for head_idx in range(local_heads)
    ]
    return jnp.stack(outputs, 1)[:, :, None, :]


def shift(array, axis, step):
    count = lax.axis_size(axis)
    return lax.ppermute(array, axis, [(i, (i + step) % count) for i in range(count)])


def trade(array, axis, bits):
    return lax.ppermute(array, axis, [(i, i ^ bits) for i in range(lax.axis_size(axis))])


def unit_index(shape, unit):
    row = lax.broadcasted_iota(jnp.int32, shape, 0)
    if unit & (unit - 1):
        return row // unit, row % unit
    return row >> (unit.bit_length() - 1), row & (unit - 1)


def head_mask(shape, heads):
    column = lax.broadcasted_iota(jnp.int32, shape, 1)
    low = unit_index(shape, heads)[1] * (shape[1] // heads)
    inside = (column >= low) & (column < low + shape[1] // heads)
    return jnp.where(inside, 1.0, 0.0).astype(jnp.bfloat16)


def own_head(block, heads, width):
    result = block[:width]
    row = lax.broadcasted_iota(jnp.int32, result.shape, 1)
    head_of = row % heads if heads & (heads - 1) else row & (heads - 1)
    for i in range(1, heads):
        result = jnp.where(head_of == i, block[i * width : (i + 1) * width], result)
    return result


def softmax_parts(scores, old_max=None):
    row_max = jnp.max(scores, axis=0, keepdims=True)
    if old_max is not None:
        row_max = jnp.maximum(row_max, old_max)
    return row_max, jnp.exp2(scores - row_max).astype(jnp.bfloat16)


def dot_queries(keys, query_block):
    return lax.dot_general(
        keys, query_block, (((1,), (1,)), ((), ())), preferred_element_type=jnp.float32
    )


def params():
    return pltpu.CompilerParams(vmem_limit_bytes=VMEM_BYTES)


def weight_kernel(ctx_count, heads, head_count, key_ref, value_ref, out_ref, flat):
    depth, slots, width = key_ref.shape
    for kind, ref in enumerate((key_ref, value_ref)):
        flat[...] = ref[...].astype(jnp.float32).reshape(depth * slots, width)
        for ctx in range(ctx_count):
            for head in range(heads):
                for core in range(head_count):
                    slot = (ctx * heads + head) * head_count + core
                    at = (kind * heads + head) * width
                    out_ref[core, ctx, :, at : at + width] = flat[
                        pl.ds(slot, depth, stride=slots), :
                    ].astype(out_ref.dtype)


def arrange_weights(key_weight, value_weight, ctx_count, heads, head_count):
    depth, width = key_weight.shape[2], key_weight.shape[5]
    slots = ctx_count * heads * head_count
    rows = min(128, depth)
    views = [w.reshape(depth, slots, width) for w in (key_weight, value_weight)]
    block = pl.BlockSpec((rows, slots, width), lambda i: (i, 0, 0))
    columns = 2 * heads * width
    return pl.pallas_call(
        functools.partial(weight_kernel, ctx_count, heads, head_count),
        grid=(depth // rows,),
        in_specs=[block, block],
        out_specs=pl.BlockSpec((head_count, ctx_count, rows, columns), lambda i: (0, 0, i, 0)),
        out_shape=jax.ShapeDtypeStruct((head_count, ctx_count, depth, columns), jnp.bfloat16),
        scratch_shapes=[pltpu.VMEM((rows * slots, width), jnp.float32)],
        compiler_params=params(),
        cost_estimate=LONG,
        name="arrange_weights",
    )(*views)


def pool_kernel(ctx_count, heads, place_ref, pool_ref, *refs):
    flat, outs = refs[-1], refs[:-1]
    length, slots, width = pool_ref.shape[1:]
    flat[...] = pool_ref[0].astype(jnp.float32).reshape(length * slots, width)
    for kind in range(2):
        for head in range(heads):
            at = (kind * heads + head) * width
            held = []
            for ctx in range(ctx_count):
                slot = (kind * ctx_count + ctx) * heads + head
                held.append(flat[pl.ds(slot, length, stride=slots), :])
            for step, out_ref in enumerate(outs):
                target = lax.rem(place_ref[1] + step, ctx_count)
                value = held[0]
                for ctx in range(1, ctx_count):
                    value = jnp.where(target == ctx, held[ctx], value)
                value = value.T if kind else value
                out_ref[0, :, at : at + width] = value.astype(out_ref.dtype)


def arrange_pool(place, prefix_pool, ctx_count, heads):
    blocks, length, all_heads, _, double = prefix_pool.shape
    width = double // 2
    slots = 2 * all_heads
    view = prefix_pool.reshape(blocks, length, all_heads, 2, width)
    view = view.transpose(0, 1, 3, 2, 4).reshape(blocks, length, slots, width)
    columns = 2 * heads * width
    out = pl.BlockSpec((1, length, columns), lambda i, place: (i, 0, 0))
    return pl.pallas_call(
        functools.partial(pool_kernel, ctx_count, heads),
        grid_spec=pltpu.PrefetchScalarGridSpec(
            num_scalar_prefetch=1,
            grid=(blocks,),
            in_specs=[pl.BlockSpec((1, length, slots, width), lambda i, place: (i, 0, 0, 0))],
            out_specs=[out] * ctx_count,
            scratch_shapes=[pltpu.VMEM((length * slots, width), jnp.float32)],
        ),
        out_shape=[jax.ShapeDtypeStruct((blocks, length, columns), jnp.bfloat16)] * ctx_count,
        compiler_params=params(),
        cost_estimate=LONG,
        name="arrange_pool",
    )(place, view)


def project_kernel(place_ref, *refs):
    token_refs, (weight_ref, out_ref, stacked) = refs[:-3], refs[-3:]
    rows = token_refs[0].shape[0]

    @pl.when(pl.program_id(0) == 0)
    def _():
        for index, token_ref in enumerate(token_refs):
            stacked[index * rows : (index + 1) * rows, :] = token_ref[...]

    out_ref[...] = jnp.dot(
        stacked[...], weight_ref[0, 0], preferred_element_type=jnp.float32
    ).astype(out_ref.dtype)


def project(place, blocks, weights, head_step, out_dtype):
    head_count, ctx_count, depth, width = weights.shape
    rows = blocks[0].shape[0]
    row_total = rows * len(blocks)
    columns = ctx_count * width

    def block_spec(block):
        if block.shape[1] == depth:
            return pl.BlockSpec((rows, depth), lambda j, place: (0, 0))
        return pl.BlockSpec((rows, depth), lambda j, place: (0, place[0]))

    return pl.pallas_call(
        project_kernel,
        grid_spec=pltpu.PrefetchScalarGridSpec(
            num_scalar_prefetch=1,
            grid=(ctx_count,),
            in_specs=[block_spec(block) for block in blocks]
            + [
                pl.BlockSpec(
                    (1, 1, depth, width),
                    lambda j, place: (
                        lax.rem(place[2] + head_step, head_count),
                        lax.rem(place[1] + j, ctx_count),
                        0,
                        0,
                    ),
                )
            ],
            out_specs=pl.BlockSpec((row_total, width), lambda j, place: (0, j)),
            scratch_shapes=[pltpu.VMEM((row_total, depth), weights.dtype)],
        ),
        out_shape=jax.ShapeDtypeStruct((row_total, columns), out_dtype),
        compiler_params=params(),
        cost_estimate=LONG,
        name="project",
    )(place, *blocks, weights)


def pick_kernel(heads, ctx_count, place_ref, table_ref, *refs):
    pool_refs, (keys, values) = refs[:ctx_count], refs[ctx_count:]
    blocks, length, columns = pool_refs[0].shape
    wide = columns // 2
    width = wide // heads
    values[wide:, :] = jnp.ones_like(values[wide:, :])
    for at in range(table_ref.shape[0]):
        entry = table_ref[at]
        here = slice(at * length, (at + 1) * length)
        step = lax.rem(place_ref[1] - entry // blocks + ctx_count, ctx_count)
        for ctx_step, pool_ref in enumerate(pool_refs):

            @pl.when(step == ctx_step)
            def _():
                block = pool_ref[entry % blocks]
                keys[here, :] = block[:, :wide]
                for head in range(heads):
                    low = wide + head * length
                    values[head * width : (head + 1) * width, here] = block[:, low : low + length]


def pick_blocks(place, table, pools, heads):
    length, columns = pools[0].shape[1:]
    count = table.shape[0] * length
    wide = columns // 2
    return pl.pallas_call(
        functools.partial(pick_kernel, heads, len(pools)),
        grid_spec=pltpu.PrefetchScalarGridSpec(
            num_scalar_prefetch=2,
            grid=(1,),
            in_specs=[pl.BlockSpec(p.shape, lambda i, *_: (0, 0, 0)) for p in pools],
            out_specs=[
                pl.BlockSpec((count, wide), lambda i, *_: (0, 0)),
                pl.BlockSpec((wide + 16, count), lambda i, *_: (0, 0)),
            ],
        ),
        out_shape=[
            jax.ShapeDtypeStruct((count, wide), jnp.bfloat16),
            jax.ShapeDtypeStruct((wide + 16, count), jnp.bfloat16),
        ],
        compiler_params=params(),
        cost_estimate=LONG,
        name="pick_blocks",
    )(place, table, *pools)


def prefix_kernel(scale, heads, query_ref, keys, values, acc_ref, stat_ref, mask):
    rows, width = query_ref.shape
    part_rows = mask.shape[0]
    wide = heads * width

    @pl.when(pl.program_id(0) == 0)
    def _():
        mask[...] = head_mask(mask.shape, heads)

    for part in range(rows // part_rows):
        here = slice(part * part_rows, (part + 1) * part_rows)
        query_block = jnp.concatenate([query_ref[here, :]] * heads, 1) * mask[...]
        row_max, weights = softmax_parts(dot_queries(keys[...], query_block) * scale)
        mixed = jnp.dot(values[...], weights, preferred_element_type=jnp.float32)
        acc_ref[:, here] = own_head(mixed, heads, width)
        half = stat_ref.shape[0] // 2
        stat_ref[:half, here] = jnp.broadcast_to(row_max, (half, part_rows))
        stat_ref[half:, here] = jnp.broadcast_to(mixed[wide : wide + 1], (half, part_rows))


def prefix_attend(query_rows, keys, values, piece, scale, heads):
    all_rows, width = query_rows.shape
    row_total = all_rows // CHUNKS
    rows = min(1024, row_total)
    steps = row_total // rows
    key_count, wide = keys.shape
    return pl.pallas_call(
        functools.partial(prefix_kernel, scale, heads),
        grid=(steps,),
        in_specs=[
            pl.BlockSpec((rows, width), lambda i: (piece * steps + i, 0)),
            pl.BlockSpec(keys.shape, lambda i: (0, 0)),
            pl.BlockSpec(values.shape, lambda i: (0, 0)),
        ],
        out_specs=[
            pl.BlockSpec((width, rows), lambda i: (0, i)),
            pl.BlockSpec((8, rows), lambda i: (0, i)),
        ],
        out_shape=[
            jax.ShapeDtypeStruct((width, row_total), jnp.float32),
            jax.ShapeDtypeStruct((8, row_total), jnp.float32),
        ],
        scratch_shapes=[pltpu.VMEM((min(512, rows), wide), jnp.bfloat16)],
        compiler_params=params(),
        cost_estimate=LONG,
        name="prefix_attend",
    )(query_rows, keys, values)


def fresh_kernel(
    scale, heads, per_token, first_row, length_ref, query_ref, acc_ref, stat_ref, fresh_ref, *rest
):
    out_ref, values, mask = rest[-3:]
    rows, width = query_ref.shape
    wide = heads * width
    step = pl.program_id(0)

    @pl.when(step == 0)
    def _():
        mask[...] = head_mask(mask.shape, heads)
        values[wide:, :] = jnp.ones_like(values[wide:, :])
        values[:wide, :] = fresh_ref[:, wide:].astype(jnp.float32).T.astype(jnp.bfloat16)

    part_rows = mask.shape[0]
    half = stat_ref.shape[0] // 2
    for part in range(rows // part_rows):
        here = slice(part * part_rows, (part + 1) * part_rows)
        query_block = jnp.concatenate([query_ref[here, :]] * heads, 1) * mask[...]
        scores = dot_queries(fresh_ref[:, :wide], query_block) * scale
        row = part * part_rows + lax.broadcasted_iota(jnp.int32, (1, part_rows), 1)
        token = first_row + step * (rows // per_token) + (
            row // per_token if per_token & (per_token - 1) else row >> (per_token.bit_length() - 1)
        )
        key_at = lax.broadcasted_iota(jnp.int32, scores.shape, 0)
        scores = jnp.where(key_at <= token, scores, -jnp.inf)
        old_max, old_total = stat_ref[:1, here], stat_ref[half : half + 1, here]
        row_max, weights = softmax_parts(scores, old_max)
        fade = jnp.exp2(old_max - row_max)
        mixed = jnp.dot(values[...], weights, preferred_element_type=jnp.float32)
        row_total = old_total * fade + mixed[wide : wide + 1]
        share = jnp.where(token < length_ref[0], 1.0 / row_total, 0.0)
        result = acc_ref[:, here] * (fade * share) + own_head(mixed, heads, width) * share
        out_ref[here, :] = result.T.astype(out_ref.dtype)


def fresh_attend(length, query_rows, acc, stat, fresh, earlier, piece, scale, heads, per_token):
    row_total, width = query_rows.shape
    piece_rows = row_total // CHUNKS
    rows = min(1024, piece_rows)
    steps = piece_rows // rows
    block = pl.BlockSpec((rows, width), lambda i, length: (piece * steps + i, 0))
    in_specs = [
        block,
        pl.BlockSpec((width, rows), lambda i, length: (0, i)),
        pl.BlockSpec((stat.shape[0], rows), lambda i, length: (0, i)),
        pl.BlockSpec(fresh.shape, lambda i, length: (0, 0)),
    ]
    operands = [length, query_rows, acc, stat, fresh]
    aliases = {}
    if earlier is not None:
        in_specs.append(pl.BlockSpec(memory_space=pl.ANY))
        operands.append(earlier)
        aliases = {5: 0}
    return pl.pallas_call(
        functools.partial(
            fresh_kernel, scale, heads, per_token, piece * (piece_rows // per_token)
        ),
        grid_spec=pltpu.PrefetchScalarGridSpec(
            num_scalar_prefetch=1,
            grid=(steps,),
            in_specs=in_specs,
            out_specs=block,
            scratch_shapes=[
                pltpu.VMEM((heads * width + 16, fresh.shape[0]), jnp.bfloat16),
                pltpu.VMEM((min(512, rows), heads * width), jnp.bfloat16),
            ],
        ),
        out_shape=jax.ShapeDtypeStruct((row_total, width), jnp.bfloat16),
        input_output_aliases=aliases,
        compiler_params=params(),
        cost_estimate=LONG,
        name="fresh_attend",
    )(*operands)


def reduced_shards(tokens, key_weight, value_weight, queries, prefix_pool, block_table, lengths):
    batch_count = lax.axis_size("batch")
    ctx_count = lax.axis_size("ctx")
    head_count = lax.axis_size("head")
    batch_at, ctx_at, head_at = (lax.axis_index(a) for a in ("batch", "ctx", "head"))
    place = jnp.stack([batch_at, ctx_at, head_at]).astype(jnp.int32)
    token_count = tokens.shape[0]
    heads = queries.shape[1]
    width = prefix_pool.shape[4] // 2
    group = queries.shape[3] // width
    per_token = heads * group
    depth = key_weight.shape[2]
    rows = token_count // CHUNKS
    scale = math.log2(math.e) / math.sqrt(width)

    def leaving(bits):
        start = (batch_at ^ bits) * depth
        return lax.dynamic_slice(tokens, (0, start), (token_count, depth))

    top = batch_count // 2
    steps = [bits for bits in range(1, batch_count) if bits != top]
    near = [trade(leaving(bits), "batch", bits) for bits in steps]

    pools = arrange_pool(place, prefix_pool, ctx_count, heads)
    pools, key_weight, value_weight, tokens = lax.optimization_barrier(
        (pools, key_weight, value_weight, tokens)
    )
    last = trade(leaving(top), "batch", top)
    pools = [shift(part, "ctx", step) if step else part for step, part in enumerate(pools)]

    weights = arrange_weights(key_weight, value_weight, ctx_count, heads, head_count)

    query_rows = queries.reshape(token_count, heads, group, width)
    query_rows = query_rows.transpose(0, 2, 1, 3).reshape(-1, width)
    cols = weights.shape[3]

    def projected(blocks):
        terms = [
            shift(project(place, blocks, weights, step, jnp.bfloat16), "head", step)
            for step in range(1, head_count)
        ]
        total = project(place, blocks, weights, 0, jnp.float32)
        total = sum((term.astype(jnp.float32) for term in terms), total)
        others = [
            total[:, step * cols : (step + 1) * cols].astype(jnp.bfloat16)
            for step in range(1, ctx_count)
        ]
        return total[:, :cols], others

    def spread(others):
        return [shift(other, "ctx", step + 1) for step, other in enumerate(others)]

    def summed(mine, others):
        return sum((other.astype(jnp.float32) for other in others), mine)

    def after(first, second):
        return lax.optimization_barrier((first, second))[1]

    def halves(block):
        return [block[i * rows : (i + 1) * rows] for i in range(CHUNKS)]

    early, others = projected([*near, tokens])
    pools = after(others, pools)
    own_at = len(near) * token_count
    keys, values = pick_blocks(place, block_table[0], pools, heads)
    if near:
        away = summed(early[:own_at], spread([other[:own_at] for other in others]))
        away = trade(away.astype(jnp.bfloat16), "batch", 1).astype(jnp.float32)
    home = summed(early[own_at:], spread([other[own_at:] for other in others]))
    states = [prefix_attend(query_rows, keys, values, 0, scale, heads)]
    last = after(states[0], last)

    mine, others = projected([last])
    keys, values = after(others, (keys, values))
    for chunk in range(1, CHUNKS):
        states.append(prefix_attend(query_rows, keys, values, chunk, scale, heads))
    mine = halves(mine)
    others = [spread(list(o)) for o in zip(*(halves(other) for other in others))]
    if near:
        home = home + away[:token_count]
        mine = [a + b for a, b in zip(mine, halves(away[token_count:]))]
    home = halves(home)
    parts = []
    for chunk in range(CHUNKS):
        if parts:
            others[chunk] = after(parts[-1], others[chunk])
        parts.append(summed(mine[chunk], others[chunk]).astype(jnp.bfloat16))
    parts = [trade(part, "batch", top) for part in parts]

    result = None
    fresh_parts = []
    for chunk in range(CHUNKS):
        if chunk:
            parts[chunk] = after(result, parts[chunk])
        fresh_parts.append((parts[chunk].astype(jnp.float32) + home[chunk]).astype(jnp.bfloat16))
        fresh = jnp.concatenate(fresh_parts, 0)
        result = fresh_attend(
            lengths, query_rows, *states[chunk], fresh, result, chunk, scale, heads, per_token
        )
    result = result.reshape(token_count, group, heads, width).transpose(0, 2, 1, 3)
    return result.reshape(token_count, heads, 1, group * width)


def solution(mesh):
    def shards(tokens, key_weight, value_weight, *rest):
        prompts = mesh.shape["batch"]
        columns = 2 * math.prod(key_weight.shape[3:])
        few_tokens = prompts * tokens.shape[0] <= columns and prompts in (2, 4)
        form = reduced_shards if few_tokens else gathered_shards
        return form(tokens, key_weight, value_weight, *rest)

    return jax.shard_map(
        shards,
        mesh=mesh,
        in_specs=(
            P(("groups", "batch"), ("ctx", "head")),
            P("ctx", "head", "batch", None, None, None),
            P("ctx", "head", "batch", None, None, None),
            P(("groups", "batch"), "ctx", "head", None),
            P(("groups", "ctx"), None, None, "head", None),
            P(("groups", "batch"), None),
            P(("groups", "batch")),
        ),
        out_specs=P(("groups", "batch"), "ctx", "head", None),
        check_vma=False,
    )
```

```python
import functools
import math

import jax
import jax.numpy as jnp
from jax import lax
from jax.experimental import pallas as pl
from jax.experimental.pallas import tpu as pltpu
from jax.sharding import PartitionSpec as P

CHUNKS = 2
VMEM_BYTES = 24 * 1024 * 1024
LONG = pl.CostEstimate(flops=10**11, bytes_accessed=1, transcendentals=0)


def attend_head(query_rows, prefix, fresh_rows, length):
    token_count = query_rows.shape[0]
    head_width = prefix.shape[1] // 2
    group_size = query_rows.shape[1] // head_width
    prefix_len = prefix.shape[0]
    key_rows = jnp.concatenate([prefix[:, :head_width], fresh_rows[:, :head_width]], 0)
    value_rows = jnp.concatenate([prefix[:, head_width:], fresh_rows[:, head_width:]], 0)
    block_len = min(token_count, 64)
    pieces = []
    for first_row in range(0, token_count, block_len):
        block_rows = query_rows[first_row : first_row + block_len].reshape(
            block_len * group_size, head_width
        )
        scores = jnp.dot(
            block_rows, key_rows.T, preferred_element_type=jnp.float32
        ) * head_width ** (-0.5)
        position = first_row + jnp.arange(block_len * group_size) // group_size
        column = jnp.arange(prefix_len + token_count) - prefix_len
        allowed = column[None, :] <= position[:, None]
        scores = jnp.where(allowed, scores, -jnp.inf)
        row_max = jnp.max(scores, axis=1, keepdims=True)
        weights = jnp.exp(scores - row_max)
        row_total = jnp.sum(weights, axis=1, keepdims=True)
        probs_bf = (weights / row_total).astype(jnp.bfloat16)
        mixed_rows = jnp.dot(probs_bf, value_rows, preferred_element_type=jnp.float32)
        is_live = position < length
        mixed_rows = jnp.where(is_live[:, None], mixed_rows, 0.0)
        pieces.append(mixed_rows.astype(jnp.bfloat16).reshape(block_len, group_size * head_width))
    return jnp.concatenate(pieces, 0)


def gathered_shards(tokens, key_weight, value_weight, queries, prefix_pool, block_table, lengths):
    token_count = tokens.shape[0]
    local_heads = queries.shape[1]
    head_width = prefix_pool.shape[4] // 2
    ctx_count = lax.axis_size("ctx")
    head_count = lax.axis_size("head")
    features = lax.all_gather(tokens, ("ctx", "head"), axis=1, tiled=True)
    key_cols, value_cols = (
        lax.all_to_all(
            lax.all_to_all(weight, "ctx", split_axis=3, concat_axis=0, tiled=True),
            "head",
            split_axis=4,
            concat_axis=1,
            tiled=True,
        )
        for weight in (key_weight, value_weight)
    )
    span_len = features.shape[1] // (ctx_count * head_count)
    feature_view = features.reshape(token_count, ctx_count, head_count, span_len)
    pieces = (
        lax.all_gather(key_cols, "batch", axis=2, tiled=True),
        lax.all_gather(value_cols, "batch", axis=2, tiled=True),
    )
    row_count = pieces[0].shape[2]

    def one_term(weight_piece):
        shaped = weight_piece.reshape(ctx_count, head_count, row_count, local_heads * head_width)
        return jnp.einsum("tchr,chrk->tk", feature_view, shaped, preferred_element_type=jnp.float32)

    new_keys = one_term(pieces[0]).astype(jnp.bfloat16).reshape(token_count, local_heads, head_width)
    new_values = one_term(pieces[1]).astype(jnp.bfloat16).reshape(token_count, local_heads, head_width)
    fresh_all = jnp.concatenate([new_keys, new_values], 2)
    pool_heads = lax.all_to_all(prefix_pool, "ctx", split_axis=2, concat_axis=0, tiled=True)
    chosen = jnp.take(pool_heads, block_table[0], axis=0)
    chosen = chosen.reshape(-1, local_heads, 2 * head_width)
    outputs = [
        attend_head(
            queries[:, head_idx, 0], chosen[:, head_idx], fresh_all[:, head_idx], lengths[0]
        )
        for head_idx in range(local_heads)
    ]
    return jnp.stack(outputs, 1)[:, :, None, :]


def shift(array, axis, step):
    count = lax.axis_size(axis)
    return lax.ppermute(array, axis, [(i, (i + step) % count) for i in range(count)])


def trade(array, axis, bits):
    return lax.ppermute(array, axis, [(i, i ^ bits) for i in range(lax.axis_size(axis))])


def after(first, second):
    return lax.optimization_barrier((first, second))


def unit_index(shape, unit):
    row = lax.broadcasted_iota(jnp.int32, shape, 0)
    if unit & (unit - 1):
        return row // unit, row % unit
    return row >> (unit.bit_length() - 1), row & (unit - 1)


def head_mask(shape, heads):
    column = lax.broadcasted_iota(jnp.int32, shape, 1)
    low = unit_index(shape, heads)[1] * (shape[1] // heads)
    inside = (column >= low) & (column < low + shape[1] // heads)
    return jnp.where(inside, 1.0, 0.0).astype(jnp.bfloat16)


def own_head(block, heads, width):
    result = block[:width]
    row = lax.broadcasted_iota(jnp.int32, result.shape, 1)
    head_of = row % heads if heads & (heads - 1) else row & (heads - 1)
    for i in range(1, heads):
        result = jnp.where(head_of == i, block[i * width : (i + 1) * width], result)
    return result


def softmax_parts(scores, old_max=None):
    row_max = jnp.max(scores, axis=0, keepdims=True)
    if old_max is not None:
        row_max = jnp.maximum(row_max, old_max)
    return row_max, jnp.exp2(scores - row_max).astype(jnp.bfloat16)


def dot_queries(keys, query_block):
    return lax.dot_general(
        keys, query_block, (((1,), (1,)), ((), ())), preferred_element_type=jnp.float32
    )


def params():
    return pltpu.CompilerParams(vmem_limit_bytes=VMEM_BYTES)


def weight_kernel(ctx_count, heads, head_count, key_ref, value_ref, out_ref, flat):
    depth, slots, width = key_ref.shape
    for kind, ref in enumerate((key_ref, value_ref)):
        flat[...] = ref[...].astype(jnp.float32).reshape(depth * slots, width)
        for ctx in range(ctx_count):
            for head in range(heads):
                for core in range(head_count):
                    slot = (ctx * heads + head) * head_count + core
                    at = (kind * heads + head) * width
                    out_ref[core, ctx, :, at : at + width] = flat[
                        pl.ds(slot, depth, stride=slots), :
                    ].astype(out_ref.dtype)


def arrange_weights(key_weight, value_weight, ctx_count, heads, head_count):
    depth, width = key_weight.shape[2], key_weight.shape[5]
    slots = ctx_count * heads * head_count
    rows = min(128, depth)
    views = [w.reshape(depth, slots, width) for w in (key_weight, value_weight)]
    block = pl.BlockSpec((rows, slots, width), lambda i: (i, 0, 0))
    columns = 2 * heads * width
    return pl.pallas_call(
        functools.partial(weight_kernel, ctx_count, heads, head_count),
        grid=(depth // rows,),
        in_specs=[block, block],
        out_specs=pl.BlockSpec((head_count, ctx_count, rows, columns), lambda i: (0, 0, i, 0)),
        out_shape=jax.ShapeDtypeStruct((head_count, ctx_count, depth, columns), jnp.bfloat16),
        scratch_shapes=[pltpu.VMEM((rows * slots, width), jnp.float32)],
        compiler_params=params(),
        cost_estimate=LONG,
        name="arrange_weights",
    )(*views)


def pool_kernel(ctx_count, heads, place_ref, pool_ref, *refs):
    flat, outs = refs[-1], refs[:-1]
    length, slots, width = pool_ref.shape[1:]
    flat[...] = pool_ref[0].astype(jnp.float32).reshape(length * slots, width)
    for kind in range(2):
        for head in range(heads):
            at = (kind * heads + head) * width
            held = []
            for ctx in range(ctx_count):
                slot = (kind * ctx_count + ctx) * heads + head
                held.append(flat[pl.ds(slot, length, stride=slots), :])
            for step, out_ref in enumerate(outs):
                target = lax.rem(place_ref[1] + step, ctx_count)
                value = held[0]
                for ctx in range(1, ctx_count):
                    value = jnp.where(target == ctx, held[ctx], value)
                value = value.T if kind else value
                out_ref[0, :, at : at + width] = value.astype(out_ref.dtype)


def arrange_pool(place, prefix_pool, ctx_count, heads):
    blocks, length, all_heads, _, double = prefix_pool.shape
    width = double // 2
    slots = 2 * all_heads
    view = prefix_pool.reshape(blocks, length, all_heads, 2, width)
    view = view.transpose(0, 1, 3, 2, 4).reshape(blocks, length, slots, width)
    columns = 2 * heads * width
    out = pl.BlockSpec((1, length, columns), lambda i, place: (i, 0, 0))
    return pl.pallas_call(
        functools.partial(pool_kernel, ctx_count, heads),
        grid_spec=pltpu.PrefetchScalarGridSpec(
            num_scalar_prefetch=1,
            grid=(blocks,),
            in_specs=[pl.BlockSpec((1, length, slots, width), lambda i, place: (i, 0, 0, 0))],
            out_specs=[out] * ctx_count,
            scratch_shapes=[pltpu.VMEM((length * slots, width), jnp.float32)],
        ),
        out_shape=[jax.ShapeDtypeStruct((blocks, length, columns), jnp.bfloat16)] * ctx_count,
        compiler_params=params(),
        cost_estimate=LONG,
        name="arrange_pool",
    )(place, view)


def project_kernel(place_ref, *refs):
    token_refs, (weight_ref, out_ref, stacked) = refs[:-3], refs[-3:]

    @pl.when(pl.program_id(0) == 0)
    def _():
        at = 0
        for token_ref in token_refs:
            rows = token_ref.shape[0]
            stacked[at : at + rows, :] = token_ref[...]
            at += rows

    out_ref[0] = jnp.dot(
        stacked[...], weight_ref[0, 0], preferred_element_type=jnp.float32
    ).astype(out_ref.dtype)


def project(place, blocks, weights, head_step, out_dtype):
    head_count, ctx_count, depth, width = weights.shape
    row_total = sum(block.shape[0] for block in blocks)

    def block_spec(block):
        if block.shape[1] == depth:
            return pl.BlockSpec(block.shape, lambda j, place: (0, 0))
        return pl.BlockSpec((block.shape[0], depth), lambda j, place: (0, place[0]))

    return pl.pallas_call(
        project_kernel,
        grid_spec=pltpu.PrefetchScalarGridSpec(
            num_scalar_prefetch=1,
            grid=(ctx_count,),
            in_specs=[block_spec(block) for block in blocks]
            + [
                pl.BlockSpec(
                    (1, 1, depth, width),
                    lambda j, place: (
                        lax.rem(place[2] + head_step, head_count),
                        lax.rem(place[1] + j, ctx_count),
                        0,
                        0,
                    ),
                )
            ],
            out_specs=pl.BlockSpec((1, row_total, width), lambda j, place: (j, 0, 0)),
            scratch_shapes=[pltpu.VMEM((row_total, depth), weights.dtype)],
        ),
        out_shape=jax.ShapeDtypeStruct((ctx_count, row_total, width), out_dtype),
        compiler_params=params(),
        cost_estimate=LONG,
        name="project",
    )(place, *blocks, weights)


def pick_kernel(heads, ctx_count, place_ref, table_ref, *refs):
    pool_refs, (keys, values) = refs[:ctx_count], refs[ctx_count:]
    blocks, length, columns = pool_refs[0].shape
    wide = columns // 2
    width = wide // heads
    values[wide:, :] = jnp.ones_like(values[wide:, :])
    for at in range(table_ref.shape[0]):
        entry = table_ref[at]
        here = slice(at * length, (at + 1) * length)
        step = lax.rem(place_ref[1] - entry // blocks + ctx_count, ctx_count)
        for ctx_step, pool_ref in enumerate(pool_refs):

            @pl.when(step == ctx_step)
            def _():
                block = pool_ref[entry % blocks]
                keys[here, :] = block[:, :wide]
                for head in range(heads):
                    low = wide + head * length
                    values[head * width : (head + 1) * width, here] = block[:, low : low + length]


def pick_blocks(place, table, pools, heads):
    length, columns = pools[0].shape[1:]
    count = table.shape[0] * length
    wide = columns // 2
    return pl.pallas_call(
        functools.partial(pick_kernel, heads, len(pools)),
        grid_spec=pltpu.PrefetchScalarGridSpec(
            num_scalar_prefetch=2,
            grid=(1,),
            in_specs=[pl.BlockSpec(p.shape, lambda i, *_: (0, 0, 0)) for p in pools],
            out_specs=[
                pl.BlockSpec((count, wide), lambda i, *_: (0, 0)),
                pl.BlockSpec((wide + 16, count), lambda i, *_: (0, 0)),
            ],
        ),
        out_shape=[
            jax.ShapeDtypeStruct((count, wide), jnp.bfloat16),
            jax.ShapeDtypeStruct((wide + 16, count), jnp.bfloat16),
        ],
        compiler_params=params(),
        cost_estimate=LONG,
        name="pick_blocks",
    )(place, table, *pools)


def prefix_kernel(scale, heads, query_ref, keys, values, acc_ref, stat_ref, mask):
    rows, width = query_ref.shape
    part_rows = mask.shape[0]
    wide = heads * width

    @pl.when(pl.program_id(0) == 0)
    def _():
        mask[...] = head_mask(mask.shape, heads)

    for part in range(rows // part_rows):
        here = slice(part * part_rows, (part + 1) * part_rows)
        query_block = jnp.concatenate([query_ref[here, :]] * heads, 1) * mask[...]
        row_max, weights = softmax_parts(dot_queries(keys[...], query_block) * scale)
        mixed = jnp.dot(values[...], weights, preferred_element_type=jnp.float32)
        acc_ref[:, here] = own_head(mixed, heads, width)
        half = stat_ref.shape[0] // 2
        stat_ref[:half, here] = jnp.broadcast_to(row_max, (half, part_rows))
        stat_ref[half:, here] = jnp.broadcast_to(mixed[wide : wide + 1], (half, part_rows))


def prefix_attend(query_rows, keys, values, piece, scale, heads):
    all_rows, width = query_rows.shape
    row_total = all_rows // CHUNKS
    rows = min(1024, row_total)
    steps = row_total // rows
    key_count, wide = keys.shape
    return pl.pallas_call(
        functools.partial(prefix_kernel, scale, heads),
        grid=(steps,),
        in_specs=[
            pl.BlockSpec((rows, width), lambda i: (piece * steps + i, 0)),
            pl.BlockSpec(keys.shape, lambda i: (0, 0)),
            pl.BlockSpec(values.shape, lambda i: (0, 0)),
        ],
        out_specs=[
            pl.BlockSpec((width, rows), lambda i: (0, i)),
            pl.BlockSpec((8, rows), lambda i: (0, i)),
        ],
        out_shape=[
            jax.ShapeDtypeStruct((width, row_total), jnp.float32),
            jax.ShapeDtypeStruct((8, row_total), jnp.float32),
        ],
        scratch_shapes=[pltpu.VMEM((min(512, rows), wide), jnp.bfloat16)],
        compiler_params=params(),
        cost_estimate=LONG,
        name="prefix_attend",
    )(query_rows, keys, values)


def fresh_kernel(
    scale, heads, per_token, first_row, parts, length_ref, query_ref, acc_ref, stat_ref, *rest
):
    out_ref, keys, values, mask = rest[-4:]
    rows, width = query_ref.shape
    wide = heads * width
    step = pl.program_id(0)

    @pl.when(step == 0)
    def _():
        mask[...] = head_mask(mask.shape, heads)
        values[wide:, :] = jnp.ones_like(values[wide:, :])
        for index in range(parts):
            one, other = rest[2 * index], rest[2 * index + 1]
            here = slice(index * one.shape[0], (index + 1) * one.shape[0])
            fresh = (one[...].astype(jnp.float32) + other[...]).astype(jnp.bfloat16)
            keys[here, :] = fresh[:, :wide]
            values[:wide, here] = fresh[:, wide:].astype(jnp.float32).T.astype(jnp.bfloat16)

    part_rows = mask.shape[0]
    half = stat_ref.shape[0] // 2
    for part in range(rows // part_rows):
        here = slice(part * part_rows, (part + 1) * part_rows)
        query_block = jnp.concatenate([query_ref[here, :]] * heads, 1) * mask[...]
        scores = dot_queries(keys[...], query_block) * scale
        row = part * part_rows + lax.broadcasted_iota(jnp.int32, (1, part_rows), 1)
        token = first_row + step * (rows // per_token) + (
            row // per_token if per_token & (per_token - 1) else row >> (per_token.bit_length() - 1)
        )
        key_at = lax.broadcasted_iota(jnp.int32, scores.shape, 0)
        scores = jnp.where(key_at <= token, scores, -jnp.inf)
        old_max, old_total = stat_ref[:1, here], stat_ref[half : half + 1, here]
        row_max, weights = softmax_parts(scores, old_max)
        fade = jnp.exp2(old_max - row_max)
        mixed = jnp.dot(values[...], weights, preferred_element_type=jnp.float32)
        row_total = old_total * fade + mixed[wide : wide + 1]
        share = jnp.where(token < length_ref[0], 1.0 / row_total, 0.0)
        result = acc_ref[:, here] * (fade * share) + own_head(mixed, heads, width) * share
        out_ref[here, :] = result.T.astype(out_ref.dtype)


def fresh_attend(length, query_rows, acc, stat, parts, earlier, chunk, scale, heads, per_token):
    row_total, width = query_rows.shape
    chunk_rows = row_total // CHUNKS
    rows = min(1024, chunk_rows)
    steps = chunk_rows // rows
    block = pl.BlockSpec((rows, width), lambda i, length: (chunk * steps + i, 0))
    terms = [term for pair in parts for term in pair]
    key_count = sum(pair[0].shape[0] for pair in parts)
    in_specs = [
        block,
        pl.BlockSpec((width, rows), lambda i, length: (0, i)),
        pl.BlockSpec((stat.shape[0], rows), lambda i, length: (0, i)),
    ] + [pl.BlockSpec(term.shape, lambda i, length: (0, 0)) for term in terms]
    operands = [length, query_rows, acc, stat, *terms]
    aliases = {}
    if earlier is not None:
        in_specs.append(pl.BlockSpec(memory_space=pl.ANY))
        aliases = {len(operands): 0}
        operands.append(earlier)
    return pl.pallas_call(
        functools.partial(
            fresh_kernel, scale, heads, per_token, chunk * (chunk_rows // per_token), len(parts)
        ),
        grid_spec=pltpu.PrefetchScalarGridSpec(
            num_scalar_prefetch=1,
            grid=(steps,),
            in_specs=in_specs,
            out_specs=block,
            scratch_shapes=[
                pltpu.VMEM((key_count, heads * width), jnp.bfloat16),
                pltpu.VMEM((heads * width + 16, key_count), jnp.bfloat16),
                pltpu.VMEM((min(512, rows), heads * width), jnp.bfloat16),
            ],
        ),
        out_shape=jax.ShapeDtypeStruct((row_total, width), jnp.bfloat16),
        input_output_aliases=aliases,
        compiler_params=params(),
        cost_estimate=LONG,
        name="fresh_attend",
    )(*operands)


def reduced_shards(tokens, key_weight, value_weight, queries, prefix_pool, block_table, lengths):
    batch_count = lax.axis_size("batch")
    ctx_count = lax.axis_size("ctx")
    head_count = lax.axis_size("head")
    batch_at, ctx_at, head_at = (lax.axis_index(a) for a in ("batch", "ctx", "head"))
    place = jnp.stack([batch_at, ctx_at, head_at]).astype(jnp.int32)
    token_count = tokens.shape[0]
    heads = queries.shape[1]
    width = prefix_pool.shape[4] // 2
    group = queries.shape[3] // width
    per_token = heads * group
    depth = key_weight.shape[2]
    rows = token_count // CHUNKS
    scale = math.log2(math.e) / math.sqrt(width)

    def leaving(bits, first, count):
        start = (batch_at ^ bits) * depth
        return lax.dynamic_slice(tokens, (first, start), (count, depth))

    top = batch_count // 2
    steps = [bits for bits in range(1, batch_count) if bits != top]
    pieces = [leaving(bits, 0, token_count) for bits in steps] + [leaving(top, 0, rows)]
    pieces, prefix_pool = after(pieces, prefix_pool)
    arrived = [trade(piece, "batch", bits) for piece, bits in zip(pieces, [*steps, top])]
    arrived, last = after(arrived, leaving(top, rows, rows))
    last = trade(last, "batch", top)

    pools = arrange_pool(place, prefix_pool, ctx_count, heads)
    pools, (key_weight, value_weight) = after(pools, (key_weight, value_weight))
    pools = [shift(part, "ctx", step) if step else part for step, part in enumerate(pools)]

    weights = arrange_weights(key_weight, value_weight, ctx_count, heads, head_count)

    query_rows = queries.reshape(token_count, heads, group, width)
    query_rows = query_rows.transpose(0, 2, 1, 3).reshape(-1, width)
    def projected(blocks):
        terms = [
            shift(project(place, blocks, weights, step, jnp.bfloat16), "head", step)
            for step in range(1, head_count)
        ]
        total = project(place, blocks, weights, 0, jnp.float32)

        def of(step):
            return sum((term[step].astype(jnp.float32) for term in terms), total[step])

        return of(0), [of(step).astype(jnp.bfloat16) for step in range(1, ctx_count)]

    def spread(others, here=slice(None)):
        return [shift(other[here], "ctx", step + 1) for step, other in enumerate(others)]

    def summed(mine, others):
        return sum((other.astype(jnp.float32) for other in others), mine)

    mine, others = projected([*arrived, tokens])
    far, near = slice(0, len(steps) * token_count), slice(len(steps) * token_count, None)
    far_others = spread(others, far)
    others, pools = after(others, pools)
    near_others = spread(others, near)
    keys, values = pick_blocks(place, block_table[0], pools, heads)
    states = [prefix_attend(query_rows, keys, values, 0, scale, heads)]
    states[0], last = after(states[0], last)

    last_mine, last_others = projected([last])
    last_others, (keys, values) = after(last_others, (keys, values))
    last_others = spread(last_others)
    states.append(prefix_attend(query_rows, keys, values, 1, scale, heads))

    mine = [mine[far], summed(mine[near], near_others)]
    away, home = mine[1][:rows], mine[1][rows:]
    if steps:
        far = trade(summed(mine[0], far_others).astype(jnp.bfloat16), "batch", 1)
        home = home + far[:token_count].astype(jnp.float32)
        away = away + far[token_count : token_count + rows].astype(jnp.float32)
        far, last_others = after(far, last_others)
        last_mine = last_mine + far[token_count + rows :].astype(jnp.float32)
    away = [away, summed(last_mine, last_others)]
    away = [trade(part.astype(jnp.bfloat16), "batch", top) for part in away]
    parts = [(away[0], home[:rows]), (away[1], home[rows:])]

    result = None
    for chunk in range(CHUNKS):
        result = fresh_attend(
            lengths,
            query_rows,
            *states[chunk],
            parts[: chunk + 1],
            result,
            chunk,
            scale,
            heads,
            per_token,
        )
    result = result.reshape(token_count, group, heads, width).transpose(0, 2, 1, 3)
    return result.reshape(token_count, heads, 1, group * width)


def solution(mesh):
    def shards(tokens, key_weight, value_weight, *rest):
        prompts = mesh.shape["batch"]
        columns = 2 * math.prod(key_weight.shape[3:])
        few_tokens = prompts * tokens.shape[0] <= columns and prompts in (2, 4)
        form = reduced_shards if few_tokens else gathered_shards
        return form(tokens, key_weight, value_weight, *rest)

    return jax.shard_map(
        shards,
        mesh=mesh,
        in_specs=(
            P(("groups", "batch"), ("ctx", "head")),
            P("ctx", "head", "batch", None, None, None),
            P("ctx", "head", "batch", None, None, None),
            P(("groups", "batch"), "ctx", "head", None),
            P(("groups", "ctx"), None, None, "head", None),
            P(("groups", "batch"), None),
            P(("groups", "batch")),
        ),
        out_specs=P(("groups", "batch"), "ctx", "head", None),
        check_vma=False,
    )
```

```python
import functools
import math

import jax
import jax.numpy as jnp
from jax import lax
from jax.experimental import pallas as pl
from jax.experimental.pallas import tpu as pltpu
from jax.sharding import PartitionSpec as P

CHUNKS = 2
PART = 512
ONES = 16
VMEM_BYTES = 24 * 1024 * 1024
LONG = pl.CostEstimate(flops=10**11, bytes_accessed=1, transcendentals=0)
COSTS = {}


def cost(name):
    return COSTS.get(name, LONG)


def attend_head(query_rows, prefix, fresh_rows, length):
    token_count = query_rows.shape[0]
    head_width = prefix.shape[1] // 2
    group_size = query_rows.shape[1] // head_width
    prefix_len = prefix.shape[0]
    key_rows = jnp.concatenate([prefix[:, :head_width], fresh_rows[:, :head_width]], 0)
    value_rows = jnp.concatenate([prefix[:, head_width:], fresh_rows[:, head_width:]], 0)
    block_len = min(token_count, 64)
    pieces = []
    for first_row in range(0, token_count, block_len):
        block_rows = query_rows[first_row : first_row + block_len].reshape(
            block_len * group_size, head_width
        )
        scores = jnp.dot(
            block_rows, key_rows.T, preferred_element_type=jnp.float32
        ) * head_width ** (-0.5)
        position = first_row + jnp.arange(block_len * group_size) // group_size
        column = jnp.arange(prefix_len + token_count) - prefix_len
        allowed = column[None, :] <= position[:, None]
        scores = jnp.where(allowed, scores, -jnp.inf)
        row_max = jnp.max(scores, axis=1, keepdims=True)
        weights = jnp.exp(scores - row_max)
        row_total = jnp.sum(weights, axis=1, keepdims=True)
        probs_bf = (weights / row_total).astype(jnp.bfloat16)
        mixed_rows = jnp.dot(probs_bf, value_rows, preferred_element_type=jnp.float32)
        is_live = position < length
        mixed_rows = jnp.where(is_live[:, None], mixed_rows, 0.0)
        pieces.append(mixed_rows.astype(jnp.bfloat16).reshape(block_len, group_size * head_width))
    return jnp.concatenate(pieces, 0)


def gathered_shards(tokens, key_weight, value_weight, queries, prefix_pool, block_table, lengths):
    token_count = tokens.shape[0]
    local_heads = queries.shape[1]
    head_width = prefix_pool.shape[4] // 2
    ctx_count = lax.axis_size("ctx")
    head_count = lax.axis_size("head")
    features = lax.all_gather(tokens, ("ctx", "head"), axis=1, tiled=True)
    key_cols, value_cols = (
        lax.all_to_all(
            lax.all_to_all(weight, "ctx", split_axis=3, concat_axis=0, tiled=True),
            "head",
            split_axis=4,
            concat_axis=1,
            tiled=True,
        )
        for weight in (key_weight, value_weight)
    )
    span_len = features.shape[1] // (ctx_count * head_count)
    feature_view = features.reshape(token_count, ctx_count, head_count, span_len)
    pieces = (
        lax.all_gather(key_cols, "batch", axis=2, tiled=True),
        lax.all_gather(value_cols, "batch", axis=2, tiled=True),
    )
    row_count = pieces[0].shape[2]

    def one_term(weight_piece):
        shaped = weight_piece.reshape(ctx_count, head_count, row_count, local_heads * head_width)
        return jnp.einsum("tchr,chrk->tk", feature_view, shaped, preferred_element_type=jnp.float32)

    new_keys = one_term(pieces[0]).astype(jnp.bfloat16).reshape(token_count, local_heads, head_width)
    new_values = one_term(pieces[1]).astype(jnp.bfloat16).reshape(token_count, local_heads, head_width)
    fresh_all = jnp.concatenate([new_keys, new_values], 2)
    pool_heads = lax.all_to_all(prefix_pool, "ctx", split_axis=2, concat_axis=0, tiled=True)
    chosen = jnp.take(pool_heads, block_table[0], axis=0)
    chosen = chosen.reshape(-1, local_heads, 2 * head_width)
    outputs = [
        attend_head(
            queries[:, head_idx, 0], chosen[:, head_idx], fresh_all[:, head_idx], lengths[0]
        )
        for head_idx in range(local_heads)
    ]
    return jnp.stack(outputs, 1)[:, :, None, :]


def shift(array, axis, step):
    count = lax.axis_size(axis)
    return lax.ppermute(array, axis, [(i, (i + step) % count) for i in range(count)])


def trade(array, axis, bits):
    return lax.ppermute(array, axis, [(i, i ^ bits) for i in range(lax.axis_size(axis))])


def after(first, second):
    return lax.optimization_barrier((first, second))


def softmax_parts(scores, old_max=None):
    row_max = jnp.max(scores, axis=0, keepdims=True)
    if old_max is not None:
        row_max = jnp.maximum(row_max, old_max)
    return row_max, jnp.exp2(scores - row_max).astype(jnp.bfloat16)


def dot_queries(keys, query_block):
    return lax.dot_general(
        keys, query_block, (((1,), (1,)), ((), ())), preferred_element_type=jnp.float32
    )


def params():
    return pltpu.CompilerParams(vmem_limit_bytes=VMEM_BYTES)


def weight_kernel(ctx_count, heads, head_count, key_ref, value_ref, out_ref, flat):
    depth, slots, width = key_ref.shape
    for kind, ref in enumerate((key_ref, value_ref)):
        flat[...] = ref[...].astype(jnp.float32).reshape(depth * slots, width)
        for ctx in range(ctx_count):
            for head in range(heads):
                for core in range(head_count):
                    slot = (ctx * heads + head) * head_count + core
                    at = (kind * heads + head) * width
                    out_ref[core, ctx, :, at : at + width] = flat[
                        pl.ds(slot, depth, stride=slots), :
                    ].astype(out_ref.dtype)


def arrange_weights(key_weight, value_weight, ctx_count, heads, head_count):
    depth, width = key_weight.shape[2], key_weight.shape[5]
    slots = ctx_count * heads * head_count
    rows = min(128, depth)
    views = [w.reshape(depth, slots, width) for w in (key_weight, value_weight)]
    block = pl.BlockSpec((rows, slots, width), lambda i: (i, 0, 0))
    columns = 2 * heads * width
    return pl.pallas_call(
        functools.partial(weight_kernel, ctx_count, heads, head_count),
        grid=(depth // rows,),
        in_specs=[block, block],
        out_specs=pl.BlockSpec((head_count, ctx_count, rows, columns), lambda i: (0, 0, i, 0)),
        out_shape=jax.ShapeDtypeStruct((head_count, ctx_count, depth, columns), jnp.bfloat16),
        scratch_shapes=[pltpu.VMEM((rows * slots, width), jnp.float32)],
        compiler_params=params(),
        cost_estimate=cost("arrange_weights"),
        name="arrange_weights",
    )(*views)


def pool_kernel(ctx_count, heads, place_ref, pool_ref, *refs):
    flat, outs = refs[-1], refs[:-1]
    length, slots, width = pool_ref.shape[1:]
    flat[...] = pool_ref[0].astype(jnp.float32).reshape(length * slots, width)
    for kind in range(2):
        for head in range(heads):
            at = (kind * heads + head) * width
            held = []
            for ctx in range(ctx_count):
                slot = (kind * ctx_count + ctx) * heads + head
                held.append(flat[pl.ds(slot, length, stride=slots), :])
            for step, out_ref in enumerate(outs):
                target = lax.rem(place_ref[1] + step, ctx_count)
                value = held[0]
                for ctx in range(1, ctx_count):
                    value = jnp.where(target == ctx, held[ctx], value)
                out_ref[0, :, at : at + width] = value.astype(out_ref.dtype)


def arrange_pool(place, prefix_pool, ctx_count, heads):
    blocks, length, all_heads, _, double = prefix_pool.shape
    width = double // 2
    slots = 2 * all_heads
    view = prefix_pool.reshape(blocks, length, all_heads, 2, width)
    view = view.transpose(0, 1, 3, 2, 4).reshape(blocks, length, slots, width)
    columns = 2 * heads * width
    out = pl.BlockSpec((1, length, columns), lambda i, place: (i, 0, 0))
    return pl.pallas_call(
        functools.partial(pool_kernel, ctx_count, heads),
        grid_spec=pltpu.PrefetchScalarGridSpec(
            num_scalar_prefetch=1,
            grid=(blocks,),
            in_specs=[pl.BlockSpec((1, length, slots, width), lambda i, place: (i, 0, 0, 0))],
            out_specs=[out] * ctx_count,
            scratch_shapes=[pltpu.VMEM((length * slots, width), jnp.float32)],
        ),
        out_shape=[jax.ShapeDtypeStruct((blocks, length, columns), jnp.bfloat16)] * ctx_count,
        compiler_params=params(),
        cost_estimate=cost("arrange_pool"),
        name="arrange_pool",
    )(place, view)


def project_kernel(place_ref, *refs):
    token_refs, (weight_ref, out_ref, stacked) = refs[:-3], refs[-3:]

    @pl.when(pl.program_id(0) == 0)
    def _():
        at = 0
        for token_ref in token_refs:
            rows = token_ref.shape[0]
            stacked[at : at + rows, :] = token_ref[...]
            at += rows

    out_ref[0] = jnp.dot(
        stacked[...], weight_ref[0, 0], preferred_element_type=jnp.float32
    ).astype(out_ref.dtype)


def project(place, blocks, weights, head_step, out_dtype, name):
    head_count, ctx_count, depth, width = weights.shape
    row_total = sum(block.shape[0] for block in blocks)

    def block_spec(block):
        if block.shape[1] == depth:
            return pl.BlockSpec(block.shape, lambda j, place: (0, 0))
        return pl.BlockSpec((block.shape[0], depth), lambda j, place: (0, place[0]))

    return pl.pallas_call(
        project_kernel,
        grid_spec=pltpu.PrefetchScalarGridSpec(
            num_scalar_prefetch=1,
            grid=(ctx_count,),
            in_specs=[block_spec(block) for block in blocks]
            + [
                pl.BlockSpec(
                    (1, 1, depth, width),
                    lambda j, place: (
                        lax.rem(place[2] + head_step, head_count),
                        lax.rem(place[1] + j, ctx_count),
                        0,
                        0,
                    ),
                )
            ],
            out_specs=pl.BlockSpec((1, row_total, width), lambda j, place: (j, 0, 0)),
            scratch_shapes=[pltpu.VMEM((row_total, depth), weights.dtype)],
        ),
        out_shape=jax.ShapeDtypeStruct((ctx_count, row_total, width), out_dtype),
        compiler_params=params(),
        cost_estimate=cost(name),
        name=name,
    )(place, *blocks, weights)


def pick_kernel(heads, ctx_count, place_ref, table_ref, *refs):
    pool_refs, (keys, values) = refs[:ctx_count], refs[ctx_count:]
    blocks, length, columns = pool_refs[0].shape
    wide = columns // 2
    width = wide // heads
    values[...] = jnp.ones_like(values)
    for at in range(table_ref.shape[0]):
        entry = table_ref[at]
        here = slice(at * length, (at + 1) * length)
        step = lax.rem(place_ref[1] - entry // blocks + ctx_count, ctx_count)
        for ctx_step, pool_ref in enumerate(pool_refs):

            @pl.when(step == ctx_step)
            def _():
                block = pool_ref[entry % blocks]
                keys[here, :] = block[:, :wide]
                put_values(values, here, block[:, wide:], heads)


def put_values(values, here, block, heads):
    width = block.shape[1] // heads
    for head in range(heads):
        low = head * (width + ONES)
        values[low : low + width, here] = (
            block[:, head * width : (head + 1) * width].astype(jnp.float32).T.astype(jnp.bfloat16)
        )


def pick_blocks(place, table, pools, heads):
    length, columns = pools[0].shape[1:]
    count = table.shape[0] * length
    wide = columns // 2
    tall = wide + heads * ONES
    return pl.pallas_call(
        functools.partial(pick_kernel, heads, len(pools)),
        grid_spec=pltpu.PrefetchScalarGridSpec(
            num_scalar_prefetch=2,
            grid=(1,),
            in_specs=[pl.BlockSpec(p.shape, lambda i, *_: (0, 0, 0)) for p in pools],
            out_specs=[
                pl.BlockSpec((count, wide), lambda i, *_: (0, 0)),
                pl.BlockSpec((tall, count), lambda i, *_: (0, 0)),
            ],
        ),
        out_shape=[
            jax.ShapeDtypeStruct((count, wide), jnp.bfloat16),
            jax.ShapeDtypeStruct((tall, count), jnp.bfloat16),
        ],
        compiler_params=params(),
        cost_estimate=cost("pick_blocks"),
        name="pick_blocks",
    )(place, table, *pools)


def each_part(rows, heads):
    part_rows = min(PART, rows)
    each = part_rows // heads
    for low in range(0, rows, part_rows):
        for head in range(heads):
            at = low + head * each
            yield head, pl.ds(low + head, each, stride=heads), slice(at, at + each)


def prefix_kernel(scale, heads, query_ref, keys, values, acc_ref, stat_ref, flat):
    rows, width = query_ref.shape
    tall = width + ONES
    half = stat_ref.shape[0] // 2
    flat[...] = query_ref[...].astype(jnp.float32)
    for head, taken, here in each_part(rows, heads):
        query_block = flat[taken, :].astype(jnp.bfloat16)
        scores = dot_queries(keys[:, head * width : (head + 1) * width], query_block) * scale
        row_max, weights = softmax_parts(scores)
        mixed = jnp.dot(
            values[head * tall : (head + 1) * tall, :], weights, preferred_element_type=jnp.float32
        )
        acc_ref[:, here] = mixed[:width]
        stat_ref[:half, here] = jnp.broadcast_to(row_max, (half, row_max.shape[1]))
        stat_ref[half:, here] = jnp.broadcast_to(mixed[width : width + 1], (half, row_max.shape[1]))


def prefix_attend(query_rows, keys, values, chunk, scale, heads):
    all_rows, width = query_rows.shape
    row_total = all_rows // CHUNKS
    rows = min(1024, row_total)
    steps = row_total // rows
    return pl.pallas_call(
        functools.partial(prefix_kernel, scale, heads),
        grid=(steps,),
        in_specs=[
            pl.BlockSpec((rows, width), lambda i: (chunk * steps + i, 0)),
            pl.BlockSpec(keys.shape, lambda i: (0, 0)),
            pl.BlockSpec(values.shape, lambda i: (0, 0)),
        ],
        out_specs=[
            pl.BlockSpec((width, rows), lambda i: (0, i)),
            pl.BlockSpec((8, rows), lambda i: (0, i)),
        ],
        out_shape=[
            jax.ShapeDtypeStruct((width, row_total), jnp.float32),
            jax.ShapeDtypeStruct((8, row_total), jnp.float32),
        ],
        scratch_shapes=[pltpu.VMEM((rows, width), jnp.float32)],
        compiler_params=params(),
        cost_estimate=cost("prefix_attend"),
        name="prefix_attend",
    )(query_rows, keys, values)


def fresh_kernel(
    scale, heads, per_token, first_row, parts, length_ref, query_ref, acc_ref, stat_ref, *rest
):
    out_ref, keys, values, flat, mixed_rows = rest[-5:]
    rows, width = query_ref.shape
    wide, tall = heads * width, width + ONES
    step = pl.program_id(0)

    @pl.when(step == 0)
    def _():
        values[...] = jnp.ones_like(values)
        for index in range(parts):
            one, other = rest[2 * index], rest[2 * index + 1]
            here = slice(index * one.shape[0], (index + 1) * one.shape[0])
            fresh = (one[...].astype(jnp.float32) + other[...]).astype(jnp.bfloat16)
            keys[here, :] = fresh[:, :wide]
            put_values(values, here, fresh[:, wide:], heads)

    half = stat_ref.shape[0] // 2
    flat[...] = query_ref[...].astype(jnp.float32)
    for head, taken, here in each_part(rows, heads):
        query_block = flat[taken, :].astype(jnp.bfloat16)
        scores = dot_queries(keys[:, head * width : (head + 1) * width], query_block) * scale
        row = taken.start + heads * lax.broadcasted_iota(jnp.int32, (1, taken.size), 1)
        token = first_row + step * (rows // per_token) + (
            row // per_token if per_token & (per_token - 1) else row >> (per_token.bit_length() - 1)
        )
        key_at = lax.broadcasted_iota(jnp.int32, scores.shape, 0)
        scores = jnp.where(key_at <= token, scores, -jnp.inf)
        old_max, old_total = stat_ref[:1, here], stat_ref[half : half + 1, here]
        row_max, weights = softmax_parts(scores, old_max)
        fade = jnp.exp2(old_max - row_max)
        mixed = jnp.dot(
            values[head * tall : (head + 1) * tall, :], weights, preferred_element_type=jnp.float32
        )
        row_total = old_total * fade + mixed[width : width + 1]
        share = jnp.where(token < length_ref[0], 1.0 / row_total, 0.0)
        result = acc_ref[:, here] * (fade * share) + mixed[:width] * share
        mixed_rows[taken, :] = result.T
    out_ref[...] = mixed_rows[...].astype(out_ref.dtype)


def fresh_attend(length, query_rows, acc, stat, parts, earlier, chunk, scale, heads, per_token):
    row_total, width = query_rows.shape
    chunk_rows = row_total // CHUNKS
    rows = min(1024, chunk_rows)
    steps = chunk_rows // rows
    block = pl.BlockSpec((rows, width), lambda i, length: (chunk * steps + i, 0))
    terms = [term for pair in parts for term in pair]
    key_count = sum(pair[0].shape[0] for pair in parts)
    in_specs = [
        block,
        pl.BlockSpec((width, rows), lambda i, length: (0, i)),
        pl.BlockSpec((stat.shape[0], rows), lambda i, length: (0, i)),
    ] + [pl.BlockSpec(term.shape, lambda i, length: (0, 0)) for term in terms]
    operands = [length, query_rows, acc, stat, *terms]
    aliases = {}
    if earlier is not None:
        in_specs.append(pl.BlockSpec(memory_space=pl.ANY))
        aliases = {len(operands): 0}
        operands.append(earlier)
    return pl.pallas_call(
        functools.partial(
            fresh_kernel, scale, heads, per_token, chunk * (chunk_rows // per_token), len(parts)
        ),
        grid_spec=pltpu.PrefetchScalarGridSpec(
            num_scalar_prefetch=1,
            grid=(steps,),
            in_specs=in_specs,
            out_specs=block,
            scratch_shapes=[
                pltpu.VMEM((key_count, heads * width), jnp.bfloat16),
                pltpu.VMEM((heads * (width + ONES), key_count), jnp.bfloat16),
                pltpu.VMEM((rows, width), jnp.float32),
                pltpu.VMEM((rows, width), jnp.float32),
            ],
        ),
        out_shape=jax.ShapeDtypeStruct((row_total, width), jnp.bfloat16),
        input_output_aliases=aliases,
        compiler_params=params(),
        cost_estimate=cost("fresh_attend"),
        name="fresh_attend",
    )(*operands)


def cut_kernel(depth, bits, place_ref, tokens_ref, *refs):
    pieces, sems = refs[:-1], refs[-1]
    copies = []
    for index, piece in enumerate(pieces):
        start = pl.multiple_of((place_ref[0] ^ bits[index]) * depth, depth)
        copies.append(
            pltpu.make_async_copy(
                tokens_ref.at[:, pl.ds(start, depth)], piece, sems.at[index]
            )
        )
    for copy in copies:
        copy.start()
    for copy in copies:
        copy.wait()


def cut_tokens(place, tokens, depth, bits):
    anywhere = pl.BlockSpec(memory_space=pl.ANY)
    piece = jax.ShapeDtypeStruct((tokens.shape[0], depth), tokens.dtype)
    return pl.pallas_call(
        functools.partial(cut_kernel, depth, bits),
        grid_spec=pltpu.PrefetchScalarGridSpec(
            num_scalar_prefetch=1,
            grid=(1,),
            in_specs=[anywhere],
            out_specs=[anywhere] * len(bits),
            scratch_shapes=[pltpu.SemaphoreType.DMA((len(bits),))],
        ),
        out_shape=[piece] * len(bits),
        compiler_params=params(),
        cost_estimate=cost("cut_tokens"),
        name="cut_tokens",
    )(place, tokens)


def reduced_shards(tokens, key_weight, value_weight, queries, prefix_pool, block_table, lengths):
    batch_count = lax.axis_size("batch")
    ctx_count = lax.axis_size("ctx")
    head_count = lax.axis_size("head")
    batch_at, ctx_at, head_at = (lax.axis_index(a) for a in ("batch", "ctx", "head"))
    place = jnp.stack([batch_at, ctx_at, head_at]).astype(jnp.int32)
    token_count = tokens.shape[0]
    heads = queries.shape[1]
    width = prefix_pool.shape[4] // 2
    group = queries.shape[3] // width
    per_token = heads * group
    depth = key_weight.shape[2]
    rows = token_count // CHUNKS
    scale = math.log2(math.e) / math.sqrt(width)

    top = batch_count // 2
    steps = list(range(batch_count - 1, top, -1)) + list(range(1, top))
    pieces = cut_tokens(place, tokens, depth, [*steps, top])
    pieces, prefix_pool = after(pieces, prefix_pool)
    arrived = [trade(piece, "batch", bits) for piece, bits in zip(pieces, steps)]

    pools = arrange_pool(place, prefix_pool, ctx_count, heads)
    pools, (key_weight, value_weight) = after(pools, (key_weight, value_weight))
    pools = [shift(part, "ctx", step) if step else part for step, part in enumerate(pools)]

    weights = arrange_weights(key_weight, value_weight, ctx_count, heads, head_count)

    query_rows = queries.reshape(token_count, heads, group, width)
    query_rows = query_rows.transpose(0, 2, 1, 3).reshape(-1, width)
    def projected(blocks, name):
        terms = [
            shift(project(place, blocks, weights, step, jnp.bfloat16, name + "_away"), "head", step)
            for step in range(1, head_count)
        ]
        return [project(place, blocks, weights, 0, jnp.float32, name + "_kept"), *terms]

    def added(terms, step, here):
        return sum(term[step, here].astype(jnp.float32) for term in terms)

    def others(terms, here):
        return [added(terms, step, here).astype(jnp.bfloat16) for step in range(1, ctx_count)]

    def spread(parts):
        return [shift(part, "ctx", step + 1) for step, part in enumerate(parts)]

    def summed(terms, here, parts):
        return added(terms, 0, here) + sum(part.astype(jnp.float32) for part in parts)

    every = slice(None)
    parts_of = [slice(i * rows, (i + 1) * rows) for i in range(CHUNKS)]

    own = projected([tokens], "own")
    own[0], last = after(own[0], pieces[-1])
    last = trade(last, "batch", top)
    own_others = others(own, every)
    own_others = spread(own_others)

    if steps:
        early = projected(arrived, "early")
        cuts = [slice(i * token_count, (i + 1) * token_count) for i in range(len(steps))]
        far_others = spread(others(early, cuts[0]))
        near_others, pools = after(others(early, cuts[1]), pools)
        near_others = spread(near_others)
    keys, values = pick_blocks(place, block_table[0], pools, heads)
    states = [prefix_attend(query_rows, keys, values, 0, scale, heads)]
    states[0], last = after(states[0], last)
    if steps:
        far = summed(early, cuts[0], far_others).astype(jnp.bfloat16)
        far, last = after(far, last)
        far = trade(far, "batch", 1)

    late = projected([last], "late")
    late_others = [others(late, here) for here in parts_of]
    waiting = (keys, values, near_others) if steps else (keys, values)
    late_others[-1], waiting = after(late_others[-1], waiting)
    keys, values, *near_others = waiting
    late_others = [spread(part) for part in late_others]
    states.append(prefix_attend(query_rows, keys, values, 1, scale, heads))
    states[1], late_others[0] = after(states[1], late_others[0])

    home = summed(own, every, own_others)
    if steps:
        near_others = near_others[0]
        near = trade(summed(early, cuts[1], near_others).astype(jnp.bfloat16), "batch", 1)
        home = home + near.astype(jnp.float32)
    parts = []
    for chunk, here in enumerate(parts_of):
        part = summed(late, here, late_others[chunk])
        if steps:
            part = part + far[here].astype(jnp.float32)
            if chunk + 1 < CHUNKS:
                (far, late), late_others[chunk + 1] = after((far, late), late_others[chunk + 1])
        parts.append((trade(part.astype(jnp.bfloat16), "batch", top), home[here]))

    result = None
    for chunk in range(CHUNKS):
        result = fresh_attend(
            lengths,
            query_rows,
            *states[chunk],
            parts[: chunk + 1],
            result,
            chunk,
            scale,
            heads,
            per_token,
        )
    result = result.reshape(token_count, group, heads, width).transpose(0, 2, 1, 3)
    return result.reshape(token_count, heads, 1, group * width)


def solution(mesh):
    def shards(tokens, key_weight, value_weight, *rest):
        prompts = mesh.shape["batch"]
        columns = 2 * math.prod(key_weight.shape[3:])
        few_tokens = prompts * tokens.shape[0] <= columns and prompts in (2, 4)
        form = reduced_shards if few_tokens else gathered_shards
        return form(tokens, key_weight, value_weight, *rest)

    return jax.shard_map(
        shards,
        mesh=mesh,
        in_specs=(
            P(("groups", "batch"), ("ctx", "head")),
            P("ctx", "head", "batch", None, None, None),
            P("ctx", "head", "batch", None, None, None),
            P(("groups", "batch"), "ctx", "head", None),
            P(("groups", "ctx"), None, None, "head", None),
            P(("groups", "batch"), None),
            P(("groups", "batch")),
        ),
        out_specs=P(("groups", "batch"), "ctx", "head", None),
        check_vma=False,
    )
```

```python
import functools
import math

import jax
import jax.numpy as jnp
from jax import lax
from jax.experimental import pallas as pl
from jax.experimental.pallas import tpu as pltpu
from jax.sharding import PartitionSpec as P

CHUNKS = 2
PART = 1024
ONES = 16
VMEM_BYTES = 24 * 1024 * 1024
LONG = pl.CostEstimate(flops=10**11, bytes_accessed=1, transcendentals=0)
COSTS = {}


def cost(name):
    return COSTS.get(name, LONG)


def attend_head(query_rows, prefix, fresh_rows, length):
    token_count = query_rows.shape[0]
    head_width = prefix.shape[1] // 2
    group_size = query_rows.shape[1] // head_width
    prefix_len = prefix.shape[0]
    key_rows = jnp.concatenate([prefix[:, :head_width], fresh_rows[:, :head_width]], 0)
    value_rows = jnp.concatenate([prefix[:, head_width:], fresh_rows[:, head_width:]], 0)
    block_len = min(token_count, 64)
    pieces = []
    for first_row in range(0, token_count, block_len):
        block_rows = query_rows[first_row : first_row + block_len].reshape(
            block_len * group_size, head_width
        )
        scores = jnp.dot(
            block_rows, key_rows.T, preferred_element_type=jnp.float32
        ) * head_width ** (-0.5)
        position = first_row + jnp.arange(block_len * group_size) // group_size
        column = jnp.arange(prefix_len + token_count) - prefix_len
        allowed = column[None, :] <= position[:, None]
        scores = jnp.where(allowed, scores, -jnp.inf)
        row_max = jnp.max(scores, axis=1, keepdims=True)
        weights = jnp.exp(scores - row_max)
        row_total = jnp.sum(weights, axis=1, keepdims=True)
        probs_bf = (weights / row_total).astype(jnp.bfloat16)
        mixed_rows = jnp.dot(probs_bf, value_rows, preferred_element_type=jnp.float32)
        is_live = position < length
        mixed_rows = jnp.where(is_live[:, None], mixed_rows, 0.0)
        pieces.append(mixed_rows.astype(jnp.bfloat16).reshape(block_len, group_size * head_width))
    return jnp.concatenate(pieces, 0)


def gathered_shards(tokens, key_weight, value_weight, queries, prefix_pool, block_table, lengths):
    token_count = tokens.shape[0]
    local_heads = queries.shape[1]
    head_width = prefix_pool.shape[4] // 2
    ctx_count = lax.axis_size("ctx")
    head_count = lax.axis_size("head")
    features = lax.all_gather(tokens, ("ctx", "head"), axis=1, tiled=True)
    key_cols, value_cols = (
        lax.all_to_all(
            lax.all_to_all(weight, "ctx", split_axis=3, concat_axis=0, tiled=True),
            "head",
            split_axis=4,
            concat_axis=1,
            tiled=True,
        )
        for weight in (key_weight, value_weight)
    )
    span_len = features.shape[1] // (ctx_count * head_count)
    feature_view = features.reshape(token_count, ctx_count, head_count, span_len)
    pieces = (
        lax.all_gather(key_cols, "batch", axis=2, tiled=True),
        lax.all_gather(value_cols, "batch", axis=2, tiled=True),
    )
    row_count = pieces[0].shape[2]

    def one_term(weight_piece):
        shaped = weight_piece.reshape(ctx_count, head_count, row_count, local_heads * head_width)
        return jnp.einsum("tchr,chrk->tk", feature_view, shaped, preferred_element_type=jnp.float32)

    new_keys = one_term(pieces[0]).astype(jnp.bfloat16).reshape(token_count, local_heads, head_width)
    new_values = one_term(pieces[1]).astype(jnp.bfloat16).reshape(token_count, local_heads, head_width)
    fresh_all = jnp.concatenate([new_keys, new_values], 2)
    pool_heads = lax.all_to_all(prefix_pool, "ctx", split_axis=2, concat_axis=0, tiled=True)
    chosen = jnp.take(pool_heads, block_table[0], axis=0)
    chosen = chosen.reshape(-1, local_heads, 2 * head_width)
    outputs = [
        attend_head(
            queries[:, head_idx, 0], chosen[:, head_idx], fresh_all[:, head_idx], lengths[0]
        )
        for head_idx in range(local_heads)
    ]
    return jnp.stack(outputs, 1)[:, :, None, :]


def shift(array, axis, step):
    count = lax.axis_size(axis)
    return lax.ppermute(array, axis, [(i, (i + step) % count) for i in range(count)])


def trade(array, axis, bits):
    return lax.ppermute(array, axis, [(i, i ^ bits) for i in range(lax.axis_size(axis))])


def after(first, second):
    return lax.optimization_barrier((first, second))


def softmax_parts(scores, old_max=None):
    row_max = jnp.max(scores, axis=0, keepdims=True)
    if old_max is not None:
        row_max = jnp.maximum(row_max, old_max)
    return row_max, jnp.exp2(scores - row_max).astype(jnp.bfloat16)


def dot_queries(keys, query_block):
    return lax.dot_general(
        keys, query_block, (((1,), (1,)), ((), ())), preferred_element_type=jnp.float32
    )


def params():
    return pltpu.CompilerParams(vmem_limit_bytes=VMEM_BYTES)


def weight_kernel(ctx_count, heads, head_count, key_ref, value_ref, out_ref, flat):
    depth, slots, width = key_ref.shape
    for kind, ref in enumerate((key_ref, value_ref)):
        flat[...] = ref[...].astype(jnp.float32).reshape(depth * slots, width)
        for ctx in range(ctx_count):
            for head in range(heads):
                for core in range(head_count):
                    slot = (ctx * heads + head) * head_count + core
                    at = (kind * heads + head) * width
                    out_ref[core, ctx, :, at : at + width] = flat[
                        pl.ds(slot, depth, stride=slots), :
                    ].astype(out_ref.dtype)


def arrange_weights(key_weight, value_weight, ctx_count, heads, head_count):
    depth, width = key_weight.shape[2], key_weight.shape[5]
    slots = ctx_count * heads * head_count
    rows = min(128, depth)
    views = [w.reshape(depth, slots, width) for w in (key_weight, value_weight)]
    block = pl.BlockSpec((rows, slots, width), lambda i: (i, 0, 0))
    columns = 2 * heads * width
    return pl.pallas_call(
        functools.partial(weight_kernel, ctx_count, heads, head_count),
        grid=(depth // rows,),
        in_specs=[block, block],
        out_specs=pl.BlockSpec((head_count, ctx_count, rows, columns), lambda i: (0, 0, i, 0)),
        out_shape=jax.ShapeDtypeStruct((head_count, ctx_count, depth, columns), jnp.bfloat16),
        scratch_shapes=[pltpu.VMEM((rows * slots, width), jnp.float32)],
        compiler_params=params(),
        cost_estimate=cost("arrange_weights"),
        name="arrange_weights",
    )(*views)


def pool_kernel(ctx_count, heads, place_ref, pool_ref, *refs):
    flat, outs = refs[-1], refs[:-1]
    length, slots, width = pool_ref.shape[1:]
    flat[...] = pool_ref[0].astype(jnp.float32).reshape(length * slots, width)
    for kind in range(2):
        for head in range(heads):
            at = (kind * heads + head) * width
            held = []
            for ctx in range(ctx_count):
                slot = (kind * ctx_count + ctx) * heads + head
                held.append(flat[pl.ds(slot, length, stride=slots), :])
            for step, out_ref in enumerate(outs):
                target = lax.rem(place_ref[1] + step, ctx_count)
                value = held[0]
                for ctx in range(1, ctx_count):
                    value = jnp.where(target == ctx, held[ctx], value)
                out_ref[0, :, at : at + width] = value.astype(out_ref.dtype)


def arrange_pool(place, prefix_pool, ctx_count, heads):
    blocks, length, all_heads, _, double = prefix_pool.shape
    width = double // 2
    slots = 2 * all_heads
    view = prefix_pool.reshape(blocks, length, all_heads, 2, width)
    view = view.transpose(0, 1, 3, 2, 4).reshape(blocks, length, slots, width)
    columns = 2 * heads * width
    out = pl.BlockSpec((1, length, columns), lambda i, place: (i, 0, 0))
    return pl.pallas_call(
        functools.partial(pool_kernel, ctx_count, heads),
        grid_spec=pltpu.PrefetchScalarGridSpec(
            num_scalar_prefetch=1,
            grid=(blocks,),
            in_specs=[pl.BlockSpec((1, length, slots, width), lambda i, place: (i, 0, 0, 0))],
            out_specs=[out] * ctx_count,
            scratch_shapes=[pltpu.VMEM((length * slots, width), jnp.float32)],
        ),
        out_shape=[jax.ShapeDtypeStruct((blocks, length, columns), jnp.bfloat16)] * ctx_count,
        compiler_params=params(),
        cost_estimate=cost("arrange_pool"),
        name="arrange_pool",
    )(place, view)


def project_kernel(place_ref, *refs):
    token_refs, (weight_ref, out_ref, stacked) = refs[:-3], refs[-3:]

    @pl.when(pl.program_id(0) == 0)
    def _():
        at = 0
        for token_ref in token_refs:
            rows = token_ref.shape[0]
            stacked[at : at + rows, :] = token_ref[...]
            at += rows

    out_ref[0] = jnp.dot(
        stacked[...], weight_ref[0, 0], preferred_element_type=jnp.float32
    ).astype(out_ref.dtype)


def project(place, blocks, weights, head_step, out_dtype, name):
    head_count, ctx_count, depth, width = weights.shape
    row_total = sum(block.shape[0] for block in blocks)

    def block_spec(block):
        if block.shape[1] == depth:
            return pl.BlockSpec(block.shape, lambda j, place: (0, 0))
        return pl.BlockSpec((block.shape[0], depth), lambda j, place: (0, place[0]))

    return pl.pallas_call(
        project_kernel,
        grid_spec=pltpu.PrefetchScalarGridSpec(
            num_scalar_prefetch=1,
            grid=(ctx_count,),
            in_specs=[block_spec(block) for block in blocks]
            + [
                pl.BlockSpec(
                    (1, 1, depth, width),
                    lambda j, place: (
                        lax.rem(place[2] + head_step, head_count),
                        lax.rem(place[1] + j, ctx_count),
                        0,
                        0,
                    ),
                )
            ],
            out_specs=pl.BlockSpec((1, row_total, width), lambda j, place: (j, 0, 0)),
            scratch_shapes=[pltpu.VMEM((row_total, depth), weights.dtype)],
        ),
        out_shape=jax.ShapeDtypeStruct((ctx_count, row_total, width), out_dtype),
        compiler_params=params(),
        cost_estimate=cost(name),
        name=name,
    )(place, *blocks, weights)


def pick_kernel(heads, ctx_count, place_ref, table_ref, *refs):
    pool_refs, (keys, values) = refs[:ctx_count], refs[ctx_count:]
    blocks, length, columns = pool_refs[0].shape
    wide = columns // 2
    width = wide // heads
    values[...] = jnp.ones_like(values)
    for at in range(table_ref.shape[0]):
        entry = table_ref[at]
        here = slice(at * length, (at + 1) * length)
        step = lax.rem(place_ref[1] - entry // blocks + ctx_count, ctx_count)
        for ctx_step, pool_ref in enumerate(pool_refs):

            @pl.when(step == ctx_step)
            def _():
                block = pool_ref[entry % blocks]
                keys[here, :] = block[:, :wide]
                put_values(values, here, block[:, wide:], heads)


def put_values(values, here, block, heads):
    width = block.shape[1] // heads
    for head in range(heads):
        low = head * (width + ONES)
        values[low : low + width, here] = (
            block[:, head * width : (head + 1) * width].astype(jnp.float32).T.astype(jnp.bfloat16)
        )


def pick_blocks(place, table, pools, heads):
    length, columns = pools[0].shape[1:]
    count = table.shape[0] * length
    wide = columns // 2
    tall = wide + heads * ONES
    return pl.pallas_call(
        functools.partial(pick_kernel, heads, len(pools)),
        grid_spec=pltpu.PrefetchScalarGridSpec(
            num_scalar_prefetch=2,
            grid=(1,),
            in_specs=[pl.BlockSpec(p.shape, lambda i, *_: (0, 0, 0)) for p in pools],
            out_specs=[
                pl.BlockSpec((count, wide), lambda i, *_: (0, 0)),
                pl.BlockSpec((tall, count), lambda i, *_: (0, 0)),
            ],
        ),
        out_shape=[
            jax.ShapeDtypeStruct((count, wide), jnp.bfloat16),
            jax.ShapeDtypeStruct((tall, count), jnp.bfloat16),
        ],
        compiler_params=params(),
        cost_estimate=cost("pick_blocks"),
        name="pick_blocks",
    )(place, table, *pools)


def each_part(rows, heads):
    part_rows = min(PART, rows)
    each = part_rows // heads
    for low in range(0, rows, part_rows):
        for head in range(heads):
            at = low + head * each
            yield head, pl.ds(low + head, each, stride=heads), slice(at, at + each)


def prefix_kernel(scale, heads, query_ref, keys, values, acc_ref, stat_ref, flat):
    rows, width = query_ref.shape
    tall = width + ONES
    half = stat_ref.shape[0] // 2
    flat[...] = query_ref[...].astype(jnp.float32)
    for head, taken, here in each_part(rows, heads):
        query_block = flat[taken, :].astype(jnp.bfloat16)
        scores = dot_queries(keys[:, head * width : (head + 1) * width], query_block) * scale
        row_max, weights = softmax_parts(scores)
        mixed = jnp.dot(
            values[head * tall : (head + 1) * tall, :], weights, preferred_element_type=jnp.float32
        )
        acc_ref[:, here] = mixed[:width]
        stat_ref[:half, here] = jnp.broadcast_to(row_max, (half, row_max.shape[1]))
        stat_ref[half:, here] = jnp.broadcast_to(mixed[width : width + 1], (half, row_max.shape[1]))


def prefix_attend(query_rows, keys, values, chunk, scale, heads):
    all_rows, width = query_rows.shape
    row_total = all_rows // CHUNKS
    rows = min(1024, row_total)
    steps = row_total // rows
    return pl.pallas_call(
        functools.partial(prefix_kernel, scale, heads),
        grid=(steps,),
        in_specs=[
            pl.BlockSpec((rows, width), lambda i: (chunk * steps + i, 0)),
            pl.BlockSpec(keys.shape, lambda i: (0, 0)),
            pl.BlockSpec(values.shape, lambda i: (0, 0)),
        ],
        out_specs=[
            pl.BlockSpec((width, rows), lambda i: (0, i)),
            pl.BlockSpec((8, rows), lambda i: (0, i)),
        ],
        out_shape=[
            jax.ShapeDtypeStruct((width, row_total), jnp.float32),
            jax.ShapeDtypeStruct((8, row_total), jnp.float32),
        ],
        scratch_shapes=[pltpu.VMEM((rows, width), jnp.float32)],
        compiler_params=params(),
        cost_estimate=cost("prefix_attend"),
        name="prefix_attend",
    )(query_rows, keys, values)


def fresh_kernel(
    scale, heads, per_token, first_row, parts, length_ref, query_ref, acc_ref, stat_ref, *rest
):
    out_ref, keys, values, flat, mixed_rows = rest[-5:]
    rows, width = query_ref.shape
    wide, tall = heads * width, width + ONES
    step = pl.program_id(0)

    @pl.when(step == 0)
    def _():
        values[...] = jnp.ones_like(values)
        for index in range(parts):
            one, other = rest[2 * index], rest[2 * index + 1]
            here = slice(index * one.shape[0], (index + 1) * one.shape[0])
            fresh = (one[...].astype(jnp.float32) + other[...]).astype(jnp.bfloat16)
            keys[here, :] = fresh[:, :wide]
            put_values(values, here, fresh[:, wide:], heads)

    half = stat_ref.shape[0] // 2
    flat[...] = query_ref[...].astype(jnp.float32)
    for head, taken, here in each_part(rows, heads):
        query_block = flat[taken, :].astype(jnp.bfloat16)
        scores = dot_queries(keys[:, head * width : (head + 1) * width], query_block) * scale
        row = taken.start + heads * lax.broadcasted_iota(jnp.int32, (1, taken.size), 1)
        token = first_row + step * (rows // per_token) + (
            row // per_token if per_token & (per_token - 1) else row >> (per_token.bit_length() - 1)
        )
        key_at = lax.broadcasted_iota(jnp.int32, scores.shape, 0)
        scores = jnp.where(key_at <= token, scores, -jnp.inf)
        old_max, old_total = stat_ref[:1, here], stat_ref[half : half + 1, here]
        row_max, weights = softmax_parts(scores, old_max)
        fade = jnp.exp2(old_max - row_max)
        mixed = jnp.dot(
            values[head * tall : (head + 1) * tall, :], weights, preferred_element_type=jnp.float32
        )
        row_total = old_total * fade + mixed[width : width + 1]
        share = jnp.where(token < length_ref[0], 1.0 / row_total, 0.0)
        result = acc_ref[:, here] * (fade * share) + mixed[:width] * share
        mixed_rows[taken, :] = result.T
    out_ref[...] = mixed_rows[...].astype(out_ref.dtype)


def fresh_attend(length, query_rows, acc, stat, parts, earlier, chunk, scale, heads, per_token):
    row_total, width = query_rows.shape
    chunk_rows = row_total // CHUNKS
    rows = min(1024, chunk_rows)
    steps = chunk_rows // rows
    block = pl.BlockSpec((rows, width), lambda i, length: (chunk * steps + i, 0))
    terms = [term for pair in parts for term in pair]
    key_count = sum(pair[0].shape[0] for pair in parts)
    in_specs = [
        block,
        pl.BlockSpec((width, rows), lambda i, length: (0, i)),
        pl.BlockSpec((stat.shape[0], rows), lambda i, length: (0, i)),
    ] + [pl.BlockSpec(term.shape, lambda i, length: (0, 0)) for term in terms]
    operands = [length, query_rows, acc, stat, *terms]
    aliases = {}
    if earlier is not None:
        in_specs.append(pl.BlockSpec(memory_space=pl.ANY))
        aliases = {len(operands): 0}
        operands.append(earlier)
    return pl.pallas_call(
        functools.partial(
            fresh_kernel, scale, heads, per_token, chunk * (chunk_rows // per_token), len(parts)
        ),
        grid_spec=pltpu.PrefetchScalarGridSpec(
            num_scalar_prefetch=1,
            grid=(steps,),
            in_specs=in_specs,
            out_specs=block,
            scratch_shapes=[
                pltpu.VMEM((key_count, heads * width), jnp.bfloat16),
                pltpu.VMEM((heads * (width + ONES), key_count), jnp.bfloat16),
                pltpu.VMEM((rows, width), jnp.float32),
                pltpu.VMEM((rows, width), jnp.float32),
            ],
        ),
        out_shape=jax.ShapeDtypeStruct((row_total, width), jnp.bfloat16),
        input_output_aliases=aliases,
        compiler_params=params(),
        cost_estimate=cost("fresh_attend"),
        name="fresh_attend",
    )(*operands)


def cut_kernel(depth, bits, place_ref, tokens_ref, *refs):
    pieces, sems = refs[:-1], refs[-1]
    copies = []
    for index, piece in enumerate(pieces):
        start = pl.multiple_of((place_ref[0] ^ bits[index]) * depth, depth)
        copies.append(
            pltpu.make_async_copy(
                tokens_ref.at[:, pl.ds(start, depth)], piece, sems.at[index]
            )
        )
    for copy in copies:
        copy.start()
    for copy in copies:
        copy.wait()


def cut_tokens(place, tokens, depth, bits):
    anywhere = pl.BlockSpec(memory_space=pl.ANY)
    piece = jax.ShapeDtypeStruct((tokens.shape[0], depth), tokens.dtype)
    return pl.pallas_call(
        functools.partial(cut_kernel, depth, bits),
        grid_spec=pltpu.PrefetchScalarGridSpec(
            num_scalar_prefetch=1,
            grid=(1,),
            in_specs=[anywhere],
            out_specs=[anywhere] * len(bits),
            scratch_shapes=[pltpu.SemaphoreType.DMA((len(bits),))],
        ),
        out_shape=[piece] * len(bits),
        compiler_params=params(),
        cost_estimate=cost("cut_tokens"),
        name="cut_tokens",
    )(place, tokens)


def reduced_shards(tokens, key_weight, value_weight, queries, prefix_pool, block_table, lengths):
    batch_count = lax.axis_size("batch")
    ctx_count = lax.axis_size("ctx")
    head_count = lax.axis_size("head")
    batch_at, ctx_at, head_at = (lax.axis_index(a) for a in ("batch", "ctx", "head"))
    place = jnp.stack([batch_at, ctx_at, head_at]).astype(jnp.int32)
    token_count = tokens.shape[0]
    heads = queries.shape[1]
    width = prefix_pool.shape[4] // 2
    group = queries.shape[3] // width
    per_token = heads * group
    depth = key_weight.shape[2]
    rows = token_count // CHUNKS
    scale = math.log2(math.e) / math.sqrt(width)

    top = batch_count // 2
    steps = list(range(batch_count - 1, top, -1)) + list(range(1, top))
    pieces = cut_tokens(place, tokens, depth, [*steps, top])
    pieces, prefix_pool = after(pieces, prefix_pool)
    arrived = [trade(piece, "batch", bits) for piece, bits in zip(pieces, steps)]

    pools = arrange_pool(place, prefix_pool, ctx_count, heads)
    pools, (key_weight, value_weight) = after(pools, (key_weight, value_weight))
    pools = [shift(part, "ctx", step) if step else part for step, part in enumerate(pools)]

    weights = arrange_weights(key_weight, value_weight, ctx_count, heads, head_count)

    query_rows = queries.reshape(token_count, heads, group, width)
    query_rows = query_rows.transpose(0, 2, 1, 3).reshape(-1, width)
    def projected(blocks, name):
        terms = [
            shift(project(place, blocks, weights, step, jnp.bfloat16, name + "_away"), "head", step)
            for step in range(1, head_count)
        ]
        return [project(place, blocks, weights, 0, jnp.float32, name + "_kept"), *terms]

    def added(terms, step, here):
        return sum(term[step, here].astype(jnp.float32) for term in terms)

    def others(terms, here):
        return [added(terms, step, here).astype(jnp.bfloat16) for step in range(1, ctx_count)]

    def spread(parts):
        return [shift(part, "ctx", step + 1) for step, part in enumerate(parts)]

    def summed(terms, here, parts):
        return added(terms, 0, here) + sum(part.astype(jnp.float32) for part in parts)

    every = slice(None)
    parts_of = [slice(i * rows, (i + 1) * rows) for i in range(CHUNKS)]

    own = projected([tokens], "own")
    own[0], last = after(own[0], pieces[-1])
    last = trade(last, "batch", top)
    own_others = others(own, every)
    own_others = spread(own_others)

    if steps:
        early = projected(arrived, "early")
        cuts = [slice(i * token_count, (i + 1) * token_count) for i in range(len(steps))]
        leaving = [others(early, cut) for cut in cuts]
        leaving, pools = after(leaving, pools)
        far_others, near_others = (spread(parts) for parts in leaving)
    keys, values = pick_blocks(place, block_table[0], pools, heads)
    states = [prefix_attend(query_rows, keys, values, 0, scale, heads)]
    states[0], last = after(states[0], last)
    if steps:
        far_others, last = after(far_others, last)

    terms = [
        shift(project(place, [last], weights, step, jnp.bfloat16, "late_away"), "head", step)
        for step in range(1, head_count)
    ]
    if steps:
        far = summed(early, cuts[0], far_others).astype(jnp.bfloat16)
        far, last = after(far, last)
        far = trade(far, "batch", 1)
    late = [project(place, [last], weights, 0, jnp.float32, "late_kept"), *terms]
    late_others = [others(late, here) for here in parts_of]
    late_others[-1], (keys, values) = after(late_others[-1], (keys, values))
    late_others = [spread(part) for part in late_others]
    states.append(prefix_attend(query_rows, keys, values, 1, scale, heads))
    if steps:
        states[1], (late_others[0], near_others) = after(
            states[1], (late_others[0], near_others)
        )

    home = summed(own, every, own_others)
    if steps:
        near = trade(summed(early, cuts[1], near_others).astype(jnp.bfloat16), "batch", 1)
        home = home + near.astype(jnp.float32)
    parts = []
    for chunk, here in enumerate(parts_of):
        part = summed(late, here, late_others[chunk])
        if steps:
            part = part + far[here].astype(jnp.float32)
            if chunk + 1 < CHUNKS:
                (far, late), late_others[chunk + 1] = after((far, late), late_others[chunk + 1])
        part = part.astype(jnp.bfloat16)
        if parts:
            parts[-1], part = after(parts[-1], part)
        parts.append(trade(part, "batch", top))
    parts = [(part, home[here]) for part, here in zip(parts, parts_of)]

    result = None
    for chunk in range(CHUNKS):
        result = fresh_attend(
            lengths,
            query_rows,
            *states[chunk],
            parts[: chunk + 1],
            result,
            chunk,
            scale,
            heads,
            per_token,
        )
    result = result.reshape(token_count, group, heads, width).transpose(0, 2, 1, 3)
    return result.reshape(token_count, heads, 1, group * width)


def solution(mesh):
    def shards(tokens, key_weight, value_weight, *rest):
        prompts = mesh.shape["batch"]
        columns = 2 * math.prod(key_weight.shape[3:])
        few_tokens = prompts * tokens.shape[0] <= columns and prompts in (2, 4)
        form = reduced_shards if few_tokens else gathered_shards
        return form(tokens, key_weight, value_weight, *rest)

    return jax.shard_map(
        shards,
        mesh=mesh,
        in_specs=(
            P(("groups", "batch"), ("ctx", "head")),
            P("ctx", "head", "batch", None, None, None),
            P("ctx", "head", "batch", None, None, None),
            P(("groups", "batch"), "ctx", "head", None),
            P(("groups", "ctx"), None, None, "head", None),
            P(("groups", "batch"), None),
            P(("groups", "batch")),
        ),
        out_specs=P(("groups", "batch"), "ctx", "head", None),
        check_vma=False,
    )
```

```python
import functools
import math

import jax
import jax.numpy as jnp
from jax import lax
from jax.experimental import pallas as pl
from jax.experimental.pallas import tpu as pltpu
from jax.sharding import PartitionSpec as P

CHUNKS = 2
PART = 1024
ONES = 16
VMEM_BYTES = 24 * 1024 * 1024
LONG = pl.CostEstimate(flops=10**11, bytes_accessed=1, transcendentals=0)
COSTS = {}


def cost(name):
    return COSTS.get(name, LONG)


def attend_head(query_rows, prefix, fresh_rows, length):
    token_count = query_rows.shape[0]
    head_width = prefix.shape[1] // 2
    group_size = query_rows.shape[1] // head_width
    prefix_len = prefix.shape[0]
    key_rows = jnp.concatenate([prefix[:, :head_width], fresh_rows[:, :head_width]], 0)
    value_rows = jnp.concatenate([prefix[:, head_width:], fresh_rows[:, head_width:]], 0)
    block_len = min(token_count, 64)
    pieces = []
    for first_row in range(0, token_count, block_len):
        block_rows = query_rows[first_row : first_row + block_len].reshape(
            block_len * group_size, head_width
        )
        scores = jnp.dot(
            block_rows, key_rows.T, preferred_element_type=jnp.float32
        ) * head_width ** (-0.5)
        position = first_row + jnp.arange(block_len * group_size) // group_size
        column = jnp.arange(prefix_len + token_count) - prefix_len
        allowed = column[None, :] <= position[:, None]
        scores = jnp.where(allowed, scores, -jnp.inf)
        row_max = jnp.max(scores, axis=1, keepdims=True)
        weights = jnp.exp(scores - row_max)
        row_total = jnp.sum(weights, axis=1, keepdims=True)
        probs_bf = (weights / row_total).astype(jnp.bfloat16)
        mixed_rows = jnp.dot(probs_bf, value_rows, preferred_element_type=jnp.float32)
        is_live = position < length
        mixed_rows = jnp.where(is_live[:, None], mixed_rows, 0.0)
        pieces.append(mixed_rows.astype(jnp.bfloat16).reshape(block_len, group_size * head_width))
    return jnp.concatenate(pieces, 0)


def gathered_shards(tokens, key_weight, value_weight, queries, prefix_pool, block_table, lengths):
    token_count = tokens.shape[0]
    local_heads = queries.shape[1]
    head_width = prefix_pool.shape[4] // 2
    ctx_count = lax.axis_size("ctx")
    head_count = lax.axis_size("head")
    features = lax.all_gather(tokens, ("ctx", "head"), axis=1, tiled=True)
    key_cols, value_cols = (
        lax.all_to_all(
            lax.all_to_all(weight, "ctx", split_axis=3, concat_axis=0, tiled=True),
            "head",
            split_axis=4,
            concat_axis=1,
            tiled=True,
        )
        for weight in (key_weight, value_weight)
    )
    span_len = features.shape[1] // (ctx_count * head_count)
    feature_view = features.reshape(token_count, ctx_count, head_count, span_len)
    pieces = (
        lax.all_gather(key_cols, "batch", axis=2, tiled=True),
        lax.all_gather(value_cols, "batch", axis=2, tiled=True),
    )
    row_count = pieces[0].shape[2]

    def one_term(weight_piece):
        shaped = weight_piece.reshape(ctx_count, head_count, row_count, local_heads * head_width)
        return jnp.einsum("tchr,chrk->tk", feature_view, shaped, preferred_element_type=jnp.float32)

    new_keys = one_term(pieces[0]).astype(jnp.bfloat16).reshape(token_count, local_heads, head_width)
    new_values = one_term(pieces[1]).astype(jnp.bfloat16).reshape(token_count, local_heads, head_width)
    fresh_all = jnp.concatenate([new_keys, new_values], 2)
    pool_heads = lax.all_to_all(prefix_pool, "ctx", split_axis=2, concat_axis=0, tiled=True)
    chosen = jnp.take(pool_heads, block_table[0], axis=0)
    chosen = chosen.reshape(-1, local_heads, 2 * head_width)
    outputs = [
        attend_head(
            queries[:, head_idx, 0], chosen[:, head_idx], fresh_all[:, head_idx], lengths[0]
        )
        for head_idx in range(local_heads)
    ]
    return jnp.stack(outputs, 1)[:, :, None, :]


def shift(array, axis, step):
    count = lax.axis_size(axis)
    return lax.ppermute(array, axis, [(i, (i + step) % count) for i in range(count)])


def trade(array, axis, bits):
    return lax.ppermute(array, axis, [(i, i ^ bits) for i in range(lax.axis_size(axis))])


def after(first, second):
    return lax.optimization_barrier((first, second))


def softmax_parts(scores, old_max=None):
    row_max = jnp.max(scores, axis=0, keepdims=True)
    if old_max is not None:
        row_max = jnp.maximum(row_max, old_max)
    return row_max, jnp.exp2(scores - row_max).astype(jnp.bfloat16)


def dot_queries(keys, query_block):
    return lax.dot_general(
        keys, query_block, (((1,), (1,)), ((), ())), preferred_element_type=jnp.float32
    )


def params():
    return pltpu.CompilerParams(vmem_limit_bytes=VMEM_BYTES)


def weight_kernel(ctx_count, heads, head_count, key_ref, value_ref, out_ref, flat):
    depth, slots, width = key_ref.shape
    for kind, ref in enumerate((key_ref, value_ref)):
        flat[...] = ref[...].astype(jnp.float32).reshape(depth * slots, width)
        for ctx in range(ctx_count):
            for head in range(heads):
                for core in range(head_count):
                    slot = (ctx * heads + head) * head_count + core
                    at = (kind * heads + head) * width
                    out_ref[core, ctx, :, at : at + width] = flat[
                        pl.ds(slot, depth, stride=slots), :
                    ].astype(out_ref.dtype)


def arrange_weights(key_weight, value_weight, ctx_count, heads, head_count):
    depth, width = key_weight.shape[2], key_weight.shape[5]
    slots = ctx_count * heads * head_count
    rows = min(128, depth)
    views = [w.reshape(depth, slots, width) for w in (key_weight, value_weight)]
    block = pl.BlockSpec((rows, slots, width), lambda i: (i, 0, 0))
    columns = 2 * heads * width
    return pl.pallas_call(
        functools.partial(weight_kernel, ctx_count, heads, head_count),
        grid=(depth // rows,),
        in_specs=[block, block],
        out_specs=pl.BlockSpec((head_count, ctx_count, rows, columns), lambda i: (0, 0, i, 0)),
        out_shape=jax.ShapeDtypeStruct((head_count, ctx_count, depth, columns), jnp.bfloat16),
        scratch_shapes=[pltpu.VMEM((rows * slots, width), jnp.float32)],
        compiler_params=params(),
        cost_estimate=cost("arrange_weights"),
        name="arrange_weights",
    )(*views)


def prepare_kernel(ctx_count, heads, cuts, place_ref, tokens_ref, pool_ref, *refs):
    pieces, outs = refs[: len(cuts)], refs[len(cuts) : len(cuts) + ctx_count]
    flat, sems = refs[-2:]
    depth = pieces[0].shape[1]

    def copies():
        for index, (bits, first) in enumerate(cuts):
            start = pl.multiple_of((place_ref[0] ^ bits) * depth, depth)
            source = tokens_ref.at[pl.ds(first, pieces[index].shape[0]), pl.ds(start, depth)]
            yield pltpu.make_async_copy(source, pieces[index], sems.at[index])

    @pl.when(pl.program_id(0) == 0)
    def _():
        for copy in copies():
            copy.start()

    blocks, length, slots, width = pool_ref.shape
    length *= blocks
    flat[...] = pool_ref[...].astype(jnp.float32).reshape(length * slots, width)
    for kind in range(2):
        for head in range(heads):
            at = (kind * heads + head) * width
            held = []
            for ctx in range(ctx_count):
                slot = (kind * ctx_count + ctx) * heads + head
                held.append(flat[pl.ds(slot, length, stride=slots), :])
            for step, out_ref in enumerate(outs):
                target = lax.rem(place_ref[1] + step, ctx_count)
                value = held[0]
                for ctx in range(1, ctx_count):
                    value = jnp.where(target == ctx, held[ctx], value)
                out_ref[:, :, at : at + width] = value.astype(out_ref.dtype).reshape(
                    blocks, length // blocks, width
                )

    @pl.when(pl.program_id(0) == pl.num_programs(0) - 1)
    def _():
        for copy in copies():
            copy.wait()


def prepare(place, tokens, depth, cuts, prefix_pool, ctx_count, heads):
    blocks, length, all_heads, _, double = prefix_pool.shape
    width = double // 2
    slots = 2 * all_heads
    view = prefix_pool.reshape(blocks, length, all_heads, 2, width)
    view = view.transpose(0, 1, 3, 2, 4).reshape(blocks, length, slots, width)
    columns = 2 * heads * width
    some = 2 if blocks % 2 == 0 else 1
    out = pl.BlockSpec((some, length, columns), lambda i, place: (i, 0, 0))
    far = pl.BlockSpec(memory_space=pltpu.HBM)
    result = pl.pallas_call(
        functools.partial(
            prepare_kernel, ctx_count, heads, [(bits, first) for bits, first, _ in cuts]
        ),
        grid_spec=pltpu.PrefetchScalarGridSpec(
            num_scalar_prefetch=1,
            grid=(blocks // some,),
            in_specs=[
                far,
                pl.BlockSpec((some, length, slots, width), lambda i, place: (i, 0, 0, 0)),
            ],
            out_specs=[far] * len(cuts) + [out] * ctx_count,
            scratch_shapes=[
                pltpu.VMEM((some * length * slots, width), jnp.float32),
                pltpu.SemaphoreType.DMA((len(cuts),)),
            ],
        ),
        out_shape=[jax.ShapeDtypeStruct((rows, depth), tokens.dtype) for _, _, rows in cuts]
        + [jax.ShapeDtypeStruct((blocks, length, columns), jnp.bfloat16)] * ctx_count,
        compiler_params=params(),
        cost_estimate=cost("prepare"),
        name="prepare",
    )(place, tokens, view)
    return result[: len(cuts)], result[len(cuts) :]


def total_of(refs):
    return sum(ref[...].astype(jnp.float32).reshape(ref.shape[-2:]) for ref in refs)


def project_kernel(block_count, term_counts, place_ref, *refs):
    token_refs, weight_ref = refs[:block_count], refs[block_count]
    terms = refs[block_count + 1 : block_count + 1 + sum(term_counts)]
    out_ref, *sum_refs = refs[block_count + 1 + sum(term_counts) : -1]
    stacked = refs[-1]

    @pl.when(pl.program_id(0) == 0)
    def _():
        at = 0
        for token_ref in token_refs:
            rows = token_ref.shape[0]
            stacked[at : at + rows, :] = token_ref[...]
            at += rows
        at = 0
        for count, sum_ref in zip(term_counts, sum_refs):
            sum_ref[...] = total_of(terms[at : at + count]).astype(sum_ref.dtype)
            at += count

    out_ref[0] = jnp.dot(
        stacked[...], weight_ref[0, 0], preferred_element_type=jnp.float32
    ).astype(out_ref.dtype)


def piece_of(array, *index):
    rows, block, *leading = index
    shape = (1,) * len(leading) + (rows, array.shape[-1])
    return array, pl.BlockSpec(shape, lambda j, *_: (*leading, block, 0))


def project(place, blocks, weights, head_step, out_dtype, name, sums=()):
    head_count, ctx_count, depth, width = weights.shape
    row_total = sum(block.shape[0] for block in blocks)

    def block_spec(block):
        if block.shape[1] == depth:
            return pl.BlockSpec(block.shape, lambda j, place: (0, 0))
        return pl.BlockSpec((block.shape[0], depth), lambda j, place: (0, place[0]))

    pieces = [piece for terms in sums for piece in terms]
    sum_shapes = [terms[0][1].block_shape[-2:] for terms in sums]
    result = pl.pallas_call(
        functools.partial(project_kernel, len(blocks), [len(terms) for terms in sums]),
        grid_spec=pltpu.PrefetchScalarGridSpec(
            num_scalar_prefetch=1,
            grid=(ctx_count,),
            in_specs=[block_spec(block) for block in blocks]
            + [
                pl.BlockSpec(
                    (1, 1, depth, width),
                    lambda j, place: (
                        lax.rem(place[2] + head_step, head_count),
                        lax.rem(place[1] + j, ctx_count),
                        0,
                        0,
                    ),
                )
            ]
            + [spec for _, spec in pieces],
            out_specs=[pl.BlockSpec((1, row_total, width), lambda j, place: (j, 0, 0))]
            + [pl.BlockSpec(shape, lambda j, place: (0, 0)) for shape in sum_shapes],
            scratch_shapes=[pltpu.VMEM((row_total, depth), weights.dtype)],
        ),
        out_shape=[jax.ShapeDtypeStruct((ctx_count, row_total, width), out_dtype)]
        + [jax.ShapeDtypeStruct(shape, jnp.bfloat16) for shape in sum_shapes],
        compiler_params=params(),
        cost_estimate=cost(name),
        name=name,
    )(place, *blocks, weights, *(array for array, _ in pieces))
    return result if sums else result[0]


def pick_kernel(heads, ctx_count, place_ref, table_ref, *refs):
    pool_refs, (keys, values) = refs[:ctx_count], refs[ctx_count:]
    blocks, length, columns = pool_refs[0].shape
    wide = columns // 2
    width = wide // heads
    values[...] = jnp.ones_like(values)
    for at in range(table_ref.shape[0]):
        entry = table_ref[at]
        here = slice(at * length, (at + 1) * length)
        step = lax.rem(place_ref[1] - entry // blocks + ctx_count, ctx_count)
        for ctx_step, pool_ref in enumerate(pool_refs):

            @pl.when(step == ctx_step)
            def _():
                block = pool_ref[entry % blocks]
                keys[here, :] = block[:, :wide]
                put_values(values, here, block[:, wide:], heads)


def put_values(values, here, block, heads):
    width = block.shape[1] // heads
    for head in range(heads):
        low = head * (width + ONES)
        values[low : low + width, here] = (
            block[:, head * width : (head + 1) * width].astype(jnp.float32).T.astype(jnp.bfloat16)
        )


def pick_blocks(place, table, pools, heads):
    length, columns = pools[0].shape[1:]
    count = table.shape[0] * length
    wide = columns // 2
    tall = wide + heads * ONES
    return pl.pallas_call(
        functools.partial(pick_kernel, heads, len(pools)),
        grid_spec=pltpu.PrefetchScalarGridSpec(
            num_scalar_prefetch=2,
            grid=(1,),
            in_specs=[pl.BlockSpec(p.shape, lambda i, *_: (0, 0, 0)) for p in pools],
            out_specs=[
                pl.BlockSpec((count, wide), lambda i, *_: (0, 0)),
                pl.BlockSpec((tall, count), lambda i, *_: (0, 0)),
            ],
        ),
        out_shape=[
            jax.ShapeDtypeStruct((count, wide), jnp.bfloat16),
            jax.ShapeDtypeStruct((tall, count), jnp.bfloat16),
        ],
        compiler_params=params(),
        cost_estimate=cost("pick_blocks"),
        name="pick_blocks",
    )(place, table, *pools)


def each_part(rows, heads):
    part_rows = min(PART, rows)
    each = part_rows // heads
    for low in range(0, rows, part_rows):
        for head in range(heads):
            at = low + head * each
            yield head, pl.ds(low + head, each, stride=heads), slice(at, at + each)


def prefix_kernel(scale, heads, query_ref, keys, values, acc_ref, stat_ref, flat):
    rows, width = query_ref.shape
    tall = width + ONES
    half = stat_ref.shape[0] // 2
    flat[...] = query_ref[...].astype(jnp.float32)
    for head, taken, here in each_part(rows, heads):
        query_block = flat[taken, :].astype(jnp.bfloat16)
        scores = dot_queries(keys[:, head * width : (head + 1) * width], query_block) * scale
        row_max, weights = softmax_parts(scores)
        mixed = jnp.dot(
            values[head * tall : (head + 1) * tall, :], weights, preferred_element_type=jnp.float32
        )
        acc_ref[:, here] = mixed[:width]
        stat_ref[:half, here] = jnp.broadcast_to(row_max, (half, row_max.shape[1]))
        stat_ref[half:, here] = jnp.broadcast_to(mixed[width : width + 1], (half, row_max.shape[1]))


def prefix_attend(query_rows, keys, values, chunk, scale, heads):
    all_rows, width = query_rows.shape
    row_total = all_rows // CHUNKS
    rows = min(1024, row_total)
    steps = row_total // rows
    return pl.pallas_call(
        functools.partial(prefix_kernel, scale, heads),
        grid=(steps,),
        in_specs=[
            pl.BlockSpec((rows, width), lambda i: (chunk * steps + i, 0)),
            pl.BlockSpec(keys.shape, lambda i: (0, 0)),
            pl.BlockSpec(values.shape, lambda i: (0, 0)),
        ],
        out_specs=[
            pl.BlockSpec((width, rows), lambda i: (0, i)),
            pl.BlockSpec((8, rows), lambda i: (0, i)),
        ],
        out_shape=[
            jax.ShapeDtypeStruct((width, row_total), jnp.float32),
            jax.ShapeDtypeStruct((8, row_total), jnp.float32),
        ],
        scratch_shapes=[pltpu.VMEM((rows, width), jnp.float32)],
        compiler_params=params(),
        cost_estimate=cost("prefix_attend"),
        name="prefix_attend",
    )(query_rows, keys, values)


def fresh_kernel(
    scale, heads, per_token, first_row, counts, length_ref, query_ref, acc_ref, stat_ref, *rest
):
    early_count, term_count = counts
    earlier, terms = rest[:early_count], rest[early_count : early_count + term_count]
    out_ref, fresh_ref, keys, values, flat, mixed_rows = rest[-6:]
    rows, width = query_ref.shape
    wide, tall = heads * width, width + ONES
    step = pl.program_id(0)

    @pl.when(step == 0)
    def _():
        values[...] = jnp.ones_like(values)
        fresh_ref[...] = total_of(terms).astype(fresh_ref.dtype)
        for index, ref in enumerate([*earlier, fresh_ref]):
            here = slice(index * ref.shape[0], (index + 1) * ref.shape[0])
            fresh = ref[...]
            keys[here, :] = fresh[:, :wide]
            put_values(values, here, fresh[:, wide:], heads)

    half = stat_ref.shape[0] // 2
    flat[...] = query_ref[...].astype(jnp.float32)
    for head, taken, here in each_part(rows, heads):
        query_block = flat[taken, :].astype(jnp.bfloat16)
        scores = dot_queries(keys[:, head * width : (head + 1) * width], query_block) * scale
        row = taken.start + heads * lax.broadcasted_iota(jnp.int32, (1, taken.size), 1)
        token = first_row + step * (rows // per_token) + (
            row // per_token if per_token & (per_token - 1) else row >> (per_token.bit_length() - 1)
        )
        key_at = lax.broadcasted_iota(jnp.int32, scores.shape, 0)
        scores = jnp.where(key_at <= token, scores, -jnp.inf)
        old_max, old_total = stat_ref[:1, here], stat_ref[half : half + 1, here]
        row_max, weights = softmax_parts(scores, old_max)
        fade = jnp.exp2(old_max - row_max)
        mixed = jnp.dot(
            values[head * tall : (head + 1) * tall, :], weights, preferred_element_type=jnp.float32
        )
        row_total = old_total * fade + mixed[width : width + 1]
        share = jnp.where(token < length_ref[0], 1.0 / row_total, 0.0)
        result = acc_ref[:, here] * (fade * share) + mixed[:width] * share
        mixed_rows[taken, :] = result.T
    out_ref[...] = mixed_rows[...].astype(out_ref.dtype)


def fresh_attend(
    length, query_rows, acc, stat, earlier, pieces, result, chunk, scale, heads, per_token
):
    row_total, width = query_rows.shape
    chunk_rows = row_total // CHUNKS
    rows = min(1024, chunk_rows)
    steps = chunk_rows // rows
    block = pl.BlockSpec((rows, width), lambda i, length: (chunk * steps + i, 0))
    fresh_shape = pieces[0][1].block_shape[-2:]
    key_count = (len(earlier) + 1) * fresh_shape[0]
    whole = pl.BlockSpec(fresh_shape, lambda i, length: (0, 0))
    in_specs = [
        block,
        pl.BlockSpec((width, rows), lambda i, length: (0, i)),
        pl.BlockSpec((stat.shape[0], rows), lambda i, length: (0, i)),
        *(whole for _ in earlier),
        *(spec for _, spec in pieces),
    ]
    operands = [length, query_rows, acc, stat, *earlier, *(array for array, _ in pieces)]
    aliases = {}
    if result is not None:
        in_specs.append(pl.BlockSpec(memory_space=pl.ANY))
        aliases = {len(operands): 0}
        operands.append(result)
    return pl.pallas_call(
        functools.partial(
            fresh_kernel,
            scale,
            heads,
            per_token,
            chunk * (chunk_rows // per_token),
            (len(earlier), len(pieces)),
        ),
        grid_spec=pltpu.PrefetchScalarGridSpec(
            num_scalar_prefetch=1,
            grid=(steps,),
            in_specs=in_specs,
            out_specs=[block, whole],
            scratch_shapes=[
                pltpu.VMEM((key_count, heads * width), jnp.bfloat16),
                pltpu.VMEM((heads * (width + ONES), key_count), jnp.bfloat16),
                pltpu.VMEM((rows, width), jnp.float32),
                pltpu.VMEM((rows, width), jnp.float32),
            ],
        ),
        out_shape=[
            jax.ShapeDtypeStruct((row_total, width), jnp.bfloat16),
            jax.ShapeDtypeStruct(fresh_shape, jnp.bfloat16),
        ],
        input_output_aliases=aliases,
        compiler_params=params(),
        cost_estimate=cost("fresh_attend"),
        name="fresh_attend",
    )(*operands)


def reduced_shards(tokens, key_weight, value_weight, queries, prefix_pool, block_table, lengths):
    batch_count = lax.axis_size("batch")
    ctx_count = lax.axis_size("ctx")
    head_count = lax.axis_size("head")
    batch_at, ctx_at, head_at = (lax.axis_index(a) for a in ("batch", "ctx", "head"))
    place = jnp.stack([batch_at, ctx_at, head_at]).astype(jnp.int32)
    token_count = tokens.shape[0]
    heads = queries.shape[1]
    width = prefix_pool.shape[4] // 2
    group = queries.shape[3] // width
    per_token = heads * group
    depth = key_weight.shape[2]
    rows = token_count // CHUNKS
    scale = math.log2(math.e) / math.sqrt(width)

    top = batch_count // 2
    steps = list(range(batch_count - 1, top, -1)) + list(range(1, top))
    cuts = [(bits, i * rows, rows) for bits in steps for i in range(CHUNKS)]
    cuts.append((top, 0, token_count))
    pieces, pools = prepare(place, tokens, depth, cuts, prefix_pool, ctx_count, heads)
    arrived = [trade(piece, "batch", bits) for piece, (bits, _, _) in zip(pieces, cuts[:-1])]
    pools, (key_weight, value_weight) = after(pools, (key_weight, value_weight))
    pools = [shift(part, "ctx", step) if step else part for step, part in enumerate(pools)]

    weights = arrange_weights(key_weight, value_weight, ctx_count, heads, head_count)

    query_rows = queries.reshape(token_count, heads, group, width)
    query_rows = query_rows.transpose(0, 2, 1, 3).reshape(-1, width)
    def projected(blocks, name):
        terms = [
            shift(project(place, blocks, weights, step, jnp.bfloat16, name + "_away"), "head", step)
            for step in range(1, head_count)
        ]
        return [project(place, blocks, weights, 0, jnp.float32, name + "_kept"), *terms]

    def added(terms, step, here):
        return sum(term[step, here].astype(jnp.float32) for term in terms)

    def others(terms, here):
        return [added(terms, step, here).astype(jnp.bfloat16) for step in range(1, ctx_count)]

    def spread(parts):
        return [shift(part, "ctx", step + 1) for step, part in enumerate(parts)]

    every = slice(None)
    parts_of = [slice(i * rows, (i + 1) * rows) for i in range(CHUNKS)]

    last = trade(pieces[-1], "batch", top)

    sums = [[], []]
    if steps:
        early = projected(arrived, "early")
        cuts = [slice(i * token_count, (i + 1) * token_count) for i in range(len(steps))]
        leaving = [others(early, cut) for cut in cuts]
        leaving, pools = after(leaving, pools)
        sums = [
            [
                [piece_of(t, token_count, i, 0) for t in early]
                + [piece_of(p, token_count, 0) for p in spread(parts)]
            ]
            for i, parts in enumerate(leaving)
        ]
    keys, values = pick_blocks(place, block_table[0], pools, heads)
    states = [prefix_attend(query_rows, keys, values, 0, scale, heads)]
    states[0], last = after(states[0], last)

    def late_project(step, dtype, name, sums):
        result = project(place, [last, tokens], weights, step, dtype, name, sums)
        return result if sums else (result,)

    terms = []
    for step in range(1, head_count):
        term, *far = late_project(step, jnp.bfloat16, "late_away", sums[0] + sums[1] if step == 1 else [])
        terms.append(shift(term, "head", step))
    kept, *_ = late_project(0, jnp.float32, "late_kept", [])
    far, near = far[:1], far[1:]
    late = [kept, *terms]
    far, near = ([trade(part, "batch", 1) for part in parts] for parts in (far, near))
    own_at = slice(token_count, 2 * token_count)
    late_others = [others(late, here) for here in [*parts_of, own_at]]
    late_others[-1], (keys, values) = after(late_others[-1], (keys, values))
    *late_others, own_others = [spread(part) for part in late_others]
    states.append(prefix_attend(query_rows, keys, values, 1, scale, heads))
    states[1], late_others[0] = after(states[1], late_others[0])

    away = []
    for chunk, here in enumerate(parts_of):
        part = added(late, 0, here) + sum(p.astype(jnp.float32) for p in late_others[chunk])
        part = part + sum(p[here].astype(jnp.float32) for p in far)
        if chunk + 1 < CHUNKS:
            (far, late), late_others[chunk + 1] = after((far, late), late_others[chunk + 1])
        part = part.astype(jnp.bfloat16)
        if away:
            away[-1], part = after(away[-1], part)
        away.append(trade(part, "batch", top))

    result = None
    fresh = []
    for chunk in range(CHUNKS):
        pieces = [piece_of(t, rows, CHUNKS + chunk, 0) for t in late]
        pieces += [piece_of(part, rows, chunk) for part in (*own_others, *near)]
        pieces.append(piece_of(away[chunk], rows, 0))
        result, new = fresh_attend(
            lengths,
            query_rows,
            *states[chunk],
            fresh,
            pieces,
            result,
            chunk,
            scale,
            heads,
            per_token,
        )
        fresh.append(new)
    result = result.reshape(token_count, group, heads, width).transpose(0, 2, 1, 3)
    return result.reshape(token_count, heads, 1, group * width)


def solution(mesh):
    def shards(tokens, key_weight, value_weight, *rest):
        prompts = mesh.shape["batch"]
        columns = 2 * math.prod(key_weight.shape[3:])
        few_tokens = prompts * tokens.shape[0] <= columns and prompts in (2, 4)
        form = reduced_shards if few_tokens else gathered_shards
        return form(tokens, key_weight, value_weight, *rest)

    return jax.shard_map(
        shards,
        mesh=mesh,
        in_specs=(
            P(("groups", "batch"), ("ctx", "head")),
            P("ctx", "head", "batch", None, None, None),
            P("ctx", "head", "batch", None, None, None),
            P(("groups", "batch"), "ctx", "head", None),
            P(("groups", "ctx"), None, None, "head", None),
            P(("groups", "batch"), None),
            P(("groups", "batch")),
        ),
        out_specs=P(("groups", "batch"), "ctx", "head", None),
        check_vma=False,
    )
```

```python
import functools
import math

import jax
import jax.numpy as jnp
from jax import lax
from jax.experimental import pallas as pl
from jax.experimental.pallas import tpu as pltpu
from jax.sharding import PartitionSpec as P

CHUNKS = 2
PART = 1024
ONES = 16
VMEM_BYTES = 24 * 1024 * 1024
LONG = pl.CostEstimate(flops=10**11, bytes_accessed=1, transcendentals=0)
COSTS = {}


def cost(name):
    return COSTS.get(name, LONG)


def attend_head(query_rows, prefix, fresh_rows, length):
    token_count = query_rows.shape[0]
    head_width = prefix.shape[1] // 2
    group_size = query_rows.shape[1] // head_width
    prefix_len = prefix.shape[0]
    key_rows = jnp.concatenate([prefix[:, :head_width], fresh_rows[:, :head_width]], 0)
    value_rows = jnp.concatenate([prefix[:, head_width:], fresh_rows[:, head_width:]], 0)
    block_len = min(token_count, 64)
    pieces = []
    for first_row in range(0, token_count, block_len):
        block_rows = query_rows[first_row : first_row + block_len].reshape(
            block_len * group_size, head_width
        )
        scores = jnp.dot(
            block_rows, key_rows.T, preferred_element_type=jnp.float32
        ) * head_width ** (-0.5)
        position = first_row + jnp.arange(block_len * group_size) // group_size
        column = jnp.arange(prefix_len + token_count) - prefix_len
        allowed = column[None, :] <= position[:, None]
        scores = jnp.where(allowed, scores, -jnp.inf)
        row_max = jnp.max(scores, axis=1, keepdims=True)
        weights = jnp.exp(scores - row_max)
        row_total = jnp.sum(weights, axis=1, keepdims=True)
        probs_bf = (weights / row_total).astype(jnp.bfloat16)
        mixed_rows = jnp.dot(probs_bf, value_rows, preferred_element_type=jnp.float32)
        is_live = position < length
        mixed_rows = jnp.where(is_live[:, None], mixed_rows, 0.0)
        pieces.append(mixed_rows.astype(jnp.bfloat16).reshape(block_len, group_size * head_width))
    return jnp.concatenate(pieces, 0)


def gathered_shards(tokens, key_weight, value_weight, queries, prefix_pool, block_table, lengths):
    token_count = tokens.shape[0]
    local_heads = queries.shape[1]
    head_width = prefix_pool.shape[4] // 2
    ctx_count = lax.axis_size("ctx")
    head_count = lax.axis_size("head")
    features = lax.all_gather(tokens, ("ctx", "head"), axis=1, tiled=True)
    key_cols, value_cols = (
        lax.all_to_all(
            lax.all_to_all(weight, "ctx", split_axis=3, concat_axis=0, tiled=True),
            "head",
            split_axis=4,
            concat_axis=1,
            tiled=True,
        )
        for weight in (key_weight, value_weight)
    )
    span_len = features.shape[1] // (ctx_count * head_count)
    feature_view = features.reshape(token_count, ctx_count, head_count, span_len)
    pieces = (
        lax.all_gather(key_cols, "batch", axis=2, tiled=True),
        lax.all_gather(value_cols, "batch", axis=2, tiled=True),
    )
    row_count = pieces[0].shape[2]

    def one_term(weight_piece):
        shaped = weight_piece.reshape(ctx_count, head_count, row_count, local_heads * head_width)
        return jnp.einsum("tchr,chrk->tk", feature_view, shaped, preferred_element_type=jnp.float32)

    new_keys = one_term(pieces[0]).astype(jnp.bfloat16).reshape(token_count, local_heads, head_width)
    new_values = one_term(pieces[1]).astype(jnp.bfloat16).reshape(token_count, local_heads, head_width)
    fresh_all = jnp.concatenate([new_keys, new_values], 2)
    pool_heads = lax.all_to_all(prefix_pool, "ctx", split_axis=2, concat_axis=0, tiled=True)
    chosen = jnp.take(pool_heads, block_table[0], axis=0)
    chosen = chosen.reshape(-1, local_heads, 2 * head_width)
    outputs = [
        attend_head(
            queries[:, head_idx, 0], chosen[:, head_idx], fresh_all[:, head_idx], lengths[0]
        )
        for head_idx in range(local_heads)
    ]
    return jnp.stack(outputs, 1)[:, :, None, :]


def shift(array, axis, step):
    count = lax.axis_size(axis)
    return lax.ppermute(array, axis, [(i, (i + step) % count) for i in range(count)])


def trade(array, axis, bits):
    return lax.ppermute(array, axis, [(i, i ^ bits) for i in range(lax.axis_size(axis))])


def after(first, second):
    return lax.optimization_barrier((first, second))


def softmax_parts(scores, old_max=None):
    row_max = jnp.max(scores, axis=0, keepdims=True)
    if old_max is not None:
        row_max = jnp.maximum(row_max, old_max)
    return row_max, jnp.exp2(scores - row_max).astype(jnp.bfloat16)


def dot_queries(keys, query_block):
    return lax.dot_general(
        keys, query_block, (((1,), (1,)), ((), ())), preferred_element_type=jnp.float32
    )


def params():
    return pltpu.CompilerParams(vmem_limit_bytes=VMEM_BYTES)


def weight_kernel(ctx_count, heads, head_count, key_ref, value_ref, out_ref, flat):
    depth, slots, width = key_ref.shape
    for kind, ref in enumerate((key_ref, value_ref)):
        flat[...] = ref[...].astype(jnp.float32).reshape(depth * slots, width)
        for ctx in range(ctx_count):
            for head in range(heads):
                for core in range(head_count):
                    slot = (ctx * heads + head) * head_count + core
                    at = (kind * heads + head) * width
                    out_ref[core, ctx, :, at : at + width] = flat[
                        pl.ds(slot, depth, stride=slots), :
                    ].astype(out_ref.dtype)


def arrange_weights(key_weight, value_weight, ctx_count, heads, head_count):
    depth, width = key_weight.shape[2], key_weight.shape[5]
    slots = ctx_count * heads * head_count
    rows = min(128, depth)
    views = [w.reshape(depth, slots, width) for w in (key_weight, value_weight)]
    block = pl.BlockSpec((rows, slots, width), lambda i: (i, 0, 0))
    columns = 2 * heads * width
    return pl.pallas_call(
        functools.partial(weight_kernel, ctx_count, heads, head_count),
        grid=(depth // rows,),
        in_specs=[block, block],
        out_specs=pl.BlockSpec((head_count, ctx_count, rows, columns), lambda i: (0, 0, i, 0)),
        out_shape=jax.ShapeDtypeStruct((head_count, ctx_count, depth, columns), jnp.bfloat16),
        scratch_shapes=[pltpu.VMEM((rows * slots, width), jnp.float32)],
        compiler_params=params(),
        cost_estimate=cost("arrange_weights"),
        name="arrange_weights",
    )(*views)


def prepare_kernel(ctx_count, heads, cuts, place_ref, tokens_ref, pool_ref, *refs):
    pieces, outs = refs[: len(cuts)], refs[len(cuts) : len(cuts) + ctx_count]
    held_pool, flat, sems, pool_sems = refs[-4:]
    depth = pieces[0].shape[1]
    step_at = pl.program_id(0)
    some = outs[0].shape[0]
    steps = pool_ref.shape[0] // some

    def copies():
        for index, (bits, first) in enumerate(cuts):
            start = pl.multiple_of((place_ref[0] ^ bits) * depth, depth)
            source = tokens_ref.at[pl.ds(first, pieces[index].shape[0]), pl.ds(start, depth)]
            yield pltpu.make_async_copy(source, pieces[index], sems.at[index])

    def pool_copy(index):
        here = pl.ds(index * some, some)
        return pltpu.make_async_copy(pool_ref.at[here], held_pool.at[here], pool_sems.at[index])

    @pl.when(step_at == 0)
    def _():
        for copy in copies():
            copy.start()
        for index in range(steps):
            pool_copy(index).start()

    pool_copy(step_at).wait()
    _, length, slots, width = pool_ref.shape
    length *= some
    block = held_pool[pl.ds(step_at * some, some)]
    flat[...] = block.astype(jnp.float32).reshape(length * slots, width)
    for kind in range(2):
        for head in range(heads):
            at = (kind * heads + head) * width
            held = []
            for ctx in range(ctx_count):
                slot = (kind * ctx_count + ctx) * heads + head
                held.append(flat[pl.ds(slot, length, stride=slots), :])
            for step, out_ref in enumerate(outs):
                target = lax.rem(place_ref[1] + step, ctx_count)
                value = held[0]
                for ctx in range(1, ctx_count):
                    value = jnp.where(target == ctx, held[ctx], value)
                out_ref[:, :, at : at + width] = value.astype(out_ref.dtype).reshape(
                    some, length // some, width
                )

    @pl.when(step_at == steps - 1)
    def _():
        for copy in copies():
            copy.wait()


def prepare(place, tokens, depth, cuts, prefix_pool, ctx_count, heads):
    blocks, length, all_heads, _, double = prefix_pool.shape
    width = double // 2
    slots = 2 * all_heads
    view = prefix_pool.reshape(blocks, length, all_heads, 2, width)
    view = view.transpose(0, 1, 3, 2, 4).reshape(blocks, length, slots, width)
    columns = 2 * heads * width
    some = 2 if blocks % 2 == 0 else 1
    out = pl.BlockSpec((some, length, columns), lambda i, place: (i, 0, 0))
    far = pl.BlockSpec(memory_space=pltpu.HBM)
    result = pl.pallas_call(
        functools.partial(
            prepare_kernel, ctx_count, heads, [(bits, first) for bits, first, _ in cuts]
        ),
        grid_spec=pltpu.PrefetchScalarGridSpec(
            num_scalar_prefetch=1,
            grid=(blocks // some,),
            in_specs=[far, far],
            out_specs=[far] * len(cuts) + [out] * ctx_count,
            scratch_shapes=[
                pltpu.VMEM(view.shape, view.dtype),
                pltpu.VMEM((some * length * slots, width), jnp.float32),
                pltpu.SemaphoreType.DMA((len(cuts),)),
                pltpu.SemaphoreType.DMA((blocks // some,)),
            ],
        ),
        out_shape=[jax.ShapeDtypeStruct((rows, depth), tokens.dtype) for _, _, rows in cuts]
        + [jax.ShapeDtypeStruct((blocks, length, columns), jnp.bfloat16)] * ctx_count,
        compiler_params=params(),
        cost_estimate=cost("prepare"),
        name="prepare",
    )(place, tokens, view)
    return result[: len(cuts)], result[len(cuts) :]


def total_of(refs):
    return sum(ref[...].astype(jnp.float32).reshape(ref.shape[-2:]) for ref in refs)


def project_kernel(block_count, term_counts, place_ref, *refs):
    token_refs, weight_ref = refs[:block_count], refs[block_count]
    terms = refs[block_count + 1 : block_count + 1 + sum(term_counts)]
    out_ref, *sum_refs = refs[block_count + 1 + sum(term_counts) : -1]
    stacked = refs[-1]

    @pl.when(pl.program_id(0) == 0)
    def _():
        at = 0
        for token_ref in token_refs:
            rows = token_ref.shape[0]
            stacked[at : at + rows, :] = token_ref[...]
            at += rows
        at = 0
        for count, sum_ref in zip(term_counts, sum_refs):
            sum_ref[...] = total_of(terms[at : at + count]).astype(sum_ref.dtype)
            at += count

    out_ref[0] = jnp.dot(
        stacked[...], weight_ref[0, 0], preferred_element_type=jnp.float32
    ).astype(out_ref.dtype)


def piece_of(array, *index):
    rows, block, *leading = index
    shape = (1,) * len(leading) + (rows, array.shape[-1])
    return array, pl.BlockSpec(shape, lambda j, *_: (*leading, block, 0))


def project(place, blocks, weights, head_step, out_dtype, name, sums=()):
    head_count, ctx_count, depth, width = weights.shape
    row_total = sum(block.shape[0] for block in blocks)

    def block_spec(block):
        if block.shape[1] == depth:
            return pl.BlockSpec(block.shape, lambda j, place: (0, 0))
        return pl.BlockSpec((block.shape[0], depth), lambda j, place: (0, place[0]))

    pieces = [piece for terms in sums for piece in terms]
    sum_shapes = [terms[0][1].block_shape[-2:] for terms in sums]
    result = pl.pallas_call(
        functools.partial(project_kernel, len(blocks), [len(terms) for terms in sums]),
        grid_spec=pltpu.PrefetchScalarGridSpec(
            num_scalar_prefetch=1,
            grid=(ctx_count,),
            in_specs=[block_spec(block) for block in blocks]
            + [
                pl.BlockSpec(
                    (1, 1, depth, width),
                    lambda j, place: (
                        lax.rem(place[2] + head_step, head_count),
                        lax.rem(place[1] + j, ctx_count),
                        0,
                        0,
                    ),
                )
            ]
            + [spec for _, spec in pieces],
            out_specs=[pl.BlockSpec((1, row_total, width), lambda j, place: (j, 0, 0))]
            + [pl.BlockSpec(shape, lambda j, place: (0, 0)) for shape in sum_shapes],
            scratch_shapes=[pltpu.VMEM((row_total, depth), weights.dtype)],
        ),
        out_shape=[jax.ShapeDtypeStruct((ctx_count, row_total, width), out_dtype)]
        + [jax.ShapeDtypeStruct(shape, jnp.bfloat16) for shape in sum_shapes],
        compiler_params=params(),
        cost_estimate=cost(name),
        name=name,
    )(place, *blocks, weights, *(array for array, _ in pieces))
    return result if sums else result[0]


def pick_kernel(heads, ctx_count, place_ref, table_ref, *refs):
    pool_refs, (keys, values) = refs[:ctx_count], refs[ctx_count:]
    blocks, length, columns = pool_refs[0].shape
    wide = columns // 2
    width = wide // heads
    values[...] = jnp.ones_like(values)
    for at in range(table_ref.shape[0]):
        entry = table_ref[at]
        here = slice(at * length, (at + 1) * length)
        step = lax.rem(place_ref[1] - entry // blocks + ctx_count, ctx_count)
        for ctx_step, pool_ref in enumerate(pool_refs):

            @pl.when(step == ctx_step)
            def _():
                block = pool_ref[entry % blocks]
                keys[here, :] = block[:, :wide]
                put_values(values, here, block[:, wide:], heads)


def put_values(values, here, block, heads):
    width = block.shape[1] // heads
    for head in range(heads):
        low = head * (width + ONES)
        values[low : low + width, here] = (
            block[:, head * width : (head + 1) * width].astype(jnp.float32).T.astype(jnp.bfloat16)
        )


def pick_blocks(place, table, pools, heads):
    length, columns = pools[0].shape[1:]
    count = table.shape[0] * length
    wide = columns // 2
    tall = wide + heads * ONES
    return pl.pallas_call(
        functools.partial(pick_kernel, heads, len(pools)),
        grid_spec=pltpu.PrefetchScalarGridSpec(
            num_scalar_prefetch=2,
            grid=(1,),
            in_specs=[pl.BlockSpec(p.shape, lambda i, *_: (0, 0, 0)) for p in pools],
            out_specs=[
                pl.BlockSpec((count, wide), lambda i, *_: (0, 0)),
                pl.BlockSpec((tall, count), lambda i, *_: (0, 0)),
            ],
        ),
        out_shape=[
            jax.ShapeDtypeStruct((count, wide), jnp.bfloat16),
            jax.ShapeDtypeStruct((tall, count), jnp.bfloat16),
        ],
        compiler_params=params(),
        cost_estimate=cost("pick_blocks"),
        name="pick_blocks",
    )(place, table, *pools)


def each_part(rows, heads):
    part_rows = min(PART, rows)
    each = part_rows // heads
    for low in range(0, rows, part_rows):
        for head in range(heads):
            at = low + head * each
            yield head, pl.ds(low + head, each, stride=heads), slice(at, at + each)


def prefix_kernel(scale, heads, query_ref, keys, values, *refs):
    acc_ref, stat_ref, flat = refs[-3:]
    rows, width = query_ref.shape
    tall = width + ONES
    half = stat_ref.shape[0] // 2
    flat[...] = query_ref[...].astype(jnp.float32)
    for head, taken, here in each_part(rows, heads):
        query_block = flat[taken, :].astype(jnp.bfloat16)
        scores = dot_queries(keys[:, head * width : (head + 1) * width], query_block) * scale
        row_max, weights = softmax_parts(scores)
        mixed = jnp.dot(
            values[head * tall : (head + 1) * tall, :], weights, preferred_element_type=jnp.float32
        )
        acc_ref[:, here] = mixed[:width]
        stat_ref[:half, here] = jnp.broadcast_to(row_max, (half, row_max.shape[1]))
        stat_ref[half:, here] = jnp.broadcast_to(mixed[width : width + 1], (half, row_max.shape[1]))


def prefix_attend(query_rows, keys, values, chunk, scale, heads, part=(0, 1), state=None):
    all_rows, width = query_rows.shape
    row_total = all_rows // CHUNKS
    at, count = part
    rows = min(1024, row_total // count)
    steps = row_total // rows // count
    first = chunk * count * steps + at * steps
    out_specs = [
        pl.BlockSpec((width, rows), lambda i: (0, at * steps + i)),
        pl.BlockSpec((8, rows), lambda i: (0, at * steps + i)),
    ]
    in_specs = [
        pl.BlockSpec((rows, width), lambda i: (first + i, 0)),
        pl.BlockSpec(keys.shape, lambda i: (0, 0)),
        pl.BlockSpec(values.shape, lambda i: (0, 0)),
    ]
    operands = [query_rows, keys, values]
    aliases = {}
    if state is not None:
        in_specs += [pl.BlockSpec(memory_space=pl.ANY)] * 2
        operands += state
        aliases = {3: 0, 4: 1}
    return pl.pallas_call(
        functools.partial(prefix_kernel, scale, heads),
        grid=(steps,),
        in_specs=in_specs,
        out_specs=out_specs,
        out_shape=[
            jax.ShapeDtypeStruct((width, row_total), jnp.float32),
            jax.ShapeDtypeStruct((8, row_total), jnp.float32),
        ],
        input_output_aliases=aliases,
        scratch_shapes=[pltpu.VMEM((rows, width), jnp.float32)],
        compiler_params=params(),
        cost_estimate=cost("prefix_attend"),
        name="prefix_attend",
    )(*operands)


def fresh_kernel(
    scale, heads, per_token, first_row, counts, length_ref, query_ref, acc_ref, stat_ref, *rest
):
    early_count, term_count = counts
    earlier, terms = rest[:early_count], rest[early_count : early_count + term_count]
    out_ref, fresh_ref, keys, values, flat, mixed_rows = rest[-6:]
    rows, width = query_ref.shape
    wide, tall = heads * width, width + ONES
    step = pl.program_id(0)

    @pl.when(step == 0)
    def _():
        values[...] = jnp.ones_like(values)
        fresh_ref[...] = total_of(terms).astype(fresh_ref.dtype)
        for index, ref in enumerate([*earlier, fresh_ref]):
            here = slice(index * ref.shape[0], (index + 1) * ref.shape[0])
            fresh = ref[...]
            keys[here, :] = fresh[:, :wide]
            put_values(values, here, fresh[:, wide:], heads)

    half = stat_ref.shape[0] // 2
    flat[...] = query_ref[...].astype(jnp.float32)
    for head, taken, here in each_part(rows, heads):
        query_block = flat[taken, :].astype(jnp.bfloat16)
        scores = dot_queries(keys[:, head * width : (head + 1) * width], query_block) * scale
        row = taken.start + heads * lax.broadcasted_iota(jnp.int32, (1, taken.size), 1)
        token = first_row + step * (rows // per_token) + (
            row // per_token if per_token & (per_token - 1) else row >> (per_token.bit_length() - 1)
        )
        key_at = lax.broadcasted_iota(jnp.int32, scores.shape, 0)
        scores = jnp.where(key_at <= token, scores, -jnp.inf)
        old_max, old_total = stat_ref[:1, here], stat_ref[half : half + 1, here]
        row_max, weights = softmax_parts(scores, old_max)
        fade = jnp.exp2(old_max - row_max)
        mixed = jnp.dot(
            values[head * tall : (head + 1) * tall, :], weights, preferred_element_type=jnp.float32
        )
        row_total = old_total * fade + mixed[width : width + 1]
        share = jnp.where(token < length_ref[0], 1.0 / row_total, 0.0)
        result = acc_ref[:, here] * (fade * share) + mixed[:width] * share
        mixed_rows[taken, :] = result.T
    out_ref[...] = mixed_rows[...].astype(out_ref.dtype)


def fresh_attend(
    length, query_rows, acc, stat, earlier, pieces, result, chunk, scale, heads, per_token
):
    row_total, width = query_rows.shape
    chunk_rows = row_total // CHUNKS
    rows = min(1024, chunk_rows)
    steps = chunk_rows // rows
    block = pl.BlockSpec((rows, width), lambda i, length: (chunk * steps + i, 0))
    fresh_shape = pieces[0][1].block_shape[-2:]
    key_count = (len(earlier) + 1) * fresh_shape[0]
    whole = pl.BlockSpec(fresh_shape, lambda i, length: (0, 0))
    in_specs = [
        block,
        pl.BlockSpec((width, rows), lambda i, length: (0, i)),
        pl.BlockSpec((stat.shape[0], rows), lambda i, length: (0, i)),
        *(whole for _ in earlier),
        *(spec for _, spec in pieces),
    ]
    operands = [length, query_rows, acc, stat, *earlier, *(array for array, _ in pieces)]
    aliases = {}
    if result is not None:
        in_specs.append(pl.BlockSpec(memory_space=pl.ANY))
        aliases = {len(operands): 0}
        operands.append(result)
    return pl.pallas_call(
        functools.partial(
            fresh_kernel,
            scale,
            heads,
            per_token,
            chunk * (chunk_rows // per_token),
            (len(earlier), len(pieces)),
        ),
        grid_spec=pltpu.PrefetchScalarGridSpec(
            num_scalar_prefetch=1,
            grid=(steps,),
            in_specs=in_specs,
            out_specs=[block, whole],
            scratch_shapes=[
                pltpu.VMEM((key_count, heads * width), jnp.bfloat16),
                pltpu.VMEM((heads * (width + ONES), key_count), jnp.bfloat16),
                pltpu.VMEM((rows, width), jnp.float32),
                pltpu.VMEM((rows, width), jnp.float32),
            ],
        ),
        out_shape=[
            jax.ShapeDtypeStruct((row_total, width), jnp.bfloat16),
            jax.ShapeDtypeStruct(fresh_shape, jnp.bfloat16),
        ],
        input_output_aliases=aliases,
        compiler_params=params(),
        cost_estimate=cost("fresh_attend"),
        name="fresh_attend",
    )(*operands)


def reduced_shards(tokens, key_weight, value_weight, queries, prefix_pool, block_table, lengths):
    batch_count = lax.axis_size("batch")
    ctx_count = lax.axis_size("ctx")
    head_count = lax.axis_size("head")
    batch_at, ctx_at, head_at = (lax.axis_index(a) for a in ("batch", "ctx", "head"))
    place = jnp.stack([batch_at, ctx_at, head_at]).astype(jnp.int32)
    token_count = tokens.shape[0]
    heads = queries.shape[1]
    width = prefix_pool.shape[4] // 2
    group = queries.shape[3] // width
    per_token = heads * group
    depth = key_weight.shape[2]
    rows = token_count // CHUNKS
    scale = math.log2(math.e) / math.sqrt(width)

    top = batch_count // 2
    steps = list(range(batch_count - 1, top, -1)) + list(range(1, top))
    cuts = [(bits, 0, token_count) for bits in [*steps, top]]
    pieces, pools = prepare(place, tokens, depth, cuts, prefix_pool, ctx_count, heads)
    arrived = [trade(piece, "batch", bits) for piece, (bits, _, _) in zip(pieces, cuts[:-1])]
    pools, (key_weight, value_weight) = after(pools, (key_weight, value_weight))
    pools = [shift(part, "ctx", step) if step else part for step, part in enumerate(pools)]

    weights = arrange_weights(key_weight, value_weight, ctx_count, heads, head_count)
    weights, last = after(weights, pieces[-1])
    last = trade(last, "batch", top)

    query_rows = queries.reshape(token_count, heads, group, width)
    query_rows = query_rows.transpose(0, 2, 1, 3).reshape(-1, width)
    def projected(blocks, name):
        terms = [
            shift(project(place, blocks, weights, step, jnp.bfloat16, name + "_away"), "head", step)
            for step in range(1, head_count)
        ]
        return [project(place, blocks, weights, 0, jnp.float32, name + "_kept"), *terms]

    def added(terms, step, here):
        return sum(term[step, here].astype(jnp.float32) for term in terms)

    def others(terms, here):
        return [added(terms, step, here).astype(jnp.bfloat16) for step in range(1, ctx_count)]

    def spread(parts):
        return [shift(part, "ctx", step + 1) for step, part in enumerate(parts)]

    every = slice(None)
    parts_of = [slice(i * rows, (i + 1) * rows) for i in range(CHUNKS)]

    sums = [[], []]
    if steps:
        early = projected(arrived, "early")
        cuts = [slice(i * token_count, (i + 1) * token_count) for i in range(len(steps))]
        leaving = [others(early, cut) for cut in cuts]
        leaving, pools = after(leaving, pools)
        sums = [
            [
                [piece_of(t, token_count, i, 0) for t in early]
                + [piece_of(p, token_count, 0) for p in spread(parts)]
            ]
            for i, parts in enumerate(leaving)
        ]
    keys, values = pick_blocks(place, block_table[0], pools, heads)
    states = [prefix_attend(query_rows, keys, values, 0, scale, heads)]
    states[0], last = after(states[0], last)

    def late_project(step, dtype, name, sums):
        result = project(place, [last, tokens], weights, step, dtype, name, sums)
        return result if sums else (result,)

    terms = []
    for step in range(1, head_count):
        term, *far = late_project(step, jnp.bfloat16, "late_away", sums[0] + sums[1] if step == 1 else [])
        terms.append(shift(term, "head", step))
    kept, *_ = late_project(0, jnp.float32, "late_kept", [])
    far, near = far[:1], far[1:]
    late = [kept, *terms]
    far = [trade(part, "batch", 1) for part in far]
    own_at = slice(token_count, 2 * token_count)
    *late_others, own_others = [others(late, here) for here in [*parts_of, own_at]]
    late_others[0] = spread(late_others[0])
    late_others[1], (keys, values) = after(late_others[1], (keys, values))
    state = prefix_attend(query_rows, keys, values, 1, scale, heads, (0, 2))
    state, (late_others[1], own_others, near) = after(state, (late_others[1], own_others, near))
    late_others[1], own_others = spread(late_others[1]), spread(own_others)
    near = [trade(part, "batch", 1) for part in near]

    away = []
    for chunk, here in enumerate(parts_of):
        part = added(late, 0, here) + sum(p.astype(jnp.float32) for p in late_others[chunk])
        part = part + sum(p[here].astype(jnp.float32) for p in far)
        part = part.astype(jnp.bfloat16)
        if chunk == 0:
            (far, late), late_others[1] = after((far, late), late_others[1])
            part, state = after(part, state)
        else:
            away[-1], part = after(away[-1], part)
        away.append(trade(part, "batch", top))
    states.append(prefix_attend(query_rows, keys, values, 1, scale, heads, (1, 2), state))

    result = None
    fresh = []
    for chunk in range(CHUNKS):
        pieces = [piece_of(t, rows, CHUNKS + chunk, 0) for t in late]
        pieces += [piece_of(part, rows, chunk) for part in (*own_others, *near)]
        pieces.append(piece_of(away[chunk], rows, 0))
        result, new = fresh_attend(
            lengths,
            query_rows,
            *states[chunk],
            fresh,
            pieces,
            result,
            chunk,
            scale,
            heads,
            per_token,
        )
        fresh.append(new)
    result = result.reshape(token_count, group, heads, width).transpose(0, 2, 1, 3)
    return result.reshape(token_count, heads, 1, group * width)


def solution(mesh):
    def shards(tokens, key_weight, value_weight, *rest):
        prompts = mesh.shape["batch"]
        columns = 2 * math.prod(key_weight.shape[3:])
        few_tokens = prompts * tokens.shape[0] <= columns and prompts in (2, 4)
        form = reduced_shards if few_tokens else gathered_shards
        return form(tokens, key_weight, value_weight, *rest)

    return jax.shard_map(
        shards,
        mesh=mesh,
        in_specs=(
            P(("groups", "batch"), ("ctx", "head")),
            P("ctx", "head", "batch", None, None, None),
            P("ctx", "head", "batch", None, None, None),
            P(("groups", "batch"), "ctx", "head", None),
            P(("groups", "ctx"), None, None, "head", None),
            P(("groups", "batch"), None),
            P(("groups", "batch")),
        ),
        out_specs=P(("groups", "batch"), "ctx", "head", None),
        check_vma=False,
    )
```

```python
import functools
import math

import jax
import jax.numpy as jnp
from jax import lax
from jax.experimental import pallas as pl
from jax.experimental.pallas import tpu as pltpu
from jax.sharding import PartitionSpec as P

CHUNKS = 2
PART = 1024
ONES = 16
VMEM_BYTES = 16 * 1024 * 1024
MOST_VMEM_BYTES = 60 * 1024 * 1024
LONG = pl.CostEstimate(flops=10**11, bytes_accessed=1, transcendentals=0)
COSTS = {}


def cost(name):
    return COSTS.get(name, LONG)


def attend_head(query_rows, prefix, fresh_rows, length):
    token_count = query_rows.shape[0]
    head_width = prefix.shape[1] // 2
    group_size = query_rows.shape[1] // head_width
    prefix_len = prefix.shape[0]
    key_rows = jnp.concatenate([prefix[:, :head_width], fresh_rows[:, :head_width]], 0)
    value_rows = jnp.concatenate([prefix[:, head_width:], fresh_rows[:, head_width:]], 0)
    block_len = min(token_count, 64)
    pieces = []
    for first_row in range(0, token_count, block_len):
        block_rows = query_rows[first_row : first_row + block_len].reshape(
            block_len * group_size, head_width
        )
        scores = jnp.dot(
            block_rows, key_rows.T, preferred_element_type=jnp.float32
        ) * head_width ** (-0.5)
        position = first_row + jnp.arange(block_len * group_size) // group_size
        column = jnp.arange(prefix_len + token_count) - prefix_len
        allowed = column[None, :] <= position[:, None]
        scores = jnp.where(allowed, scores, -jnp.inf)
        row_max = jnp.max(scores, axis=1, keepdims=True)
        weights = jnp.exp(scores - row_max)
        row_total = jnp.sum(weights, axis=1, keepdims=True)
        probs_bf = (weights / row_total).astype(jnp.bfloat16)
        mixed_rows = jnp.dot(probs_bf, value_rows, preferred_element_type=jnp.float32)
        is_live = position < length
        mixed_rows = jnp.where(is_live[:, None], mixed_rows, 0.0)
        pieces.append(mixed_rows.astype(jnp.bfloat16).reshape(block_len, group_size * head_width))
    return jnp.concatenate(pieces, 0)


def gathered_shards(tokens, key_weight, value_weight, queries, prefix_pool, block_table, lengths):
    token_count = tokens.shape[0]
    local_heads = queries.shape[1]
    head_width = prefix_pool.shape[4] // 2
    ctx_count = lax.axis_size("ctx")
    head_count = lax.axis_size("head")
    features = lax.all_gather(tokens, ("ctx", "head"), axis=1, tiled=True)
    key_cols, value_cols = (
        lax.all_to_all(
            lax.all_to_all(weight, "ctx", split_axis=3, concat_axis=0, tiled=True),
            "head",
            split_axis=4,
            concat_axis=1,
            tiled=True,
        )
        for weight in (key_weight, value_weight)
    )
    span_len = features.shape[1] // (ctx_count * head_count)
    feature_view = features.reshape(token_count, ctx_count, head_count, span_len)
    pieces = (
        lax.all_gather(key_cols, "batch", axis=2, tiled=True),
        lax.all_gather(value_cols, "batch", axis=2, tiled=True),
    )
    row_count = pieces[0].shape[2]

    def one_term(weight_piece):
        shaped = weight_piece.reshape(ctx_count, head_count, row_count, local_heads * head_width)
        return jnp.einsum("tchr,chrk->tk", feature_view, shaped, preferred_element_type=jnp.float32)

    new_keys = one_term(pieces[0]).astype(jnp.bfloat16).reshape(token_count, local_heads, head_width)
    new_values = one_term(pieces[1]).astype(jnp.bfloat16).reshape(token_count, local_heads, head_width)
    fresh_all = jnp.concatenate([new_keys, new_values], 2)
    pool_heads = lax.all_to_all(prefix_pool, "ctx", split_axis=2, concat_axis=0, tiled=True)
    chosen = jnp.take(pool_heads, block_table[0], axis=0)
    chosen = chosen.reshape(-1, local_heads, 2 * head_width)
    outputs = [
        attend_head(
            queries[:, head_idx, 0], chosen[:, head_idx], fresh_all[:, head_idx], lengths[0]
        )
        for head_idx in range(local_heads)
    ]
    return jnp.stack(outputs, 1)[:, :, None, :]


def shift(array, axis, step):
    count = lax.axis_size(axis)
    return lax.ppermute(array, axis, [(i, (i + step) % count) for i in range(count)])


def trade(array, axis, bits):
    return lax.ppermute(array, axis, [(i, i ^ bits) for i in range(lax.axis_size(axis))])


def after(first, second):
    return lax.optimization_barrier((first, second))


def softmax_parts(scores, old_max=None):
    row_max = jnp.max(scores, axis=0, keepdims=True)
    if old_max is not None:
        row_max = jnp.maximum(row_max, old_max)
    return row_max, jnp.exp2(scores - row_max).astype(jnp.bfloat16)


def dot_queries(keys, query_block):
    return lax.dot_general(
        keys, query_block, (((1,), (1,)), ((), ())), preferred_element_type=jnp.float32
    )


def params(limit=None):
    return pltpu.CompilerParams(vmem_limit_bytes=limit or VMEM_BYTES)


def weight_kernel(ctx_count, heads, head_count, key_ref, value_ref, out_ref, flat):
    depth, slots, width = key_ref.shape
    for kind, ref in enumerate((key_ref, value_ref)):
        flat[...] = ref[...].astype(jnp.float32).reshape(depth * slots, width)
        for ctx in range(ctx_count):
            for head in range(heads):
                for core in range(head_count):
                    slot = (ctx * heads + head) * head_count + core
                    at = (kind * heads + head) * width
                    out_ref[core, ctx, :, at : at + width] = flat[
                        pl.ds(slot, depth, stride=slots), :
                    ].astype(out_ref.dtype)


def arrange_weights(key_weight, value_weight, ctx_count, heads, head_count):
    depth, width = key_weight.shape[2], key_weight.shape[5]
    slots = ctx_count * heads * head_count
    rows = min(128, depth)
    views = [w.reshape(depth, slots, width) for w in (key_weight, value_weight)]
    block = pl.BlockSpec((rows, slots, width), lambda i: (i, 0, 0))
    columns = 2 * heads * width
    return pl.pallas_call(
        functools.partial(weight_kernel, ctx_count, heads, head_count),
        grid=(depth // rows,),
        in_specs=[block, block],
        out_specs=pl.BlockSpec((head_count, ctx_count, rows, columns), lambda i: (0, 0, i, 0)),
        out_shape=jax.ShapeDtypeStruct((head_count, ctx_count, depth, columns), jnp.bfloat16),
        scratch_shapes=[pltpu.VMEM((rows * slots, width), jnp.float32)],
        compiler_params=params(),
        cost_estimate=cost("arrange_weights"),
        name="arrange_weights",
    )(*views)


def cut_kernel(bits, place_ref, tokens_ref, *refs):
    pieces, sems = refs[:-1], refs[-1]
    depth = pieces[0].shape[1]
    copies = []
    for index, piece in enumerate(pieces):
        start = pl.multiple_of((place_ref[0] ^ bits[index]) * depth, depth)
        source = tokens_ref.at[:, pl.ds(start, depth)]
        copies.append(pltpu.make_async_copy(source, piece, sems.at[index]))
    for copy in copies:
        copy.start()
    for copy in copies:
        copy.wait()


def cut_tokens(place, tokens, depth, bits):
    far = pl.BlockSpec(memory_space=pltpu.HBM)
    piece = jax.ShapeDtypeStruct((tokens.shape[0], depth), tokens.dtype)
    return pl.pallas_call(
        functools.partial(cut_kernel, bits),
        grid_spec=pltpu.PrefetchScalarGridSpec(
            num_scalar_prefetch=1,
            grid=(1,),
            in_specs=[far],
            out_specs=[far] * len(bits),
            scratch_shapes=[pltpu.SemaphoreType.DMA((len(bits),))],
        ),
        out_shape=[piece] * len(bits),
        compiler_params=params(MOST_VMEM_BYTES),
        cost_estimate=cost("cut_tokens"),
        name="cut_tokens",
    )(place, tokens)


def pool_kernel(ctx_count, heads, place_ref, pool_ref, *refs):
    outs, flat = refs[:-1], refs[-1]
    some, length, slots, width = pool_ref.shape
    length *= some
    flat[...] = pool_ref[...].astype(jnp.float32).reshape(length * slots, width)
    for kind in range(2):
        for head in range(heads):
            at = (kind * heads + head) * width
            held = []
            for ctx in range(ctx_count):
                slot = (kind * ctx_count + ctx) * heads + head
                held.append(flat[pl.ds(slot, length, stride=slots), :])
            for step, out_ref in enumerate(outs):
                target = lax.rem(place_ref[1] + step, ctx_count)
                value = held[0]
                for ctx in range(1, ctx_count):
                    value = jnp.where(target == ctx, held[ctx], value)
                out_ref[:, :, at : at + width] = value.astype(out_ref.dtype).reshape(
                    some, length // some, width
                )


def arrange_pool(place, prefix_pool, ctx_count, heads):
    blocks, length, all_heads, _, double = prefix_pool.shape
    width = double // 2
    slots = 2 * all_heads
    view = prefix_pool.reshape(blocks, length, all_heads, 2, width)
    view = view.transpose(0, 1, 3, 2, 4).reshape(blocks, length, slots, width)
    columns = 2 * heads * width
    some = 2 if blocks % 2 == 0 else 1
    out = pl.BlockSpec((some, length, columns), lambda i, place: (i, 0, 0))
    return pl.pallas_call(
        functools.partial(pool_kernel, ctx_count, heads),
        grid_spec=pltpu.PrefetchScalarGridSpec(
            num_scalar_prefetch=1,
            grid=(blocks // some,),
            in_specs=[pl.BlockSpec((some, length, slots, width), lambda i, place: (i, 0, 0, 0))],
            out_specs=[out] * ctx_count,
            scratch_shapes=[pltpu.VMEM((some * length * slots, width), jnp.float32)],
        ),
        out_shape=[jax.ShapeDtypeStruct((blocks, length, columns), jnp.bfloat16)] * ctx_count,
        compiler_params=params(),
        cost_estimate=cost("arrange_pool"),
        name="arrange_pool",
    )(place, view)


def total_of(refs):
    return sum(ref[...].astype(jnp.float32).reshape(ref.shape[-2:]) for ref in refs)


def project_kernel(block_count, term_counts, place_ref, *refs):
    token_refs, weight_ref = refs[:block_count], refs[block_count]
    terms = refs[block_count + 1 : block_count + 1 + sum(term_counts)]
    out_ref, *sum_refs = refs[block_count + 1 + sum(term_counts) : -1]
    stacked = refs[-1]

    @pl.when(pl.program_id(0) == 0)
    def _():
        at = 0
        for token_ref in token_refs:
            rows = token_ref.shape[0]
            stacked[at : at + rows, :] = token_ref[...]
            at += rows
        at = 0
        for count, sum_ref in zip(term_counts, sum_refs):
            sum_ref[...] = total_of(terms[at : at + count]).astype(sum_ref.dtype)
            at += count

    out_ref[0] = jnp.dot(
        stacked[...], weight_ref[0, 0], preferred_element_type=jnp.float32
    ).astype(out_ref.dtype)


def piece_of(array, *index):
    rows, block, *leading = index
    shape = (1,) * len(leading) + (rows, array.shape[-1])
    return array, pl.BlockSpec(shape, lambda j, *_: (*leading, block, 0))


def project(place, blocks, weights, head_step, out_dtype, name, sums=()):
    head_count, ctx_count, depth, width = weights.shape
    row_total = sum(block.shape[0] for block in blocks)

    def block_spec(block):
        if block.shape[1] == depth:
            return pl.BlockSpec(block.shape, lambda j, place: (0, 0))
        return pl.BlockSpec((block.shape[0], depth), lambda j, place: (0, place[0]))

    pieces = [piece for terms in sums for piece in terms]
    sum_shapes = [terms[0][1].block_shape[-2:] for terms in sums]
    result = pl.pallas_call(
        functools.partial(project_kernel, len(blocks), [len(terms) for terms in sums]),
        grid_spec=pltpu.PrefetchScalarGridSpec(
            num_scalar_prefetch=1,
            grid=(ctx_count,),
            in_specs=[block_spec(block) for block in blocks]
            + [
                pl.BlockSpec(
                    (1, 1, depth, width),
                    lambda j, place: (
                        lax.rem(place[2] + head_step, head_count),
                        lax.rem(place[1] + j, ctx_count),
                        0,
                        0,
                    ),
                )
            ]
            + [spec for _, spec in pieces],
            out_specs=[pl.BlockSpec((1, row_total, width), lambda j, place: (j, 0, 0))]
            + [pl.BlockSpec(shape, lambda j, place: (0, 0)) for shape in sum_shapes],
            scratch_shapes=[pltpu.VMEM((row_total, depth), weights.dtype)],
        ),
        out_shape=[jax.ShapeDtypeStruct((ctx_count, row_total, width), out_dtype)]
        + [jax.ShapeDtypeStruct(shape, jnp.bfloat16) for shape in sum_shapes],
        compiler_params=params(),
        cost_estimate=cost(name),
        name=name,
    )(place, *blocks, weights, *(array for array, _ in pieces))
    return result if sums else result[0]


def pick_kernel(heads, ctx_count, place_ref, table_ref, *refs):
    pool_refs, (keys, values) = refs[:ctx_count], refs[ctx_count:]
    blocks, length, columns = pool_refs[0].shape
    wide = columns // 2
    width = wide // heads
    values[...] = jnp.ones_like(values)
    for at in range(table_ref.shape[0]):
        entry = table_ref[at]
        here = slice(at * length, (at + 1) * length)
        step = lax.rem(place_ref[1] - entry // blocks + ctx_count, ctx_count)
        for ctx_step, pool_ref in enumerate(pool_refs):

            @pl.when(step == ctx_step)
            def _():
                block = pool_ref[entry % blocks]
                keys[here, :] = block[:, :wide]
                put_values(values, here, block[:, wide:], heads)


def put_values(values, here, block, heads):
    width = block.shape[1] // heads
    for head in range(heads):
        low = head * (width + ONES)
        values[low : low + width, here] = (
            block[:, head * width : (head + 1) * width].astype(jnp.float32).T.astype(jnp.bfloat16)
        )


def pick_blocks(place, table, pools, heads):
    length, columns = pools[0].shape[1:]
    count = table.shape[0] * length
    wide = columns // 2
    tall = wide + heads * ONES
    return pl.pallas_call(
        functools.partial(pick_kernel, heads, len(pools)),
        grid_spec=pltpu.PrefetchScalarGridSpec(
            num_scalar_prefetch=2,
            grid=(1,),
            in_specs=[pl.BlockSpec(p.shape, lambda i, *_: (0, 0, 0)) for p in pools],
            out_specs=[
                pl.BlockSpec((count, wide), lambda i, *_: (0, 0)),
                pl.BlockSpec((tall, count), lambda i, *_: (0, 0)),
            ],
        ),
        out_shape=[
            jax.ShapeDtypeStruct((count, wide), jnp.bfloat16),
            jax.ShapeDtypeStruct((tall, count), jnp.bfloat16),
        ],
        compiler_params=params(),
        cost_estimate=cost("pick_blocks"),
        name="pick_blocks",
    )(place, table, *pools)


def each_part(rows, heads):
    part_rows = min(PART, rows)
    each = part_rows // heads
    for low in range(0, rows, part_rows):
        for head in range(heads):
            at = low + head * each
            yield head, pl.ds(low + head, each, stride=heads), slice(at, at + each)


def prefix_kernel(scale, heads, query_ref, keys, values, *refs):
    acc_ref, stat_ref, flat = refs[-3:]
    rows, width = query_ref.shape
    tall = width + ONES
    half = stat_ref.shape[0] // 2
    flat[...] = query_ref[...].astype(jnp.float32)
    for head, taken, here in each_part(rows, heads):
        query_block = flat[taken, :].astype(jnp.bfloat16)
        scores = dot_queries(keys[:, head * width : (head + 1) * width], query_block) * scale
        row_max, weights = softmax_parts(scores)
        mixed = jnp.dot(
            values[head * tall : (head + 1) * tall, :], weights, preferred_element_type=jnp.float32
        )
        acc_ref[:, here] = mixed[:width]
        stat_ref[:half, here] = jnp.broadcast_to(row_max, (half, row_max.shape[1]))
        stat_ref[half:, here] = jnp.broadcast_to(mixed[width : width + 1], (half, row_max.shape[1]))


def prefix_attend(query_rows, keys, values, chunk, scale, heads, part=(0, 1), state=None):
    all_rows, width = query_rows.shape
    row_total = all_rows // CHUNKS
    at, count = part
    rows = min(1024, row_total // count)
    steps = row_total // rows // count
    first = chunk * count * steps + at * steps
    out_specs = [
        pl.BlockSpec((width, rows), lambda i: (0, at * steps + i)),
        pl.BlockSpec((8, rows), lambda i: (0, at * steps + i)),
    ]
    in_specs = [
        pl.BlockSpec((rows, width), lambda i: (first + i, 0)),
        pl.BlockSpec(keys.shape, lambda i: (0, 0)),
        pl.BlockSpec(values.shape, lambda i: (0, 0)),
    ]
    operands = [query_rows, keys, values]
    aliases = {}
    if state is not None:
        in_specs += [pl.BlockSpec(memory_space=pl.ANY)] * 2
        operands += state
        aliases = {3: 0, 4: 1}
    return pl.pallas_call(
        functools.partial(prefix_kernel, scale, heads),
        grid=(steps,),
        in_specs=in_specs,
        out_specs=out_specs,
        out_shape=[
            jax.ShapeDtypeStruct((width, row_total), jnp.float32),
            jax.ShapeDtypeStruct((8, row_total), jnp.float32),
        ],
        input_output_aliases=aliases,
        scratch_shapes=[pltpu.VMEM((rows, width), jnp.float32)],
        compiler_params=params(),
        cost_estimate=cost("prefix_attend"),
        name="prefix_attend",
    )(*operands)


def fresh_kernel(
    scale, heads, per_token, first_row, counts, length_ref, query_ref, acc_ref, stat_ref, *rest
):
    early_count, term_count = counts
    earlier, terms = rest[:early_count], rest[early_count : early_count + term_count]
    out_ref, fresh_ref, keys, values, flat, mixed_rows = rest[-6:]
    rows, width = query_ref.shape
    wide, tall = heads * width, width + ONES
    step = pl.program_id(0)

    @pl.when(step == 0)
    def _():
        values[...] = jnp.ones_like(values)
        fresh_ref[...] = total_of(terms).astype(fresh_ref.dtype)
        for index, ref in enumerate([*earlier, fresh_ref]):
            here = slice(index * ref.shape[0], (index + 1) * ref.shape[0])
            fresh = ref[...]
            keys[here, :] = fresh[:, :wide]
            put_values(values, here, fresh[:, wide:], heads)

    half = stat_ref.shape[0] // 2
    flat[...] = query_ref[...].astype(jnp.float32)
    for head, taken, here in each_part(rows, heads):
        query_block = flat[taken, :].astype(jnp.bfloat16)
        scores = dot_queries(keys[:, head * width : (head + 1) * width], query_block) * scale
        row = taken.start + heads * lax.broadcasted_iota(jnp.int32, (1, taken.size), 1)
        token = first_row + step * (rows // per_token) + (
            row // per_token if per_token & (per_token - 1) else row >> (per_token.bit_length() - 1)
        )
        key_at = lax.broadcasted_iota(jnp.int32, scores.shape, 0)
        scores = jnp.where(key_at <= token, scores, -jnp.inf)
        old_max, old_total = stat_ref[:1, here], stat_ref[half : half + 1, here]
        row_max, weights = softmax_parts(scores, old_max)
        fade = jnp.exp2(old_max - row_max)
        mixed = jnp.dot(
            values[head * tall : (head + 1) * tall, :], weights, preferred_element_type=jnp.float32
        )
        row_total = old_total * fade + mixed[width : width + 1]
        share = jnp.where(token < length_ref[0], 1.0 / row_total, 0.0)
        result = acc_ref[:, here] * (fade * share) + mixed[:width] * share
        mixed_rows[taken, :] = result.T
    out_ref[...] = mixed_rows[...].astype(out_ref.dtype)


def fresh_attend(
    length, query_rows, acc, stat, earlier, pieces, result, chunk, scale, heads, per_token
):
    row_total, width = query_rows.shape
    chunk_rows = row_total // CHUNKS
    rows = min(1024, chunk_rows)
    steps = chunk_rows // rows
    block = pl.BlockSpec((rows, width), lambda i, length: (chunk * steps + i, 0))
    fresh_shape = pieces[0][1].block_shape[-2:]
    key_count = (len(earlier) + 1) * fresh_shape[0]
    whole = pl.BlockSpec(fresh_shape, lambda i, length: (0, 0))
    in_specs = [
        block,
        pl.BlockSpec((width, rows), lambda i, length: (0, i)),
        pl.BlockSpec((stat.shape[0], rows), lambda i, length: (0, i)),
        *(whole for _ in earlier),
        *(spec for _, spec in pieces),
    ]
    operands = [length, query_rows, acc, stat, *earlier, *(array for array, _ in pieces)]
    aliases = {}
    if result is not None:
        in_specs.append(pl.BlockSpec(memory_space=pl.ANY))
        aliases = {len(operands): 0}
        operands.append(result)
    return pl.pallas_call(
        functools.partial(
            fresh_kernel,
            scale,
            heads,
            per_token,
            chunk * (chunk_rows // per_token),
            (len(earlier), len(pieces)),
        ),
        grid_spec=pltpu.PrefetchScalarGridSpec(
            num_scalar_prefetch=1,
            grid=(steps,),
            in_specs=in_specs,
            out_specs=[block, whole],
            scratch_shapes=[
                pltpu.VMEM((key_count, heads * width), jnp.bfloat16),
                pltpu.VMEM((heads * (width + ONES), key_count), jnp.bfloat16),
                pltpu.VMEM((rows, width), jnp.float32),
                pltpu.VMEM((rows, width), jnp.float32),
            ],
        ),
        out_shape=[
            jax.ShapeDtypeStruct((row_total, width), jnp.bfloat16),
            jax.ShapeDtypeStruct(fresh_shape, jnp.bfloat16),
        ],
        input_output_aliases=aliases,
        compiler_params=params(),
        cost_estimate=cost("fresh_attend"),
        name="fresh_attend",
    )(*operands)


def reduced_shards(tokens, key_weight, value_weight, queries, prefix_pool, block_table, lengths):
    batch_count = lax.axis_size("batch")
    ctx_count = lax.axis_size("ctx")
    head_count = lax.axis_size("head")
    batch_at, ctx_at, head_at = (lax.axis_index(a) for a in ("batch", "ctx", "head"))
    place = jnp.stack([batch_at, ctx_at, head_at]).astype(jnp.int32)
    token_count = tokens.shape[0]
    heads = queries.shape[1]
    width = prefix_pool.shape[4] // 2
    group = queries.shape[3] // width
    per_token = heads * group
    depth = key_weight.shape[2]
    rows = token_count // CHUNKS
    scale = math.log2(math.e) / math.sqrt(width)

    top = batch_count // 2
    steps = list(range(batch_count - 1, top, -1)) + list(range(1, top))
    pieces = cut_tokens(place, tokens, depth, [*steps, top])
    pieces, prefix_pool = after(pieces, prefix_pool)
    arrived = [trade(piece, "batch", bits) for piece, bits in zip(pieces, steps)]
    pools = arrange_pool(place, prefix_pool, ctx_count, heads)
    pools, (key_weight, value_weight) = after(pools, (key_weight, value_weight))
    pools = [shift(part, "ctx", step) if step else part for step, part in enumerate(pools)]

    weights = arrange_weights(key_weight, value_weight, ctx_count, heads, head_count)
    weights, last = after(weights, pieces[-1])
    last = trade(last, "batch", top)

    query_rows = queries.reshape(token_count, heads, group, width)
    query_rows = query_rows.transpose(0, 2, 1, 3).reshape(-1, width)
    def projected(blocks, name):
        terms = [
            shift(project(place, blocks, weights, step, jnp.bfloat16, name + "_away"), "head", step)
            for step in range(1, head_count)
        ]
        return [project(place, blocks, weights, 0, jnp.float32, name + "_kept"), *terms]

    def added(terms, step, here):
        return sum(term[step, here].astype(jnp.float32) for term in terms)

    def others(terms, here):
        return [added(terms, step, here).astype(jnp.bfloat16) for step in range(1, ctx_count)]

    def spread(parts):
        return [shift(part, "ctx", step + 1) for step, part in enumerate(parts)]

    every = slice(None)
    parts_of = [slice(i * rows, (i + 1) * rows) for i in range(CHUNKS)]

    sums = [[], []]
    if steps:
        early = projected(arrived, "early")
        cuts = [slice(i * token_count, (i + 1) * token_count) for i in range(len(steps))]
        leaving = [others(early, cut) for cut in cuts]
        leaving, pools = after(leaving, pools)
        sums = [
            [
                [piece_of(t, token_count, i, 0) for t in early]
                + [piece_of(p, token_count, 0) for p in spread(parts)]
            ]
            for i, parts in enumerate(leaving)
        ]
    keys, values = pick_blocks(place, block_table[0], pools, heads)
    states = [prefix_attend(query_rows, keys, values, 0, scale, heads)]
    states[0], last = after(states[0], last)

    def late_project(step, dtype, name, sums):
        result = project(place, [last, tokens], weights, step, dtype, name, sums)
        return result if sums else (result,)

    terms = []
    for step in range(1, head_count):
        term, *far = late_project(step, jnp.bfloat16, "late_away", sums[0] + sums[1] if step == 1 else [])
        terms.append(shift(term, "head", step))
    kept, *_ = late_project(0, jnp.float32, "late_kept", [])
    far, near = far[:1], far[1:]
    late = [kept, *terms]
    far = [trade(part, "batch", 1) for part in far]
    own_at = slice(token_count, 2 * token_count)
    *late_others, own_others = [others(late, here) for here in [*parts_of, own_at]]
    late_others[0] = spread(late_others[0])
    late_others[1], (keys, values) = after(late_others[1], (keys, values))
    state = prefix_attend(query_rows, keys, values, 1, scale, heads, (0, 2))
    state, (late_others[1], own_others, near) = after(state, (late_others[1], own_others, near))
    late_others[1], own_others = spread(late_others[1]), spread(own_others)
    near = [trade(part, "batch", 1) for part in near]

    away = []
    for chunk, here in enumerate(parts_of):
        part = added(late, 0, here) + sum(p.astype(jnp.float32) for p in late_others[chunk])
        part = part + sum(p[here].astype(jnp.float32) for p in far)
        part = part.astype(jnp.bfloat16)
        if chunk == 0:
            (far, late), late_others[1] = after((far, late), late_others[1])
            part, state = after(part, state)
        else:
            away[-1], part = after(away[-1], part)
        away.append(trade(part, "batch", top))
    states.append(prefix_attend(query_rows, keys, values, 1, scale, heads, (1, 2), state))

    result = None
    fresh = []
    for chunk in range(CHUNKS):
        pieces = [piece_of(t, rows, CHUNKS + chunk, 0) for t in late]
        pieces += [piece_of(part, rows, chunk) for part in (*own_others, *near)]
        pieces.append(piece_of(away[chunk], rows, 0))
        result, new = fresh_attend(
            lengths,
            query_rows,
            *states[chunk],
            fresh,
            pieces,
            result,
            chunk,
            scale,
            heads,
            per_token,
        )
        fresh.append(new)
    result = result.reshape(token_count, group, heads, width).transpose(0, 2, 1, 3)
    return result.reshape(token_count, heads, 1, group * width)


def solution(mesh):
    def shards(tokens, key_weight, value_weight, *rest):
        prompts = mesh.shape["batch"]
        columns = 2 * math.prod(key_weight.shape[3:])
        few_tokens = prompts * tokens.shape[0] <= columns and prompts in (2, 4)
        form = reduced_shards if few_tokens else gathered_shards
        return form(tokens, key_weight, value_weight, *rest)

    return jax.shard_map(
        shards,
        mesh=mesh,
        in_specs=(
            P(("groups", "batch"), ("ctx", "head")),
            P("ctx", "head", "batch", None, None, None),
            P("ctx", "head", "batch", None, None, None),
            P(("groups", "batch"), "ctx", "head", None),
            P(("groups", "ctx"), None, None, "head", None),
            P(("groups", "batch"), None),
            P(("groups", "batch")),
        ),
        out_specs=P(("groups", "batch"), "ctx", "head", None),
        check_vma=False,
    )
```

```python
import functools
import math

import jax
import jax.numpy as jnp
from jax import lax
from jax.experimental import pallas as pl
from jax.experimental.pallas import tpu as pltpu
from jax.sharding import PartitionSpec as P

CHUNKS = 2
PART = 1024
ONES = 16
VMEM_BYTES = 16 * 1024 * 1024
MOST_VMEM_BYTES = 60 * 1024 * 1024
LONG = pl.CostEstimate(flops=10**11, bytes_accessed=1, transcendentals=0)
COSTS = {}


def cost(name):
    return COSTS.get(name, LONG)


def attend_head(query_rows, prefix, fresh_rows, length):
    token_count = query_rows.shape[0]
    head_width = prefix.shape[1] // 2
    group_size = query_rows.shape[1] // head_width
    prefix_len = prefix.shape[0]
    key_rows = jnp.concatenate([prefix[:, :head_width], fresh_rows[:, :head_width]], 0)
    value_rows = jnp.concatenate([prefix[:, head_width:], fresh_rows[:, head_width:]], 0)
    block_len = min(token_count, 64)
    pieces = []
    for first_row in range(0, token_count, block_len):
        block_rows = query_rows[first_row : first_row + block_len].reshape(
            block_len * group_size, head_width
        )
        scores = jnp.dot(
            block_rows, key_rows.T, preferred_element_type=jnp.float32
        ) * head_width ** (-0.5)
        position = first_row + jnp.arange(block_len * group_size) // group_size
        column = jnp.arange(prefix_len + token_count) - prefix_len
        allowed = column[None, :] <= position[:, None]
        scores = jnp.where(allowed, scores, -jnp.inf)
        row_max = jnp.max(scores, axis=1, keepdims=True)
        weights = jnp.exp(scores - row_max)
        row_total = jnp.sum(weights, axis=1, keepdims=True)
        probs_bf = (weights / row_total).astype(jnp.bfloat16)
        mixed_rows = jnp.dot(probs_bf, value_rows, preferred_element_type=jnp.float32)
        is_live = position < length
        mixed_rows = jnp.where(is_live[:, None], mixed_rows, 0.0)
        pieces.append(mixed_rows.astype(jnp.bfloat16).reshape(block_len, group_size * head_width))
    return jnp.concatenate(pieces, 0)


def gathered_shards(tokens, key_weight, value_weight, queries, prefix_pool, block_table, lengths):
    token_count = tokens.shape[0]
    local_heads = queries.shape[1]
    head_width = prefix_pool.shape[4] // 2
    ctx_count = lax.axis_size("ctx")
    head_count = lax.axis_size("head")
    features = lax.all_gather(tokens, ("ctx", "head"), axis=1, tiled=True)
    key_cols, value_cols = (
        lax.all_to_all(
            lax.all_to_all(weight, "ctx", split_axis=3, concat_axis=0, tiled=True),
            "head",
            split_axis=4,
            concat_axis=1,
            tiled=True,
        )
        for weight in (key_weight, value_weight)
    )
    span_len = features.shape[1] // (ctx_count * head_count)
    feature_view = features.reshape(token_count, ctx_count, head_count, span_len)
    pieces = (
        lax.all_gather(key_cols, "batch", axis=2, tiled=True),
        lax.all_gather(value_cols, "batch", axis=2, tiled=True),
    )
    row_count = pieces[0].shape[2]

    def one_term(weight_piece):
        shaped = weight_piece.reshape(ctx_count, head_count, row_count, local_heads * head_width)
        return jnp.einsum("tchr,chrk->tk", feature_view, shaped, preferred_element_type=jnp.float32)

    new_keys = one_term(pieces[0]).astype(jnp.bfloat16).reshape(token_count, local_heads, head_width)
    new_values = one_term(pieces[1]).astype(jnp.bfloat16).reshape(token_count, local_heads, head_width)
    fresh_all = jnp.concatenate([new_keys, new_values], 2)
    pool_heads = lax.all_to_all(prefix_pool, "ctx", split_axis=2, concat_axis=0, tiled=True)
    chosen = jnp.take(pool_heads, block_table[0], axis=0)
    chosen = chosen.reshape(-1, local_heads, 2 * head_width)
    outputs = [
        attend_head(
            queries[:, head_idx, 0], chosen[:, head_idx], fresh_all[:, head_idx], lengths[0]
        )
        for head_idx in range(local_heads)
    ]
    return jnp.stack(outputs, 1)[:, :, None, :]


def shift(array, axis, step):
    count = lax.axis_size(axis)
    return lax.ppermute(array, axis, [(i, (i + step) % count) for i in range(count)])


def trade(array, axis, bits):
    return lax.ppermute(array, axis, [(i, i ^ bits) for i in range(lax.axis_size(axis))])


def after(first, second):
    return lax.optimization_barrier((first, second))


def softmax_parts(scores, old_max=None):
    row_max = jnp.max(scores, axis=0, keepdims=True)
    if old_max is not None:
        row_max = jnp.maximum(row_max, old_max)
    return row_max, jnp.exp2(scores - row_max).astype(jnp.bfloat16)


def dot_queries(keys, query_block):
    return lax.dot_general(
        keys, query_block, (((1,), (1,)), ((), ())), preferred_element_type=jnp.float32
    )


def params(limit=None):
    return pltpu.CompilerParams(vmem_limit_bytes=limit or VMEM_BYTES)


def weight_kernel(ctx_count, heads, head_count, key_ref, value_ref, out_ref, flat):
    depth, slots, width = key_ref.shape
    for kind, ref in enumerate((key_ref, value_ref)):
        flat[...] = ref[...].astype(jnp.float32).reshape(depth * slots, width)
        for ctx in range(ctx_count):
            for head in range(heads):
                for core in range(head_count):
                    slot = (ctx * heads + head) * head_count + core
                    at = (kind * heads + head) * width
                    out_ref[core, ctx, :, at : at + width] = flat[
                        pl.ds(slot, depth, stride=slots), :
                    ].astype(out_ref.dtype)


def arrange_weights(key_weight, value_weight, ctx_count, heads, head_count):
    depth, width = key_weight.shape[2], key_weight.shape[5]
    slots = ctx_count * heads * head_count
    rows = min(128, depth)
    views = [w.reshape(depth, slots, width) for w in (key_weight, value_weight)]
    block = pl.BlockSpec((rows, slots, width), lambda i: (i, 0, 0))
    columns = 2 * heads * width
    return pl.pallas_call(
        functools.partial(weight_kernel, ctx_count, heads, head_count),
        grid=(depth // rows,),
        in_specs=[block, block],
        out_specs=pl.BlockSpec((head_count, ctx_count, rows, columns), lambda i: (0, 0, i, 0)),
        out_shape=jax.ShapeDtypeStruct((head_count, ctx_count, depth, columns), jnp.bfloat16),
        scratch_shapes=[pltpu.VMEM((rows * slots, width), jnp.float32)],
        compiler_params=params(),
        cost_estimate=cost("arrange_weights"),
        name="arrange_weights",
    )(*views)


def cut_kernel(bits, place_ref, tokens_ref, *refs):
    pieces, (held, sems) = refs[:-2], refs[-2:]
    depth = pieces[0].shape[1]
    inward, outward = [], []
    for index, piece in enumerate(pieces):
        start = pl.multiple_of((place_ref[0] ^ bits[index]) * depth, depth)
        source = tokens_ref.at[:, pl.ds(start, depth)]
        inward.append(pltpu.make_async_copy(source, held.at[index], sems.at[0, index]))
        outward.append(pltpu.make_async_copy(held.at[index], piece, sems.at[1, index]))
    for copy in inward:
        copy.start()
    for copy, onward in zip(inward, outward):
        copy.wait()
        onward.start()
    for copy in outward:
        copy.wait()


def cut_tokens(place, tokens, depth, bits):
    far = pl.BlockSpec(memory_space=pltpu.HBM)
    piece = jax.ShapeDtypeStruct((tokens.shape[0], depth), tokens.dtype)
    return pl.pallas_call(
        functools.partial(cut_kernel, bits),
        grid_spec=pltpu.PrefetchScalarGridSpec(
            num_scalar_prefetch=1,
            grid=(1,),
            in_specs=[far],
            out_specs=[far] * len(bits),
            scratch_shapes=[
                pltpu.VMEM((len(bits), *piece.shape), tokens.dtype),
                pltpu.SemaphoreType.DMA((2, len(bits))),
            ],
        ),
        out_shape=[piece] * len(bits),
        compiler_params=params(MOST_VMEM_BYTES),
        cost_estimate=cost("cut_tokens"),
        name="cut_tokens",
    )(place, tokens)


def pool_kernel(ctx_count, heads, place_ref, pool_ref, *refs):
    outs, flat = refs[:-1], refs[-1]
    some, length, slots, width = pool_ref.shape
    length *= some
    flat[...] = pool_ref[...].astype(jnp.float32).reshape(length * slots, width)
    for kind in range(2):
        for head in range(heads):
            at = (kind * heads + head) * width
            held = []
            for ctx in range(ctx_count):
                slot = (kind * ctx_count + ctx) * heads + head
                held.append(flat[pl.ds(slot, length, stride=slots), :])
            for step, out_ref in enumerate(outs):
                target = lax.rem(place_ref[1] + step, ctx_count)
                value = held[0]
                for ctx in range(1, ctx_count):
                    value = jnp.where(target == ctx, held[ctx], value)
                out_ref[:, :, at : at + width] = value.astype(out_ref.dtype).reshape(
                    some, length // some, width
                )


def arrange_pool(place, prefix_pool, ctx_count, heads):
    blocks, length, all_heads, _, double = prefix_pool.shape
    width = double // 2
    slots = 2 * all_heads
    view = prefix_pool.reshape(blocks, length, all_heads, 2, width)
    view = view.transpose(0, 1, 3, 2, 4).reshape(blocks, length, slots, width)
    columns = 2 * heads * width
    some = 2 if blocks % 2 == 0 else 1
    out = pl.BlockSpec((some, length, columns), lambda i, place: (i, 0, 0))
    return pl.pallas_call(
        functools.partial(pool_kernel, ctx_count, heads),
        grid_spec=pltpu.PrefetchScalarGridSpec(
            num_scalar_prefetch=1,
            grid=(blocks // some,),
            in_specs=[pl.BlockSpec((some, length, slots, width), lambda i, place: (i, 0, 0, 0))],
            out_specs=[out] * ctx_count,
            scratch_shapes=[pltpu.VMEM((some * length * slots, width), jnp.float32)],
        ),
        out_shape=[jax.ShapeDtypeStruct((blocks, length, columns), jnp.bfloat16)] * ctx_count,
        compiler_params=params(),
        cost_estimate=cost("arrange_pool"),
        name="arrange_pool",
    )(place, view)


def total_of(refs):
    return sum(ref[...].astype(jnp.float32).reshape(ref.shape[-2:]) for ref in refs)


def project_kernel(block_count, term_counts, place_ref, *refs):
    token_refs, weight_ref = refs[:block_count], refs[block_count]
    terms = refs[block_count + 1 : block_count + 1 + sum(term_counts)]
    out_ref, *sum_refs = refs[block_count + 1 + sum(term_counts) : -1]
    stacked = refs[-1]

    @pl.when(pl.program_id(0) == 0)
    def _():
        at = 0
        for token_ref in token_refs:
            rows = token_ref.shape[0]
            stacked[at : at + rows, :] = token_ref[...]
            at += rows
        at = 0
        for count, sum_ref in zip(term_counts, sum_refs):
            sum_ref[...] = total_of(terms[at : at + count]).astype(sum_ref.dtype)
            at += count

    out_ref[0] = jnp.dot(
        stacked[...], weight_ref[0, 0], preferred_element_type=jnp.float32
    ).astype(out_ref.dtype)


def piece_of(array, *index):
    rows, block, *leading = index
    shape = (1,) * len(leading) + (rows, array.shape[-1])
    return array, pl.BlockSpec(shape, lambda j, *_: (*leading, block, 0))


def project(place, blocks, weights, head_step, out_dtype, name, sums=()):
    head_count, ctx_count, depth, width = weights.shape
    row_total = sum(block.shape[0] for block in blocks)

    def block_spec(block):
        if block.shape[1] == depth:
            return pl.BlockSpec(block.shape, lambda j, place: (0, 0))
        return pl.BlockSpec((block.shape[0], depth), lambda j, place: (0, place[0]))

    pieces = [piece for terms in sums for piece in terms]
    sum_shapes = [terms[0][1].block_shape[-2:] for terms in sums]
    result = pl.pallas_call(
        functools.partial(project_kernel, len(blocks), [len(terms) for terms in sums]),
        grid_spec=pltpu.PrefetchScalarGridSpec(
            num_scalar_prefetch=1,
            grid=(ctx_count,),
            in_specs=[block_spec(block) for block in blocks]
            + [
                pl.BlockSpec(
                    (1, 1, depth, width),
                    lambda j, place: (
                        lax.rem(place[2] + head_step, head_count),
                        lax.rem(place[1] + j, ctx_count),
                        0,
                        0,
                    ),
                )
            ]
            + [spec for _, spec in pieces],
            out_specs=[pl.BlockSpec((1, row_total, width), lambda j, place: (j, 0, 0))]
            + [pl.BlockSpec(shape, lambda j, place: (0, 0)) for shape in sum_shapes],
            scratch_shapes=[pltpu.VMEM((row_total, depth), weights.dtype)],
        ),
        out_shape=[jax.ShapeDtypeStruct((ctx_count, row_total, width), out_dtype)]
        + [jax.ShapeDtypeStruct(shape, jnp.bfloat16) for shape in sum_shapes],
        compiler_params=params(),
        cost_estimate=cost(name),
        name=name,
    )(place, *blocks, weights, *(array for array, _ in pieces))
    return result if sums else result[0]


def pick_kernel(heads, ctx_count, place_ref, table_ref, *refs):
    pool_refs, (keys, values) = refs[:ctx_count], refs[ctx_count:]
    blocks, length, columns = pool_refs[0].shape
    wide = columns // 2
    width = wide // heads
    values[...] = jnp.ones_like(values)
    for at in range(table_ref.shape[0]):
        entry = table_ref[at]
        here = slice(at * length, (at + 1) * length)
        step = lax.rem(place_ref[1] - entry // blocks + ctx_count, ctx_count)
        for ctx_step, pool_ref in enumerate(pool_refs):

            @pl.when(step == ctx_step)
            def _():
                block = pool_ref[entry % blocks]
                keys[here, :] = block[:, :wide]
                put_values(values, here, block[:, wide:], heads)


def put_values(values, here, block, heads):
    width = block.shape[1] // heads
    for head in range(heads):
        low = head * (width + ONES)
        values[low : low + width, here] = (
            block[:, head * width : (head + 1) * width].astype(jnp.float32).T.astype(jnp.bfloat16)
        )


def pick_blocks(place, table, pools, heads):
    length, columns = pools[0].shape[1:]
    count = table.shape[0] * length
    wide = columns // 2
    tall = wide + heads * ONES
    return pl.pallas_call(
        functools.partial(pick_kernel, heads, len(pools)),
        grid_spec=pltpu.PrefetchScalarGridSpec(
            num_scalar_prefetch=2,
            grid=(1,),
            in_specs=[pl.BlockSpec(p.shape, lambda i, *_: (0, 0, 0)) for p in pools],
            out_specs=[
                pl.BlockSpec((count, wide), lambda i, *_: (0, 0)),
                pl.BlockSpec((tall, count), lambda i, *_: (0, 0)),
            ],
        ),
        out_shape=[
            jax.ShapeDtypeStruct((count, wide), jnp.bfloat16),
            jax.ShapeDtypeStruct((tall, count), jnp.bfloat16),
        ],
        compiler_params=params(),
        cost_estimate=cost("pick_blocks"),
        name="pick_blocks",
    )(place, table, *pools)


def each_part(rows, heads):
    part_rows = min(PART, rows)
    each = part_rows // heads
    for low in range(0, rows, part_rows):
        for head in range(heads):
            at = low + head * each
            yield head, pl.ds(low + head, each, stride=heads), slice(at, at + each)


def prefix_kernel(scale, heads, query_ref, keys, values, *refs):
    acc_ref, stat_ref, flat = refs[-3:]
    rows, width = query_ref.shape
    tall = width + ONES
    half = stat_ref.shape[0] // 2
    flat[...] = query_ref[...].astype(jnp.float32)
    for head, taken, here in each_part(rows, heads):
        query_block = flat[taken, :].astype(jnp.bfloat16)
        scores = dot_queries(keys[:, head * width : (head + 1) * width], query_block) * scale
        row_max, weights = softmax_parts(scores)
        mixed = jnp.dot(
            values[head * tall : (head + 1) * tall, :], weights, preferred_element_type=jnp.float32
        )
        acc_ref[:, here] = mixed[:width]
        stat_ref[:half, here] = jnp.broadcast_to(row_max, (half, row_max.shape[1]))
        stat_ref[half:, here] = jnp.broadcast_to(mixed[width : width + 1], (half, row_max.shape[1]))


def prefix_attend(query_rows, keys, values, chunk, scale, heads, part=(0, 1), state=None):
    all_rows, width = query_rows.shape
    row_total = all_rows // CHUNKS
    at, count = part
    rows = min(1024, row_total // count)
    steps = row_total // rows // count
    first = chunk * count * steps + at * steps
    out_specs = [
        pl.BlockSpec((width, rows), lambda i: (0, at * steps + i)),
        pl.BlockSpec((8, rows), lambda i: (0, at * steps + i)),
    ]
    in_specs = [
        pl.BlockSpec((rows, width), lambda i: (first + i, 0)),
        pl.BlockSpec(keys.shape, lambda i: (0, 0)),
        pl.BlockSpec(values.shape, lambda i: (0, 0)),
    ]
    operands = [query_rows, keys, values]
    aliases = {}
    if state is not None:
        in_specs += [pl.BlockSpec(memory_space=pl.ANY)] * 2
        operands += state
        aliases = {3: 0, 4: 1}
    return pl.pallas_call(
        functools.partial(prefix_kernel, scale, heads),
        grid=(steps,),
        in_specs=in_specs,
        out_specs=out_specs,
        out_shape=[
            jax.ShapeDtypeStruct((width, row_total), jnp.float32),
            jax.ShapeDtypeStruct((8, row_total), jnp.float32),
        ],
        input_output_aliases=aliases,
        scratch_shapes=[pltpu.VMEM((rows, width), jnp.float32)],
        compiler_params=params(),
        cost_estimate=cost("prefix_attend"),
        name="prefix_attend",
    )(*operands)


def fresh_kernel(
    scale, heads, per_token, first_row, counts, length_ref, query_ref, acc_ref, stat_ref, *rest
):
    early_count, term_count = counts
    earlier, terms = rest[:early_count], rest[early_count : early_count + term_count]
    out_ref, fresh_ref, keys, values, flat, mixed_rows = rest[-6:]
    rows, width = query_ref.shape
    wide, tall = heads * width, width + ONES
    step = pl.program_id(0)

    @pl.when(step == 0)
    def _():
        values[...] = jnp.ones_like(values)
        fresh_ref[...] = total_of(terms).astype(fresh_ref.dtype)
        for index, ref in enumerate([*earlier, fresh_ref]):
            here = slice(index * ref.shape[0], (index + 1) * ref.shape[0])
            fresh = ref[...]
            keys[here, :] = fresh[:, :wide]
            put_values(values, here, fresh[:, wide:], heads)

    half = stat_ref.shape[0] // 2
    flat[...] = query_ref[...].astype(jnp.float32)
    for head, taken, here in each_part(rows, heads):
        query_block = flat[taken, :].astype(jnp.bfloat16)
        scores = dot_queries(keys[:, head * width : (head + 1) * width], query_block) * scale
        row = taken.start + heads * lax.broadcasted_iota(jnp.int32, (1, taken.size), 1)
        token = first_row + step * (rows // per_token) + (
            row // per_token if per_token & (per_token - 1) else row >> (per_token.bit_length() - 1)
        )
        key_at = lax.broadcasted_iota(jnp.int32, scores.shape, 0)
        scores = jnp.where(key_at <= token, scores, -jnp.inf)
        old_max, old_total = stat_ref[:1, here], stat_ref[half : half + 1, here]
        row_max, weights = softmax_parts(scores, old_max)
        fade = jnp.exp2(old_max - row_max)
        mixed = jnp.dot(
            values[head * tall : (head + 1) * tall, :], weights, preferred_element_type=jnp.float32
        )
        row_total = old_total * fade + mixed[width : width + 1]
        share = jnp.where(token < length_ref[0], 1.0 / row_total, 0.0)
        result = acc_ref[:, here] * (fade * share) + mixed[:width] * share
        mixed_rows[taken, :] = result.T
    out_ref[...] = mixed_rows[...].astype(out_ref.dtype)


def fresh_attend(
    length, query_rows, acc, stat, earlier, pieces, result, chunk, scale, heads, per_token
):
    row_total, width = query_rows.shape
    chunk_rows = row_total // CHUNKS
    rows = min(1024, chunk_rows)
    steps = chunk_rows // rows
    block = pl.BlockSpec((rows, width), lambda i, length: (chunk * steps + i, 0))
    fresh_shape = pieces[0][1].block_shape[-2:]
    key_count = (len(earlier) + 1) * fresh_shape[0]
    whole = pl.BlockSpec(fresh_shape, lambda i, length: (0, 0))
    in_specs = [
        block,
        pl.BlockSpec((width, rows), lambda i, length: (0, i)),
        pl.BlockSpec((stat.shape[0], rows), lambda i, length: (0, i)),
        *(whole for _ in earlier),
        *(spec for _, spec in pieces),
    ]
    operands = [length, query_rows, acc, stat, *earlier, *(array for array, _ in pieces)]
    aliases = {}
    if result is not None:
        in_specs.append(pl.BlockSpec(memory_space=pl.ANY))
        aliases = {len(operands): 0}
        operands.append(result)
    return pl.pallas_call(
        functools.partial(
            fresh_kernel,
            scale,
            heads,
            per_token,
            chunk * (chunk_rows // per_token),
            (len(earlier), len(pieces)),
        ),
        grid_spec=pltpu.PrefetchScalarGridSpec(
            num_scalar_prefetch=1,
            grid=(steps,),
            in_specs=in_specs,
            out_specs=[block, whole],
            scratch_shapes=[
                pltpu.VMEM((key_count, heads * width), jnp.bfloat16),
                pltpu.VMEM((heads * (width + ONES), key_count), jnp.bfloat16),
                pltpu.VMEM((rows, width), jnp.float32),
                pltpu.VMEM((rows, width), jnp.float32),
            ],
        ),
        out_shape=[
            jax.ShapeDtypeStruct((row_total, width), jnp.bfloat16),
            jax.ShapeDtypeStruct(fresh_shape, jnp.bfloat16),
        ],
        input_output_aliases=aliases,
        compiler_params=params(),
        cost_estimate=cost("fresh_attend"),
        name="fresh_attend",
    )(*operands)


def reduced_shards(tokens, key_weight, value_weight, queries, prefix_pool, block_table, lengths):
    batch_count = lax.axis_size("batch")
    ctx_count = lax.axis_size("ctx")
    head_count = lax.axis_size("head")
    batch_at, ctx_at, head_at = (lax.axis_index(a) for a in ("batch", "ctx", "head"))
    place = jnp.stack([batch_at, ctx_at, head_at]).astype(jnp.int32)
    token_count = tokens.shape[0]
    heads = queries.shape[1]
    width = prefix_pool.shape[4] // 2
    group = queries.shape[3] // width
    per_token = heads * group
    depth = key_weight.shape[2]
    rows = token_count // CHUNKS
    scale = math.log2(math.e) / math.sqrt(width)

    top = batch_count // 2
    steps = list(range(batch_count - 1, top, -1)) + list(range(1, top))
    pieces = cut_tokens(place, tokens, depth, [*steps, top])
    pieces, prefix_pool = after(pieces, prefix_pool)
    arrived = [trade(piece, "batch", bits) for piece, bits in zip(pieces, steps)]
    pools = arrange_pool(place, prefix_pool, ctx_count, heads)
    pools, (key_weight, value_weight) = after(pools, (key_weight, value_weight))
    pools = [shift(part, "ctx", step) if step else part for step, part in enumerate(pools)]

    weights = arrange_weights(key_weight, value_weight, ctx_count, heads, head_count)
    weights, last = after(weights, pieces[-1])
    last = trade(last, "batch", top)

    query_rows = queries.reshape(token_count, heads, group, width)
    query_rows = query_rows.transpose(0, 2, 1, 3).reshape(-1, width)
    def projected(blocks, name):
        terms = [
            shift(project(place, blocks, weights, step, jnp.bfloat16, name + "_away"), "head", step)
            for step in range(1, head_count)
        ]
        return [project(place, blocks, weights, 0, jnp.float32, name + "_kept"), *terms]

    def added(terms, step, here):
        return sum(term[step, here].astype(jnp.float32) for term in terms)

    def others(terms, here):
        return [added(terms, step, here).astype(jnp.bfloat16) for step in range(1, ctx_count)]

    def spread(parts):
        return [shift(part, "ctx", step + 1) for step, part in enumerate(parts)]

    every = slice(None)
    parts_of = [slice(i * rows, (i + 1) * rows) for i in range(CHUNKS)]

    sums = [[], []]
    if steps:
        early = projected(arrived, "early")
        cuts = [slice(i * token_count, (i + 1) * token_count) for i in range(len(steps))]
        leaving = [others(early, cut) for cut in cuts]
        leaving, pools = after(leaving, pools)
        sums = [
            [
                [piece_of(t, token_count, i, 0) for t in early]
                + [piece_of(p, token_count, 0) for p in spread(parts)]
            ]
            for i, parts in enumerate(leaving)
        ]
    keys, values = pick_blocks(place, block_table[0], pools, heads)
    states = [prefix_attend(query_rows, keys, values, 0, scale, heads)]
    states[0], last = after(states[0], last)

    def late_project(step, dtype, name, sums):
        result = project(place, [last, tokens], weights, step, dtype, name, sums)
        return result if sums else (result,)

    terms = []
    for step in range(1, head_count):
        term, *far = late_project(step, jnp.bfloat16, "late_away", sums[0] + sums[1] if step == 1 else [])
        terms.append(shift(term, "head", step))
    kept, *_ = late_project(0, jnp.float32, "late_kept", [])
    far, near = far[:1], far[1:]
    late = [kept, *terms]
    far = [trade(part, "batch", 1) for part in far]
    own_at = slice(token_count, 2 * token_count)
    *late_others, own_others = [others(late, here) for here in [*parts_of, own_at]]
    late_others[0] = spread(late_others[0])
    late_others[1], (keys, values) = after(late_others[1], (keys, values))
    state = prefix_attend(query_rows, keys, values, 1, scale, heads, (0, 2))
    state, (late_others[1], own_others, near) = after(state, (late_others[1], own_others, near))
    late_others[1], own_others = spread(late_others[1]), spread(own_others)
    near = [trade(part, "batch", 1) for part in near]

    away = []
    for chunk, here in enumerate(parts_of):
        part = added(late, 0, here) + sum(p.astype(jnp.float32) for p in late_others[chunk])
        part = part + sum(p[here].astype(jnp.float32) for p in far)
        part = part.astype(jnp.bfloat16)
        if chunk == 0:
            (far, late), late_others[1] = after((far, late), late_others[1])
            part, state = after(part, state)
        else:
            away[-1], part = after(away[-1], part)
        away.append(trade(part, "batch", top))
    states.append(prefix_attend(query_rows, keys, values, 1, scale, heads, (1, 2), state))

    result = None
    fresh = []
    for chunk in range(CHUNKS):
        pieces = [piece_of(t, rows, CHUNKS + chunk, 0) for t in late]
        pieces += [piece_of(part, rows, chunk) for part in (*own_others, *near)]
        pieces.append(piece_of(away[chunk], rows, 0))
        result, new = fresh_attend(
            lengths,
            query_rows,
            *states[chunk],
            fresh,
            pieces,
            result,
            chunk,
            scale,
            heads,
            per_token,
        )
        fresh.append(new)
    result = result.reshape(token_count, group, heads, width).transpose(0, 2, 1, 3)
    return result.reshape(token_count, heads, 1, group * width)


def solution(mesh):
    def shards(tokens, key_weight, value_weight, *rest):
        prompts = mesh.shape["batch"]
        columns = 2 * math.prod(key_weight.shape[3:])
        few_tokens = prompts * tokens.shape[0] <= columns and prompts in (2, 4)
        form = reduced_shards if few_tokens else gathered_shards
        return form(tokens, key_weight, value_weight, *rest)

    return jax.shard_map(
        shards,
        mesh=mesh,
        in_specs=(
            P(("groups", "batch"), ("ctx", "head")),
            P("ctx", "head", "batch", None, None, None),
            P("ctx", "head", "batch", None, None, None),
            P(("groups", "batch"), "ctx", "head", None),
            P(("groups", "ctx"), None, None, "head", None),
            P(("groups", "batch"), None),
            P(("groups", "batch")),
        ),
        out_specs=P(("groups", "batch"), "ctx", "head", None),
        check_vma=False,
    )
```

```python
import functools
import math

import jax
import jax.numpy as jnp
from jax import lax
from jax.experimental import pallas as pl
from jax.experimental.pallas import tpu as pltpu
from jax.sharding import PartitionSpec as P

CHUNKS = 2
PART = 1024
ONES = 16
VMEM_BYTES = 16 * 1024 * 1024
MOST_VMEM_BYTES = 60 * 1024 * 1024
LONG = pl.CostEstimate(flops=10**11, bytes_accessed=1, transcendentals=0)
COSTS = {}


def cost(name):
    return COSTS.get(name, LONG)


def attend_head(query_rows, prefix, fresh_rows, length):
    token_count = query_rows.shape[0]
    head_width = prefix.shape[1] // 2
    group_size = query_rows.shape[1] // head_width
    prefix_len = prefix.shape[0]
    key_rows = jnp.concatenate([prefix[:, :head_width], fresh_rows[:, :head_width]], 0)
    value_rows = jnp.concatenate([prefix[:, head_width:], fresh_rows[:, head_width:]], 0)
    block_len = min(token_count, 64)
    pieces = []
    for first_row in range(0, token_count, block_len):
        block_rows = query_rows[first_row : first_row + block_len].reshape(
            block_len * group_size, head_width
        )
        scores = jnp.dot(
            block_rows, key_rows.T, preferred_element_type=jnp.float32
        ) * head_width ** (-0.5)
        position = first_row + jnp.arange(block_len * group_size) // group_size
        column = jnp.arange(prefix_len + token_count) - prefix_len
        allowed = column[None, :] <= position[:, None]
        scores = jnp.where(allowed, scores, -jnp.inf)
        row_max = jnp.max(scores, axis=1, keepdims=True)
        weights = jnp.exp(scores - row_max)
        row_total = jnp.sum(weights, axis=1, keepdims=True)
        probs_bf = (weights / row_total).astype(jnp.bfloat16)
        mixed_rows = jnp.dot(probs_bf, value_rows, preferred_element_type=jnp.float32)
        is_live = position < length
        mixed_rows = jnp.where(is_live[:, None], mixed_rows, 0.0)
        pieces.append(mixed_rows.astype(jnp.bfloat16).reshape(block_len, group_size * head_width))
    return jnp.concatenate(pieces, 0)


def gathered_shards(tokens, key_weight, value_weight, queries, prefix_pool, block_table, lengths):
    token_count = tokens.shape[0]
    local_heads = queries.shape[1]
    head_width = prefix_pool.shape[4] // 2
    ctx_count = lax.axis_size("ctx")
    head_count = lax.axis_size("head")
    features = lax.all_gather(tokens, ("ctx", "head"), axis=1, tiled=True)
    key_cols, value_cols = (
        lax.all_to_all(
            lax.all_to_all(weight, "ctx", split_axis=3, concat_axis=0, tiled=True),
            "head",
            split_axis=4,
            concat_axis=1,
            tiled=True,
        )
        for weight in (key_weight, value_weight)
    )
    span_len = features.shape[1] // (ctx_count * head_count)
    feature_view = features.reshape(token_count, ctx_count, head_count, span_len)
    pieces = (
        lax.all_gather(key_cols, "batch", axis=2, tiled=True),
        lax.all_gather(value_cols, "batch", axis=2, tiled=True),
    )
    row_count = pieces[0].shape[2]

    def one_term(weight_piece):
        shaped = weight_piece.reshape(ctx_count, head_count, row_count, local_heads * head_width)
        return jnp.einsum("tchr,chrk->tk", feature_view, shaped, preferred_element_type=jnp.float32)

    new_keys = one_term(pieces[0]).astype(jnp.bfloat16).reshape(token_count, local_heads, head_width)
    new_values = one_term(pieces[1]).astype(jnp.bfloat16).reshape(token_count, local_heads, head_width)
    fresh_all = jnp.concatenate([new_keys, new_values], 2)
    pool_heads = lax.all_to_all(prefix_pool, "ctx", split_axis=2, concat_axis=0, tiled=True)
    chosen = jnp.take(pool_heads, block_table[0], axis=0)
    chosen = chosen.reshape(-1, local_heads, 2 * head_width)
    outputs = [
        attend_head(
            queries[:, head_idx, 0], chosen[:, head_idx], fresh_all[:, head_idx], lengths[0]
        )
        for head_idx in range(local_heads)
    ]
    return jnp.stack(outputs, 1)[:, :, None, :]


def shift(array, axis, step):
    count = lax.axis_size(axis)
    return lax.ppermute(array, axis, [(i, (i + step) % count) for i in range(count)])


def trade(array, axis, bits):
    return lax.ppermute(array, axis, [(i, i ^ bits) for i in range(lax.axis_size(axis))])


def after(first, second):
    return lax.optimization_barrier((first, second))


def softmax_parts(scores, old_max=None):
    row_max = jnp.max(scores, axis=0, keepdims=True)
    if old_max is not None:
        row_max = jnp.maximum(row_max, old_max)
    return row_max, jnp.exp2(scores - row_max).astype(jnp.bfloat16)


def dot_queries(keys, query_block):
    return lax.dot_general(
        keys, query_block, (((1,), (1,)), ((), ())), preferred_element_type=jnp.float32
    )


def params(limit=None):
    return pltpu.CompilerParams(vmem_limit_bytes=limit or VMEM_BYTES)


def weight_kernel(ctx_count, heads, head_count, key_ref, value_ref, out_ref, flat):
    depth, slots, width = key_ref.shape
    for kind, ref in enumerate((key_ref, value_ref)):
        flat[...] = ref[...].astype(jnp.float32).reshape(depth * slots, width)
        for ctx in range(ctx_count):
            for head in range(heads):
                for core in range(head_count):
                    slot = (ctx * heads + head) * head_count + core
                    at = (kind * heads + head) * width
                    out_ref[core, ctx, :, at : at + width] = flat[
                        pl.ds(slot, depth, stride=slots), :
                    ].astype(out_ref.dtype)


def arrange_weights(key_weight, value_weight, ctx_count, heads, head_count):
    depth, width = key_weight.shape[2], key_weight.shape[5]
    slots = ctx_count * heads * head_count
    rows = min(128, depth)
    views = [w.reshape(depth, slots, width) for w in (key_weight, value_weight)]
    block = pl.BlockSpec((rows, slots, width), lambda i: (i, 0, 0))
    columns = 2 * heads * width
    return pl.pallas_call(
        functools.partial(weight_kernel, ctx_count, heads, head_count),
        grid=(depth // rows,),
        in_specs=[block, block],
        out_specs=pl.BlockSpec((head_count, ctx_count, rows, columns), lambda i: (0, 0, i, 0)),
        out_shape=jax.ShapeDtypeStruct((head_count, ctx_count, depth, columns), jnp.bfloat16),
        scratch_shapes=[pltpu.VMEM((rows * slots, width), jnp.float32)],
        compiler_params=params(),
        cost_estimate=cost("arrange_weights"),
        name="arrange_weights",
    )(*views)


def prepare_kernel(ctx_count, heads, bits, place_ref, tokens_ref, pool_ref, *refs):
    pieces, outs = refs[: len(bits)], refs[len(bits) : len(bits) + ctx_count]
    held_tokens, flat, sems = refs[-3:]
    step_at, last_step = pl.program_id(0), pl.num_programs(0) - 1
    depth = pieces[0].shape[1]

    def inward(index):
        start = pl.multiple_of((place_ref[0] ^ bits[index]) * depth, depth)
        source = tokens_ref.at[:, pl.ds(start, depth)]
        return pltpu.make_async_copy(source, held_tokens.at[index], sems.at[0, index])

    def outward(index):
        return pltpu.make_async_copy(held_tokens.at[index], pieces[index], sems.at[1, index])

    @pl.when(step_at == 0)
    def _():
        for index in range(len(bits)):
            inward(index).start()

    some, length, slots, width = pool_ref.shape
    length *= some
    flat[...] = pool_ref[...].astype(jnp.float32).reshape(length * slots, width)
    for kind in range(2):
        for head in range(heads):
            at = (kind * heads + head) * width
            held = []
            for ctx in range(ctx_count):
                slot = (kind * ctx_count + ctx) * heads + head
                held.append(flat[pl.ds(slot, length, stride=slots), :])
            for step, out_ref in enumerate(outs):
                target = lax.rem(place_ref[1] + step, ctx_count)
                value = held[0]
                for ctx in range(1, ctx_count):
                    value = jnp.where(target == ctx, held[ctx], value)
                out_ref[:, :, at : at + width] = value.astype(out_ref.dtype).reshape(
                    some, length // some, width
                )

    @pl.when(step_at == 0)
    def _():
        for index in range(len(bits)):
            inward(index).wait()
            outward(index).start()

    @pl.when(step_at == last_step)
    def _():
        for index in range(len(bits)):
            outward(index).wait()


def prepare(place, tokens, depth, bits, prefix_pool, ctx_count, heads):
    blocks, length, all_heads, _, double = prefix_pool.shape
    width = double // 2
    slots = 2 * all_heads
    view = prefix_pool.reshape(blocks, length, all_heads, 2, width)
    view = view.transpose(0, 1, 3, 2, 4).reshape(blocks, length, slots, width)
    columns = 2 * heads * width
    some = 2 if blocks % 2 == 0 else 1
    out = pl.BlockSpec((some, length, columns), lambda i, place: (i, 0, 0))
    far = pl.BlockSpec(memory_space=pltpu.HBM)
    piece = jax.ShapeDtypeStruct((tokens.shape[0], depth), tokens.dtype)
    result = pl.pallas_call(
        functools.partial(prepare_kernel, ctx_count, heads, bits),
        grid_spec=pltpu.PrefetchScalarGridSpec(
            num_scalar_prefetch=1,
            grid=(blocks // some,),
            in_specs=[
                far,
                pl.BlockSpec((some, length, slots, width), lambda i, place: (i, 0, 0, 0)),
            ],
            out_specs=[far] * len(bits) + [out] * ctx_count,
            scratch_shapes=[
                pltpu.VMEM((len(bits), *piece.shape), tokens.dtype),
                pltpu.VMEM((some * length * slots, width), jnp.float32),
                pltpu.SemaphoreType.DMA((2, len(bits))),
            ],
        ),
        out_shape=[piece] * len(bits)
        + [jax.ShapeDtypeStruct((blocks, length, columns), jnp.bfloat16)] * ctx_count,
        compiler_params=params(MOST_VMEM_BYTES),
        cost_estimate=cost("prepare"),
        name="prepare",
    )(place, tokens, view)
    return result[: len(bits)], result[len(bits) :]


def total_of(refs):
    return sum(ref[...].astype(jnp.float32).reshape(ref.shape[-2:]) for ref in refs)


def project_kernel(block_count, term_counts, place_ref, *refs):
    token_refs, weight_ref = refs[:block_count], refs[block_count]
    terms = refs[block_count + 1 : block_count + 1 + sum(term_counts)]
    out_ref, *sum_refs = refs[block_count + 1 + sum(term_counts) : -1]
    stacked = refs[-1]

    @pl.when(pl.program_id(0) == 0)
    def _():
        at = 0
        for token_ref in token_refs:
            rows = token_ref.shape[0]
            stacked[at : at + rows, :] = token_ref[...]
            at += rows
        at = 0
        for count, sum_ref in zip(term_counts, sum_refs):
            sum_ref[...] = total_of(terms[at : at + count]).astype(sum_ref.dtype)
            at += count

    out_ref[0] = jnp.dot(
        stacked[...], weight_ref[0, 0], preferred_element_type=jnp.float32
    ).astype(out_ref.dtype)


def piece_of(array, *index):
    rows, block, *leading = index
    shape = (1,) * len(leading) + (rows, array.shape[-1])
    return array, pl.BlockSpec(shape, lambda j, *_: (*leading, block, 0))


def project(place, blocks, weights, head_step, out_dtype, name, sums=()):
    head_count, ctx_count, depth, width = weights.shape
    row_total = sum(block.shape[0] for block in blocks)

    def block_spec(block):
        if block.shape[1] == depth:
            return pl.BlockSpec(block.shape, lambda j, place: (0, 0))
        return pl.BlockSpec((block.shape[0], depth), lambda j, place: (0, place[0]))

    pieces = [piece for terms in sums for piece in terms]
    sum_shapes = [terms[0][1].block_shape[-2:] for terms in sums]
    result = pl.pallas_call(
        functools.partial(project_kernel, len(blocks), [len(terms) for terms in sums]),
        grid_spec=pltpu.PrefetchScalarGridSpec(
            num_scalar_prefetch=1,
            grid=(ctx_count,),
            in_specs=[block_spec(block) for block in blocks]
            + [
                pl.BlockSpec(
                    (1, 1, depth, width),
                    lambda j, place: (
                        lax.rem(place[2] + head_step, head_count),
                        lax.rem(place[1] + j, ctx_count),
                        0,
                        0,
                    ),
                )
            ]
            + [spec for _, spec in pieces],
            out_specs=[pl.BlockSpec((1, row_total, width), lambda j, place: (j, 0, 0))]
            + [pl.BlockSpec(shape, lambda j, place: (0, 0)) for shape in sum_shapes],
            scratch_shapes=[pltpu.VMEM((row_total, depth), weights.dtype)],
        ),
        out_shape=[jax.ShapeDtypeStruct((ctx_count, row_total, width), out_dtype)]
        + [jax.ShapeDtypeStruct(shape, jnp.bfloat16) for shape in sum_shapes],
        compiler_params=params(),
        cost_estimate=cost(name),
        name=name,
    )(place, *blocks, weights, *(array for array, _ in pieces))
    return result if sums else result[0]


def pick_kernel(heads, ctx_count, place_ref, table_ref, *refs):
    pool_refs, (keys, values) = refs[:ctx_count], refs[ctx_count:]
    blocks, length, columns = pool_refs[0].shape
    wide = columns // 2
    width = wide // heads
    values[...] = jnp.ones_like(values)
    for at in range(table_ref.shape[0]):
        entry = table_ref[at]
        here = slice(at * length, (at + 1) * length)
        step = lax.rem(place_ref[1] - entry // blocks + ctx_count, ctx_count)
        for ctx_step, pool_ref in enumerate(pool_refs):

            @pl.when(step == ctx_step)
            def _():
                block = pool_ref[entry % blocks]
                keys[here, :] = block[:, :wide]
                put_values(values, here, block[:, wide:], heads)


def put_values(values, here, block, heads):
    width = block.shape[1] // heads
    for head in range(heads):
        low = head * (width + ONES)
        values[low : low + width, here] = (
            block[:, head * width : (head + 1) * width].astype(jnp.float32).T.astype(jnp.bfloat16)
        )


def pick_blocks(place, table, pools, heads):
    length, columns = pools[0].shape[1:]
    count = table.shape[0] * length
    wide = columns // 2
    tall = wide + heads * ONES
    return pl.pallas_call(
        functools.partial(pick_kernel, heads, len(pools)),
        grid_spec=pltpu.PrefetchScalarGridSpec(
            num_scalar_prefetch=2,
            grid=(1,),
            in_specs=[pl.BlockSpec(p.shape, lambda i, *_: (0, 0, 0)) for p in pools],
            out_specs=[
                pl.BlockSpec((count, wide), lambda i, *_: (0, 0)),
                pl.BlockSpec((tall, count), lambda i, *_: (0, 0)),
            ],
        ),
        out_shape=[
            jax.ShapeDtypeStruct((count, wide), jnp.bfloat16),
            jax.ShapeDtypeStruct((tall, count), jnp.bfloat16),
        ],
        compiler_params=params(),
        cost_estimate=cost("pick_blocks"),
        name="pick_blocks",
    )(place, table, *pools)


def each_part(rows, heads):
    part_rows = min(PART, rows)
    each = part_rows // heads
    for low in range(0, rows, part_rows):
        for head in range(heads):
            at = low + head * each
            yield head, pl.ds(low + head, each, stride=heads), slice(at, at + each)


def prefix_kernel(scale, heads, query_ref, keys, values, *refs):
    acc_ref, stat_ref, flat = refs[-3:]
    rows, width = query_ref.shape
    tall = width + ONES
    half = stat_ref.shape[0] // 2
    flat[...] = query_ref[...].astype(jnp.float32)
    for head, taken, here in each_part(rows, heads):
        query_block = flat[taken, :].astype(jnp.bfloat16)
        scores = dot_queries(keys[:, head * width : (head + 1) * width], query_block) * scale
        row_max, weights = softmax_parts(scores)
        mixed = jnp.dot(
            values[head * tall : (head + 1) * tall, :], weights, preferred_element_type=jnp.float32
        )
        acc_ref[:, here] = mixed[:width]
        stat_ref[:half, here] = jnp.broadcast_to(row_max, (half, row_max.shape[1]))
        stat_ref[half:, here] = jnp.broadcast_to(mixed[width : width + 1], (half, row_max.shape[1]))


def prefix_attend(query_rows, keys, values, chunk, scale, heads, part=(0, 1), state=None):
    all_rows, width = query_rows.shape
    row_total = all_rows // CHUNKS
    at, count = part
    rows = min(1024, row_total // count)
    steps = row_total // rows // count
    first = chunk * count * steps + at * steps
    out_specs = [
        pl.BlockSpec((width, rows), lambda i: (0, at * steps + i)),
        pl.BlockSpec((8, rows), lambda i: (0, at * steps + i)),
    ]
    in_specs = [
        pl.BlockSpec((rows, width), lambda i: (first + i, 0)),
        pl.BlockSpec(keys.shape, lambda i: (0, 0)),
        pl.BlockSpec(values.shape, lambda i: (0, 0)),
    ]
    operands = [query_rows, keys, values]
    aliases = {}
    if state is not None:
        in_specs += [pl.BlockSpec(memory_space=pl.ANY)] * 2
        operands += state
        aliases = {3: 0, 4: 1}
    return pl.pallas_call(
        functools.partial(prefix_kernel, scale, heads),
        grid=(steps,),
        in_specs=in_specs,
        out_specs=out_specs,
        out_shape=[
            jax.ShapeDtypeStruct((width, row_total), jnp.float32),
            jax.ShapeDtypeStruct((8, row_total), jnp.float32),
        ],
        input_output_aliases=aliases,
        scratch_shapes=[pltpu.VMEM((rows, width), jnp.float32)],
        compiler_params=params(),
        cost_estimate=cost("prefix_attend"),
        name="prefix_attend",
    )(*operands)


def fresh_kernel(
    scale, heads, per_token, first_row, counts, length_ref, query_ref, acc_ref, stat_ref, *rest
):
    early_count, term_count = counts
    earlier, terms = rest[:early_count], rest[early_count : early_count + term_count]
    out_ref, fresh_ref, keys, values, flat, mixed_rows = rest[-6:]
    rows, width = query_ref.shape
    wide, tall = heads * width, width + ONES
    step = pl.program_id(0)

    @pl.when(step == 0)
    def _():
        values[...] = jnp.ones_like(values)
        fresh_ref[...] = total_of(terms).astype(fresh_ref.dtype)
        for index, ref in enumerate([*earlier, fresh_ref]):
            here = slice(index * ref.shape[0], (index + 1) * ref.shape[0])
            fresh = ref[...]
            keys[here, :] = fresh[:, :wide]
            put_values(values, here, fresh[:, wide:], heads)

    half = stat_ref.shape[0] // 2
    flat[...] = query_ref[...].astype(jnp.float32)
    for head, taken, here in each_part(rows, heads):
        query_block = flat[taken, :].astype(jnp.bfloat16)
        scores = dot_queries(keys[:, head * width : (head + 1) * width], query_block) * scale
        row = taken.start + heads * lax.broadcasted_iota(jnp.int32, (1, taken.size), 1)
        token = first_row + step * (rows // per_token) + (
            row // per_token if per_token & (per_token - 1) else row >> (per_token.bit_length() - 1)
        )
        key_at = lax.broadcasted_iota(jnp.int32, scores.shape, 0)
        scores = jnp.where(key_at <= token, scores, -jnp.inf)
        old_max, old_total = stat_ref[:1, here], stat_ref[half : half + 1, here]
        row_max, weights = softmax_parts(scores, old_max)
        fade = jnp.exp2(old_max - row_max)
        mixed = jnp.dot(
            values[head * tall : (head + 1) * tall, :], weights, preferred_element_type=jnp.float32
        )
        row_total = old_total * fade + mixed[width : width + 1]
        share = jnp.where(token < length_ref[0], 1.0 / row_total, 0.0)
        result = acc_ref[:, here] * (fade * share) + mixed[:width] * share
        mixed_rows[taken, :] = result.T
    out_ref[...] = mixed_rows[...].astype(out_ref.dtype)


def fresh_attend(
    length, query_rows, acc, stat, earlier, pieces, result, chunk, scale, heads, per_token
):
    row_total, width = query_rows.shape
    chunk_rows = row_total // CHUNKS
    rows = min(1024, chunk_rows)
    steps = chunk_rows // rows
    block = pl.BlockSpec((rows, width), lambda i, length: (chunk * steps + i, 0))
    fresh_shape = pieces[0][1].block_shape[-2:]
    key_count = (len(earlier) + 1) * fresh_shape[0]
    whole = pl.BlockSpec(fresh_shape, lambda i, length: (0, 0))
    in_specs = [
        block,
        pl.BlockSpec((width, rows), lambda i, length: (0, i)),
        pl.BlockSpec((stat.shape[0], rows), lambda i, length: (0, i)),
        *(whole for _ in earlier),
        *(spec for _, spec in pieces),
    ]
    operands = [length, query_rows, acc, stat, *earlier, *(array for array, _ in pieces)]
    aliases = {}
    if result is not None:
        in_specs.append(pl.BlockSpec(memory_space=pl.ANY))
        aliases = {len(operands): 0}
        operands.append(result)
    return pl.pallas_call(
        functools.partial(
            fresh_kernel,
            scale,
            heads,
            per_token,
            chunk * (chunk_rows // per_token),
            (len(earlier), len(pieces)),
        ),
        grid_spec=pltpu.PrefetchScalarGridSpec(
            num_scalar_prefetch=1,
            grid=(steps,),
            in_specs=in_specs,
            out_specs=[block, whole],
            scratch_shapes=[
                pltpu.VMEM((key_count, heads * width), jnp.bfloat16),
                pltpu.VMEM((heads * (width + ONES), key_count), jnp.bfloat16),
                pltpu.VMEM((rows, width), jnp.float32),
                pltpu.VMEM((rows, width), jnp.float32),
            ],
        ),
        out_shape=[
            jax.ShapeDtypeStruct((row_total, width), jnp.bfloat16),
            jax.ShapeDtypeStruct(fresh_shape, jnp.bfloat16),
        ],
        input_output_aliases=aliases,
        compiler_params=params(),
        cost_estimate=cost("fresh_attend"),
        name="fresh_attend",
    )(*operands)


def reduced_shards(tokens, key_weight, value_weight, queries, prefix_pool, block_table, lengths):
    batch_count = lax.axis_size("batch")
    ctx_count = lax.axis_size("ctx")
    head_count = lax.axis_size("head")
    batch_at, ctx_at, head_at = (lax.axis_index(a) for a in ("batch", "ctx", "head"))
    place = jnp.stack([batch_at, ctx_at, head_at]).astype(jnp.int32)
    token_count = tokens.shape[0]
    heads = queries.shape[1]
    width = prefix_pool.shape[4] // 2
    group = queries.shape[3] // width
    per_token = heads * group
    depth = key_weight.shape[2]
    rows = token_count // CHUNKS
    scale = math.log2(math.e) / math.sqrt(width)

    top = batch_count // 2
    steps = list(range(batch_count - 1, top, -1)) + list(range(1, top))
    pieces, pools = prepare(
        place, tokens, depth, [*steps, top], prefix_pool, ctx_count, heads
    )
    arrived = [trade(piece, "batch", bits) for piece, bits in zip(pieces, steps)]
    pools, (key_weight, value_weight) = after(pools, (key_weight, value_weight))
    pools = [shift(part, "ctx", step) if step else part for step, part in enumerate(pools)]

    weights = arrange_weights(key_weight, value_weight, ctx_count, heads, head_count)
    weights, last = after(weights, pieces[-1])
    last = trade(last, "batch", top)

    query_rows = queries.reshape(token_count, heads, group, width)
    query_rows = query_rows.transpose(0, 2, 1, 3).reshape(-1, width)
    def projected(blocks, name):
        terms = [
            shift(project(place, blocks, weights, step, jnp.bfloat16, name + "_away"), "head", step)
            for step in range(1, head_count)
        ]
        return [project(place, blocks, weights, 0, jnp.float32, name + "_kept"), *terms]

    def added(terms, step, here):
        return sum(term[step, here].astype(jnp.float32) for term in terms)

    def others(terms, here):
        return [added(terms, step, here).astype(jnp.bfloat16) for step in range(1, ctx_count)]

    def spread(parts):
        return [shift(part, "ctx", step + 1) for step, part in enumerate(parts)]

    every = slice(None)
    parts_of = [slice(i * rows, (i + 1) * rows) for i in range(CHUNKS)]

    keys, values = pick_blocks(place, block_table[0], pools, heads)
    state = prefix_attend(query_rows, keys, values, 0, scale, heads, (0, 2))

    sums, near = [], []
    if steps:
        state, arrived = after(state, arrived)
        early = projected(arrived, "early")
        far_rows, near_rows = slice(0, token_count), slice(token_count, 2 * token_count)
        far = others(early, far_rows)
        near = sum(term[:, near_rows].astype(jnp.float32) for term in early)
        near = near.astype(jnp.bfloat16)
        (far, near), (keys, values) = after((far, near), (keys, values))
        far, near = spread(far), [trade(near, "batch", 1)]
        sums = [
            [piece_of(t, token_count, 0, 0) for t in early]
            + [piece_of(part, token_count, 0) for part in far]
        ]
    states = [prefix_attend(query_rows, keys, values, 0, scale, heads, (1, 2), state)]
    state = prefix_attend(query_rows, keys, values, 1, scale, heads, (0, 2))
    (states[0], state), last = after((states[0], state), last)

    def late_project(step, dtype, name, sums):
        result = project(place, [last, tokens], weights, step, dtype, name, sums)
        return result if sums else (result,)

    terms = []
    for step in range(1, head_count):
        term, *far = late_project(step, jnp.bfloat16, "late_away", sums if step == 1 else [])
        terms.append(shift(term, "head", step))
    kept, *_ = late_project(0, jnp.float32, "late_kept", [])
    late = [kept, *terms]
    far = [trade(part, "batch", 1) for part in far]
    own_at = slice(token_count, 2 * token_count)
    late_others = [others(late, here) for here in parts_of]
    late_others[0] = spread(late_others[0])
    own_others = []
    for step in range(1, ctx_count):
        part = added(late, step, own_at) + sum(part[step].astype(jnp.float32) for part in near)
        own_others.append(part.astype(jnp.bfloat16))
    (late_others[1], own_others), (keys, values) = after(
        (late_others[1], own_others), (keys, values)
    )
    states.append(prefix_attend(query_rows, keys, values, 1, scale, heads, (1, 2), state))
    states[1], (late_others[1], own_others) = after(states[1], (late_others[1], own_others))
    late_others[1], own_others = spread(late_others[1]), spread(own_others)

    away = []
    for chunk, here in enumerate(parts_of):
        part = added(late, 0, here) + sum(p.astype(jnp.float32) for p in late_others[chunk])
        part = part + sum(p[here].astype(jnp.float32) for p in far)
        part = part.astype(jnp.bfloat16)
        if chunk == 0:
            (far, late), late_others[1] = after((far, late), late_others[1])
        else:
            away[-1], part = after(away[-1], part)
        away.append(trade(part, "batch", top))

    result = None
    fresh = []
    for chunk in range(CHUNKS):
        pieces = [piece_of(t, rows, CHUNKS + chunk, 0) for t in late]
        pieces += [piece_of(part, rows, chunk, 0) for part in near]
        pieces += [piece_of(part, rows, chunk) for part in own_others]
        pieces.append(piece_of(away[chunk], rows, 0))
        result, new = fresh_attend(
            lengths,
            query_rows,
            *states[chunk],
            fresh,
            pieces,
            result,
            chunk,
            scale,
            heads,
            per_token,
        )
        fresh.append(new)
    result = result.reshape(token_count, group, heads, width).transpose(0, 2, 1, 3)
    return result.reshape(token_count, heads, 1, group * width)


def solution(mesh):
    def shards(tokens, key_weight, value_weight, *rest):
        prompts = mesh.shape["batch"]
        columns = 2 * math.prod(key_weight.shape[3:])
        few_tokens = prompts * tokens.shape[0] <= columns and prompts in (2, 4)
        form = reduced_shards if few_tokens else gathered_shards
        return form(tokens, key_weight, value_weight, *rest)

    return jax.shard_map(
        shards,
        mesh=mesh,
        in_specs=(
            P(("groups", "batch"), ("ctx", "head")),
            P("ctx", "head", "batch", None, None, None),
            P("ctx", "head", "batch", None, None, None),
            P(("groups", "batch"), "ctx", "head", None),
            P(("groups", "ctx"), None, None, "head", None),
            P(("groups", "batch"), None),
            P(("groups", "batch")),
        ),
        out_specs=P(("groups", "batch"), "ctx", "head", None),
        check_vma=False,
    )
```

```python
import functools
import math

import jax
import jax.numpy as jnp
from jax import lax
from jax.experimental import pallas as pl
from jax.experimental.pallas import tpu as pltpu
from jax.sharding import PartitionSpec as P

CHUNKS = 2
PART = 1024
ONES = 16
VMEM_BYTES = 16 * 1024 * 1024
MOST_VMEM_BYTES = 60 * 1024 * 1024
LONG = pl.CostEstimate(flops=10**11, bytes_accessed=1, transcendentals=0)
COSTS = {}


def cost(name):
    return COSTS.get(name, LONG)


def attend_head(query_rows, prefix, fresh_rows, length):
    token_count = query_rows.shape[0]
    head_width = prefix.shape[1] // 2
    group_size = query_rows.shape[1] // head_width
    prefix_len = prefix.shape[0]
    key_rows = jnp.concatenate([prefix[:, :head_width], fresh_rows[:, :head_width]], 0)
    value_rows = jnp.concatenate([prefix[:, head_width:], fresh_rows[:, head_width:]], 0)
    block_len = min(token_count, 64)
    pieces = []
    for first_row in range(0, token_count, block_len):
        block_rows = query_rows[first_row : first_row + block_len].reshape(
            block_len * group_size, head_width
        )
        scores = jnp.dot(
            block_rows, key_rows.T, preferred_element_type=jnp.float32
        ) * head_width ** (-0.5)
        position = first_row + jnp.arange(block_len * group_size) // group_size
        column = jnp.arange(prefix_len + token_count) - prefix_len
        allowed = column[None, :] <= position[:, None]
        scores = jnp.where(allowed, scores, -jnp.inf)
        row_max = jnp.max(scores, axis=1, keepdims=True)
        weights = jnp.exp(scores - row_max)
        row_total = jnp.sum(weights, axis=1, keepdims=True)
        probs_bf = (weights / row_total).astype(jnp.bfloat16)
        mixed_rows = jnp.dot(probs_bf, value_rows, preferred_element_type=jnp.float32)
        is_live = position < length
        mixed_rows = jnp.where(is_live[:, None], mixed_rows, 0.0)
        pieces.append(mixed_rows.astype(jnp.bfloat16).reshape(block_len, group_size * head_width))
    return jnp.concatenate(pieces, 0)


def gathered_shards(tokens, key_weight, value_weight, queries, prefix_pool, block_table, lengths):
    token_count = tokens.shape[0]
    local_heads = queries.shape[1]
    head_width = prefix_pool.shape[4] // 2
    ctx_count = lax.axis_size("ctx")
    head_count = lax.axis_size("head")
    features = lax.all_gather(tokens, ("ctx", "head"), axis=1, tiled=True)
    key_cols, value_cols = (
        lax.all_to_all(
            lax.all_to_all(weight, "ctx", split_axis=3, concat_axis=0, tiled=True),
            "head",
            split_axis=4,
            concat_axis=1,
            tiled=True,
        )
        for weight in (key_weight, value_weight)
    )
    span_len = features.shape[1] // (ctx_count * head_count)
    feature_view = features.reshape(token_count, ctx_count, head_count, span_len)
    pieces = (
        lax.all_gather(key_cols, "batch", axis=2, tiled=True),
        lax.all_gather(value_cols, "batch", axis=2, tiled=True),
    )
    row_count = pieces[0].shape[2]

    def one_term(weight_piece):
        shaped = weight_piece.reshape(ctx_count, head_count, row_count, local_heads * head_width)
        return jnp.einsum("tchr,chrk->tk", feature_view, shaped, preferred_element_type=jnp.float32)

    new_keys = one_term(pieces[0]).astype(jnp.bfloat16).reshape(token_count, local_heads, head_width)
    new_values = one_term(pieces[1]).astype(jnp.bfloat16).reshape(token_count, local_heads, head_width)
    fresh_all = jnp.concatenate([new_keys, new_values], 2)
    pool_heads = lax.all_to_all(prefix_pool, "ctx", split_axis=2, concat_axis=0, tiled=True)
    chosen = jnp.take(pool_heads, block_table[0], axis=0)
    chosen = chosen.reshape(-1, local_heads, 2 * head_width)
    outputs = [
        attend_head(
            queries[:, head_idx, 0], chosen[:, head_idx], fresh_all[:, head_idx], lengths[0]
        )
        for head_idx in range(local_heads)
    ]
    return jnp.stack(outputs, 1)[:, :, None, :]


def shift(array, axis, step):
    count = lax.axis_size(axis)
    return lax.ppermute(array, axis, [(i, (i + step) % count) for i in range(count)])


def trade(array, axis, bits):
    return lax.ppermute(array, axis, [(i, i ^ bits) for i in range(lax.axis_size(axis))])


def after(first, second):
    return lax.optimization_barrier((first, second))


def softmax_parts(scores, old_max=None):
    row_max = jnp.max(scores, axis=0, keepdims=True)
    if old_max is not None:
        row_max = jnp.maximum(row_max, old_max)
    return row_max, jnp.exp2(scores - row_max).astype(jnp.bfloat16)


def dot_queries(keys, query_block):
    return lax.dot_general(
        keys, query_block, (((1,), (1,)), ((), ())), preferred_element_type=jnp.float32
    )


def params(limit=None):
    return pltpu.CompilerParams(vmem_limit_bytes=limit or VMEM_BYTES)


def weight_kernel(ctx_count, heads, head_count, key_ref, value_ref, out_ref, flat):
    depth, slots, width = key_ref.shape
    for kind, ref in enumerate((key_ref, value_ref)):
        flat[...] = ref[...].astype(jnp.float32).reshape(depth * slots, width)
        for ctx in range(ctx_count):
            for head in range(heads):
                for core in range(head_count):
                    slot = (ctx * heads + head) * head_count + core
                    at = (kind * heads + head) * width
                    out_ref[core, ctx, :, at : at + width] = flat[
                        pl.ds(slot, depth, stride=slots), :
                    ].astype(out_ref.dtype)


def arrange_weights(key_weight, value_weight, ctx_count, heads, head_count):
    depth, width = key_weight.shape[2], key_weight.shape[5]
    slots = ctx_count * heads * head_count
    rows = min(128, depth)
    views = [w.reshape(depth, slots, width) for w in (key_weight, value_weight)]
    block = pl.BlockSpec((rows, slots, width), lambda i: (i, 0, 0))
    columns = 2 * heads * width
    return pl.pallas_call(
        functools.partial(weight_kernel, ctx_count, heads, head_count),
        grid=(depth // rows,),
        in_specs=[block, block],
        out_specs=pl.BlockSpec((head_count, ctx_count, rows, columns), lambda i: (0, 0, i, 0)),
        out_shape=jax.ShapeDtypeStruct((head_count, ctx_count, depth, columns), jnp.bfloat16),
        scratch_shapes=[pltpu.VMEM((rows * slots, width), jnp.float32)],
        compiler_params=params(),
        cost_estimate=cost("arrange_weights"),
        name="arrange_weights",
    )(*views)


def cut_kernel(bits, place_ref, tokens_ref, *refs):
    pieces, (held, sems) = refs[:-2], refs[-2:]
    depth = pieces[0].shape[1]
    inward, outward = [], []
    for index, piece in enumerate(pieces):
        start = pl.multiple_of((place_ref[0] ^ bits[index]) * depth, depth)
        source = tokens_ref.at[:, pl.ds(start, depth)]
        inward.append(pltpu.make_async_copy(source, held.at[index], sems.at[0, index]))
        outward.append(pltpu.make_async_copy(held.at[index], piece, sems.at[1, index]))
    for copy in inward:
        copy.start()
    for copy, onward in zip(inward, outward):
        copy.wait()
        onward.start()
    for copy in outward:
        copy.wait()


def cut_tokens(place, tokens, depth, bits):
    far = pl.BlockSpec(memory_space=pltpu.HBM)
    piece = jax.ShapeDtypeStruct((tokens.shape[0], depth), tokens.dtype)
    return pl.pallas_call(
        functools.partial(cut_kernel, bits),
        grid_spec=pltpu.PrefetchScalarGridSpec(
            num_scalar_prefetch=1,
            grid=(1,),
            in_specs=[far],
            out_specs=[far] * len(bits),
            scratch_shapes=[
                pltpu.VMEM((len(bits), *piece.shape), tokens.dtype),
                pltpu.SemaphoreType.DMA((2, len(bits))),
            ],
        ),
        out_shape=[piece] * len(bits),
        compiler_params=params(MOST_VMEM_BYTES),
        cost_estimate=cost("cut_tokens"),
        name="cut_tokens",
    )(place, tokens)


def pool_kernel(ctx_count, heads, place_ref, pool_ref, *refs):
    outs, flat = refs[:-1], refs[-1]
    some, length, slots, width = pool_ref.shape
    length *= some
    flat[...] = pool_ref[...].astype(jnp.float32).reshape(length * slots, width)
    for kind in range(2):
        for head in range(heads):
            at = (kind * heads + head) * width
            held = []
            for ctx in range(ctx_count):
                slot = (kind * ctx_count + ctx) * heads + head
                held.append(flat[pl.ds(slot, length, stride=slots), :])
            for step, out_ref in enumerate(outs):
                target = lax.rem(place_ref[1] + step, ctx_count)
                value = held[0]
                for ctx in range(1, ctx_count):
                    value = jnp.where(target == ctx, held[ctx], value)
                out_ref[:, :, at : at + width] = value.astype(out_ref.dtype).reshape(
                    some, length // some, width
                )


def arrange_pool(place, prefix_pool, ctx_count, heads):
    blocks, length, all_heads, _, double = prefix_pool.shape
    width = double // 2
    slots = 2 * all_heads
    view = prefix_pool.reshape(blocks, length, all_heads, 2, width)
    view = view.transpose(0, 1, 3, 2, 4).reshape(blocks, length, slots, width)
    columns = 2 * heads * width
    some = 2 if blocks % 2 == 0 else 1
    out = pl.BlockSpec((some, length, columns), lambda i, place: (i, 0, 0))
    return pl.pallas_call(
        functools.partial(pool_kernel, ctx_count, heads),
        grid_spec=pltpu.PrefetchScalarGridSpec(
            num_scalar_prefetch=1,
            grid=(blocks // some,),
            in_specs=[pl.BlockSpec((some, length, slots, width), lambda i, place: (i, 0, 0, 0))],
            out_specs=[out] * ctx_count,
            scratch_shapes=[pltpu.VMEM((some * length * slots, width), jnp.float32)],
        ),
        out_shape=[jax.ShapeDtypeStruct((blocks, length, columns), jnp.bfloat16)] * ctx_count,
        compiler_params=params(),
        cost_estimate=cost("arrange_pool"),
        name="arrange_pool",
    )(place, view)


def total_of(refs):
    return sum(ref[...].astype(jnp.float32).reshape(ref.shape[-2:]) for ref in refs)


def project_kernel(block_count, term_counts, place_ref, *refs):
    token_refs, weight_ref = refs[:block_count], refs[block_count]
    terms = refs[block_count + 1 : block_count + 1 + sum(term_counts)]
    out_ref, *sum_refs = refs[block_count + 1 + sum(term_counts) : -1]
    stacked = refs[-1]

    @pl.when(pl.program_id(0) == 0)
    def _():
        at = 0
        for token_ref in token_refs:
            rows = token_ref.shape[0]
            stacked[at : at + rows, :] = token_ref[...]
            at += rows
        at = 0
        for count, sum_ref in zip(term_counts, sum_refs):
            sum_ref[...] = total_of(terms[at : at + count]).astype(sum_ref.dtype)
            at += count

    out_ref[0] = jnp.dot(
        stacked[...], weight_ref[0, 0], preferred_element_type=jnp.float32
    ).astype(out_ref.dtype)


def piece_of(array, *index):
    rows, block, *leading = index
    shape = (1,) * len(leading) + (rows, array.shape[-1])
    return array, pl.BlockSpec(shape, lambda j, *_: (*leading, block, 0))


def project(place, blocks, weights, head_step, out_dtype, name, sums=()):
    head_count, ctx_count, depth, width = weights.shape
    row_total = sum(block.shape[0] for block in blocks)

    def block_spec(block):
        if block.shape[1] == depth:
            return pl.BlockSpec(block.shape, lambda j, place: (0, 0))
        return pl.BlockSpec((block.shape[0], depth), lambda j, place: (0, place[0]))

    pieces = [piece for terms in sums for piece in terms]
    sum_shapes = [terms[0][1].block_shape[-2:] for terms in sums]
    result = pl.pallas_call(
        functools.partial(project_kernel, len(blocks), [len(terms) for terms in sums]),
        grid_spec=pltpu.PrefetchScalarGridSpec(
            num_scalar_prefetch=1,
            grid=(ctx_count,),
            in_specs=[block_spec(block) for block in blocks]
            + [
                pl.BlockSpec(
                    (1, 1, depth, width),
                    lambda j, place: (
                        lax.rem(place[2] + head_step, head_count),
                        lax.rem(place[1] + j, ctx_count),
                        0,
                        0,
                    ),
                )
            ]
            + [spec for _, spec in pieces],
            out_specs=[pl.BlockSpec((1, row_total, width), lambda j, place: (j, 0, 0))]
            + [pl.BlockSpec(shape, lambda j, place: (0, 0)) for shape in sum_shapes],
            scratch_shapes=[pltpu.VMEM((row_total, depth), weights.dtype)],
        ),
        out_shape=[jax.ShapeDtypeStruct((ctx_count, row_total, width), out_dtype)]
        + [jax.ShapeDtypeStruct(shape, jnp.bfloat16) for shape in sum_shapes],
        compiler_params=params(),
        cost_estimate=cost(name),
        name=name,
    )(place, *blocks, weights, *(array for array, _ in pieces))
    return result if sums else result[0]


def pick_kernel(heads, ctx_count, place_ref, table_ref, *refs):
    pool_refs, (keys, values) = refs[:ctx_count], refs[ctx_count:]
    blocks, length, columns = pool_refs[0].shape
    wide = columns // 2
    width = wide // heads
    values[...] = jnp.ones_like(values)
    for at in range(table_ref.shape[0]):
        entry = table_ref[at]
        here = slice(at * length, (at + 1) * length)
        step = lax.rem(place_ref[1] - entry // blocks + ctx_count, ctx_count)
        for ctx_step, pool_ref in enumerate(pool_refs):

            @pl.when(step == ctx_step)
            def _():
                block = pool_ref[entry % blocks]
                keys[here, :] = block[:, :wide]
                put_values(values, here, block[:, wide:], heads)


def put_values(values, here, block, heads):
    width = block.shape[1] // heads
    for head in range(heads):
        low = head * (width + ONES)
        values[low : low + width, here] = (
            block[:, head * width : (head + 1) * width].astype(jnp.float32).T.astype(jnp.bfloat16)
        )


def pick_blocks(place, table, pools, heads):
    length, columns = pools[0].shape[1:]
    count = table.shape[0] * length
    wide = columns // 2
    tall = wide + heads * ONES
    return pl.pallas_call(
        functools.partial(pick_kernel, heads, len(pools)),
        grid_spec=pltpu.PrefetchScalarGridSpec(
            num_scalar_prefetch=2,
            grid=(1,),
            in_specs=[pl.BlockSpec(p.shape, lambda i, *_: (0, 0, 0)) for p in pools],
            out_specs=[
                pl.BlockSpec((count, wide), lambda i, *_: (0, 0)),
                pl.BlockSpec((tall, count), lambda i, *_: (0, 0)),
            ],
        ),
        out_shape=[
            jax.ShapeDtypeStruct((count, wide), jnp.bfloat16),
            jax.ShapeDtypeStruct((tall, count), jnp.bfloat16),
        ],
        compiler_params=params(),
        cost_estimate=cost("pick_blocks"),
        name="pick_blocks",
    )(place, table, *pools)


def each_part(rows, heads):
    part_rows = min(PART, rows)
    each = part_rows // heads
    for low in range(0, rows, part_rows):
        for head in range(heads):
            at = low + head * each
            yield head, pl.ds(low + head, each, stride=heads), slice(at, at + each)


def prefix_kernel(scale, heads, query_ref, keys, values, *refs):
    acc_ref, stat_ref, flat = refs[-3:]
    rows, width = query_ref.shape
    tall = width + ONES
    half = stat_ref.shape[0] // 2
    flat[...] = query_ref[...].astype(jnp.float32)
    for head, taken, here in each_part(rows, heads):
        query_block = flat[taken, :].astype(jnp.bfloat16)
        scores = dot_queries(keys[:, head * width : (head + 1) * width], query_block) * scale
        row_max, weights = softmax_parts(scores)
        mixed = jnp.dot(
            values[head * tall : (head + 1) * tall, :], weights, preferred_element_type=jnp.float32
        )
        acc_ref[:, here] = mixed[:width]
        stat_ref[:half, here] = jnp.broadcast_to(row_max, (half, row_max.shape[1]))
        stat_ref[half:, here] = jnp.broadcast_to(mixed[width : width + 1], (half, row_max.shape[1]))


def prefix_attend(query_rows, keys, values, chunk, scale, heads, part=(0, 1), state=None):
    all_rows, width = query_rows.shape
    row_total = all_rows // CHUNKS
    at, count = part
    rows = min(1024, row_total // count)
    steps = row_total // rows // count
    first = chunk * count * steps + at * steps
    out_specs = [
        pl.BlockSpec((width, rows), lambda i: (0, at * steps + i)),
        pl.BlockSpec((8, rows), lambda i: (0, at * steps + i)),
    ]
    in_specs = [
        pl.BlockSpec((rows, width), lambda i: (first + i, 0)),
        pl.BlockSpec(keys.shape, lambda i: (0, 0)),
        pl.BlockSpec(values.shape, lambda i: (0, 0)),
    ]
    operands = [query_rows, keys, values]
    aliases = {}
    if state is not None:
        in_specs += [pl.BlockSpec(memory_space=pl.ANY)] * 2
        operands += state
        aliases = {3: 0, 4: 1}
    return pl.pallas_call(
        functools.partial(prefix_kernel, scale, heads),
        grid=(steps,),
        in_specs=in_specs,
        out_specs=out_specs,
        out_shape=[
            jax.ShapeDtypeStruct((width, row_total), jnp.float32),
            jax.ShapeDtypeStruct((8, row_total), jnp.float32),
        ],
        input_output_aliases=aliases,
        scratch_shapes=[pltpu.VMEM((rows, width), jnp.float32)],
        compiler_params=params(),
        cost_estimate=cost("prefix_attend"),
        name="prefix_attend",
    )(*operands)


def fresh_kernel(
    scale, heads, per_token, first_row, counts, length_ref, query_ref, acc_ref, stat_ref, *rest
):
    early_count, term_count = counts
    earlier, terms = rest[:early_count], rest[early_count : early_count + term_count]
    out_ref, fresh_ref, keys, values, flat, mixed_rows = rest[-6:]
    rows, width = query_ref.shape
    wide, tall = heads * width, width + ONES
    step = pl.program_id(0)

    @pl.when(step == 0)
    def _():
        values[...] = jnp.ones_like(values)
        fresh_ref[...] = total_of(terms).astype(fresh_ref.dtype)
        for index, ref in enumerate([*earlier, fresh_ref]):
            here = slice(index * ref.shape[0], (index + 1) * ref.shape[0])
            fresh = ref[...]
            keys[here, :] = fresh[:, :wide]
            put_values(values, here, fresh[:, wide:], heads)

    half = stat_ref.shape[0] // 2
    flat[...] = query_ref[...].astype(jnp.float32)
    for head, taken, here in each_part(rows, heads):
        query_block = flat[taken, :].astype(jnp.bfloat16)
        scores = dot_queries(keys[:, head * width : (head + 1) * width], query_block) * scale
        row = taken.start + heads * lax.broadcasted_iota(jnp.int32, (1, taken.size), 1)
        token = first_row + step * (rows // per_token) + (
            row // per_token if per_token & (per_token - 1) else row >> (per_token.bit_length() - 1)
        )
        key_at = lax.broadcasted_iota(jnp.int32, scores.shape, 0)
        scores = jnp.where(key_at <= token, scores, -jnp.inf)
        old_max, old_total = stat_ref[:1, here], stat_ref[half : half + 1, here]
        row_max, weights = softmax_parts(scores, old_max)
        fade = jnp.exp2(old_max - row_max)
        mixed = jnp.dot(
            values[head * tall : (head + 1) * tall, :], weights, preferred_element_type=jnp.float32
        )
        row_total = old_total * fade + mixed[width : width + 1]
        share = jnp.where(token < length_ref[0], 1.0 / row_total, 0.0)
        result = acc_ref[:, here] * (fade * share) + mixed[:width] * share
        mixed_rows[taken, :] = result.T
    out_ref[...] = mixed_rows[...].astype(out_ref.dtype)


def fresh_attend(
    length, query_rows, acc, stat, earlier, pieces, result, chunk, scale, heads, per_token
):
    row_total, width = query_rows.shape
    chunk_rows = row_total // CHUNKS
    rows = min(1024, chunk_rows)
    steps = chunk_rows // rows
    block = pl.BlockSpec((rows, width), lambda i, length: (chunk * steps + i, 0))
    fresh_shape = pieces[0][1].block_shape[-2:]
    key_count = (len(earlier) + 1) * fresh_shape[0]
    whole = pl.BlockSpec(fresh_shape, lambda i, length: (0, 0))
    in_specs = [
        block,
        pl.BlockSpec((width, rows), lambda i, length: (0, i)),
        pl.BlockSpec((stat.shape[0], rows), lambda i, length: (0, i)),
        *(whole for _ in earlier),
        *(spec for _, spec in pieces),
    ]
    operands = [length, query_rows, acc, stat, *earlier, *(array for array, _ in pieces)]
    aliases = {}
    if result is not None:
        in_specs.append(pl.BlockSpec(memory_space=pl.ANY))
        aliases = {len(operands): 0}
        operands.append(result)
    return pl.pallas_call(
        functools.partial(
            fresh_kernel,
            scale,
            heads,
            per_token,
            chunk * (chunk_rows // per_token),
            (len(earlier), len(pieces)),
        ),
        grid_spec=pltpu.PrefetchScalarGridSpec(
            num_scalar_prefetch=1,
            grid=(steps,),
            in_specs=in_specs,
            out_specs=[block, whole],
            scratch_shapes=[
                pltpu.VMEM((key_count, heads * width), jnp.bfloat16),
                pltpu.VMEM((heads * (width + ONES), key_count), jnp.bfloat16),
                pltpu.VMEM((rows, width), jnp.float32),
                pltpu.VMEM((rows, width), jnp.float32),
            ],
        ),
        out_shape=[
            jax.ShapeDtypeStruct((row_total, width), jnp.bfloat16),
            jax.ShapeDtypeStruct(fresh_shape, jnp.bfloat16),
        ],
        input_output_aliases=aliases,
        compiler_params=params(),
        cost_estimate=cost("fresh_attend"),
        name="fresh_attend",
    )(*operands)


def reduced_shards(tokens, key_weight, value_weight, queries, prefix_pool, block_table, lengths):
    batch_count = lax.axis_size("batch")
    ctx_count = lax.axis_size("ctx")
    head_count = lax.axis_size("head")
    batch_at, ctx_at, head_at = (lax.axis_index(a) for a in ("batch", "ctx", "head"))
    place = jnp.stack([batch_at, ctx_at, head_at]).astype(jnp.int32)
    token_count = tokens.shape[0]
    heads = queries.shape[1]
    width = prefix_pool.shape[4] // 2
    group = queries.shape[3] // width
    per_token = heads * group
    depth = key_weight.shape[2]
    rows = token_count // CHUNKS
    scale = math.log2(math.e) / math.sqrt(width)

    top = batch_count // 2
    steps = list(range(batch_count - 1, top, -1)) + list(range(1, top))
    pieces = cut_tokens(place, tokens, depth, steps)
    pieces, prefix_pool = after(pieces, prefix_pool)
    arrived = [trade(piece, "batch", bits) for piece, bits in zip(pieces, steps)]
    pools = arrange_pool(place, prefix_pool, ctx_count, heads)
    pools, (key_weight, value_weight) = after(pools, (key_weight, value_weight))
    pools = [shift(part, "ctx", step) if step else part for step, part in enumerate(pools)]

    weights = arrange_weights(key_weight, value_weight, ctx_count, heads, head_count)
    weights, late_tokens = after(weights, tokens)
    (last,) = cut_tokens(place, late_tokens, depth, [top])
    last = trade(last, "batch", top)

    query_rows = queries.reshape(token_count, heads, group, width)
    query_rows = query_rows.transpose(0, 2, 1, 3).reshape(-1, width)
    def projected(blocks, name):
        terms = [
            shift(project(place, blocks, weights, step, jnp.bfloat16, name + "_away"), "head", step)
            for step in range(1, head_count)
        ]
        return [project(place, blocks, weights, 0, jnp.float32, name + "_kept"), *terms]

    def added(terms, step, here):
        return sum(term[step, here].astype(jnp.float32) for term in terms)

    def others(terms, here):
        return [added(terms, step, here).astype(jnp.bfloat16) for step in range(1, ctx_count)]

    def spread(parts):
        return [shift(part, "ctx", step + 1) for step, part in enumerate(parts)]

    every = slice(None)
    parts_of = [slice(i * rows, (i + 1) * rows) for i in range(CHUNKS)]

    sums, near = [], []
    if steps:
        early = projected(arrived, "early")
        far_rows, near_rows = slice(0, token_count), slice(token_count, 2 * token_count)
        far = others(early, far_rows)
        near = sum(term[:, near_rows].astype(jnp.float32) for term in early)
        near = near.astype(jnp.bfloat16)
        far, pools = after(far, pools)
        far, near = spread(far), [trade(near, "batch", 1)]
        sums = [
            [piece_of(t, token_count, 0, 0) for t in early]
            + [piece_of(part, token_count, 0) for part in far]
        ]
    keys, values = pick_blocks(place, block_table[0], pools, heads)
    state = prefix_attend(query_rows, keys, values, 0, scale, heads, (0, 2))
    state, last = after(state, last)

    def late_project(step, dtype, name, sums):
        result = project(place, [last, tokens], weights, step, dtype, name, sums)
        return result if sums else (result,)

    terms = []
    for step in range(1, head_count):
        term, *far = late_project(step, jnp.bfloat16, "late_away", sums if step == 1 else [])
        terms.append(shift(term, "head", step))
    kept, *_ = late_project(0, jnp.float32, "late_kept", [])
    late = [kept, *terms]
    far = [trade(part, "batch", 1) for part in far]
    own_at = slice(token_count, 2 * token_count)
    late_others = [others(late, here) for here in parts_of]
    late_others[0] = spread(late_others[0])
    own_others = []
    for step in range(1, ctx_count):
        part = added(late, step, own_at) + sum(part[step].astype(jnp.float32) for part in near)
        own_others.append(part.astype(jnp.bfloat16))
    (late_others[1], own_others), (keys, values) = after(
        (late_others[1], own_others), (keys, values)
    )
    states = [prefix_attend(query_rows, keys, values, 0, scale, heads, (1, 2), state)]
    states[0], (late_others[1], own_others) = after(states[0], (late_others[1], own_others))
    late_others[1], own_others = spread(late_others[1]), spread(own_others)

    away = []
    for chunk, here in enumerate(parts_of):
        part = added(late, 0, here) + sum(p.astype(jnp.float32) for p in late_others[chunk])
        part = part + sum(p[here].astype(jnp.float32) for p in far)
        part = part.astype(jnp.bfloat16)
        if chunk == 0:
            (far, late), late_others[1] = after((far, late), late_others[1])
            part, (keys, values) = after(part, (keys, values))
            state = prefix_attend(query_rows, keys, values, 1, scale, heads, (0, 2))
            state = prefix_attend(query_rows, keys, values, 1, scale, heads, (1, 2), state)
            states.append(state)
        else:
            away[-1], part = after(away[-1], part)
        away.append(trade(part, "batch", top))

    result = None
    fresh = []
    for chunk in range(CHUNKS):
        pieces = [piece_of(t, rows, CHUNKS + chunk, 0) for t in late]
        pieces += [piece_of(part, rows, chunk, 0) for part in near]
        pieces += [piece_of(part, rows, chunk) for part in own_others]
        pieces.append(piece_of(away[chunk], rows, 0))
        result, new = fresh_attend(
            lengths,
            query_rows,
            *states[chunk],
            fresh,
            pieces,
            result,
            chunk,
            scale,
            heads,
            per_token,
        )
        fresh.append(new)
    result = result.reshape(token_count, group, heads, width).transpose(0, 2, 1, 3)
    return result.reshape(token_count, heads, 1, group * width)


def solution(mesh):
    def shards(tokens, key_weight, value_weight, *rest):
        prompts = mesh.shape["batch"]
        columns = 2 * math.prod(key_weight.shape[3:])
        few_tokens = prompts * tokens.shape[0] <= columns and prompts in (2, 4)
        form = reduced_shards if few_tokens else gathered_shards
        return form(tokens, key_weight, value_weight, *rest)

    return jax.shard_map(
        shards,
        mesh=mesh,
        in_specs=(
            P(("groups", "batch"), ("ctx", "head")),
            P("ctx", "head", "batch", None, None, None),
            P("ctx", "head", "batch", None, None, None),
            P(("groups", "batch"), "ctx", "head", None),
            P(("groups", "ctx"), None, None, "head", None),
            P(("groups", "batch"), None),
            P(("groups", "batch")),
        ),
        out_specs=P(("groups", "batch"), "ctx", "head", None),
        check_vma=False,
    )
```

```python
import functools
import math

import jax
import jax.numpy as jnp
from jax import lax
from jax.experimental import pallas as pl
from jax.experimental.pallas import tpu as pltpu
from jax.sharding import PartitionSpec as P

CHUNKS = 2
PART = 1024
ONES = 16
VMEM_BYTES = 16 * 1024 * 1024
MOST_VMEM_BYTES = 60 * 1024 * 1024
LONG = pl.CostEstimate(flops=10**11, bytes_accessed=1, transcendentals=0)
COSTS = {}


def cost(name):
    return COSTS.get(name, LONG)


def attend_head(query_rows, prefix, fresh_rows, length):
    token_count = query_rows.shape[0]
    head_width = prefix.shape[1] // 2
    group_size = query_rows.shape[1] // head_width
    prefix_len = prefix.shape[0]
    key_rows = jnp.concatenate([prefix[:, :head_width], fresh_rows[:, :head_width]], 0)
    value_rows = jnp.concatenate([prefix[:, head_width:], fresh_rows[:, head_width:]], 0)
    block_len = min(token_count, 64)
    pieces = []
    for first_row in range(0, token_count, block_len):
        block_rows = query_rows[first_row : first_row + block_len].reshape(
            block_len * group_size, head_width
        )
        scores = jnp.dot(
            block_rows, key_rows.T, preferred_element_type=jnp.float32
        ) * head_width ** (-0.5)
        position = first_row + jnp.arange(block_len * group_size) // group_size
        column = jnp.arange(prefix_len + token_count) - prefix_len
        allowed = column[None, :] <= position[:, None]
        scores = jnp.where(allowed, scores, -jnp.inf)
        row_max = jnp.max(scores, axis=1, keepdims=True)
        weights = jnp.exp(scores - row_max)
        row_total = jnp.sum(weights, axis=1, keepdims=True)
        probs_bf = (weights / row_total).astype(jnp.bfloat16)
        mixed_rows = jnp.dot(probs_bf, value_rows, preferred_element_type=jnp.float32)
        is_live = position < length
        mixed_rows = jnp.where(is_live[:, None], mixed_rows, 0.0)
        pieces.append(mixed_rows.astype(jnp.bfloat16).reshape(block_len, group_size * head_width))
    return jnp.concatenate(pieces, 0)


def gathered_shards(tokens, key_weight, value_weight, queries, prefix_pool, block_table, lengths):
    token_count = tokens.shape[0]
    local_heads = queries.shape[1]
    head_width = prefix_pool.shape[4] // 2
    ctx_count = lax.axis_size("ctx")
    head_count = lax.axis_size("head")
    features = lax.all_gather(tokens, ("ctx", "head"), axis=1, tiled=True)
    key_cols, value_cols = (
        lax.all_to_all(
            lax.all_to_all(weight, "ctx", split_axis=3, concat_axis=0, tiled=True),
            "head",
            split_axis=4,
            concat_axis=1,
            tiled=True,
        )
        for weight in (key_weight, value_weight)
    )
    span_len = features.shape[1] // (ctx_count * head_count)
    feature_view = features.reshape(token_count, ctx_count, head_count, span_len)
    pieces = (
        lax.all_gather(key_cols, "batch", axis=2, tiled=True),
        lax.all_gather(value_cols, "batch", axis=2, tiled=True),
    )
    row_count = pieces[0].shape[2]

    def one_term(weight_piece):
        shaped = weight_piece.reshape(ctx_count, head_count, row_count, local_heads * head_width)
        return jnp.einsum("tchr,chrk->tk", feature_view, shaped, preferred_element_type=jnp.float32)

    new_keys = one_term(pieces[0]).astype(jnp.bfloat16).reshape(token_count, local_heads, head_width)
    new_values = one_term(pieces[1]).astype(jnp.bfloat16).reshape(token_count, local_heads, head_width)
    fresh_all = jnp.concatenate([new_keys, new_values], 2)
    pool_heads = lax.all_to_all(prefix_pool, "ctx", split_axis=2, concat_axis=0, tiled=True)
    chosen = jnp.take(pool_heads, block_table[0], axis=0)
    chosen = chosen.reshape(-1, local_heads, 2 * head_width)
    outputs = [
        attend_head(
            queries[:, head_idx, 0], chosen[:, head_idx], fresh_all[:, head_idx], lengths[0]
        )
        for head_idx in range(local_heads)
    ]
    return jnp.stack(outputs, 1)[:, :, None, :]


def shift(array, axis, step):
    count = lax.axis_size(axis)
    return lax.ppermute(array, axis, [(i, (i + step) % count) for i in range(count)])


def trade(array, axis, bits):
    return lax.ppermute(array, axis, [(i, i ^ bits) for i in range(lax.axis_size(axis))])


def after(first, second):
    return lax.optimization_barrier((first, second))


def softmax_parts(scores, old_max=None):
    row_max = jnp.max(scores, axis=0, keepdims=True)
    if old_max is not None:
        row_max = jnp.maximum(row_max, old_max)
    return row_max, jnp.exp2(scores - row_max).astype(jnp.bfloat16)


def dot_queries(keys, query_block):
    return lax.dot_general(
        keys, query_block, (((1,), (1,)), ((), ())), preferred_element_type=jnp.float32
    )


def params(limit=None):
    return pltpu.CompilerParams(vmem_limit_bytes=limit or VMEM_BYTES)


def weight_kernel(ctx_count, heads, head_count, key_ref, value_ref, out_ref, flat):
    depth, slots, width = key_ref.shape
    for kind, ref in enumerate((key_ref, value_ref)):
        flat[...] = ref[...].astype(jnp.float32).reshape(depth * slots, width)
        for ctx in range(ctx_count):
            for head in range(heads):
                for core in range(head_count):
                    slot = (ctx * heads + head) * head_count + core
                    at = (kind * heads + head) * width
                    out_ref[core, ctx, :, at : at + width] = flat[
                        pl.ds(slot, depth, stride=slots), :
                    ].astype(out_ref.dtype)


def arrange_weights(key_weight, value_weight, ctx_count, heads, head_count):
    depth, width = key_weight.shape[2], key_weight.shape[5]
    slots = ctx_count * heads * head_count
    rows = min(128, depth)
    views = [w.reshape(depth, slots, width) for w in (key_weight, value_weight)]
    block = pl.BlockSpec((rows, slots, width), lambda i: (i, 0, 0))
    columns = 2 * heads * width
    return pl.pallas_call(
        functools.partial(weight_kernel, ctx_count, heads, head_count),
        grid=(depth // rows,),
        in_specs=[block, block],
        out_specs=pl.BlockSpec((head_count, ctx_count, rows, columns), lambda i: (0, 0, i, 0)),
        out_shape=jax.ShapeDtypeStruct((head_count, ctx_count, depth, columns), jnp.bfloat16),
        scratch_shapes=[pltpu.VMEM((rows * slots, width), jnp.float32)],
        compiler_params=params(),
        cost_estimate=cost("arrange_weights"),
        name="arrange_weights",
    )(*views)


def cut_kernel(bits, place_ref, tokens_ref, *refs):
    pieces, (held, sems) = refs[:-2], refs[-2:]
    depth = pieces[0].shape[1]
    inward, outward = [], []
    for index, piece in enumerate(pieces):
        start = pl.multiple_of((place_ref[0] ^ bits[index]) * depth, depth)
        source = tokens_ref.at[:, pl.ds(start, depth)]
        inward.append(pltpu.make_async_copy(source, held.at[index], sems.at[0, index]))
        outward.append(pltpu.make_async_copy(held.at[index], piece, sems.at[1, index]))
    for copy in inward:
        copy.start()
    for copy, onward in zip(inward, outward):
        copy.wait()
        onward.start()
    for copy in outward:
        copy.wait()


def cut_tokens(place, tokens, depth, bits):
    far = pl.BlockSpec(memory_space=pltpu.HBM)
    piece = jax.ShapeDtypeStruct((tokens.shape[0], depth), tokens.dtype)
    return pl.pallas_call(
        functools.partial(cut_kernel, bits),
        grid_spec=pltpu.PrefetchScalarGridSpec(
            num_scalar_prefetch=1,
            grid=(1,),
            in_specs=[far],
            out_specs=[far] * len(bits),
            scratch_shapes=[
                pltpu.VMEM((len(bits), *piece.shape), tokens.dtype),
                pltpu.SemaphoreType.DMA((2, len(bits))),
            ],
        ),
        out_shape=[piece] * len(bits),
        compiler_params=params(MOST_VMEM_BYTES),
        cost_estimate=cost("cut_tokens"),
        name="cut_tokens",
    )(place, tokens)


def pool_kernel(ctx_count, heads, place_ref, pool_ref, *refs):
    outs, flat = refs[:-1], refs[-1]
    some, length, slots, width = pool_ref.shape
    length *= some
    flat[...] = pool_ref[...].astype(jnp.float32).reshape(length * slots, width)
    for kind in range(2):
        for head in range(heads):
            at = (kind * heads + head) * width
            held = []
            for ctx in range(ctx_count):
                slot = (kind * ctx_count + ctx) * heads + head
                held.append(flat[pl.ds(slot, length, stride=slots), :])
            for step, out_ref in enumerate(outs):
                target = lax.rem(place_ref[1] + step, ctx_count)
                value = held[0]
                for ctx in range(1, ctx_count):
                    value = jnp.where(target == ctx, held[ctx], value)
                out_ref[:, :, at : at + width] = value.astype(out_ref.dtype).reshape(
                    some, length // some, width
                )


def arrange_pool(place, prefix_pool, ctx_count, heads):
    blocks, length, all_heads, _, double = prefix_pool.shape
    width = double // 2
    slots = 2 * all_heads
    view = prefix_pool.reshape(blocks, length, all_heads, 2, width)
    view = view.transpose(0, 1, 3, 2, 4).reshape(blocks, length, slots, width)
    columns = 2 * heads * width
    some = 2 if blocks % 2 == 0 else 1
    out = pl.BlockSpec((some, length, columns), lambda i, place: (i, 0, 0))
    return pl.pallas_call(
        functools.partial(pool_kernel, ctx_count, heads),
        grid_spec=pltpu.PrefetchScalarGridSpec(
            num_scalar_prefetch=1,
            grid=(blocks // some,),
            in_specs=[pl.BlockSpec((some, length, slots, width), lambda i, place: (i, 0, 0, 0))],
            out_specs=[out] * ctx_count,
            scratch_shapes=[pltpu.VMEM((some * length * slots, width), jnp.float32)],
        ),
        out_shape=[jax.ShapeDtypeStruct((blocks, length, columns), jnp.bfloat16)] * ctx_count,
        compiler_params=params(),
        cost_estimate=cost("arrange_pool"),
        name="arrange_pool",
    )(place, view)


def total_of(refs):
    return sum(ref[...].astype(jnp.float32).reshape(ref.shape[-2:]) for ref in refs)


def project_kernel(block_count, term_counts, place_ref, *refs):
    token_refs, weight_ref = refs[:block_count], refs[block_count]
    terms = refs[block_count + 1 : block_count + 1 + sum(term_counts)]
    out_ref, *sum_refs = refs[block_count + 1 + sum(term_counts) : -1]
    stacked = refs[-1]

    @pl.when(pl.program_id(0) == 0)
    def _():
        at = 0
        for token_ref in token_refs:
            rows = token_ref.shape[0]
            stacked[at : at + rows, :] = token_ref[...]
            at += rows
        at = 0
        for count, sum_ref in zip(term_counts, sum_refs):
            sum_ref[...] = total_of(terms[at : at + count]).astype(sum_ref.dtype)
            at += count

    out_ref[0] = jnp.dot(
        stacked[...], weight_ref[0, 0], preferred_element_type=jnp.float32
    ).astype(out_ref.dtype)


def piece_of(array, *index):
    rows, block, *leading = index
    shape = (1,) * len(leading) + (rows, array.shape[-1])
    return array, pl.BlockSpec(shape, lambda j, *_: (*leading, block, 0))


def project(place, blocks, weights, head_step, out_dtype, name, sums=()):
    head_count, ctx_count, depth, width = weights.shape
    row_total = sum(block.shape[0] for block in blocks)

    def block_spec(block):
        if block.shape[1] == depth:
            return pl.BlockSpec(block.shape, lambda j, place: (0, 0))
        return pl.BlockSpec((block.shape[0], depth), lambda j, place: (0, place[0]))

    pieces = [piece for terms in sums for piece in terms]
    sum_shapes = [terms[0][1].block_shape[-2:] for terms in sums]
    result = pl.pallas_call(
        functools.partial(project_kernel, len(blocks), [len(terms) for terms in sums]),
        grid_spec=pltpu.PrefetchScalarGridSpec(
            num_scalar_prefetch=1,
            grid=(ctx_count,),
            in_specs=[block_spec(block) for block in blocks]
            + [
                pl.BlockSpec(
                    (1, 1, depth, width),
                    lambda j, place: (
                        lax.rem(place[2] + head_step, head_count),
                        lax.rem(place[1] + j, ctx_count),
                        0,
                        0,
                    ),
                )
            ]
            + [spec for _, spec in pieces],
            out_specs=[pl.BlockSpec((1, row_total, width), lambda j, place: (j, 0, 0))]
            + [pl.BlockSpec(shape, lambda j, place: (0, 0)) for shape in sum_shapes],
            scratch_shapes=[pltpu.VMEM((row_total, depth), weights.dtype)],
        ),
        out_shape=[jax.ShapeDtypeStruct((ctx_count, row_total, width), out_dtype)]
        + [jax.ShapeDtypeStruct(shape, jnp.bfloat16) for shape in sum_shapes],
        compiler_params=params(),
        cost_estimate=cost(name),
        name=name,
    )(place, *blocks, weights, *(array for array, _ in pieces))
    return result if sums else result[0]


def pick_kernel(heads, ctx_count, place_ref, table_ref, *refs):
    pool_refs, (keys, values) = refs[:ctx_count], refs[ctx_count:]
    blocks, length, columns = pool_refs[0].shape
    wide = columns // 2
    width = wide // heads
    values[...] = jnp.ones_like(values)
    for at in range(table_ref.shape[0]):
        entry = table_ref[at]
        here = slice(at * length, (at + 1) * length)
        step = lax.rem(place_ref[1] - entry // blocks + ctx_count, ctx_count)
        for ctx_step, pool_ref in enumerate(pool_refs):

            @pl.when(step == ctx_step)
            def _():
                block = pool_ref[entry % blocks]
                keys[here, :] = block[:, :wide]
                put_values(values, here, block[:, wide:], heads)


def put_values(values, here, block, heads):
    width = block.shape[1] // heads
    for head in range(heads):
        low = head * (width + ONES)
        values[low : low + width, here] = (
            block[:, head * width : (head + 1) * width].astype(jnp.float32).T.astype(jnp.bfloat16)
        )


def pick_blocks(place, table, pools, heads):
    length, columns = pools[0].shape[1:]
    count = table.shape[0] * length
    wide = columns // 2
    tall = wide + heads * ONES
    return pl.pallas_call(
        functools.partial(pick_kernel, heads, len(pools)),
        grid_spec=pltpu.PrefetchScalarGridSpec(
            num_scalar_prefetch=2,
            grid=(1,),
            in_specs=[pl.BlockSpec(p.shape, lambda i, *_: (0, 0, 0)) for p in pools],
            out_specs=[
                pl.BlockSpec((count, wide), lambda i, *_: (0, 0)),
                pl.BlockSpec((tall, count), lambda i, *_: (0, 0)),
            ],
        ),
        out_shape=[
            jax.ShapeDtypeStruct((count, wide), jnp.bfloat16),
            jax.ShapeDtypeStruct((tall, count), jnp.bfloat16),
        ],
        compiler_params=params(),
        cost_estimate=cost("pick_blocks"),
        name="pick_blocks",
    )(place, table, *pools)


def each_part(rows, heads):
    part_rows = min(PART, rows)
    each = part_rows // heads
    for low in range(0, rows, part_rows):
        for head in range(heads):
            at = low + head * each
            yield head, pl.ds(low + head, each, stride=heads), slice(at, at + each)


def prefix_kernel(scale, heads, query_ref, keys, values, *refs):
    acc_ref, stat_ref, flat = refs[-3:]
    rows, width = query_ref.shape
    tall = width + ONES
    half = stat_ref.shape[0] // 2
    flat[...] = query_ref[...].astype(jnp.float32)
    for head, taken, here in each_part(rows, heads):
        query_block = flat[taken, :].astype(jnp.bfloat16)
        scores = dot_queries(keys[:, head * width : (head + 1) * width], query_block) * scale
        row_max, weights = softmax_parts(scores)
        mixed = jnp.dot(
            values[head * tall : (head + 1) * tall, :], weights, preferred_element_type=jnp.float32
        )
        acc_ref[:, here] = mixed[:width]
        stat_ref[:half, here] = jnp.broadcast_to(row_max, (half, row_max.shape[1]))
        stat_ref[half:, here] = jnp.broadcast_to(mixed[width : width + 1], (half, row_max.shape[1]))


def prefix_attend(query_rows, keys, values, chunk, scale, heads, part=(0, 1), state=None):
    all_rows, width = query_rows.shape
    row_total = all_rows // CHUNKS
    at, count = part
    rows = min(1024, row_total // count)
    steps = row_total // rows // count
    first = chunk * count * steps + at * steps
    out_specs = [
        pl.BlockSpec((width, rows), lambda i: (0, at * steps + i)),
        pl.BlockSpec((8, rows), lambda i: (0, at * steps + i)),
    ]
    in_specs = [
        pl.BlockSpec((rows, width), lambda i: (first + i, 0)),
        pl.BlockSpec(keys.shape, lambda i: (0, 0)),
        pl.BlockSpec(values.shape, lambda i: (0, 0)),
    ]
    operands = [query_rows, keys, values]
    aliases = {}
    if state is not None:
        in_specs += [pl.BlockSpec(memory_space=pl.ANY)] * 2
        operands += state
        aliases = {3: 0, 4: 1}
    return pl.pallas_call(
        functools.partial(prefix_kernel, scale, heads),
        grid=(steps,),
        in_specs=in_specs,
        out_specs=out_specs,
        out_shape=[
            jax.ShapeDtypeStruct((width, row_total), jnp.float32),
            jax.ShapeDtypeStruct((8, row_total), jnp.float32),
        ],
        input_output_aliases=aliases,
        scratch_shapes=[pltpu.VMEM((rows, width), jnp.float32)],
        compiler_params=params(),
        cost_estimate=cost("prefix_attend"),
        name="prefix_attend",
    )(*operands)


def fresh_kernel(
    scale, heads, per_token, first_row, counts, length_ref, query_ref, acc_ref, stat_ref, *rest
):
    early_count, term_count = counts
    earlier, terms = rest[:early_count], rest[early_count : early_count + term_count]
    out_ref, fresh_ref, keys, values, flat, mixed_rows = rest[-6:]
    rows, width = query_ref.shape
    wide, tall = heads * width, width + ONES
    step = pl.program_id(0)

    @pl.when(step == 0)
    def _():
        values[...] = jnp.ones_like(values)
        fresh_ref[...] = total_of(terms).astype(fresh_ref.dtype)
        for index, ref in enumerate([*earlier, fresh_ref]):
            here = slice(index * ref.shape[0], (index + 1) * ref.shape[0])
            fresh = ref[...]
            keys[here, :] = fresh[:, :wide]
            put_values(values, here, fresh[:, wide:], heads)

    half = stat_ref.shape[0] // 2
    flat[...] = query_ref[...].astype(jnp.float32)
    for head, taken, here in each_part(rows, heads):
        query_block = flat[taken, :].astype(jnp.bfloat16)
        scores = dot_queries(keys[:, head * width : (head + 1) * width], query_block) * scale
        row = taken.start + heads * lax.broadcasted_iota(jnp.int32, (1, taken.size), 1)
        token = first_row + step * (rows // per_token) + (
            row // per_token if per_token & (per_token - 1) else row >> (per_token.bit_length() - 1)
        )
        key_at = lax.broadcasted_iota(jnp.int32, scores.shape, 0)
        scores = jnp.where(key_at <= token, scores, -jnp.inf)
        old_max, old_total = stat_ref[:1, here], stat_ref[half : half + 1, here]
        row_max, weights = softmax_parts(scores, old_max)
        fade = jnp.exp2(old_max - row_max)
        mixed = jnp.dot(
            values[head * tall : (head + 1) * tall, :], weights, preferred_element_type=jnp.float32
        )
        row_total = old_total * fade + mixed[width : width + 1]
        share = jnp.where(token < length_ref[0], 1.0 / row_total, 0.0)
        result = acc_ref[:, here] * (fade * share) + mixed[:width] * share
        mixed_rows[taken, :] = result.T
    out_ref[...] = mixed_rows[...].astype(out_ref.dtype)


def fresh_attend(
    length, query_rows, acc, stat, earlier, pieces, result, chunk, scale, heads, per_token
):
    row_total, width = query_rows.shape
    chunk_rows = row_total // CHUNKS
    rows = min(1024, chunk_rows)
    steps = chunk_rows // rows
    block = pl.BlockSpec((rows, width), lambda i, length: (chunk * steps + i, 0))
    fresh_shape = pieces[0][1].block_shape[-2:]
    key_count = (len(earlier) + 1) * fresh_shape[0]
    whole = pl.BlockSpec(fresh_shape, lambda i, length: (0, 0))
    in_specs = [
        block,
        pl.BlockSpec((width, rows), lambda i, length: (0, i)),
        pl.BlockSpec((stat.shape[0], rows), lambda i, length: (0, i)),
        *(whole for _ in earlier),
        *(spec for _, spec in pieces),
    ]
    operands = [length, query_rows, acc, stat, *earlier, *(array for array, _ in pieces)]
    aliases = {}
    if result is not None:
        in_specs.append(pl.BlockSpec(memory_space=pl.ANY))
        aliases = {len(operands): 0}
        operands.append(result)
    return pl.pallas_call(
        functools.partial(
            fresh_kernel,
            scale,
            heads,
            per_token,
            chunk * (chunk_rows // per_token),
            (len(earlier), len(pieces)),
        ),
        grid_spec=pltpu.PrefetchScalarGridSpec(
            num_scalar_prefetch=1,
            grid=(steps,),
            in_specs=in_specs,
            out_specs=[block, whole],
            scratch_shapes=[
                pltpu.VMEM((key_count, heads * width), jnp.bfloat16),
                pltpu.VMEM((heads * (width + ONES), key_count), jnp.bfloat16),
                pltpu.VMEM((rows, width), jnp.float32),
                pltpu.VMEM((rows, width), jnp.float32),
            ],
        ),
        out_shape=[
            jax.ShapeDtypeStruct((row_total, width), jnp.bfloat16),
            jax.ShapeDtypeStruct(fresh_shape, jnp.bfloat16),
        ],
        input_output_aliases=aliases,
        compiler_params=params(),
        cost_estimate=cost("fresh_attend"),
        name="fresh_attend",
    )(*operands)


def reduced_shards(tokens, key_weight, value_weight, queries, prefix_pool, block_table, lengths):
    batch_count = lax.axis_size("batch")
    ctx_count = lax.axis_size("ctx")
    head_count = lax.axis_size("head")
    batch_at, ctx_at, head_at = (lax.axis_index(a) for a in ("batch", "ctx", "head"))
    place = jnp.stack([batch_at, ctx_at, head_at]).astype(jnp.int32)
    token_count = tokens.shape[0]
    heads = queries.shape[1]
    width = prefix_pool.shape[4] // 2
    group = queries.shape[3] // width
    per_token = heads * group
    depth = key_weight.shape[2]
    rows = token_count // CHUNKS
    scale = math.log2(math.e) / math.sqrt(width)

    top = batch_count // 2
    steps = list(range(batch_count - 1, top, -1)) + list(range(1, top))
    pieces = cut_tokens(place, tokens, depth, [*steps, top])
    pieces, prefix_pool = after(pieces, prefix_pool)
    arrived = [trade(piece, "batch", bits) for piece, bits in zip(pieces, steps)]
    pools = arrange_pool(place, prefix_pool, ctx_count, heads)
    pools, (key_weight, value_weight) = after(pools, (key_weight, value_weight))
    pools = [shift(part, "ctx", step) if step else part for step, part in enumerate(pools)]

    weights = arrange_weights(key_weight, value_weight, ctx_count, heads, head_count)

    query_rows = queries.reshape(token_count, heads, group, width)
    query_rows = query_rows.transpose(0, 2, 1, 3).reshape(-1, width)
    def projected(blocks, name, sums=()):
        terms = [
            shift(
                project(place, blocks, weights, step, jnp.bfloat16, name + "_away"), "head", step
            )
            for step in range(1, head_count)
        ]
        kept = project(place, blocks, weights, 0, jnp.float32, name + "_kept", sums)
        kept, *made = kept if sums else [kept]
        return [kept, *terms], made

    def added(terms, step, here):
        return sum(term[step, here].astype(jnp.float32) for term in terms)

    def others(terms, here):
        return [added(terms, step, here).astype(jnp.bfloat16) for step in range(1, ctx_count)]

    def spread(parts):
        return [shift(part, "ctx", step + 1) for step, part in enumerate(parts)]

    every = slice(None)
    parts_of = [slice(i * rows, (i + 1) * rows) for i in range(CHUNKS)]

    weights, last = after(weights, pieces[-1])
    last = trade(last, "batch", top)
    own, _ = projected([tokens], "own")

    sums = [[], []]
    own_others = []
    if steps:
        sums = [[piece_of(t, token_count, 0, step) for t in own] for step in range(1, ctx_count)]
        early, own_others = projected(arrived, "early", sums)
        own_others = spread(own_others)
        cuts = [slice(i * token_count, (i + 1) * token_count) for i in range(len(steps))]
        leaving = [others(early, cut) for cut in cuts]
        leaving, pools = after(leaving, pools)
        sums = [
            [
                [piece_of(t, token_count, i, 0) for t in early]
                + [piece_of(p, token_count, 0) for p in spread(parts)]
            ]
            for i, parts in enumerate(leaving)
        ]
    keys, values = pick_blocks(place, block_table[0], pools, heads)
    states = [prefix_attend(query_rows, keys, values, 0, scale, heads)]
    states[0], last = after(states[0], last)

    def late_project(step, dtype, name, sums):
        result = project(place, [last], weights, step, dtype, name, sums)
        return result if sums else (result,)

    terms = []
    for step in range(1, head_count):
        term, *far = late_project(step, jnp.bfloat16, "late_away", sums[0] + sums[1] if step == 1 else [])
        terms.append(shift(term, "head", step))
    kept, *_ = late_project(0, jnp.float32, "late_kept", [])
    far, near = far[:1], far[1:]
    late = [kept, *terms]
    far = [trade(part, "batch", 1) for part in far]
    late_others = [others(late, here) for here in parts_of]
    late_others[0] = spread(late_others[0])
    late_others[1], (keys, values) = after(late_others[1], (keys, values))
    state = prefix_attend(query_rows, keys, values, 1, scale, heads, (0, 2))

    away = []
    for chunk, here in enumerate(parts_of):
        part = added(late, 0, here) + sum(p.astype(jnp.float32) for p in late_others[chunk])
        part = part + sum(p[here].astype(jnp.float32) for p in far)
        part = part.astype(jnp.bfloat16)
        if chunk == 0:
            state, part = after(state, part)
            part, (state, late_others[1], near) = after(part, (state, late_others[1], near))
            late_others[1] = spread(late_others[1])
            near = [trade(piece, "batch", 1) for piece in near]
            (far, late), late_others[1] = after((far, late), late_others[1])
            states.append(
                prefix_attend(query_rows, keys, values, 1, scale, heads, (1, 2), state)
            )
        else:
            away[-1], part = after(away[-1], part)
        away.append(trade(part, "batch", top))

    result = None
    fresh = []
    for chunk in range(CHUNKS):
        pieces = [piece_of(t, rows, chunk, 0) for t in own]
        pieces += [piece_of(part, rows, chunk) for part in (*own_others, *near)]
        pieces.append(piece_of(away[chunk], rows, 0))
        result, new = fresh_attend(
            lengths,
            query_rows,
            *states[chunk],
            fresh,
            pieces,
            result,
            chunk,
            scale,
            heads,
            per_token,
        )
        fresh.append(new)
    result = result.reshape(token_count, group, heads, width).transpose(0, 2, 1, 3)
    return result.reshape(token_count, heads, 1, group * width)


def solution(mesh):
    def shards(tokens, key_weight, value_weight, *rest):
        prompts = mesh.shape["batch"]
        columns = 2 * math.prod(key_weight.shape[3:])
        few_tokens = prompts * tokens.shape[0] <= columns and prompts == 4
        form = reduced_shards if few_tokens else gathered_shards
        return form(tokens, key_weight, value_weight, *rest)

    return jax.shard_map(
        shards,
        mesh=mesh,
        in_specs=(
            P(("groups", "batch"), ("ctx", "head")),
            P("ctx", "head", "batch", None, None, None),
            P("ctx", "head", "batch", None, None, None),
            P(("groups", "batch"), "ctx", "head", None),
            P(("groups", "ctx"), None, None, "head", None),
            P(("groups", "batch"), None),
            P(("groups", "batch")),
        ),
        out_specs=P(("groups", "batch"), "ctx", "head", None),
        check_vma=False,
    )
```

```python
import functools
import math

import jax
import jax.numpy as jnp
from jax import lax
from jax.experimental import pallas as pl
from jax.experimental.pallas import tpu as pltpu
from jax.sharding import PartitionSpec as P

CHUNKS = 2
PART = 1024
ONES = 16
VMEM_BYTES = 16 * 1024 * 1024
MOST_VMEM_BYTES = 60 * 1024 * 1024
LONG = pl.CostEstimate(flops=10**11, bytes_accessed=1, transcendentals=0)
COSTS = {}


def cost(name):
    return COSTS.get(name, LONG)


def attend_head(query_rows, prefix, fresh_rows, length):
    token_count = query_rows.shape[0]
    head_width = prefix.shape[1] // 2
    group_size = query_rows.shape[1] // head_width
    prefix_len = prefix.shape[0]
    key_rows = jnp.concatenate([prefix[:, :head_width], fresh_rows[:, :head_width]], 0)
    value_rows = jnp.concatenate([prefix[:, head_width:], fresh_rows[:, head_width:]], 0)
    block_len = min(token_count, 64)
    pieces = []
    for first_row in range(0, token_count, block_len):
        block_rows = query_rows[first_row : first_row + block_len].reshape(
            block_len * group_size, head_width
        )
        scores = jnp.dot(
            block_rows, key_rows.T, preferred_element_type=jnp.float32
        ) * head_width ** (-0.5)
        position = first_row + jnp.arange(block_len * group_size) // group_size
        column = jnp.arange(prefix_len + token_count) - prefix_len
        allowed = column[None, :] <= position[:, None]
        scores = jnp.where(allowed, scores, -jnp.inf)
        row_max = jnp.max(scores, axis=1, keepdims=True)
        weights = jnp.exp(scores - row_max)
        row_total = jnp.sum(weights, axis=1, keepdims=True)
        probs_bf = (weights / row_total).astype(jnp.bfloat16)
        mixed_rows = jnp.dot(probs_bf, value_rows, preferred_element_type=jnp.float32)
        is_live = position < length
        mixed_rows = jnp.where(is_live[:, None], mixed_rows, 0.0)
        pieces.append(mixed_rows.astype(jnp.bfloat16).reshape(block_len, group_size * head_width))
    return jnp.concatenate(pieces, 0)


def gathered_shards(tokens, key_weight, value_weight, queries, prefix_pool, block_table, lengths):
    token_count = tokens.shape[0]
    local_heads = queries.shape[1]
    head_width = prefix_pool.shape[4] // 2
    ctx_count = lax.axis_size("ctx")
    head_count = lax.axis_size("head")
    features = lax.all_gather(tokens, ("ctx", "head"), axis=1, tiled=True)
    key_cols, value_cols = (
        lax.all_to_all(
            lax.all_to_all(weight, "ctx", split_axis=3, concat_axis=0, tiled=True),
            "head",
            split_axis=4,
            concat_axis=1,
            tiled=True,
        )
        for weight in (key_weight, value_weight)
    )
    span_len = features.shape[1] // (ctx_count * head_count)
    feature_view = features.reshape(token_count, ctx_count, head_count, span_len)
    pieces = (
        lax.all_gather(key_cols, "batch", axis=2, tiled=True),
        lax.all_gather(value_cols, "batch", axis=2, tiled=True),
    )
    row_count = pieces[0].shape[2]

    def one_term(weight_piece):
        shaped = weight_piece.reshape(ctx_count, head_count, row_count, local_heads * head_width)
        return jnp.einsum("tchr,chrk->tk", feature_view, shaped, preferred_element_type=jnp.float32)

    new_keys = one_term(pieces[0]).astype(jnp.bfloat16).reshape(token_count, local_heads, head_width)
    new_values = one_term(pieces[1]).astype(jnp.bfloat16).reshape(token_count, local_heads, head_width)
    fresh_all = jnp.concatenate([new_keys, new_values], 2)
    pool_heads = lax.all_to_all(prefix_pool, "ctx", split_axis=2, concat_axis=0, tiled=True)
    chosen = jnp.take(pool_heads, block_table[0], axis=0)
    chosen = chosen.reshape(-1, local_heads, 2 * head_width)
    outputs = [
        attend_head(
            queries[:, head_idx, 0], chosen[:, head_idx], fresh_all[:, head_idx], lengths[0]
        )
        for head_idx in range(local_heads)
    ]
    return jnp.stack(outputs, 1)[:, :, None, :]


def shift(array, axis, step):
    count = lax.axis_size(axis)
    return lax.ppermute(array, axis, [(i, (i + step) % count) for i in range(count)])


def trade(array, axis, bits):
    return lax.ppermute(array, axis, [(i, i ^ bits) for i in range(lax.axis_size(axis))])


def after(first, second):
    return lax.optimization_barrier((first, second))


def softmax_parts(scores, old_max=None):
    row_max = jnp.max(scores, axis=0, keepdims=True)
    if old_max is not None:
        row_max = jnp.maximum(row_max, old_max)
    return row_max, jnp.exp2(scores - row_max).astype(jnp.bfloat16)


def dot_queries(keys, query_block):
    return lax.dot_general(
        keys, query_block, (((1,), (1,)), ((), ())), preferred_element_type=jnp.float32
    )


def params(limit=None):
    return pltpu.CompilerParams(vmem_limit_bytes=limit or VMEM_BYTES)


def weight_kernel(ctx_count, heads, head_count, key_ref, value_ref, out_ref, flat):
    depth, slots, width = key_ref.shape
    for kind, ref in enumerate((key_ref, value_ref)):
        flat[...] = ref[...].astype(jnp.float32).reshape(depth * slots, width)
        for ctx in range(ctx_count):
            for head in range(heads):
                for core in range(head_count):
                    slot = (ctx * heads + head) * head_count + core
                    at = (kind * heads + head) * width
                    out_ref[core, ctx, :, at : at + width] = flat[
                        pl.ds(slot, depth, stride=slots), :
                    ].astype(out_ref.dtype)


def arrange_weights(key_weight, value_weight, ctx_count, heads, head_count):
    depth, width = key_weight.shape[2], key_weight.shape[5]
    slots = ctx_count * heads * head_count
    rows = min(128, depth)
    views = [w.reshape(depth, slots, width) for w in (key_weight, value_weight)]
    block = pl.BlockSpec((rows, slots, width), lambda i: (i, 0, 0))
    columns = 2 * heads * width
    return pl.pallas_call(
        functools.partial(weight_kernel, ctx_count, heads, head_count),
        grid=(depth // rows,),
        in_specs=[block, block],
        out_specs=pl.BlockSpec((head_count, ctx_count, rows, columns), lambda i: (0, 0, i, 0)),
        out_shape=jax.ShapeDtypeStruct((head_count, ctx_count, depth, columns), jnp.bfloat16),
        scratch_shapes=[pltpu.VMEM((rows * slots, width), jnp.float32)],
        compiler_params=params(),
        cost_estimate=cost("arrange_weights"),
        name="arrange_weights",
    )(*views)


def cut_kernel(bits, place_ref, tokens_ref, *refs):
    pieces, (held, sems) = refs[:-2], refs[-2:]
    depth = pieces[0].shape[1]
    inward, outward = [], []
    for index, piece in enumerate(pieces):
        start = pl.multiple_of((place_ref[0] ^ bits[index]) * depth, depth)
        source = tokens_ref.at[:, pl.ds(start, depth)]
        inward.append(pltpu.make_async_copy(source, held.at[index], sems.at[0, index]))
        outward.append(pltpu.make_async_copy(held.at[index], piece, sems.at[1, index]))
    for copy in inward:
        copy.start()
    for copy, onward in zip(inward, outward):
        copy.wait()
        onward.start()
    for copy in outward:
        copy.wait()


def cut_tokens(place, tokens, depth, bits):
    far = pl.BlockSpec(memory_space=pltpu.HBM)
    piece = jax.ShapeDtypeStruct((tokens.shape[0], depth), tokens.dtype)
    return pl.pallas_call(
        functools.partial(cut_kernel, bits),
        grid_spec=pltpu.PrefetchScalarGridSpec(
            num_scalar_prefetch=1,
            grid=(1,),
            in_specs=[far],
            out_specs=[far] * len(bits),
            scratch_shapes=[
                pltpu.VMEM((len(bits), *piece.shape), tokens.dtype),
                pltpu.SemaphoreType.DMA((2, len(bits))),
            ],
        ),
        out_shape=[piece] * len(bits),
        compiler_params=params(MOST_VMEM_BYTES),
        cost_estimate=cost("cut_tokens"),
        name="cut_tokens",
    )(place, tokens)


def pool_kernel(ctx_count, heads, place_ref, pool_ref, *refs):
    outs, flat = refs[:-1], refs[-1]
    some, length, slots, width = pool_ref.shape
    length *= some
    flat[...] = pool_ref[...].astype(jnp.float32).reshape(length * slots, width)
    for kind in range(2):
        for head in range(heads):
            at = (kind * heads + head) * width
            held = []
            for ctx in range(ctx_count):
                slot = (kind * ctx_count + ctx) * heads + head
                held.append(flat[pl.ds(slot, length, stride=slots), :])
            for step, out_ref in enumerate(outs):
                target = lax.rem(place_ref[1] + step, ctx_count)
                value = held[0]
                for ctx in range(1, ctx_count):
                    value = jnp.where(target == ctx, held[ctx], value)
                out_ref[:, :, at : at + width] = value.astype(out_ref.dtype).reshape(
                    some, length // some, width
                )


def arrange_pool(place, prefix_pool, ctx_count, heads):
    blocks, length, all_heads, _, double = prefix_pool.shape
    width = double // 2
    slots = 2 * all_heads
    view = prefix_pool.reshape(blocks, length, all_heads, 2, width)
    view = view.transpose(0, 1, 3, 2, 4).reshape(blocks, length, slots, width)
    columns = 2 * heads * width
    some = 2 if blocks % 2 == 0 else 1
    out = pl.BlockSpec((some, length, columns), lambda i, place: (i, 0, 0))
    return pl.pallas_call(
        functools.partial(pool_kernel, ctx_count, heads),
        grid_spec=pltpu.PrefetchScalarGridSpec(
            num_scalar_prefetch=1,
            grid=(blocks // some,),
            in_specs=[pl.BlockSpec((some, length, slots, width), lambda i, place: (i, 0, 0, 0))],
            out_specs=[out] * ctx_count,
            scratch_shapes=[pltpu.VMEM((some * length * slots, width), jnp.float32)],
        ),
        out_shape=[jax.ShapeDtypeStruct((blocks, length, columns), jnp.bfloat16)] * ctx_count,
        compiler_params=params(),
        cost_estimate=cost("arrange_pool"),
        name="arrange_pool",
    )(place, view)


def total_of(refs):
    return sum(ref[...].astype(jnp.float32).reshape(ref.shape[-2:]) for ref in refs)


def project_kernel(block_count, term_counts, place_ref, *refs):
    token_refs, weight_ref = refs[:block_count], refs[block_count]
    terms = refs[block_count + 1 : block_count + 1 + sum(term_counts)]
    out_ref, *sum_refs = refs[block_count + 1 + sum(term_counts) : -1]
    stacked = refs[-1]

    @pl.when(pl.program_id(0) == 0)
    def _():
        at = 0
        for token_ref in token_refs:
            rows = token_ref.shape[0]
            stacked[at : at + rows, :] = token_ref[...]
            at += rows
        at = 0
        for count, sum_ref in zip(term_counts, sum_refs):
            sum_ref[...] = total_of(terms[at : at + count]).astype(sum_ref.dtype)
            at += count

    out_ref[0] = jnp.dot(
        stacked[...], weight_ref[0, 0], preferred_element_type=jnp.float32
    ).astype(out_ref.dtype)


def piece_of(array, *index):
    rows, block, *leading = index
    shape = (1,) * len(leading) + (rows, array.shape[-1])
    return array, pl.BlockSpec(shape, lambda j, *_: (*leading, block, 0))


def project(place, blocks, weights, head_step, out_dtype, name, sums=()):
    head_count, ctx_count, depth, width = weights.shape
    row_total = sum(block.shape[0] for block in blocks)

    def block_spec(block):
        if block.shape[1] == depth:
            return pl.BlockSpec(block.shape, lambda j, place: (0, 0))
        return pl.BlockSpec((block.shape[0], depth), lambda j, place: (0, place[0]))

    pieces = [piece for terms in sums for piece in terms]
    sum_shapes = [terms[0][1].block_shape[-2:] for terms in sums]
    result = pl.pallas_call(
        functools.partial(project_kernel, len(blocks), [len(terms) for terms in sums]),
        grid_spec=pltpu.PrefetchScalarGridSpec(
            num_scalar_prefetch=1,
            grid=(ctx_count,),
            in_specs=[block_spec(block) for block in blocks]
            + [
                pl.BlockSpec(
                    (1, 1, depth, width),
                    lambda j, place: (
                        lax.rem(place[2] + head_step, head_count),
                        lax.rem(place[1] + j, ctx_count),
                        0,
                        0,
                    ),
                )
            ]
            + [spec for _, spec in pieces],
            out_specs=[pl.BlockSpec((1, row_total, width), lambda j, place: (j, 0, 0))]
            + [pl.BlockSpec(shape, lambda j, place: (0, 0)) for shape in sum_shapes],
            scratch_shapes=[pltpu.VMEM((row_total, depth), weights.dtype)],
        ),
        out_shape=[jax.ShapeDtypeStruct((ctx_count, row_total, width), out_dtype)]
        + [jax.ShapeDtypeStruct(shape, jnp.bfloat16) for shape in sum_shapes],
        compiler_params=params(),
        cost_estimate=cost(name),
        name=name,
    )(place, *blocks, weights, *(array for array, _ in pieces))
    return result if sums else result[0]


def pick_kernel(heads, ctx_count, place_ref, table_ref, *refs):
    pool_refs, (keys, values) = refs[:ctx_count], refs[ctx_count:]
    blocks, length, columns = pool_refs[0].shape
    wide = columns // 2
    width = wide // heads
    values[...] = jnp.ones_like(values)
    for at in range(table_ref.shape[0]):
        entry = table_ref[at]
        here = slice(at * length, (at + 1) * length)
        step = lax.rem(place_ref[1] - entry // blocks + ctx_count, ctx_count)
        for ctx_step, pool_ref in enumerate(pool_refs):

            @pl.when(step == ctx_step)
            def _():
                block = pool_ref[entry % blocks]
                keys[here, :] = block[:, :wide]
                put_values(values, here, block[:, wide:], heads)


def put_values(values, here, block, heads):
    width = block.shape[1] // heads
    for head in range(heads):
        low = head * (width + ONES)
        values[low : low + width, here] = (
            block[:, head * width : (head + 1) * width].astype(jnp.float32).T.astype(jnp.bfloat16)
        )


def pick_blocks(place, table, pools, heads):
    length, columns = pools[0].shape[1:]
    count = table.shape[0] * length
    wide = columns // 2
    tall = wide + heads * ONES
    return pl.pallas_call(
        functools.partial(pick_kernel, heads, len(pools)),
        grid_spec=pltpu.PrefetchScalarGridSpec(
            num_scalar_prefetch=2,
            grid=(1,),
            in_specs=[pl.BlockSpec(p.shape, lambda i, *_: (0, 0, 0)) for p in pools],
            out_specs=[
                pl.BlockSpec((count, wide), lambda i, *_: (0, 0)),
                pl.BlockSpec((tall, count), lambda i, *_: (0, 0)),
            ],
        ),
        out_shape=[
            jax.ShapeDtypeStruct((count, wide), jnp.bfloat16),
            jax.ShapeDtypeStruct((tall, count), jnp.bfloat16),
        ],
        compiler_params=params(),
        cost_estimate=cost("pick_blocks"),
        name="pick_blocks",
    )(place, table, *pools)


def each_part(rows, heads):
    part_rows = min(PART, rows)
    each = part_rows // heads
    for low in range(0, rows, part_rows):
        for head in range(heads):
            at = low + head * each
            yield head, pl.ds(low + head, each, stride=heads), slice(at, at + each)


def prefix_kernel(scale, heads, query_ref, keys, values, *refs):
    acc_ref, stat_ref, flat = refs[-3:]
    rows, width = query_ref.shape
    tall = width + ONES
    half = stat_ref.shape[0] // 2
    flat[...] = query_ref[...].astype(jnp.float32)
    for head, taken, here in each_part(rows, heads):
        query_block = flat[taken, :].astype(jnp.bfloat16)
        scores = dot_queries(keys[:, head * width : (head + 1) * width], query_block) * scale
        row_max, weights = softmax_parts(scores)
        mixed = jnp.dot(
            values[head * tall : (head + 1) * tall, :], weights, preferred_element_type=jnp.float32
        )
        acc_ref[:, here] = mixed[:width]
        stat_ref[:half, here] = jnp.broadcast_to(row_max, (half, row_max.shape[1]))
        stat_ref[half:, here] = jnp.broadcast_to(mixed[width : width + 1], (half, row_max.shape[1]))


def prefix_attend(query_rows, keys, values, chunk, scale, heads, part=(0, 1), state=None):
    all_rows, width = query_rows.shape
    row_total = all_rows // CHUNKS
    at, count = part
    rows = min(1024, row_total // count)
    steps = row_total // rows // count
    first = chunk * count * steps + at * steps
    out_specs = [
        pl.BlockSpec((width, rows), lambda i: (0, at * steps + i)),
        pl.BlockSpec((8, rows), lambda i: (0, at * steps + i)),
    ]
    in_specs = [
        pl.BlockSpec((rows, width), lambda i: (first + i, 0)),
        pl.BlockSpec(keys.shape, lambda i: (0, 0)),
        pl.BlockSpec(values.shape, lambda i: (0, 0)),
    ]
    operands = [query_rows, keys, values]
    aliases = {}
    if state is not None:
        in_specs += [pl.BlockSpec(memory_space=pl.ANY)] * 2
        operands += state
        aliases = {3: 0, 4: 1}
    return pl.pallas_call(
        functools.partial(prefix_kernel, scale, heads),
        grid=(steps,),
        in_specs=in_specs,
        out_specs=out_specs,
        out_shape=[
            jax.ShapeDtypeStruct((width, row_total), jnp.float32),
            jax.ShapeDtypeStruct((8, row_total), jnp.float32),
        ],
        input_output_aliases=aliases,
        scratch_shapes=[pltpu.VMEM((rows, width), jnp.float32)],
        compiler_params=params(),
        cost_estimate=cost("prefix_attend"),
        name="prefix_attend",
    )(*operands)


def fresh_kernel(
    scale, heads, per_token, first_row, counts, length_ref, query_ref, acc_ref, stat_ref, *rest
):
    early_count, term_count = counts
    earlier, terms = rest[:early_count], rest[early_count : early_count + term_count]
    out_ref, fresh_ref, keys, values, flat, mixed_rows = rest[-6:]
    rows, width = query_ref.shape
    wide, tall = heads * width, width + ONES
    step = pl.program_id(0)

    @pl.when(step == 0)
    def _():
        values[...] = jnp.ones_like(values)
        fresh_ref[...] = total_of(terms).astype(fresh_ref.dtype)
        for index, ref in enumerate([*earlier, fresh_ref]):
            here = slice(index * ref.shape[0], (index + 1) * ref.shape[0])
            fresh = ref[...]
            keys[here, :] = fresh[:, :wide]
            put_values(values, here, fresh[:, wide:], heads)

    half = stat_ref.shape[0] // 2
    flat[...] = query_ref[...].astype(jnp.float32)
    for head, taken, here in each_part(rows, heads):
        query_block = flat[taken, :].astype(jnp.bfloat16)
        scores = dot_queries(keys[:, head * width : (head + 1) * width], query_block) * scale
        row = taken.start + heads * lax.broadcasted_iota(jnp.int32, (1, taken.size), 1)
        token = first_row + step * (rows // per_token) + (
            row // per_token if per_token & (per_token - 1) else row >> (per_token.bit_length() - 1)
        )
        key_at = lax.broadcasted_iota(jnp.int32, scores.shape, 0)
        scores = jnp.where(key_at <= token, scores, -jnp.inf)
        old_max, old_total = stat_ref[:1, here], stat_ref[half : half + 1, here]
        row_max, weights = softmax_parts(scores, old_max)
        fade = jnp.exp2(old_max - row_max)
        mixed = jnp.dot(
            values[head * tall : (head + 1) * tall, :], weights, preferred_element_type=jnp.float32
        )
        row_total = old_total * fade + mixed[width : width + 1]
        share = jnp.where(token < length_ref[0], 1.0 / row_total, 0.0)
        result = acc_ref[:, here] * (fade * share) + mixed[:width] * share
        mixed_rows[taken, :] = result.T
    out_ref[...] = mixed_rows[...].astype(out_ref.dtype)


def fresh_attend(
    length, query_rows, acc, stat, earlier, pieces, result, chunk, scale, heads, per_token
):
    row_total, width = query_rows.shape
    chunk_rows = row_total // CHUNKS
    rows = min(1024, chunk_rows)
    steps = chunk_rows // rows
    block = pl.BlockSpec((rows, width), lambda i, length: (chunk * steps + i, 0))
    fresh_shape = pieces[0][1].block_shape[-2:]
    key_count = (len(earlier) + 1) * fresh_shape[0]
    whole = pl.BlockSpec(fresh_shape, lambda i, length: (0, 0))
    in_specs = [
        block,
        pl.BlockSpec((width, rows), lambda i, length: (0, i)),
        pl.BlockSpec((stat.shape[0], rows), lambda i, length: (0, i)),
        *(whole for _ in earlier),
        *(spec for _, spec in pieces),
    ]
    operands = [length, query_rows, acc, stat, *earlier, *(array for array, _ in pieces)]
    aliases = {}
    if result is not None:
        in_specs.append(pl.BlockSpec(memory_space=pl.ANY))
        aliases = {len(operands): 0}
        operands.append(result)
    return pl.pallas_call(
        functools.partial(
            fresh_kernel,
            scale,
            heads,
            per_token,
            chunk * (chunk_rows // per_token),
            (len(earlier), len(pieces)),
        ),
        grid_spec=pltpu.PrefetchScalarGridSpec(
            num_scalar_prefetch=1,
            grid=(steps,),
            in_specs=in_specs,
            out_specs=[block, whole],
            scratch_shapes=[
                pltpu.VMEM((key_count, heads * width), jnp.bfloat16),
                pltpu.VMEM((heads * (width + ONES), key_count), jnp.bfloat16),
                pltpu.VMEM((rows, width), jnp.float32),
                pltpu.VMEM((rows, width), jnp.float32),
            ],
        ),
        out_shape=[
            jax.ShapeDtypeStruct((row_total, width), jnp.bfloat16),
            jax.ShapeDtypeStruct(fresh_shape, jnp.bfloat16),
        ],
        input_output_aliases=aliases,
        compiler_params=params(),
        cost_estimate=cost("fresh_attend"),
        name="fresh_attend",
    )(*operands)


def reduced_shards(tokens, key_weight, value_weight, queries, prefix_pool, block_table, lengths):
    batch_count = lax.axis_size("batch")
    ctx_count = lax.axis_size("ctx")
    head_count = lax.axis_size("head")
    batch_at, ctx_at, head_at = (lax.axis_index(a) for a in ("batch", "ctx", "head"))
    place = jnp.stack([batch_at, ctx_at, head_at]).astype(jnp.int32)
    token_count = tokens.shape[0]
    heads = queries.shape[1]
    width = prefix_pool.shape[4] // 2
    group = queries.shape[3] // width
    per_token = heads * group
    depth = key_weight.shape[2]
    rows = token_count // CHUNKS
    scale = math.log2(math.e) / math.sqrt(width)

    top = batch_count // 2
    steps = list(range(batch_count - 1, top, -1)) + list(range(1, top))
    pieces = cut_tokens(place, tokens, depth, [*steps, top])
    pieces, prefix_pool = after(pieces, prefix_pool)
    arrived = [trade(piece, "batch", bits) for piece, bits in zip(pieces, steps)]
    pools = arrange_pool(place, prefix_pool, ctx_count, heads)
    pools, (key_weight, value_weight) = after(pools, (key_weight, value_weight))
    pools = [shift(part, "ctx", step) if step else part for step, part in enumerate(pools)]

    weights = arrange_weights(key_weight, value_weight, ctx_count, heads, head_count)

    query_rows = queries.reshape(token_count, heads, group, width)
    query_rows = query_rows.transpose(0, 2, 1, 3).reshape(-1, width)
    def projected(blocks, name):
        terms = [
            shift(project(place, blocks, weights, step, jnp.bfloat16, name + "_away"), "head", step)
            for step in range(1, head_count)
        ]
        return [project(place, blocks, weights, 0, jnp.float32, name + "_kept"), *terms]

    def added(terms, step, here):
        return sum(term[step, here].astype(jnp.float32) for term in terms)

    def others(terms, here):
        return [added(terms, step, here).astype(jnp.bfloat16) for step in range(1, ctx_count)]

    def spread(parts):
        return [shift(part, "ctx", step + 1) for step, part in enumerate(parts)]

    every = slice(None)
    parts_of = [slice(i * rows, (i + 1) * rows) for i in range(CHUNKS)]

    weights, last = after(weights, pieces[-1])
    last = trade(last, "batch", top)
    own = projected([tokens], "own")
    own_others = spread(others(own, every))

    sums = [[], []]
    if steps:
        early = projected(arrived, "early")
        cuts = [slice(i * token_count, (i + 1) * token_count) for i in range(len(steps))]
        leaving = [others(early, cut) for cut in cuts]
        leaving, pools = after(leaving, pools)
        sums = [
            [
                [piece_of(t, token_count, i, 0) for t in early]
                + [piece_of(p, token_count, 0) for p in spread(parts)]
            ]
            for i, parts in enumerate(leaving)
        ]
    keys, values = pick_blocks(place, block_table[0], pools, heads)
    states = [prefix_attend(query_rows, keys, values, 0, scale, heads)]
    states[0], last = after(states[0], last)

    def late_project(step, dtype, name, sums):
        result = project(place, [last], weights, step, dtype, name, sums)
        return result if sums else (result,)

    terms = []
    for step in range(1, head_count):
        term, *far = late_project(step, jnp.bfloat16, "late_away", sums[0] + sums[1] if step == 1 else [])
        terms.append(shift(term, "head", step))
    kept, *_ = late_project(0, jnp.float32, "late_kept", [])
    far, near = far[:1], far[1:]
    late = [kept, *terms]
    far = [trade(part, "batch", 1) for part in far]
    late_others = [others(late, here) for here in parts_of]
    late_others[0] = spread(late_others[0])
    late_others[1], (keys, values) = after(late_others[1], (keys, values))
    state = prefix_attend(query_rows, keys, values, 1, scale, heads, (0, 2))
    state, (late_others[1], near) = after(state, (late_others[1], near))
    late_others[1] = spread(late_others[1])
    near = [trade(part, "batch", 1) for part in near]

    away = []
    for chunk, here in enumerate(parts_of):
        part = added(late, 0, here) + sum(p.astype(jnp.float32) for p in late_others[chunk])
        part = part + sum(p[here].astype(jnp.float32) for p in far)
        part = part.astype(jnp.bfloat16)
        if chunk == 0:
            (far, late), late_others[1] = after((far, late), late_others[1])
            part, state = after(part, state)
        else:
            away[-1], part = after(away[-1], part)
        away.append(trade(part, "batch", top))
    states.append(prefix_attend(query_rows, keys, values, 1, scale, heads, (1, 2), state))
    home = added(own, 0, every) + sum(p.astype(jnp.float32) for p in (*own_others, *near))
    home, away[0] = after(home, away[0])

    result = None
    fresh = []
    for chunk in range(CHUNKS):
        pieces = [piece_of(home, rows, chunk), piece_of(away[chunk], rows, 0)]
        result, new = fresh_attend(
            lengths,
            query_rows,
            *states[chunk],
            fresh,
            pieces,
            result,
            chunk,
            scale,
            heads,
            per_token,
        )
        fresh.append(new)
    result = result.reshape(token_count, group, heads, width).transpose(0, 2, 1, 3)
    return result.reshape(token_count, heads, 1, group * width)


def solution(mesh):
    def shards(tokens, key_weight, value_weight, *rest):
        prompts = mesh.shape["batch"]
        columns = 2 * math.prod(key_weight.shape[3:])
        few_tokens = prompts * tokens.shape[0] <= columns and prompts in (2, 4)
        form = reduced_shards if few_tokens else gathered_shards
        return form(tokens, key_weight, value_weight, *rest)

    return jax.shard_map(
        shards,
        mesh=mesh,
        in_specs=(
            P(("groups", "batch"), ("ctx", "head")),
            P("ctx", "head", "batch", None, None, None),
            P("ctx", "head", "batch", None, None, None),
            P(("groups", "batch"), "ctx", "head", None),
            P(("groups", "ctx"), None, None, "head", None),
            P(("groups", "batch"), None),
            P(("groups", "batch")),
        ),
        out_specs=P(("groups", "batch"), "ctx", "head", None),
        check_vma=False,
    )
```

```python
import functools
import math

import jax
import jax.numpy as jnp
from jax import lax
from jax.experimental import pallas as pl
from jax.experimental.pallas import tpu as pltpu
from jax.sharding import PartitionSpec as P

CHUNKS = 2
PART = 1024
ONES = 16
VMEM_BYTES = 16 * 1024 * 1024
MOST_VMEM_BYTES = 60 * 1024 * 1024
LONG = pl.CostEstimate(flops=10**11, bytes_accessed=1, transcendentals=0)
COSTS = {}


def cost(name):
    return COSTS.get(name, LONG)


def attend_head(query_rows, prefix, fresh_rows, length):
    token_count = query_rows.shape[0]
    head_width = prefix.shape[1] // 2
    group_size = query_rows.shape[1] // head_width
    prefix_len = prefix.shape[0]
    key_rows = jnp.concatenate([prefix[:, :head_width], fresh_rows[:, :head_width]], 0)
    value_rows = jnp.concatenate([prefix[:, head_width:], fresh_rows[:, head_width:]], 0)
    block_len = min(token_count, 64)
    pieces = []
    for first_row in range(0, token_count, block_len):
        block_rows = query_rows[first_row : first_row + block_len].reshape(
            block_len * group_size, head_width
        )
        scores = jnp.dot(
            block_rows, key_rows.T, preferred_element_type=jnp.float32
        ) * head_width ** (-0.5)
        position = first_row + jnp.arange(block_len * group_size) // group_size
        column = jnp.arange(prefix_len + token_count) - prefix_len
        allowed = column[None, :] <= position[:, None]
        scores = jnp.where(allowed, scores, -jnp.inf)
        row_max = jnp.max(scores, axis=1, keepdims=True)
        weights = jnp.exp(scores - row_max)
        row_total = jnp.sum(weights, axis=1, keepdims=True)
        probs_bf = (weights / row_total).astype(jnp.bfloat16)
        mixed_rows = jnp.dot(probs_bf, value_rows, preferred_element_type=jnp.float32)
        is_live = position < length
        mixed_rows = jnp.where(is_live[:, None], mixed_rows, 0.0)
        pieces.append(mixed_rows.astype(jnp.bfloat16).reshape(block_len, group_size * head_width))
    return jnp.concatenate(pieces, 0)


def gathered_shards(tokens, key_weight, value_weight, queries, prefix_pool, block_table, lengths):
    token_count = tokens.shape[0]
    local_heads = queries.shape[1]
    head_width = prefix_pool.shape[4] // 2
    ctx_count = lax.axis_size("ctx")
    head_count = lax.axis_size("head")
    features = lax.all_gather(tokens, ("ctx", "head"), axis=1, tiled=True)
    key_cols, value_cols = (
        lax.all_to_all(
            lax.all_to_all(weight, "ctx", split_axis=3, concat_axis=0, tiled=True),
            "head",
            split_axis=4,
            concat_axis=1,
            tiled=True,
        )
        for weight in (key_weight, value_weight)
    )
    span_len = features.shape[1] // (ctx_count * head_count)
    feature_view = features.reshape(token_count, ctx_count, head_count, span_len)
    pieces = (
        lax.all_gather(key_cols, "batch", axis=2, tiled=True),
        lax.all_gather(value_cols, "batch", axis=2, tiled=True),
    )
    row_count = pieces[0].shape[2]

    def one_term(weight_piece):
        shaped = weight_piece.reshape(ctx_count, head_count, row_count, local_heads * head_width)
        return jnp.einsum("tchr,chrk->tk", feature_view, shaped, preferred_element_type=jnp.float32)

    new_keys = one_term(pieces[0]).astype(jnp.bfloat16).reshape(token_count, local_heads, head_width)
    new_values = one_term(pieces[1]).astype(jnp.bfloat16).reshape(token_count, local_heads, head_width)
    fresh_all = jnp.concatenate([new_keys, new_values], 2)
    pool_heads = lax.all_to_all(prefix_pool, "ctx", split_axis=2, concat_axis=0, tiled=True)
    chosen = jnp.take(pool_heads, block_table[0], axis=0)
    chosen = chosen.reshape(-1, local_heads, 2 * head_width)
    outputs = [
        attend_head(
            queries[:, head_idx, 0], chosen[:, head_idx], fresh_all[:, head_idx], lengths[0]
        )
        for head_idx in range(local_heads)
    ]
    return jnp.stack(outputs, 1)[:, :, None, :]


def shift(array, axis, step):
    count = lax.axis_size(axis)
    return lax.ppermute(array, axis, [(i, (i + step) % count) for i in range(count)])


def trade(array, axis, bits):
    return lax.ppermute(array, axis, [(i, i ^ bits) for i in range(lax.axis_size(axis))])


def after(first, second):
    return lax.optimization_barrier((first, second))


def softmax_parts(scores, old_max=None):
    row_max = jnp.max(scores, axis=0, keepdims=True)
    if old_max is not None:
        row_max = jnp.maximum(row_max, old_max)
    return row_max, jnp.exp2(scores - row_max).astype(jnp.bfloat16)


def dot_queries(keys, query_block):
    return lax.dot_general(
        keys, query_block, (((1,), (1,)), ((), ())), preferred_element_type=jnp.float32
    )


def params(limit=None):
    return pltpu.CompilerParams(vmem_limit_bytes=limit or VMEM_BYTES)


def weight_kernel(ctx_count, heads, head_count, key_ref, value_ref, out_ref, flat):
    depth, slots, width = key_ref.shape
    for kind, ref in enumerate((key_ref, value_ref)):
        flat[...] = ref[...].astype(jnp.float32).reshape(depth * slots, width)
        for ctx in range(ctx_count):
            for head in range(heads):
                for core in range(head_count):
                    slot = (ctx * heads + head) * head_count + core
                    at = (kind * heads + head) * width
                    out_ref[core, ctx, :, at : at + width] = flat[
                        pl.ds(slot, depth, stride=slots), :
                    ].astype(out_ref.dtype)


def arrange_weights(key_weight, value_weight, ctx_count, heads, head_count):
    depth, width = key_weight.shape[2], key_weight.shape[5]
    slots = ctx_count * heads * head_count
    rows = min(128, depth)
    views = [w.reshape(depth, slots, width) for w in (key_weight, value_weight)]
    block = pl.BlockSpec((rows, slots, width), lambda i: (i, 0, 0))
    columns = 2 * heads * width
    return pl.pallas_call(
        functools.partial(weight_kernel, ctx_count, heads, head_count),
        grid=(depth // rows,),
        in_specs=[block, block],
        out_specs=pl.BlockSpec((head_count, ctx_count, rows, columns), lambda i: (0, 0, i, 0)),
        out_shape=jax.ShapeDtypeStruct((head_count, ctx_count, depth, columns), jnp.bfloat16),
        scratch_shapes=[pltpu.VMEM((rows * slots, width), jnp.float32)],
        compiler_params=params(),
        cost_estimate=cost("arrange_weights"),
        name="arrange_weights",
    )(*views)


def cut_kernel(bits, place_ref, tokens_ref, *refs):
    pieces, (held, sems) = refs[:-2], refs[-2:]
    depth = pieces[0].shape[1]
    inward, outward = [], []
    for index, piece in enumerate(pieces):
        start = pl.multiple_of((place_ref[0] ^ bits[index]) * depth, depth)
        source = tokens_ref.at[:, pl.ds(start, depth)]
        inward.append(pltpu.make_async_copy(source, held.at[index], sems.at[0, index]))
        outward.append(pltpu.make_async_copy(held.at[index], piece, sems.at[1, index]))
    for copy in inward:
        copy.start()
    for copy, onward in zip(inward, outward):
        copy.wait()
        onward.start()
    for copy in outward:
        copy.wait()


def cut_tokens(place, tokens, depth, bits):
    far = pl.BlockSpec(memory_space=pltpu.HBM)
    piece = jax.ShapeDtypeStruct((tokens.shape[0], depth), tokens.dtype)
    return pl.pallas_call(
        functools.partial(cut_kernel, bits),
        grid_spec=pltpu.PrefetchScalarGridSpec(
            num_scalar_prefetch=1,
            grid=(1,),
            in_specs=[far],
            out_specs=[far] * len(bits),
            scratch_shapes=[
                pltpu.VMEM((len(bits), *piece.shape), tokens.dtype),
                pltpu.SemaphoreType.DMA((2, len(bits))),
            ],
        ),
        out_shape=[piece] * len(bits),
        compiler_params=params(MOST_VMEM_BYTES),
        cost_estimate=cost("cut_tokens"),
        name="cut_tokens",
    )(place, tokens)


def pool_kernel(ctx_count, heads, place_ref, pool_ref, *refs):
    outs, flat = refs[:-1], refs[-1]
    some, length, slots, width = pool_ref.shape
    length *= some
    flat[...] = pool_ref[...].astype(jnp.float32).reshape(length * slots, width)
    for kind in range(2):
        for head in range(heads):
            at = (kind * heads + head) * width
            held = []
            for ctx in range(ctx_count):
                slot = (kind * ctx_count + ctx) * heads + head
                held.append(flat[pl.ds(slot, length, stride=slots), :])
            for step, out_ref in enumerate(outs):
                target = lax.rem(place_ref[1] + step, ctx_count)
                value = held[0]
                for ctx in range(1, ctx_count):
                    value = jnp.where(target == ctx, held[ctx], value)
                out_ref[:, :, at : at + width] = value.astype(out_ref.dtype).reshape(
                    some, length // some, width
                )


def arrange_pool(place, prefix_pool, ctx_count, heads):
    blocks, length, all_heads, _, double = prefix_pool.shape
    width = double // 2
    slots = 2 * all_heads
    view = prefix_pool.reshape(blocks, length, all_heads, 2, width)
    view = view.transpose(0, 1, 3, 2, 4).reshape(blocks, length, slots, width)
    columns = 2 * heads * width
    some = 2 if blocks % 2 == 0 else 1
    out = pl.BlockSpec((some, length, columns), lambda i, place: (i, 0, 0))
    return pl.pallas_call(
        functools.partial(pool_kernel, ctx_count, heads),
        grid_spec=pltpu.PrefetchScalarGridSpec(
            num_scalar_prefetch=1,
            grid=(blocks // some,),
            in_specs=[pl.BlockSpec((some, length, slots, width), lambda i, place: (i, 0, 0, 0))],
            out_specs=[out] * ctx_count,
            scratch_shapes=[pltpu.VMEM((some * length * slots, width), jnp.float32)],
        ),
        out_shape=[jax.ShapeDtypeStruct((blocks, length, columns), jnp.bfloat16)] * ctx_count,
        compiler_params=params(),
        cost_estimate=cost("arrange_pool"),
        name="arrange_pool",
    )(place, view)


def total_of(refs):
    return sum(ref[...].astype(jnp.float32).reshape(ref.shape[-2:]) for ref in refs)


def project_kernel(block_count, term_counts, place_ref, *refs):
    token_refs, weight_ref = refs[:block_count], refs[block_count]
    terms = refs[block_count + 1 : block_count + 1 + sum(term_counts)]
    out_ref, *sum_refs = refs[block_count + 1 + sum(term_counts) : -1]
    stacked = refs[-1]

    @pl.when(pl.program_id(0) == 0)
    def _():
        at = 0
        for token_ref in token_refs:
            rows = token_ref.shape[0]
            stacked[at : at + rows, :] = token_ref[...]
            at += rows
        at = 0
        for count, sum_ref in zip(term_counts, sum_refs):
            sum_ref[...] = total_of(terms[at : at + count]).astype(sum_ref.dtype)
            at += count

    out_ref[0] = jnp.dot(
        stacked[...], weight_ref[0, 0], preferred_element_type=jnp.float32
    ).astype(out_ref.dtype)


def piece_of(array, *index):
    rows, block, *leading = index
    shape = (1,) * len(leading) + (rows, array.shape[-1])
    return array, pl.BlockSpec(shape, lambda j, *_: (*leading, block, 0))


def project(place, blocks, weights, head_step, out_dtype, name, sums=()):
    head_count, ctx_count, depth, width = weights.shape
    row_total = sum(block.shape[0] for block in blocks)

    def block_spec(block):
        if block.shape[1] == depth:
            return pl.BlockSpec(block.shape, lambda j, place: (0, 0))
        return pl.BlockSpec((block.shape[0], depth), lambda j, place: (0, place[0]))

    pieces = [piece for terms in sums for piece in terms]
    sum_shapes = [terms[0][1].block_shape[-2:] for terms in sums]
    result = pl.pallas_call(
        functools.partial(project_kernel, len(blocks), [len(terms) for terms in sums]),
        grid_spec=pltpu.PrefetchScalarGridSpec(
            num_scalar_prefetch=1,
            grid=(ctx_count,),
            in_specs=[block_spec(block) for block in blocks]
            + [
                pl.BlockSpec(
                    (1, 1, depth, width),
                    lambda j, place: (
                        lax.rem(place[2] + head_step, head_count),
                        lax.rem(place[1] + j, ctx_count),
                        0,
                        0,
                    ),
                )
            ]
            + [spec for _, spec in pieces],
            out_specs=[pl.BlockSpec((1, row_total, width), lambda j, place: (j, 0, 0))]
            + [pl.BlockSpec(shape, lambda j, place: (0, 0)) for shape in sum_shapes],
            scratch_shapes=[pltpu.VMEM((row_total, depth), weights.dtype)],
        ),
        out_shape=[jax.ShapeDtypeStruct((ctx_count, row_total, width), out_dtype)]
        + [jax.ShapeDtypeStruct(shape, jnp.bfloat16) for shape in sum_shapes],
        compiler_params=params(),
        cost_estimate=cost(name),
        name=name,
    )(place, *blocks, weights, *(array for array, _ in pieces))
    return result if sums else result[0]


def pick_kernel(heads, ctx_count, place_ref, table_ref, *refs):
    pool_refs, (keys, values) = refs[:ctx_count], refs[ctx_count:]
    blocks, length, columns = pool_refs[0].shape
    wide = columns // 2
    width = wide // heads
    values[...] = jnp.ones_like(values)
    for at in range(table_ref.shape[0]):
        entry = table_ref[at]
        here = slice(at * length, (at + 1) * length)
        step = lax.rem(place_ref[1] - entry // blocks + ctx_count, ctx_count)
        for ctx_step, pool_ref in enumerate(pool_refs):

            @pl.when(step == ctx_step)
            def _():
                block = pool_ref[entry % blocks]
                keys[here, :] = block[:, :wide]
                put_values(values, here, block[:, wide:], heads)


def put_values(values, here, block, heads):
    width = block.shape[1] // heads
    for head in range(heads):
        low = head * (width + ONES)
        values[low : low + width, here] = (
            block[:, head * width : (head + 1) * width].astype(jnp.float32).T.astype(jnp.bfloat16)
        )


def pick_blocks(place, table, pools, heads):
    length, columns = pools[0].shape[1:]
    count = table.shape[0] * length
    wide = columns // 2
    tall = wide + heads * ONES
    return pl.pallas_call(
        functools.partial(pick_kernel, heads, len(pools)),
        grid_spec=pltpu.PrefetchScalarGridSpec(
            num_scalar_prefetch=2,
            grid=(1,),
            in_specs=[pl.BlockSpec(p.shape, lambda i, *_: (0, 0, 0)) for p in pools],
            out_specs=[
                pl.BlockSpec((count, wide), lambda i, *_: (0, 0)),
                pl.BlockSpec((tall, count), lambda i, *_: (0, 0)),
            ],
        ),
        out_shape=[
            jax.ShapeDtypeStruct((count, wide), jnp.bfloat16),
            jax.ShapeDtypeStruct((tall, count), jnp.bfloat16),
        ],
        compiler_params=params(),
        cost_estimate=cost("pick_blocks"),
        name="pick_blocks",
    )(place, table, *pools)


def each_part(rows, heads):
    part_rows = min(PART, rows)
    each = part_rows // heads
    for low in range(0, rows, part_rows):
        for head in range(heads):
            at = low + head * each
            yield head, pl.ds(low + head, each, stride=heads), slice(at, at + each)


def prefix_kernel(scale, heads, query_ref, keys, values, *refs):
    acc_ref, stat_ref, flat = refs[-3:]
    rows, width = query_ref.shape
    tall = width + ONES
    half = stat_ref.shape[0] // 2
    flat[...] = query_ref[...].astype(jnp.float32)
    for head, taken, here in each_part(rows, heads):
        query_block = flat[taken, :].astype(jnp.bfloat16)
        scores = dot_queries(keys[:, head * width : (head + 1) * width], query_block) * scale
        row_max, weights = softmax_parts(scores)
        mixed = jnp.dot(
            values[head * tall : (head + 1) * tall, :], weights, preferred_element_type=jnp.float32
        )
        acc_ref[:, here] = mixed[:width]
        stat_ref[:half, here] = jnp.broadcast_to(row_max, (half, row_max.shape[1]))
        stat_ref[half:, here] = jnp.broadcast_to(mixed[width : width + 1], (half, row_max.shape[1]))


def prefix_attend(query_rows, keys, values, chunk, scale, heads, part=(0, 1), state=None):
    all_rows, width = query_rows.shape
    row_total = all_rows // CHUNKS
    at, count = part
    rows = min(1024, row_total // count)
    steps = row_total // rows // count
    first = chunk * count * steps + at * steps
    out_specs = [
        pl.BlockSpec((width, rows), lambda i: (0, at * steps + i)),
        pl.BlockSpec((8, rows), lambda i: (0, at * steps + i)),
    ]
    in_specs = [
        pl.BlockSpec((rows, width), lambda i: (first + i, 0)),
        pl.BlockSpec(keys.shape, lambda i: (0, 0)),
        pl.BlockSpec(values.shape, lambda i: (0, 0)),
    ]
    operands = [query_rows, keys, values]
    aliases = {}
    if state is not None:
        in_specs += [pl.BlockSpec(memory_space=pl.ANY)] * 2
        operands += state
        aliases = {3: 0, 4: 1}
    return pl.pallas_call(
        functools.partial(prefix_kernel, scale, heads),
        grid=(steps,),
        in_specs=in_specs,
        out_specs=out_specs,
        out_shape=[
            jax.ShapeDtypeStruct((width, row_total), jnp.float32),
            jax.ShapeDtypeStruct((8, row_total), jnp.float32),
        ],
        input_output_aliases=aliases,
        scratch_shapes=[pltpu.VMEM((rows, width), jnp.float32)],
        compiler_params=params(),
        cost_estimate=cost("prefix_attend"),
        name="prefix_attend",
    )(*operands)


def fresh_kernel(
    scale, heads, per_token, first_row, counts, length_ref, query_ref, acc_ref, stat_ref, *rest
):
    early_count, term_count = counts
    earlier, terms = rest[:early_count], rest[early_count : early_count + term_count]
    out_ref, fresh_ref, keys, values, flat, mixed_rows = rest[-6:]
    rows, width = query_ref.shape
    wide, tall = heads * width, width + ONES
    step = pl.program_id(0)

    @pl.when(step == 0)
    def _():
        values[...] = jnp.ones_like(values)
        fresh_ref[...] = total_of(terms).astype(fresh_ref.dtype)
        for index, ref in enumerate([*earlier, fresh_ref]):
            here = slice(index * ref.shape[0], (index + 1) * ref.shape[0])
            fresh = ref[...]
            keys[here, :] = fresh[:, :wide]
            put_values(values, here, fresh[:, wide:], heads)

    half = stat_ref.shape[0] // 2
    flat[...] = query_ref[...].astype(jnp.float32)
    for head, taken, here in each_part(rows, heads):
        query_block = flat[taken, :].astype(jnp.bfloat16)
        scores = dot_queries(keys[:, head * width : (head + 1) * width], query_block) * scale
        row = taken.start + heads * lax.broadcasted_iota(jnp.int32, (1, taken.size), 1)
        token = first_row + step * (rows // per_token) + (
            row // per_token if per_token & (per_token - 1) else row >> (per_token.bit_length() - 1)
        )
        key_at = lax.broadcasted_iota(jnp.int32, scores.shape, 0)
        scores = jnp.where(key_at <= token, scores, -jnp.inf)
        old_max, old_total = stat_ref[:1, here], stat_ref[half : half + 1, here]
        row_max, weights = softmax_parts(scores, old_max)
        fade = jnp.exp2(old_max - row_max)
        mixed = jnp.dot(
            values[head * tall : (head + 1) * tall, :], weights, preferred_element_type=jnp.float32
        )
        row_total = old_total * fade + mixed[width : width + 1]
        share = jnp.where(token < length_ref[0], 1.0 / row_total, 0.0)
        result = acc_ref[:, here] * (fade * share) + mixed[:width] * share
        mixed_rows[taken, :] = result.T
    out_ref[...] = mixed_rows[...].astype(out_ref.dtype)


def fresh_attend(
    length, query_rows, acc, stat, earlier, pieces, result, chunk, scale, heads, per_token
):
    row_total, width = query_rows.shape
    chunk_rows = row_total // CHUNKS
    rows = min(1024, chunk_rows)
    steps = chunk_rows // rows
    block = pl.BlockSpec((rows, width), lambda i, length: (chunk * steps + i, 0))
    fresh_shape = pieces[0][1].block_shape[-2:]
    key_count = (len(earlier) + 1) * fresh_shape[0]
    whole = pl.BlockSpec(fresh_shape, lambda i, length: (0, 0))
    in_specs = [
        block,
        pl.BlockSpec((width, rows), lambda i, length: (0, i)),
        pl.BlockSpec((stat.shape[0], rows), lambda i, length: (0, i)),
        *(whole for _ in earlier),
        *(spec for _, spec in pieces),
    ]
    operands = [length, query_rows, acc, stat, *earlier, *(array for array, _ in pieces)]
    aliases = {}
    if result is not None:
        in_specs.append(pl.BlockSpec(memory_space=pl.ANY))
        aliases = {len(operands): 0}
        operands.append(result)
    return pl.pallas_call(
        functools.partial(
            fresh_kernel,
            scale,
            heads,
            per_token,
            chunk * (chunk_rows // per_token),
            (len(earlier), len(pieces)),
        ),
        grid_spec=pltpu.PrefetchScalarGridSpec(
            num_scalar_prefetch=1,
            grid=(steps,),
            in_specs=in_specs,
            out_specs=[block, whole],
            scratch_shapes=[
                pltpu.VMEM((key_count, heads * width), jnp.bfloat16),
                pltpu.VMEM((heads * (width + ONES), key_count), jnp.bfloat16),
                pltpu.VMEM((rows, width), jnp.float32),
                pltpu.VMEM((rows, width), jnp.float32),
            ],
        ),
        out_shape=[
            jax.ShapeDtypeStruct((row_total, width), jnp.bfloat16),
            jax.ShapeDtypeStruct(fresh_shape, jnp.bfloat16),
        ],
        input_output_aliases=aliases,
        compiler_params=params(),
        cost_estimate=cost("fresh_attend"),
        name="fresh_attend",
    )(*operands)


def reduced_shards(tokens, key_weight, value_weight, queries, prefix_pool, block_table, lengths):
    batch_count = lax.axis_size("batch")
    ctx_count = lax.axis_size("ctx")
    head_count = lax.axis_size("head")
    batch_at, ctx_at, head_at = (lax.axis_index(a) for a in ("batch", "ctx", "head"))
    place = jnp.stack([batch_at, ctx_at, head_at]).astype(jnp.int32)
    token_count = tokens.shape[0]
    heads = queries.shape[1]
    width = prefix_pool.shape[4] // 2
    group = queries.shape[3] // width
    per_token = heads * group
    depth = key_weight.shape[2]
    rows = token_count // CHUNKS
    scale = math.log2(math.e) / math.sqrt(width)

    top = batch_count // 2
    steps = list(range(batch_count - 1, top, -1)) + list(range(1, top))
    pieces = cut_tokens(place, tokens, depth, [*steps, top])
    pieces, prefix_pool = after(pieces, prefix_pool)
    arrived = [trade(piece, "batch", bits) for piece, bits in zip(pieces, steps)]
    pools = arrange_pool(place, prefix_pool, ctx_count, heads)
    pools, (key_weight, value_weight) = after(pools, (key_weight, value_weight))
    pools = [shift(part, "ctx", step) if step else part for step, part in enumerate(pools)]

    weights = arrange_weights(key_weight, value_weight, ctx_count, heads, head_count)
    weights, last = after(weights, pieces[-1])
    last = trade(last, "batch", top)

    query_rows = queries.reshape(token_count, heads, group, width)
    query_rows = query_rows.transpose(0, 2, 1, 3).reshape(-1, width)
    def projected(blocks, name):
        terms = [
            shift(project(place, blocks, weights, step, jnp.bfloat16, name + "_away"), "head", step)
            for step in range(1, head_count)
        ]
        return [project(place, blocks, weights, 0, jnp.float32, name + "_kept"), *terms]

    def added(terms, step, here):
        return sum(term[step, here].astype(jnp.float32) for term in terms)

    def others(terms, here):
        return [added(terms, step, here).astype(jnp.bfloat16) for step in range(1, ctx_count)]

    def spread(parts):
        return [shift(part, "ctx", step + 1) for step, part in enumerate(parts)]

    every = slice(None)
    parts_of = [slice(i * rows, (i + 1) * rows) for i in range(CHUNKS)]

    sums = [[], []]
    if steps:
        early = projected(arrived, "early")
        cuts = [slice(i * token_count, (i + 1) * token_count) for i in range(len(steps))]
        leaving = [others(early, cut) for cut in cuts]
        leaving, pools = after(leaving, pools)
        sums = [
            [
                [piece_of(t, token_count, i, 0) for t in early]
                + [piece_of(p, token_count, 0) for p in spread(parts)]
            ]
            for i, parts in enumerate(leaving)
        ]
    keys, values = pick_blocks(place, block_table[0], pools, heads)
    states = [prefix_attend(query_rows, keys, values, 0, scale, heads)]
    states[0], last = after(states[0], last)

    def late_project(step, dtype, name, sums):
        result = project(place, [last, tokens], weights, step, dtype, name, sums)
        return result if sums else (result,)

    terms = []
    for step in range(1, head_count):
        term, *far = late_project(step, jnp.bfloat16, "late_away", sums[0] + sums[1] if step == 1 else [])
        terms.append(shift(term, "head", step))
    kept, *_ = late_project(0, jnp.float32, "late_kept", [])
    far, near = far[:1], far[1:]
    late = [kept, *terms]
    far, near = ([trade(part, "batch", 1) for part in parts] for parts in (far, near))
    own_at = slice(token_count, 2 * token_count)
    *late_others, own_others = [others(late, here) for here in [*parts_of, own_at]]
    late_others[0] = spread(late_others[0])
    late_others[1], (keys, values) = after(late_others[1], (keys, values))
    state = prefix_attend(query_rows, keys, values, 1, scale, heads, (0, 2))
    state, (late_others[1], own_others) = after(state, (late_others[1], own_others))
    late_others[1] = spread(late_others[1])

    away = []
    for chunk, here in enumerate(parts_of):
        part = added(late, 0, here) + sum(p.astype(jnp.float32) for p in late_others[chunk])
        part = part + sum(p[here].astype(jnp.float32) for p in far)
        part = part.astype(jnp.bfloat16)
        if chunk == 0:
            (far, late), late_others[1] = after((far, late), late_others[1])
            part, (state, own_others) = after(part, (state, own_others))
            own_others = spread(own_others)
        else:
            away[-1], part = after(away[-1], part)
        away.append(trade(part, "batch", top))
    states.append(prefix_attend(query_rows, keys, values, 1, scale, heads, (1, 2), state))

    result = None
    fresh = []
    for chunk in range(CHUNKS):
        pieces = [piece_of(t, rows, CHUNKS + chunk, 0) for t in late]
        pieces += [piece_of(part, rows, chunk) for part in (*own_others, *near)]
        pieces.append(piece_of(away[chunk], rows, 0))
        result, new = fresh_attend(
            lengths,
            query_rows,
            *states[chunk],
            fresh,
            pieces,
            result,
            chunk,
            scale,
            heads,
            per_token,
        )
        fresh.append(new)
    result = result.reshape(token_count, group, heads, width).transpose(0, 2, 1, 3)
    return result.reshape(token_count, heads, 1, group * width)


def solution(mesh):
    def shards(tokens, key_weight, value_weight, *rest):
        prompts = mesh.shape["batch"]
        columns = 2 * math.prod(key_weight.shape[3:])
        few_tokens = prompts * tokens.shape[0] <= columns and prompts in (2, 4)
        form = reduced_shards if few_tokens else gathered_shards
        return form(tokens, key_weight, value_weight, *rest)

    return jax.shard_map(
        shards,
        mesh=mesh,
        in_specs=(
            P(("groups", "batch"), ("ctx", "head")),
            P("ctx", "head", "batch", None, None, None),
            P("ctx", "head", "batch", None, None, None),
            P(("groups", "batch"), "ctx", "head", None),
            P(("groups", "ctx"), None, None, "head", None),
            P(("groups", "batch"), None),
            P(("groups", "batch")),
        ),
        out_specs=P(("groups", "batch"), "ctx", "head", None),
        check_vma=False,
    )
```

```python
import functools
import math

import jax
import jax.numpy as jnp
from jax import lax
from jax.experimental import pallas as pl
from jax.experimental.pallas import tpu as pltpu
from jax.sharding import PartitionSpec as P

CHUNKS = 2
PART = 1024
ONES = 16
VMEM_BYTES = 16 * 1024 * 1024
MOST_VMEM_BYTES = 60 * 1024 * 1024
LONG = pl.CostEstimate(flops=2 * 10**10, bytes_accessed=1, transcendentals=0)
COSTS = {}


def cost(name):
    return COSTS.get(name, LONG)


def attend_head(query_rows, prefix, fresh_rows, length):
    token_count = query_rows.shape[0]
    head_width = prefix.shape[1] // 2
    group_size = query_rows.shape[1] // head_width
    prefix_len = prefix.shape[0]
    key_rows = jnp.concatenate([prefix[:, :head_width], fresh_rows[:, :head_width]], 0)
    value_rows = jnp.concatenate([prefix[:, head_width:], fresh_rows[:, head_width:]], 0)
    block_len = min(token_count, 64)
    pieces = []
    for first_row in range(0, token_count, block_len):
        block_rows = query_rows[first_row : first_row + block_len].reshape(
            block_len * group_size, head_width
        )
        scores = jnp.dot(
            block_rows, key_rows.T, preferred_element_type=jnp.float32
        ) * head_width ** (-0.5)
        position = first_row + jnp.arange(block_len * group_size) // group_size
        column = jnp.arange(prefix_len + token_count) - prefix_len
        allowed = column[None, :] <= position[:, None]
        scores = jnp.where(allowed, scores, -jnp.inf)
        row_max = jnp.max(scores, axis=1, keepdims=True)
        weights = jnp.exp(scores - row_max)
        row_total = jnp.sum(weights, axis=1, keepdims=True)
        probs_bf = (weights / row_total).astype(jnp.bfloat16)
        mixed_rows = jnp.dot(probs_bf, value_rows, preferred_element_type=jnp.float32)
        is_live = position < length
        mixed_rows = jnp.where(is_live[:, None], mixed_rows, 0.0)
        pieces.append(mixed_rows.astype(jnp.bfloat16).reshape(block_len, group_size * head_width))
    return jnp.concatenate(pieces, 0)


def gathered_shards(tokens, key_weight, value_weight, queries, prefix_pool, block_table, lengths):
    token_count = tokens.shape[0]
    local_heads = queries.shape[1]
    head_width = prefix_pool.shape[4] // 2
    ctx_count = lax.axis_size("ctx")
    head_count = lax.axis_size("head")
    features = lax.all_gather(tokens, ("ctx", "head"), axis=1, tiled=True)
    key_cols, value_cols = (
        lax.all_to_all(
            lax.all_to_all(weight, "ctx", split_axis=3, concat_axis=0, tiled=True),
            "head",
            split_axis=4,
            concat_axis=1,
            tiled=True,
        )
        for weight in (key_weight, value_weight)
    )
    span_len = features.shape[1] // (ctx_count * head_count)
    feature_view = features.reshape(token_count, ctx_count, head_count, span_len)
    pieces = (
        lax.all_gather(key_cols, "batch", axis=2, tiled=True),
        lax.all_gather(value_cols, "batch", axis=2, tiled=True),
    )
    row_count = pieces[0].shape[2]

    def one_term(weight_piece):
        shaped = weight_piece.reshape(ctx_count, head_count, row_count, local_heads * head_width)
        return jnp.einsum("tchr,chrk->tk", feature_view, shaped, preferred_element_type=jnp.float32)

    new_keys = one_term(pieces[0]).astype(jnp.bfloat16).reshape(token_count, local_heads, head_width)
    new_values = one_term(pieces[1]).astype(jnp.bfloat16).reshape(token_count, local_heads, head_width)
    fresh_all = jnp.concatenate([new_keys, new_values], 2)
    pool_heads = lax.all_to_all(prefix_pool, "ctx", split_axis=2, concat_axis=0, tiled=True)
    chosen = jnp.take(pool_heads, block_table[0], axis=0)
    chosen = chosen.reshape(-1, local_heads, 2 * head_width)
    outputs = [
        attend_head(
            queries[:, head_idx, 0], chosen[:, head_idx], fresh_all[:, head_idx], lengths[0]
        )
        for head_idx in range(local_heads)
    ]
    return jnp.stack(outputs, 1)[:, :, None, :]


def shift(array, axis, step):
    count = lax.axis_size(axis)
    return lax.ppermute(array, axis, [(i, (i + step) % count) for i in range(count)])


def trade(array, axis, bits):
    return lax.ppermute(array, axis, [(i, i ^ bits) for i in range(lax.axis_size(axis))])


def after(first, second):
    return lax.optimization_barrier((first, second))


def softmax_parts(scores, old_max=None):
    row_max = jnp.max(scores, axis=0, keepdims=True)
    if old_max is not None:
        row_max = jnp.maximum(row_max, old_max)
    return row_max, jnp.exp2(scores - row_max).astype(jnp.bfloat16)


def dot_queries(keys, query_block):
    return lax.dot_general(
        keys, query_block, (((1,), (1,)), ((), ())), preferred_element_type=jnp.float32
    )


def params(limit=None):
    return pltpu.CompilerParams(vmem_limit_bytes=limit or VMEM_BYTES)


def weight_kernel(ctx_count, heads, head_count, key_ref, value_ref, out_ref, flat):
    depth, slots, width = key_ref.shape
    for kind, ref in enumerate((key_ref, value_ref)):
        flat[...] = ref[...].astype(jnp.float32).reshape(depth * slots, width)
        for ctx in range(ctx_count):
            for head in range(heads):
                for core in range(head_count):
                    slot = (ctx * heads + head) * head_count + core
                    at = (kind * heads + head) * width
                    out_ref[core, ctx, :, at : at + width] = flat[
                        pl.ds(slot, depth, stride=slots), :
                    ].astype(out_ref.dtype)


def arrange_weights(key_weight, value_weight, ctx_count, heads, head_count):
    depth, width = key_weight.shape[2], key_weight.shape[5]
    slots = ctx_count * heads * head_count
    rows = min(128, depth)
    views = [w.reshape(depth, slots, width) for w in (key_weight, value_weight)]
    block = pl.BlockSpec((rows, slots, width), lambda i: (i, 0, 0))
    columns = 2 * heads * width
    return pl.pallas_call(
        functools.partial(weight_kernel, ctx_count, heads, head_count),
        grid=(depth // rows,),
        in_specs=[block, block],
        out_specs=pl.BlockSpec((head_count, ctx_count, rows, columns), lambda i: (0, 0, i, 0)),
        out_shape=jax.ShapeDtypeStruct((head_count, ctx_count, depth, columns), jnp.bfloat16),
        scratch_shapes=[pltpu.VMEM((rows * slots, width), jnp.float32)],
        compiler_params=params(),
        cost_estimate=cost("arrange_weights"),
        name="arrange_weights",
    )(*views)


def cut_kernel(bits, place_ref, tokens_ref, *refs):
    pieces, (held, sems) = refs[:-2], refs[-2:]
    depth = pieces[0].shape[1]
    inward, outward = [], []
    for index, piece in enumerate(pieces):
        start = pl.multiple_of((place_ref[0] ^ bits[index]) * depth, depth)
        source = tokens_ref.at[:, pl.ds(start, depth)]
        inward.append(pltpu.make_async_copy(source, held.at[index], sems.at[0, index]))
        outward.append(pltpu.make_async_copy(held.at[index], piece, sems.at[1, index]))
    for copy in inward:
        copy.start()
    for copy, onward in zip(inward, outward):
        copy.wait()
        onward.start()
    for copy in outward:
        copy.wait()


def cut_tokens(place, tokens, depth, bits):
    far = pl.BlockSpec(memory_space=pltpu.HBM)
    piece = jax.ShapeDtypeStruct((tokens.shape[0], depth), tokens.dtype)
    return pl.pallas_call(
        functools.partial(cut_kernel, bits),
        grid_spec=pltpu.PrefetchScalarGridSpec(
            num_scalar_prefetch=1,
            grid=(1,),
            in_specs=[far],
            out_specs=[far] * len(bits),
            scratch_shapes=[
                pltpu.VMEM((len(bits), *piece.shape), tokens.dtype),
                pltpu.SemaphoreType.DMA((2, len(bits))),
            ],
        ),
        out_shape=[piece] * len(bits),
        compiler_params=params(MOST_VMEM_BYTES),
        cost_estimate=cost("cut_tokens"),
        name="cut_tokens",
    )(place, tokens)


def pool_kernel(ctx_count, heads, place_ref, pool_ref, *refs):
    outs, flat = refs[:-1], refs[-1]
    some, length, slots, width = pool_ref.shape
    length *= some
    flat[...] = pool_ref[...].astype(jnp.float32).reshape(length * slots, width)
    for kind in range(2):
        for head in range(heads):
            at = (kind * heads + head) * width
            held = []
            for ctx in range(ctx_count):
                slot = (kind * ctx_count + ctx) * heads + head
                held.append(flat[pl.ds(slot, length, stride=slots), :])
            for step, out_ref in enumerate(outs):
                target = lax.rem(place_ref[1] + step, ctx_count)
                value = held[0]
                for ctx in range(1, ctx_count):
                    value = jnp.where(target == ctx, held[ctx], value)
                out_ref[:, :, at : at + width] = value.astype(out_ref.dtype).reshape(
                    some, length // some, width
                )


def arrange_pool(place, prefix_pool, ctx_count, heads):
    blocks, length, all_heads, _, double = prefix_pool.shape
    width = double // 2
    slots = 2 * all_heads
    view = prefix_pool.reshape(blocks, length, all_heads, 2, width)
    view = view.transpose(0, 1, 3, 2, 4).reshape(blocks, length, slots, width)
    columns = 2 * heads * width
    some = 2 if blocks % 2 == 0 else 1
    out = pl.BlockSpec((some, length, columns), lambda i, place: (i, 0, 0))
    return pl.pallas_call(
        functools.partial(pool_kernel, ctx_count, heads),
        grid_spec=pltpu.PrefetchScalarGridSpec(
            num_scalar_prefetch=1,
            grid=(blocks // some,),
            in_specs=[pl.BlockSpec((some, length, slots, width), lambda i, place: (i, 0, 0, 0))],
            out_specs=[out] * ctx_count,
            scratch_shapes=[pltpu.VMEM((some * length * slots, width), jnp.float32)],
        ),
        out_shape=[jax.ShapeDtypeStruct((blocks, length, columns), jnp.bfloat16)] * ctx_count,
        compiler_params=params(),
        cost_estimate=cost("arrange_pool"),
        name="arrange_pool",
    )(place, view)


def total_of(refs):
    return sum(ref[...].astype(jnp.float32).reshape(ref.shape[-2:]) for ref in refs)


def project_kernel(block_count, term_counts, place_ref, *refs):
    token_refs, weight_ref = refs[:block_count], refs[block_count]
    terms = refs[block_count + 1 : block_count + 1 + sum(term_counts)]
    out_ref, *sum_refs = refs[block_count + 1 + sum(term_counts) : -1]
    stacked = refs[-1]

    @pl.when(pl.program_id(0) == 0)
    def _():
        at = 0
        for token_ref in token_refs:
            rows = token_ref.shape[0]
            stacked[at : at + rows, :] = token_ref[...]
            at += rows
        at = 0
        for count, sum_ref in zip(term_counts, sum_refs):
            sum_ref[...] = total_of(terms[at : at + count]).astype(sum_ref.dtype)
            at += count

    out_ref[0] = jnp.dot(
        stacked[...], weight_ref[0, 0], preferred_element_type=jnp.float32
    ).astype(out_ref.dtype)


def piece_of(array, *index):
    rows, block, *leading = index
    shape = (1,) * len(leading) + (rows, array.shape[-1])
    return array, pl.BlockSpec(shape, lambda j, *_: (*leading, block, 0))


def project(place, blocks, weights, head_step, out_dtype, name, sums=()):
    head_count, ctx_count, depth, width = weights.shape
    row_total = sum(block.shape[0] for block in blocks)

    def block_spec(block):
        if block.shape[1] == depth:
            return pl.BlockSpec(block.shape, lambda j, place: (0, 0))
        return pl.BlockSpec((block.shape[0], depth), lambda j, place: (0, place[0]))

    pieces = [piece for terms in sums for piece in terms]
    sum_shapes = [terms[0][1].block_shape[-2:] for terms in sums]
    result = pl.pallas_call(
        functools.partial(project_kernel, len(blocks), [len(terms) for terms in sums]),
        grid_spec=pltpu.PrefetchScalarGridSpec(
            num_scalar_prefetch=1,
            grid=(ctx_count,),
            in_specs=[block_spec(block) for block in blocks]
            + [
                pl.BlockSpec(
                    (1, 1, depth, width),
                    lambda j, place: (
                        lax.rem(place[2] + head_step, head_count),
                        lax.rem(place[1] + j, ctx_count),
                        0,
                        0,
                    ),
                )
            ]
            + [spec for _, spec in pieces],
            out_specs=[pl.BlockSpec((1, row_total, width), lambda j, place: (j, 0, 0))]
            + [pl.BlockSpec(shape, lambda j, place: (0, 0)) for shape in sum_shapes],
            scratch_shapes=[pltpu.VMEM((row_total, depth), weights.dtype)],
        ),
        out_shape=[jax.ShapeDtypeStruct((ctx_count, row_total, width), out_dtype)]
        + [jax.ShapeDtypeStruct(shape, jnp.bfloat16) for shape in sum_shapes],
        compiler_params=params(),
        cost_estimate=cost(name),
        name=name,
    )(place, *blocks, weights, *(array for array, _ in pieces))
    return result if sums else result[0]


def pick_kernel(heads, ctx_count, place_ref, table_ref, *refs):
    pool_refs, (keys, values) = refs[:ctx_count], refs[ctx_count:]
    blocks, length, columns = pool_refs[0].shape
    wide = columns // 2
    width = wide // heads
    values[...] = jnp.ones_like(values)
    for at in range(table_ref.shape[0]):
        entry = table_ref[at]
        here = slice(at * length, (at + 1) * length)
        step = lax.rem(place_ref[1] - entry // blocks + ctx_count, ctx_count)
        for ctx_step, pool_ref in enumerate(pool_refs):

            @pl.when(step == ctx_step)
            def _():
                block = pool_ref[entry % blocks]
                keys[here, :] = block[:, :wide]
                put_values(values, here, block[:, wide:], heads)


def put_values(values, here, block, heads):
    width = block.shape[1] // heads
    for head in range(heads):
        low = head * (width + ONES)
        values[low : low + width, here] = (
            block[:, head * width : (head + 1) * width].astype(jnp.float32).T.astype(jnp.bfloat16)
        )


def pick_blocks(place, table, pools, heads):
    length, columns = pools[0].shape[1:]
    count = table.shape[0] * length
    wide = columns // 2
    tall = wide + heads * ONES
    return pl.pallas_call(
        functools.partial(pick_kernel, heads, len(pools)),
        grid_spec=pltpu.PrefetchScalarGridSpec(
            num_scalar_prefetch=2,
            grid=(1,),
            in_specs=[pl.BlockSpec(p.shape, lambda i, *_: (0, 0, 0)) for p in pools],
            out_specs=[
                pl.BlockSpec((count, wide), lambda i, *_: (0, 0)),
                pl.BlockSpec((tall, count), lambda i, *_: (0, 0)),
            ],
        ),
        out_shape=[
            jax.ShapeDtypeStruct((count, wide), jnp.bfloat16),
            jax.ShapeDtypeStruct((tall, count), jnp.bfloat16),
        ],
        compiler_params=params(),
        cost_estimate=cost("pick_blocks"),
        name="pick_blocks",
    )(place, table, *pools)


def each_part(rows, heads):
    part_rows = min(PART, rows)
    each = part_rows // heads
    for low in range(0, rows, part_rows):
        for head in range(heads):
            at = low + head * each
            yield head, pl.ds(low + head, each, stride=heads), slice(at, at + each)


def prefix_kernel(scale, heads, query_ref, keys, values, *refs):
    acc_ref, stat_ref, flat = refs[-3:]
    rows, width = query_ref.shape
    tall = width + ONES
    half = stat_ref.shape[0] // 2
    flat[...] = query_ref[...].astype(jnp.float32)
    for head, taken, here in each_part(rows, heads):
        query_block = flat[taken, :].astype(jnp.bfloat16)
        scores = dot_queries(keys[:, head * width : (head + 1) * width], query_block) * scale
        row_max, weights = softmax_parts(scores)
        mixed = jnp.dot(
            values[head * tall : (head + 1) * tall, :], weights, preferred_element_type=jnp.float32
        )
        acc_ref[:, here] = mixed[:width]
        stat_ref[:half, here] = jnp.broadcast_to(row_max, (half, row_max.shape[1]))
        stat_ref[half:, here] = jnp.broadcast_to(mixed[width : width + 1], (half, row_max.shape[1]))


def prefix_attend(query_rows, keys, values, chunk, scale, heads, part=(0, 1), state=None):
    all_rows, width = query_rows.shape
    row_total = all_rows // CHUNKS
    at, count = part
    rows = min(1024, row_total // count)
    steps = row_total // rows // count
    first = chunk * count * steps + at * steps
    out_specs = [
        pl.BlockSpec((width, rows), lambda i: (0, at * steps + i)),
        pl.BlockSpec((8, rows), lambda i: (0, at * steps + i)),
    ]
    in_specs = [
        pl.BlockSpec((rows, width), lambda i: (first + i, 0)),
        pl.BlockSpec(keys.shape, lambda i: (0, 0)),
        pl.BlockSpec(values.shape, lambda i: (0, 0)),
    ]
    operands = [query_rows, keys, values]
    aliases = {}
    if state is not None:
        in_specs += [pl.BlockSpec(memory_space=pl.ANY)] * 2
        operands += state
        aliases = {3: 0, 4: 1}
    return pl.pallas_call(
        functools.partial(prefix_kernel, scale, heads),
        grid=(steps,),
        in_specs=in_specs,
        out_specs=out_specs,
        out_shape=[
            jax.ShapeDtypeStruct((width, row_total), jnp.float32),
            jax.ShapeDtypeStruct((8, row_total), jnp.float32),
        ],
        input_output_aliases=aliases,
        scratch_shapes=[pltpu.VMEM((rows, width), jnp.float32)],
        compiler_params=params(),
        cost_estimate=cost("prefix_attend"),
        name="prefix_attend",
    )(*operands)


def fresh_kernel(
    scale, heads, per_token, first_row, counts, length_ref, query_ref, acc_ref, stat_ref, *rest
):
    early_count, term_count = counts
    earlier, terms = rest[:early_count], rest[early_count : early_count + term_count]
    out_ref, fresh_ref, keys, values, flat, mixed_rows = rest[-6:]
    rows, width = query_ref.shape
    wide, tall = heads * width, width + ONES
    step = pl.program_id(0)

    @pl.when(step == 0)
    def _():
        values[...] = jnp.ones_like(values)
        fresh_ref[...] = total_of(terms).astype(fresh_ref.dtype)
        for index, ref in enumerate([*earlier, fresh_ref]):
            here = slice(index * ref.shape[0], (index + 1) * ref.shape[0])
            fresh = ref[...]
            keys[here, :] = fresh[:, :wide]
            put_values(values, here, fresh[:, wide:], heads)

    half = stat_ref.shape[0] // 2
    flat[...] = query_ref[...].astype(jnp.float32)
    for head, taken, here in each_part(rows, heads):
        query_block = flat[taken, :].astype(jnp.bfloat16)
        scores = dot_queries(keys[:, head * width : (head + 1) * width], query_block) * scale
        row = taken.start + heads * lax.broadcasted_iota(jnp.int32, (1, taken.size), 1)
        token = first_row + step * (rows // per_token) + (
            row // per_token if per_token & (per_token - 1) else row >> (per_token.bit_length() - 1)
        )
        key_at = lax.broadcasted_iota(jnp.int32, scores.shape, 0)
        scores = jnp.where(key_at <= token, scores, -jnp.inf)
        old_max, old_total = stat_ref[:1, here], stat_ref[half : half + 1, here]
        row_max, weights = softmax_parts(scores, old_max)
        fade = jnp.exp2(old_max - row_max)
        mixed = jnp.dot(
            values[head * tall : (head + 1) * tall, :], weights, preferred_element_type=jnp.float32
        )
        row_total = old_total * fade + mixed[width : width + 1]
        share = jnp.where(token < length_ref[0], 1.0 / row_total, 0.0)
        result = acc_ref[:, here] * (fade * share) + mixed[:width] * share
        mixed_rows[taken, :] = result.T
    out_ref[...] = mixed_rows[...].astype(out_ref.dtype)


def fresh_attend(
    length, query_rows, acc, stat, earlier, pieces, result, chunk, scale, heads, per_token
):
    row_total, width = query_rows.shape
    chunk_rows = row_total // CHUNKS
    rows = min(1024, chunk_rows)
    steps = chunk_rows // rows
    block = pl.BlockSpec((rows, width), lambda i, length: (chunk * steps + i, 0))
    fresh_shape = pieces[0][1].block_shape[-2:]
    key_count = (len(earlier) + 1) * fresh_shape[0]
    whole = pl.BlockSpec(fresh_shape, lambda i, length: (0, 0))
    in_specs = [
        block,
        pl.BlockSpec((width, rows), lambda i, length: (0, i)),
        pl.BlockSpec((stat.shape[0], rows), lambda i, length: (0, i)),
        *(whole for _ in earlier),
        *(spec for _, spec in pieces),
    ]
    operands = [length, query_rows, acc, stat, *earlier, *(array for array, _ in pieces)]
    aliases = {}
    if result is not None:
        in_specs.append(pl.BlockSpec(memory_space=pl.ANY))
        aliases = {len(operands): 0}
        operands.append(result)
    return pl.pallas_call(
        functools.partial(
            fresh_kernel,
            scale,
            heads,
            per_token,
            chunk * (chunk_rows // per_token),
            (len(earlier), len(pieces)),
        ),
        grid_spec=pltpu.PrefetchScalarGridSpec(
            num_scalar_prefetch=1,
            grid=(steps,),
            in_specs=in_specs,
            out_specs=[block, whole],
            scratch_shapes=[
                pltpu.VMEM((key_count, heads * width), jnp.bfloat16),
                pltpu.VMEM((heads * (width + ONES), key_count), jnp.bfloat16),
                pltpu.VMEM((rows, width), jnp.float32),
                pltpu.VMEM((rows, width), jnp.float32),
            ],
        ),
        out_shape=[
            jax.ShapeDtypeStruct((row_total, width), jnp.bfloat16),
            jax.ShapeDtypeStruct(fresh_shape, jnp.bfloat16),
        ],
        input_output_aliases=aliases,
        compiler_params=params(),
        cost_estimate=cost("fresh_attend"),
        name="fresh_attend",
    )(*operands)


def reduced_shards(tokens, key_weight, value_weight, queries, prefix_pool, block_table, lengths):
    batch_count = lax.axis_size("batch")
    ctx_count = lax.axis_size("ctx")
    head_count = lax.axis_size("head")
    batch_at, ctx_at, head_at = (lax.axis_index(a) for a in ("batch", "ctx", "head"))
    place = jnp.stack([batch_at, ctx_at, head_at]).astype(jnp.int32)
    token_count = tokens.shape[0]
    heads = queries.shape[1]
    width = prefix_pool.shape[4] // 2
    group = queries.shape[3] // width
    per_token = heads * group
    depth = key_weight.shape[2]
    rows = token_count // CHUNKS
    scale = math.log2(math.e) / math.sqrt(width)

    top = batch_count // 2
    steps = list(range(batch_count - 1, top, -1)) + list(range(1, top))
    pieces = cut_tokens(place, tokens, depth, [*steps, top])
    pieces, prefix_pool = after(pieces, prefix_pool)
    arrived = [trade(piece, "batch", bits) for piece, bits in zip(pieces, steps)]
    pools = arrange_pool(place, prefix_pool, ctx_count, heads)
    pools, (key_weight, value_weight) = after(pools, (key_weight, value_weight))
    pools = [shift(part, "ctx", step) if step else part for step, part in enumerate(pools)]

    weights = arrange_weights(key_weight, value_weight, ctx_count, heads, head_count)
    weights, last = after(weights, pieces[-1])
    last = trade(last, "batch", top)

    query_rows = queries.reshape(token_count, heads, group, width)
    query_rows = query_rows.transpose(0, 2, 1, 3).reshape(-1, width)
    def projected(blocks, name):
        terms = [
            shift(project(place, blocks, weights, step, jnp.bfloat16, name + "_away"), "head", step)
            for step in range(1, head_count)
        ]
        return [project(place, blocks, weights, 0, jnp.float32, name + "_kept"), *terms]

    def added(terms, step, here):
        return sum(term[step, here].astype(jnp.float32) for term in terms)

    def others(terms, here):
        return [added(terms, step, here).astype(jnp.bfloat16) for step in range(1, ctx_count)]

    def spread(parts):
        return [shift(part, "ctx", step + 1) for step, part in enumerate(parts)]

    every = slice(None)
    parts_of = [slice(i * rows, (i + 1) * rows) for i in range(CHUNKS)]

    sums = [[], []]
    if steps:
        early = projected(arrived, "early")
        cuts = [slice(i * token_count, (i + 1) * token_count) for i in range(len(steps))]
        leaving = [others(early, cut) for cut in cuts]
        leaving, pools = after(leaving, pools)
        sums = [
            [
                [piece_of(t, token_count, i, 0) for t in early]
                + [piece_of(p, token_count, 0) for p in spread(parts)]
            ]
            for i, parts in enumerate(leaving)
        ]
    keys, values = pick_blocks(place, block_table[0], pools, heads)
    states = [prefix_attend(query_rows, keys, values, 0, scale, heads)]
    states[0], last = after(states[0], last)

    def late_project(step, dtype, name, sums):
        result = project(place, [last, tokens], weights, step, dtype, name, sums)
        return result if sums else (result,)

    terms = []
    for step in range(1, head_count):
        term, *far = late_project(step, jnp.bfloat16, "late_away", sums[0] + sums[1] if step == 1 else [])
        terms.append(shift(term, "head", step))
    kept, *_ = late_project(0, jnp.float32, "late_kept", [])
    far, near = far[:1], far[1:]
    late = [kept, *terms]
    far, near = ([trade(part, "batch", 1) for part in parts] for parts in (far, near))
    own_at = slice(token_count, 2 * token_count)
    *late_others, own_others = [others(late, here) for here in [*parts_of, own_at]]
    late_others[0] = spread(late_others[0])
    late_others[1], (keys, values) = after(late_others[1], (keys, values))
    state = prefix_attend(query_rows, keys, values, 1, scale, heads, (0, 2))
    state, (late_others[1], own_others) = after(state, (late_others[1], own_others))
    late_others[1] = spread(late_others[1])

    away = []
    for chunk, here in enumerate(parts_of):
        part = added(late, 0, here) + sum(p.astype(jnp.float32) for p in late_others[chunk])
        part = part + sum(p[here].astype(jnp.float32) for p in far)
        part = part.astype(jnp.bfloat16)
        if chunk == 0:
            (far, late), late_others[1] = after((far, late), late_others[1])
            part, (state, own_others) = after(part, (state, own_others))
            own_others = spread(own_others)
        else:
            away[-1], part = after(away[-1], part)
        away.append(trade(part, "batch", top))
    states.append(prefix_attend(query_rows, keys, values, 1, scale, heads, (1, 2), state))

    result = None
    fresh = []
    for chunk in range(CHUNKS):
        pieces = [piece_of(t, rows, CHUNKS + chunk, 0) for t in late]
        pieces += [piece_of(part, rows, chunk) for part in (*own_others, *near)]
        pieces.append(piece_of(away[chunk], rows, 0))
        result, new = fresh_attend(
            lengths,
            query_rows,
            *states[chunk],
            fresh,
            pieces,
            result,
            chunk,
            scale,
            heads,
            per_token,
        )
        fresh.append(new)
    result = result.reshape(token_count, group, heads, width).transpose(0, 2, 1, 3)
    return result.reshape(token_count, heads, 1, group * width)


def solution(mesh):
    def shards(tokens, key_weight, value_weight, *rest):
        prompts = mesh.shape["batch"]
        columns = 2 * math.prod(key_weight.shape[3:])
        few_tokens = prompts * tokens.shape[0] <= columns and prompts in (2, 4)
        form = reduced_shards if few_tokens else gathered_shards
        return form(tokens, key_weight, value_weight, *rest)

    return jax.shard_map(
        shards,
        mesh=mesh,
        in_specs=(
            P(("groups", "batch"), ("ctx", "head")),
            P("ctx", "head", "batch", None, None, None),
            P("ctx", "head", "batch", None, None, None),
            P(("groups", "batch"), "ctx", "head", None),
            P(("groups", "ctx"), None, None, "head", None),
            P(("groups", "batch"), None),
            P(("groups", "batch")),
        ),
        out_specs=P(("groups", "batch"), "ctx", "head", None),
        check_vma=False,
    )
```

```python
import functools
import math

import jax
import jax.numpy as jnp
from jax import lax
from jax.experimental import pallas as pl
from jax.experimental.pallas import tpu as pltpu
from jax.sharding import PartitionSpec as P

CHUNKS = 2
PART = 1024
ONES = 16
VMEM_BYTES = 16 * 1024 * 1024
MOST_VMEM_BYTES = 60 * 1024 * 1024
LONG = pl.CostEstimate(flops=2 * 10**10, bytes_accessed=1, transcendentals=0)
COSTS = {}


def cost(name):
    return COSTS.get(name, LONG)


def attend_head(query_rows, prefix, fresh_rows, length):
    token_count = query_rows.shape[0]
    head_width = prefix.shape[1] // 2
    group_size = query_rows.shape[1] // head_width
    prefix_len = prefix.shape[0]
    key_rows = jnp.concatenate([prefix[:, :head_width], fresh_rows[:, :head_width]], 0)
    value_rows = jnp.concatenate([prefix[:, head_width:], fresh_rows[:, head_width:]], 0)
    block_len = min(token_count, 64)
    pieces = []
    for first_row in range(0, token_count, block_len):
        block_rows = query_rows[first_row : first_row + block_len].reshape(
            block_len * group_size, head_width
        )
        scores = jnp.dot(
            block_rows, key_rows.T, preferred_element_type=jnp.float32
        ) * head_width ** (-0.5)
        position = first_row + jnp.arange(block_len * group_size) // group_size
        column = jnp.arange(prefix_len + token_count) - prefix_len
        allowed = column[None, :] <= position[:, None]
        scores = jnp.where(allowed, scores, -jnp.inf)
        row_max = jnp.max(scores, axis=1, keepdims=True)
        weights = jnp.exp(scores - row_max)
        row_total = jnp.sum(weights, axis=1, keepdims=True)
        probs_bf = (weights / row_total).astype(jnp.bfloat16)
        mixed_rows = jnp.dot(probs_bf, value_rows, preferred_element_type=jnp.float32)
        is_live = position < length
        mixed_rows = jnp.where(is_live[:, None], mixed_rows, 0.0)
        pieces.append(mixed_rows.astype(jnp.bfloat16).reshape(block_len, group_size * head_width))
    return jnp.concatenate(pieces, 0)


def gathered_shards(tokens, key_weight, value_weight, queries, prefix_pool, block_table, lengths):
    token_count = tokens.shape[0]
    local_heads = queries.shape[1]
    head_width = prefix_pool.shape[4] // 2
    ctx_count = lax.axis_size("ctx")
    head_count = lax.axis_size("head")
    features = lax.all_gather(tokens, ("ctx", "head"), axis=1, tiled=True)
    key_cols, value_cols = (
        lax.all_to_all(
            lax.all_to_all(weight, "ctx", split_axis=3, concat_axis=0, tiled=True),
            "head",
            split_axis=4,
            concat_axis=1,
            tiled=True,
        )
        for weight in (key_weight, value_weight)
    )
    span_len = features.shape[1] // (ctx_count * head_count)
    feature_view = features.reshape(token_count, ctx_count, head_count, span_len)
    pieces = (
        lax.all_gather(key_cols, "batch", axis=2, tiled=True),
        lax.all_gather(value_cols, "batch", axis=2, tiled=True),
    )
    row_count = pieces[0].shape[2]

    def one_term(weight_piece):
        shaped = weight_piece.reshape(ctx_count, head_count, row_count, local_heads * head_width)
        return jnp.einsum("tchr,chrk->tk", feature_view, shaped, preferred_element_type=jnp.float32)

    new_keys = one_term(pieces[0]).astype(jnp.bfloat16).reshape(token_count, local_heads, head_width)
    new_values = one_term(pieces[1]).astype(jnp.bfloat16).reshape(token_count, local_heads, head_width)
    fresh_all = jnp.concatenate([new_keys, new_values], 2)
    pool_heads = lax.all_to_all(prefix_pool, "ctx", split_axis=2, concat_axis=0, tiled=True)
    chosen = jnp.take(pool_heads, block_table[0], axis=0)
    chosen = chosen.reshape(-1, local_heads, 2 * head_width)
    outputs = [
        attend_head(
            queries[:, head_idx, 0], chosen[:, head_idx], fresh_all[:, head_idx], lengths[0]
        )
        for head_idx in range(local_heads)
    ]
    return jnp.stack(outputs, 1)[:, :, None, :]


def shift(array, axis, step):
    count = lax.axis_size(axis)
    return lax.ppermute(array, axis, [(i, (i + step) % count) for i in range(count)])


def trade(array, axis, bits):
    return lax.ppermute(array, axis, [(i, i ^ bits) for i in range(lax.axis_size(axis))])


def after(first, second):
    return lax.optimization_barrier((first, second))


def softmax_parts(scores, old_max=None):
    row_max = jnp.max(scores, axis=0, keepdims=True)
    if old_max is not None:
        row_max = jnp.maximum(row_max, old_max)
    return row_max, jnp.exp2(scores - row_max).astype(jnp.bfloat16)


def dot_queries(keys, query_block):
    return lax.dot_general(
        keys, query_block, (((1,), (1,)), ((), ())), preferred_element_type=jnp.float32
    )


def params(limit=None):
    return pltpu.CompilerParams(vmem_limit_bytes=limit or VMEM_BYTES)


def weight_kernel(ctx_count, heads, head_count, key_ref, value_ref, out_ref, flat):
    depth, slots, width = key_ref.shape
    for kind, ref in enumerate((key_ref, value_ref)):
        flat[...] = ref[...].astype(jnp.float32).reshape(depth * slots, width)
        for ctx in range(ctx_count):
            for head in range(heads):
                for core in range(head_count):
                    slot = (ctx * heads + head) * head_count + core
                    at = (kind * heads + head) * width
                    out_ref[core, ctx, :, at : at + width] = flat[
                        pl.ds(slot, depth, stride=slots), :
                    ].astype(out_ref.dtype)


def arrange_weights(key_weight, value_weight, ctx_count, heads, head_count):
    depth, width = key_weight.shape[2], key_weight.shape[5]
    slots = ctx_count * heads * head_count
    rows = min(128, depth)
    views = [w.reshape(depth, slots, width) for w in (key_weight, value_weight)]
    block = pl.BlockSpec((rows, slots, width), lambda i: (i, 0, 0))
    columns = 2 * heads * width
    return pl.pallas_call(
        functools.partial(weight_kernel, ctx_count, heads, head_count),
        grid=(depth // rows,),
        in_specs=[block, block],
        out_specs=pl.BlockSpec((head_count, ctx_count, rows, columns), lambda i: (0, 0, i, 0)),
        out_shape=jax.ShapeDtypeStruct((head_count, ctx_count, depth, columns), jnp.bfloat16),
        scratch_shapes=[pltpu.VMEM((rows * slots, width), jnp.float32)],
        compiler_params=params(),
        cost_estimate=cost("arrange_weights"),
        name="arrange_weights",
    )(*views)


def cut_kernel(bits, place_ref, tokens_ref, *refs):
    pieces, (held, sems) = refs[:-2], refs[-2:]
    depth = pieces[0].shape[1]
    inward, outward = [], []
    for index, piece in enumerate(pieces):
        start = pl.multiple_of((place_ref[0] ^ bits[index]) * depth, depth)
        source = tokens_ref.at[:, pl.ds(start, depth)]
        inward.append(pltpu.make_async_copy(source, held.at[index], sems.at[0, index]))
        outward.append(pltpu.make_async_copy(held.at[index], piece, sems.at[1, index]))
    for copy in inward:
        copy.start()
    for copy, onward in zip(inward, outward):
        copy.wait()
        onward.start()
    for copy in outward:
        copy.wait()


def cut_tokens(place, tokens, depth, bits):
    far = pl.BlockSpec(memory_space=pltpu.HBM)
    piece = jax.ShapeDtypeStruct((tokens.shape[0], depth), tokens.dtype)
    return pl.pallas_call(
        functools.partial(cut_kernel, bits),
        grid_spec=pltpu.PrefetchScalarGridSpec(
            num_scalar_prefetch=1,
            grid=(1,),
            in_specs=[far],
            out_specs=[far] * len(bits),
            scratch_shapes=[
                pltpu.VMEM((len(bits), *piece.shape), tokens.dtype),
                pltpu.SemaphoreType.DMA((2, len(bits))),
            ],
        ),
        out_shape=[piece] * len(bits),
        compiler_params=params(MOST_VMEM_BYTES),
        cost_estimate=cost("cut_tokens"),
        name="cut_tokens",
    )(place, tokens)


def pool_kernel(ctx_count, heads, place_ref, pool_ref, *refs):
    outs, flat = refs[:-1], refs[-1]
    some, length, slots, width = pool_ref.shape
    length *= some
    flat[...] = pool_ref[...].astype(jnp.float32).reshape(length * slots, width)
    for kind in range(2):
        for head in range(heads):
            at = (kind * heads + head) * width
            held = []
            for ctx in range(ctx_count):
                slot = (kind * ctx_count + ctx) * heads + head
                held.append(flat[pl.ds(slot, length, stride=slots), :])
            for step, out_ref in enumerate(outs):
                target = lax.rem(place_ref[1] + step, ctx_count)
                value = held[0]
                for ctx in range(1, ctx_count):
                    value = jnp.where(target == ctx, held[ctx], value)
                out_ref[:, :, at : at + width] = value.astype(out_ref.dtype).reshape(
                    some, length // some, width
                )


def arrange_pool(place, prefix_pool, ctx_count, heads):
    blocks, length, all_heads, _, double = prefix_pool.shape
    width = double // 2
    slots = 2 * all_heads
    view = prefix_pool.reshape(blocks, length, all_heads, 2, width)
    view = view.transpose(0, 1, 3, 2, 4).reshape(blocks, length, slots, width)
    columns = 2 * heads * width
    some = 2 if blocks % 2 == 0 else 1
    out = pl.BlockSpec((some, length, columns), lambda i, place: (i, 0, 0))
    return pl.pallas_call(
        functools.partial(pool_kernel, ctx_count, heads),
        grid_spec=pltpu.PrefetchScalarGridSpec(
            num_scalar_prefetch=1,
            grid=(blocks // some,),
            in_specs=[pl.BlockSpec((some, length, slots, width), lambda i, place: (i, 0, 0, 0))],
            out_specs=[out] * ctx_count,
            scratch_shapes=[pltpu.VMEM((some * length * slots, width), jnp.float32)],
        ),
        out_shape=[jax.ShapeDtypeStruct((blocks, length, columns), jnp.bfloat16)] * ctx_count,
        compiler_params=params(),
        cost_estimate=cost("arrange_pool"),
        name="arrange_pool",
    )(place, view)


def total_of(refs):
    return sum(ref[...].astype(jnp.float32).reshape(ref.shape[-2:]) for ref in refs)


def put_sums(terms, counts, sum_refs):
    at = 0
    for count, sum_ref in zip(counts, sum_refs):
        sum_ref[...] = total_of(terms[at : at + count]).astype(sum_ref.dtype)
        at += count


def project_kernel(block_count, term_counts, place_ref, *refs):
    token_refs, weight_ref = refs[:block_count], refs[block_count]
    terms = refs[block_count + 1 : block_count + 1 + sum(term_counts)]
    out_ref, *sum_refs = refs[block_count + 1 + sum(term_counts) : -1]
    stacked = refs[-1]

    @pl.when(pl.program_id(0) == 0)
    def _():
        at = 0
        for token_ref in token_refs:
            rows = token_ref.shape[0]
            stacked[at : at + rows, :] = token_ref[...]
            at += rows
        put_sums(terms, term_counts, sum_refs)

    out_ref[0] = jnp.dot(
        stacked[...], weight_ref[0, 0], preferred_element_type=jnp.float32
    ).astype(out_ref.dtype)


def piece_of(array, *index):
    rows, block, *leading = index
    shape = (1,) * len(leading) + (rows, array.shape[-1])
    return array, pl.BlockSpec(shape, lambda j, *_: (*leading, block, 0))


def project(place, blocks, weights, head_step, out_dtype, name, sums=()):
    head_count, ctx_count, depth, width = weights.shape
    row_total = sum(block.shape[0] for block in blocks)

    def block_spec(block):
        if block.shape[1] == depth:
            return pl.BlockSpec(block.shape, lambda j, place: (0, 0))
        return pl.BlockSpec((block.shape[0], depth), lambda j, place: (0, place[0]))

    pieces = [piece for terms in sums for piece in terms]
    sum_shapes = [terms[0][1].block_shape[-2:] for terms in sums]
    result = pl.pallas_call(
        functools.partial(project_kernel, len(blocks), [len(terms) for terms in sums]),
        grid_spec=pltpu.PrefetchScalarGridSpec(
            num_scalar_prefetch=1,
            grid=(ctx_count,),
            in_specs=[block_spec(block) for block in blocks]
            + [
                pl.BlockSpec(
                    (1, 1, depth, width),
                    lambda j, place: (
                        lax.rem(place[2] + head_step, head_count),
                        lax.rem(place[1] + j, ctx_count),
                        0,
                        0,
                    ),
                )
            ]
            + [spec for _, spec in pieces],
            out_specs=[pl.BlockSpec((1, row_total, width), lambda j, place: (j, 0, 0))]
            + [pl.BlockSpec(shape, lambda j, place: (0, 0)) for shape in sum_shapes],
            scratch_shapes=[pltpu.VMEM((row_total, depth), weights.dtype)],
        ),
        out_shape=[jax.ShapeDtypeStruct((ctx_count, row_total, width), out_dtype)]
        + [jax.ShapeDtypeStruct(shape, jnp.bfloat16) for shape in sum_shapes],
        compiler_params=params(),
        cost_estimate=cost(name),
        name=name,
    )(place, *blocks, weights, *(array for array, _ in pieces))
    return result if sums else result[0]


def pick_kernel(heads, ctx_count, place_ref, table_ref, *refs):
    pool_refs, (keys, values) = refs[:ctx_count], refs[ctx_count:]
    blocks, length, columns = pool_refs[0].shape
    wide = columns // 2
    width = wide // heads
    values[...] = jnp.ones_like(values)
    for at in range(table_ref.shape[0]):
        entry = table_ref[at]
        here = slice(at * length, (at + 1) * length)
        step = lax.rem(place_ref[1] - entry // blocks + ctx_count, ctx_count)
        for ctx_step, pool_ref in enumerate(pool_refs):

            @pl.when(step == ctx_step)
            def _():
                block = pool_ref[entry % blocks]
                keys[here, :] = block[:, :wide]
                put_values(values, here, block[:, wide:], heads)


def put_values(values, here, block, heads):
    width = block.shape[1] // heads
    for head in range(heads):
        low = head * (width + ONES)
        values[low : low + width, here] = (
            block[:, head * width : (head + 1) * width].astype(jnp.float32).T.astype(jnp.bfloat16)
        )


def pick_blocks(place, table, pools, heads):
    length, columns = pools[0].shape[1:]
    count = table.shape[0] * length
    wide = columns // 2
    tall = wide + heads * ONES
    return pl.pallas_call(
        functools.partial(pick_kernel, heads, len(pools)),
        grid_spec=pltpu.PrefetchScalarGridSpec(
            num_scalar_prefetch=2,
            grid=(1,),
            in_specs=[pl.BlockSpec(p.shape, lambda i, *_: (0, 0, 0)) for p in pools],
            out_specs=[
                pl.BlockSpec((count, wide), lambda i, *_: (0, 0)),
                pl.BlockSpec((tall, count), lambda i, *_: (0, 0)),
            ],
        ),
        out_shape=[
            jax.ShapeDtypeStruct((count, wide), jnp.bfloat16),
            jax.ShapeDtypeStruct((tall, count), jnp.bfloat16),
        ],
        compiler_params=params(),
        cost_estimate=cost("pick_blocks"),
        name="pick_blocks",
    )(place, table, *pools)


def each_part(rows, heads):
    part_rows = min(PART, rows)
    each = part_rows // heads
    for low in range(0, rows, part_rows):
        for head in range(heads):
            at = low + head * each
            yield head, pl.ds(low + head, each, stride=heads), slice(at, at + each)


def prefix_kernel(scale, heads, term_counts, held, query_ref, keys, values, *refs):
    terms = refs[held : held + sum(term_counts)]
    acc_ref, stat_ref, *sum_refs, flat = refs[held + sum(term_counts) :]
    rows, width = query_ref.shape
    tall = width + ONES
    half = stat_ref.shape[0] // 2

    @pl.when(pl.program_id(0) == 0)
    def _():
        put_sums(terms, term_counts, sum_refs)

    flat[...] = query_ref[...].astype(jnp.float32)
    for head, taken, here in each_part(rows, heads):
        query_block = flat[taken, :].astype(jnp.bfloat16)
        scores = dot_queries(keys[:, head * width : (head + 1) * width], query_block) * scale
        row_max, weights = softmax_parts(scores)
        mixed = jnp.dot(
            values[head * tall : (head + 1) * tall, :], weights, preferred_element_type=jnp.float32
        )
        acc_ref[:, here] = mixed[:width]
        stat_ref[:half, here] = jnp.broadcast_to(row_max, (half, row_max.shape[1]))
        stat_ref[half:, here] = jnp.broadcast_to(mixed[width : width + 1], (half, row_max.shape[1]))


def prefix_attend(
    query_rows, keys, values, chunk, scale, heads, part=(0, 1), state=None, sums=()
):
    all_rows, width = query_rows.shape
    row_total = all_rows // CHUNKS
    at, count = part
    rows = min(1024, row_total // count)
    steps = row_total // rows // count
    first = chunk * count * steps + at * steps
    out_specs = [
        pl.BlockSpec((width, rows), lambda i: (0, at * steps + i)),
        pl.BlockSpec((8, rows), lambda i: (0, at * steps + i)),
    ]
    in_specs = [
        pl.BlockSpec((rows, width), lambda i: (first + i, 0)),
        pl.BlockSpec(keys.shape, lambda i: (0, 0)),
        pl.BlockSpec(values.shape, lambda i: (0, 0)),
    ]
    operands = [query_rows, keys, values]
    aliases = {}
    if state is not None:
        in_specs += [pl.BlockSpec(memory_space=pl.ANY)] * 2
        operands += list(state)
        aliases = {3: 0, 4: 1}
    pieces = [piece for terms in sums for piece in terms]
    sum_shapes = [terms[0][1].block_shape[-2:] for terms in sums]
    in_specs += [spec for _, spec in pieces]
    operands += [array for array, _ in pieces]
    out_specs += [pl.BlockSpec(shape, lambda i: (0, 0)) for shape in sum_shapes]
    acc, stat, *made = pl.pallas_call(
        functools.partial(
            prefix_kernel, scale, heads, [len(terms) for terms in sums], len(aliases)
        ),
        grid=(steps,),
        in_specs=in_specs,
        out_specs=out_specs,
        out_shape=[
            jax.ShapeDtypeStruct((width, row_total), jnp.float32),
            jax.ShapeDtypeStruct((8, row_total), jnp.float32),
        ]
        + [jax.ShapeDtypeStruct(shape, jnp.bfloat16) for shape in sum_shapes],
        input_output_aliases=aliases,
        scratch_shapes=[pltpu.VMEM((rows, width), jnp.float32)],
        compiler_params=params(),
        cost_estimate=cost("prefix_attend"),
        name="prefix_attend",
    )(*operands)
    return ([acc, stat], made) if sums else [acc, stat]


def fresh_kernel(
    scale, heads, per_token, first_row, counts, length_ref, query_ref, acc_ref, stat_ref, *rest
):
    early_count, term_count = counts
    earlier, terms = rest[:early_count], rest[early_count : early_count + term_count]
    out_ref, fresh_ref, keys, values, flat, mixed_rows = rest[-6:]
    rows, width = query_ref.shape
    wide, tall = heads * width, width + ONES
    step = pl.program_id(0)

    @pl.when(step == 0)
    def _():
        values[...] = jnp.ones_like(values)
        fresh_ref[...] = total_of(terms).astype(fresh_ref.dtype)
        for index, ref in enumerate([*earlier, fresh_ref]):
            here = slice(index * ref.shape[0], (index + 1) * ref.shape[0])
            fresh = ref[...]
            keys[here, :] = fresh[:, :wide]
            put_values(values, here, fresh[:, wide:], heads)

    half = stat_ref.shape[0] // 2
    flat[...] = query_ref[...].astype(jnp.float32)
    for head, taken, here in each_part(rows, heads):
        query_block = flat[taken, :].astype(jnp.bfloat16)
        scores = dot_queries(keys[:, head * width : (head + 1) * width], query_block) * scale
        row = taken.start + heads * lax.broadcasted_iota(jnp.int32, (1, taken.size), 1)
        token = first_row + step * (rows // per_token) + (
            row // per_token if per_token & (per_token - 1) else row >> (per_token.bit_length() - 1)
        )
        key_at = lax.broadcasted_iota(jnp.int32, scores.shape, 0)
        scores = jnp.where(key_at <= token, scores, -jnp.inf)
        old_max, old_total = stat_ref[:1, here], stat_ref[half : half + 1, here]
        row_max, weights = softmax_parts(scores, old_max)
        fade = jnp.exp2(old_max - row_max)
        mixed = jnp.dot(
            values[head * tall : (head + 1) * tall, :], weights, preferred_element_type=jnp.float32
        )
        row_total = old_total * fade + mixed[width : width + 1]
        share = jnp.where(token < length_ref[0], 1.0 / row_total, 0.0)
        result = acc_ref[:, here] * (fade * share) + mixed[:width] * share
        mixed_rows[taken, :] = result.T
    out_ref[...] = mixed_rows[...].astype(out_ref.dtype)


def fresh_attend(
    length, query_rows, acc, stat, earlier, pieces, result, chunk, scale, heads, per_token
):
    row_total, width = query_rows.shape
    chunk_rows = row_total // CHUNKS
    rows = min(1024, chunk_rows)
    steps = chunk_rows // rows
    block = pl.BlockSpec((rows, width), lambda i, length: (chunk * steps + i, 0))
    fresh_shape = pieces[0][1].block_shape[-2:]
    key_count = (len(earlier) + 1) * fresh_shape[0]
    whole = pl.BlockSpec(fresh_shape, lambda i, length: (0, 0))
    in_specs = [
        block,
        pl.BlockSpec((width, rows), lambda i, length: (0, i)),
        pl.BlockSpec((stat.shape[0], rows), lambda i, length: (0, i)),
        *(whole for _ in earlier),
        *(spec for _, spec in pieces),
    ]
    operands = [length, query_rows, acc, stat, *earlier, *(array for array, _ in pieces)]
    aliases = {}
    if result is not None:
        in_specs.append(pl.BlockSpec(memory_space=pl.ANY))
        aliases = {len(operands): 0}
        operands.append(result)
    return pl.pallas_call(
        functools.partial(
            fresh_kernel,
            scale,
            heads,
            per_token,
            chunk * (chunk_rows // per_token),
            (len(earlier), len(pieces)),
        ),
        grid_spec=pltpu.PrefetchScalarGridSpec(
            num_scalar_prefetch=1,
            grid=(steps,),
            in_specs=in_specs,
            out_specs=[block, whole],
            scratch_shapes=[
                pltpu.VMEM((key_count, heads * width), jnp.bfloat16),
                pltpu.VMEM((heads * (width + ONES), key_count), jnp.bfloat16),
                pltpu.VMEM((rows, width), jnp.float32),
                pltpu.VMEM((rows, width), jnp.float32),
            ],
        ),
        out_shape=[
            jax.ShapeDtypeStruct((row_total, width), jnp.bfloat16),
            jax.ShapeDtypeStruct(fresh_shape, jnp.bfloat16),
        ],
        input_output_aliases=aliases,
        compiler_params=params(),
        cost_estimate=cost("fresh_attend"),
        name="fresh_attend",
    )(*operands)


def reduced_shards(tokens, key_weight, value_weight, queries, prefix_pool, block_table, lengths):
    batch_count = lax.axis_size("batch")
    ctx_count = lax.axis_size("ctx")
    head_count = lax.axis_size("head")
    batch_at, ctx_at, head_at = (lax.axis_index(a) for a in ("batch", "ctx", "head"))
    place = jnp.stack([batch_at, ctx_at, head_at]).astype(jnp.int32)
    token_count = tokens.shape[0]
    heads = queries.shape[1]
    width = prefix_pool.shape[4] // 2
    group = queries.shape[3] // width
    per_token = heads * group
    depth = key_weight.shape[2]
    rows = token_count // CHUNKS
    scale = math.log2(math.e) / math.sqrt(width)

    top = batch_count // 2
    steps = list(range(batch_count - 1, top, -1)) + list(range(1, top))
    pieces = cut_tokens(place, tokens, depth, [*steps, top])
    pieces, prefix_pool = after(pieces, prefix_pool)
    arrived = [trade(piece, "batch", bits) for piece, bits in zip(pieces, steps)]
    pools = arrange_pool(place, prefix_pool, ctx_count, heads)
    pools, (key_weight, value_weight) = after(pools, (key_weight, value_weight))
    pools = [shift(part, "ctx", step) if step else part for step, part in enumerate(pools)]

    weights = arrange_weights(key_weight, value_weight, ctx_count, heads, head_count)
    weights, last = after(weights, pieces[-1])
    last = trade(last, "batch", top)

    query_rows = queries.reshape(token_count, heads, group, width)
    query_rows = query_rows.transpose(0, 2, 1, 3).reshape(-1, width)
    def projected(blocks, name):
        terms = [
            shift(project(place, blocks, weights, step, jnp.bfloat16, name + "_away"), "head", step)
            for step in range(1, head_count)
        ]
        return [project(place, blocks, weights, 0, jnp.float32, name + "_kept"), *terms]

    def added(terms, step, here):
        return sum(term[step, here].astype(jnp.float32) for term in terms)

    def others(terms, here):
        return [added(terms, step, here).astype(jnp.bfloat16) for step in range(1, ctx_count)]

    def spread(parts):
        return [shift(part, "ctx", step + 1) for step, part in enumerate(parts)]

    every = slice(None)
    parts_of = [slice(i * rows, (i + 1) * rows) for i in range(CHUNKS)]

    sums = [[], []]
    if steps:
        early = projected(arrived, "early")
        cuts = [slice(i * token_count, (i + 1) * token_count) for i in range(len(steps))]
        leaving = [others(early, cut) for cut in cuts]
        leaving, pools = after(leaving, pools)
        sums = [
            [
                [piece_of(t, token_count, i, 0) for t in early]
                + [piece_of(p, token_count, 0) for p in spread(parts)]
            ]
            for i, parts in enumerate(leaving)
        ]
    keys, values = pick_blocks(place, block_table[0], pools, heads)
    states = [prefix_attend(query_rows, keys, values, 0, scale, heads)]
    state, far = prefix_attend(
        query_rows, keys, values, 1, scale, heads, (0, 2), None, sums[0]
    )
    far = [trade(part, "batch", 1) for part in far]
    (states[0], state), last = after((states[0], state), last)

    def late_project(step, dtype, name, sums):
        result = project(place, [last, tokens], weights, step, dtype, name, sums)
        return result if sums else (result,)

    terms, near = [], []
    for step in range(1, head_count):
        term, *made = late_project(step, jnp.bfloat16, "late_away", sums[1] if step == 1 else [])
        near += [trade(part, "batch", 1) for part in made]
        terms.append(shift(term, "head", step))
    kept, *_ = late_project(0, jnp.float32, "late_kept", [])
    late = [kept, *terms]
    own_at = slice(token_count, 2 * token_count)
    *late_others, own_others = [others(late, here) for here in [*parts_of, own_at]]
    late_others[0] = spread(late_others[0])
    late_others[1], (keys, values) = after(late_others[1], (keys, values))
    state = prefix_attend(query_rows, keys, values, 1, scale, heads, (2, 4), state)
    state, (late_others[1], own_others) = after(state, (late_others[1], own_others))
    late_others[1], own_others = spread(late_others[1]), spread(own_others)

    away = []
    for chunk, here in enumerate(parts_of):
        part = added(late, 0, here) + sum(p.astype(jnp.float32) for p in late_others[chunk])
        part = part + sum(p[here].astype(jnp.float32) for p in far)
        part = part.astype(jnp.bfloat16)
        if chunk == 0:
            (far, late), late_others[1] = after((far, late), late_others[1])
            part, state = after(part, state)
        else:
            away[-1], part = after(away[-1], part)
        away.append(trade(part, "batch", top))
    states.append(prefix_attend(query_rows, keys, values, 1, scale, heads, (3, 4), state))

    result = None
    fresh = []
    for chunk in range(CHUNKS):
        pieces = [piece_of(t, rows, CHUNKS + chunk, 0) for t in late]
        pieces += [piece_of(part, rows, chunk) for part in (*own_others, *near)]
        pieces.append(piece_of(away[chunk], rows, 0))
        result, new = fresh_attend(
            lengths,
            query_rows,
            *states[chunk],
            fresh,
            pieces,
            result,
            chunk,
            scale,
            heads,
            per_token,
        )
        fresh.append(new)
    result = result.reshape(token_count, group, heads, width).transpose(0, 2, 1, 3)
    return result.reshape(token_count, heads, 1, group * width)


def solution(mesh):
    def shards(tokens, key_weight, value_weight, *rest):
        prompts = mesh.shape["batch"]
        columns = 2 * math.prod(key_weight.shape[3:])
        few_tokens = prompts * tokens.shape[0] <= columns and prompts in (2, 4)
        form = reduced_shards if few_tokens else gathered_shards
        return form(tokens, key_weight, value_weight, *rest)

    return jax.shard_map(
        shards,
        mesh=mesh,
        in_specs=(
            P(("groups", "batch"), ("ctx", "head")),
            P("ctx", "head", "batch", None, None, None),
            P("ctx", "head", "batch", None, None, None),
            P(("groups", "batch"), "ctx", "head", None),
            P(("groups", "ctx"), None, None, "head", None),
            P(("groups", "batch"), None),
            P(("groups", "batch")),
        ),
        out_specs=P(("groups", "batch"), "ctx", "head", None),
        check_vma=False,
    )
```

```python
import functools
import math

import jax
import jax.numpy as jnp
from jax import lax
from jax.experimental import pallas as pl
from jax.experimental.pallas import tpu as pltpu
from jax.sharding import PartitionSpec as P

CHUNKS = 2
PART = 1024
ONES = 16
VMEM_BYTES = 16 * 1024 * 1024
MOST_VMEM_BYTES = 60 * 1024 * 1024
LONG = pl.CostEstimate(flops=2 * 10**10, bytes_accessed=1, transcendentals=0)
COSTS = {}


def cost(name):
    return COSTS.get(name, LONG)


def attend_head(query_rows, prefix, fresh_rows, length):
    token_count = query_rows.shape[0]
    head_width = prefix.shape[1] // 2
    group_size = query_rows.shape[1] // head_width
    prefix_len = prefix.shape[0]
    key_rows = jnp.concatenate([prefix[:, :head_width], fresh_rows[:, :head_width]], 0)
    value_rows = jnp.concatenate([prefix[:, head_width:], fresh_rows[:, head_width:]], 0)
    block_len = min(token_count, 64)
    pieces = []
    for first_row in range(0, token_count, block_len):
        block_rows = query_rows[first_row : first_row + block_len].reshape(
            block_len * group_size, head_width
        )
        scores = jnp.dot(
            block_rows, key_rows.T, preferred_element_type=jnp.float32
        ) * head_width ** (-0.5)
        position = first_row + jnp.arange(block_len * group_size) // group_size
        column = jnp.arange(prefix_len + token_count) - prefix_len
        allowed = column[None, :] <= position[:, None]
        scores = jnp.where(allowed, scores, -jnp.inf)
        row_max = jnp.max(scores, axis=1, keepdims=True)
        weights = jnp.exp(scores - row_max)
        row_total = jnp.sum(weights, axis=1, keepdims=True)
        probs_bf = (weights / row_total).astype(jnp.bfloat16)
        mixed_rows = jnp.dot(probs_bf, value_rows, preferred_element_type=jnp.float32)
        is_live = position < length
        mixed_rows = jnp.where(is_live[:, None], mixed_rows, 0.0)
        pieces.append(mixed_rows.astype(jnp.bfloat16).reshape(block_len, group_size * head_width))
    return jnp.concatenate(pieces, 0)


def gathered_shards(tokens, key_weight, value_weight, queries, prefix_pool, block_table, lengths):
    token_count = tokens.shape[0]
    local_heads = queries.shape[1]
    head_width = prefix_pool.shape[4] // 2
    ctx_count = lax.axis_size("ctx")
    head_count = lax.axis_size("head")
    features = lax.all_gather(tokens, ("ctx", "head"), axis=1, tiled=True)
    key_cols, value_cols = (
        lax.all_to_all(
            lax.all_to_all(weight, "ctx", split_axis=3, concat_axis=0, tiled=True),
            "head",
            split_axis=4,
            concat_axis=1,
            tiled=True,
        )
        for weight in (key_weight, value_weight)
    )
    span_len = features.shape[1] // (ctx_count * head_count)
    feature_view = features.reshape(token_count, ctx_count, head_count, span_len)
    pieces = (
        lax.all_gather(key_cols, "batch", axis=2, tiled=True),
        lax.all_gather(value_cols, "batch", axis=2, tiled=True),
    )
    row_count = pieces[0].shape[2]

    def one_term(weight_piece):
        shaped = weight_piece.reshape(ctx_count, head_count, row_count, local_heads * head_width)
        return jnp.einsum("tchr,chrk->tk", feature_view, shaped, preferred_element_type=jnp.float32)

    new_keys = one_term(pieces[0]).astype(jnp.bfloat16).reshape(token_count, local_heads, head_width)
    new_values = one_term(pieces[1]).astype(jnp.bfloat16).reshape(token_count, local_heads, head_width)
    fresh_all = jnp.concatenate([new_keys, new_values], 2)
    pool_heads = lax.all_to_all(prefix_pool, "ctx", split_axis=2, concat_axis=0, tiled=True)
    chosen = jnp.take(pool_heads, block_table[0], axis=0)
    chosen = chosen.reshape(-1, local_heads, 2 * head_width)
    outputs = [
        attend_head(
            queries[:, head_idx, 0], chosen[:, head_idx], fresh_all[:, head_idx], lengths[0]
        )
        for head_idx in range(local_heads)
    ]
    return jnp.stack(outputs, 1)[:, :, None, :]


def shift(array, axis, step):
    count = lax.axis_size(axis)
    return lax.ppermute(array, axis, [(i, (i + step) % count) for i in range(count)])


def trade(array, axis, bits):
    return lax.ppermute(array, axis, [(i, i ^ bits) for i in range(lax.axis_size(axis))])


def after(first, second):
    return lax.optimization_barrier((first, second))


def softmax_parts(scores, old_max=None):
    row_max = jnp.max(scores, axis=0, keepdims=True)
    if old_max is not None:
        row_max = jnp.maximum(row_max, old_max)
    return row_max, jnp.exp2(scores - row_max).astype(jnp.bfloat16)


def dot_queries(keys, query_block):
    return lax.dot_general(
        keys, query_block, (((1,), (1,)), ((), ())), preferred_element_type=jnp.float32
    )


def params(limit=None):
    return pltpu.CompilerParams(vmem_limit_bytes=limit or VMEM_BYTES)


def weight_kernel(ctx_count, heads, head_count, key_ref, value_ref, out_ref, flat):
    depth, slots, width = key_ref.shape
    for kind, ref in enumerate((key_ref, value_ref)):
        flat[...] = ref[...].astype(jnp.float32).reshape(depth * slots, width)
        for ctx in range(ctx_count):
            for head in range(heads):
                for core in range(head_count):
                    slot = (ctx * heads + head) * head_count + core
                    at = (kind * heads + head) * width
                    out_ref[core, ctx, :, at : at + width] = flat[
                        pl.ds(slot, depth, stride=slots), :
                    ].astype(out_ref.dtype)


def arrange_weights(key_weight, value_weight, ctx_count, heads, head_count):
    depth, width = key_weight.shape[2], key_weight.shape[5]
    slots = ctx_count * heads * head_count
    rows = min(128, depth)
    views = [w.reshape(depth, slots, width) for w in (key_weight, value_weight)]
    block = pl.BlockSpec((rows, slots, width), lambda i: (i, 0, 0))
    columns = 2 * heads * width
    return pl.pallas_call(
        functools.partial(weight_kernel, ctx_count, heads, head_count),
        grid=(depth // rows,),
        in_specs=[block, block],
        out_specs=pl.BlockSpec((head_count, ctx_count, rows, columns), lambda i: (0, 0, i, 0)),
        out_shape=jax.ShapeDtypeStruct((head_count, ctx_count, depth, columns), jnp.bfloat16),
        scratch_shapes=[pltpu.VMEM((rows * slots, width), jnp.float32)],
        compiler_params=params(),
        cost_estimate=cost("arrange_weights"),
        name="arrange_weights",
    )(*views)


def cut_kernel(bits, place_ref, tokens_ref, *refs):
    pieces, (held, sems) = refs[:-2], refs[-2:]
    depth = pieces[0].shape[1]
    inward, outward = [], []
    for index, piece in enumerate(pieces):
        start = pl.multiple_of((place_ref[0] ^ bits[index]) * depth, depth)
        source = tokens_ref.at[:, pl.ds(start, depth)]
        inward.append(pltpu.make_async_copy(source, held.at[index], sems.at[0, index]))
        outward.append(pltpu.make_async_copy(held.at[index], piece, sems.at[1, index]))
    for copy in inward:
        copy.start()
    for copy, onward in zip(inward, outward):
        copy.wait()
        onward.start()
    for copy in outward:
        copy.wait()


def cut_tokens(place, tokens, depth, bits):
    far = pl.BlockSpec(memory_space=pltpu.HBM)
    piece = jax.ShapeDtypeStruct((tokens.shape[0], depth), tokens.dtype)
    return pl.pallas_call(
        functools.partial(cut_kernel, bits),
        grid_spec=pltpu.PrefetchScalarGridSpec(
            num_scalar_prefetch=1,
            grid=(1,),
            in_specs=[far],
            out_specs=[far] * len(bits),
            scratch_shapes=[
                pltpu.VMEM((len(bits), *piece.shape), tokens.dtype),
                pltpu.SemaphoreType.DMA((2, len(bits))),
            ],
        ),
        out_shape=[piece] * len(bits),
        compiler_params=params(MOST_VMEM_BYTES),
        cost_estimate=cost("cut_tokens"),
        name="cut_tokens",
    )(place, tokens)


def pool_kernel(ctx_count, heads, place_ref, pool_ref, *refs):
    outs, flat = refs[:-1], refs[-1]
    some, length, slots, width = pool_ref.shape
    length *= some
    flat[...] = pool_ref[...].astype(jnp.float32).reshape(length * slots, width)
    for kind in range(2):
        for head in range(heads):
            at = (kind * heads + head) * width
            held = []
            for ctx in range(ctx_count):
                slot = (kind * ctx_count + ctx) * heads + head
                held.append(flat[pl.ds(slot, length, stride=slots), :])
            for step, out_ref in enumerate(outs):
                target = lax.rem(place_ref[1] + step, ctx_count)
                value = held[0]
                for ctx in range(1, ctx_count):
                    value = jnp.where(target == ctx, held[ctx], value)
                out_ref[:, :, at : at + width] = value.astype(out_ref.dtype).reshape(
                    some, length // some, width
                )


def arrange_pool(place, prefix_pool, ctx_count, heads):
    blocks, length, all_heads, _, double = prefix_pool.shape
    width = double // 2
    slots = 2 * all_heads
    view = prefix_pool.reshape(blocks, length, all_heads, 2, width)
    view = view.transpose(0, 1, 3, 2, 4).reshape(blocks, length, slots, width)
    columns = 2 * heads * width
    some = 2 if blocks % 2 == 0 else 1
    out = pl.BlockSpec((some, length, columns), lambda i, place: (i, 0, 0))
    return pl.pallas_call(
        functools.partial(pool_kernel, ctx_count, heads),
        grid_spec=pltpu.PrefetchScalarGridSpec(
            num_scalar_prefetch=1,
            grid=(blocks // some,),
            in_specs=[pl.BlockSpec((some, length, slots, width), lambda i, place: (i, 0, 0, 0))],
            out_specs=[out] * ctx_count,
            scratch_shapes=[pltpu.VMEM((some * length * slots, width), jnp.float32)],
        ),
        out_shape=[jax.ShapeDtypeStruct((blocks, length, columns), jnp.bfloat16)] * ctx_count,
        compiler_params=params(),
        cost_estimate=cost("arrange_pool"),
        name="arrange_pool",
    )(place, view)


def total_of(refs):
    return sum(ref[...].astype(jnp.float32).reshape(ref.shape[-2:]) for ref in refs)


def put_sums(terms, counts, sum_refs):
    at = 0
    for count, sum_ref in zip(counts, sum_refs):
        sum_ref[...] = total_of(terms[at : at + count]).astype(sum_ref.dtype)
        at += count


def project_kernel(block_count, term_counts, place_ref, *refs):
    token_refs, weight_ref = refs[:block_count], refs[block_count]
    terms = refs[block_count + 1 : block_count + 1 + sum(term_counts)]
    out_ref, *sum_refs = refs[block_count + 1 + sum(term_counts) : -1]
    stacked = refs[-1]

    @pl.when(pl.program_id(0) == 0)
    def _():
        at = 0
        for token_ref in token_refs:
            rows = token_ref.shape[0]
            stacked[at : at + rows, :] = token_ref[...]
            at += rows
        put_sums(terms, term_counts, sum_refs)

    out_ref[0] = jnp.dot(
        stacked[...], weight_ref[0, 0], preferred_element_type=jnp.float32
    ).astype(out_ref.dtype)


def piece_of(array, *index):
    rows, block, *leading = index
    shape = (1,) * len(leading) + (rows, array.shape[-1])
    return array, pl.BlockSpec(shape, lambda j, *_: (*leading, block, 0))


def project(place, blocks, weights, head_step, out_dtype, name, sums=()):
    head_count, ctx_count, depth, width = weights.shape
    row_total = sum(block.shape[0] for block in blocks)

    def block_spec(block):
        if block.shape[1] == depth:
            return pl.BlockSpec(block.shape, lambda j, place: (0, 0))
        return pl.BlockSpec((block.shape[0], depth), lambda j, place: (0, place[0]))

    pieces = [piece for terms in sums for piece in terms]
    sum_shapes = [terms[0][1].block_shape[-2:] for terms in sums]
    result = pl.pallas_call(
        functools.partial(project_kernel, len(blocks), [len(terms) for terms in sums]),
        grid_spec=pltpu.PrefetchScalarGridSpec(
            num_scalar_prefetch=1,
            grid=(ctx_count,),
            in_specs=[block_spec(block) for block in blocks]
            + [
                pl.BlockSpec(
                    (1, 1, depth, width),
                    lambda j, place: (
                        lax.rem(place[2] + head_step, head_count),
                        lax.rem(place[1] + j, ctx_count),
                        0,
                        0,
                    ),
                )
            ]
            + [spec for _, spec in pieces],
            out_specs=[pl.BlockSpec((1, row_total, width), lambda j, place: (j, 0, 0))]
            + [pl.BlockSpec(shape, lambda j, place: (0, 0)) for shape in sum_shapes],
            scratch_shapes=[pltpu.VMEM((row_total, depth), weights.dtype)],
        ),
        out_shape=[jax.ShapeDtypeStruct((ctx_count, row_total, width), out_dtype)]
        + [jax.ShapeDtypeStruct(shape, jnp.bfloat16) for shape in sum_shapes],
        compiler_params=params(),
        cost_estimate=cost(name),
        name=name,
    )(place, *blocks, weights, *(array for array, _ in pieces))
    return result if sums else result[0]


def pick_kernel(heads, ctx_count, place_ref, table_ref, *refs):
    pool_refs, (keys, values) = refs[:ctx_count], refs[ctx_count:]
    blocks, length, columns = pool_refs[0].shape
    wide = columns // 2
    width = wide // heads
    values[...] = jnp.ones_like(values)
    for at in range(table_ref.shape[0]):
        entry = table_ref[at]
        here = slice(at * length, (at + 1) * length)
        step = lax.rem(place_ref[1] - entry // blocks + ctx_count, ctx_count)
        for ctx_step, pool_ref in enumerate(pool_refs):

            @pl.when(step == ctx_step)
            def _():
                block = pool_ref[entry % blocks]
                keys[here, :] = block[:, :wide]
                put_values(values, here, block[:, wide:], heads)


def put_values(values, here, block, heads):
    width = block.shape[1] // heads
    for head in range(heads):
        low = head * (width + ONES)
        values[low : low + width, here] = (
            block[:, head * width : (head + 1) * width].astype(jnp.float32).T.astype(jnp.bfloat16)
        )


def pick_blocks(place, table, pools, heads):
    length, columns = pools[0].shape[1:]
    count = table.shape[0] * length
    wide = columns // 2
    tall = wide + heads * ONES
    return pl.pallas_call(
        functools.partial(pick_kernel, heads, len(pools)),
        grid_spec=pltpu.PrefetchScalarGridSpec(
            num_scalar_prefetch=2,
            grid=(1,),
            in_specs=[pl.BlockSpec(p.shape, lambda i, *_: (0, 0, 0)) for p in pools],
            out_specs=[
                pl.BlockSpec((count, wide), lambda i, *_: (0, 0)),
                pl.BlockSpec((tall, count), lambda i, *_: (0, 0)),
            ],
        ),
        out_shape=[
            jax.ShapeDtypeStruct((count, wide), jnp.bfloat16),
            jax.ShapeDtypeStruct((tall, count), jnp.bfloat16),
        ],
        compiler_params=params(),
        cost_estimate=cost("pick_blocks"),
        name="pick_blocks",
    )(place, table, *pools)


def each_part(rows, heads):
    part_rows = min(PART, rows)
    each = part_rows // heads
    for low in range(0, rows, part_rows):
        for head in range(heads):
            at = low + head * each
            yield head, pl.ds(low + head, each, stride=heads), slice(at, at + each)


def prefix_kernel(scale, heads, term_counts, held, query_ref, keys, values, *refs):
    terms = refs[held : held + sum(term_counts)]
    acc_ref, stat_ref, *sum_refs, flat = refs[held + sum(term_counts) :]
    rows, width = query_ref.shape
    tall = width + ONES
    half = stat_ref.shape[0] // 2

    @pl.when(pl.program_id(0) == 0)
    def _():
        put_sums(terms, term_counts, sum_refs)

    flat[...] = query_ref[...].astype(jnp.float32)
    for head, taken, here in each_part(rows, heads):
        query_block = flat[taken, :].astype(jnp.bfloat16)
        scores = dot_queries(keys[:, head * width : (head + 1) * width], query_block) * scale
        row_max, weights = softmax_parts(scores)
        mixed = jnp.dot(
            values[head * tall : (head + 1) * tall, :], weights, preferred_element_type=jnp.float32
        )
        acc_ref[:, here] = mixed[:width]
        stat_ref[:half, here] = jnp.broadcast_to(row_max, (half, row_max.shape[1]))
        stat_ref[half:, here] = jnp.broadcast_to(mixed[width : width + 1], (half, row_max.shape[1]))


def prefix_attend(
    query_rows, keys, values, chunk, scale, heads, part=(0, 1), state=None, sums=()
):
    all_rows, width = query_rows.shape
    row_total = all_rows // CHUNKS
    at, count = part
    rows = min(2048, row_total // count)
    steps = row_total // rows // count
    first = chunk * count * steps + at * steps
    out_specs = [
        pl.BlockSpec((width, rows), lambda i: (0, at * steps + i)),
        pl.BlockSpec((8, rows), lambda i: (0, at * steps + i)),
    ]
    in_specs = [
        pl.BlockSpec((rows, width), lambda i: (first + i, 0)),
        pl.BlockSpec(keys.shape, lambda i: (0, 0)),
        pl.BlockSpec(values.shape, lambda i: (0, 0)),
    ]
    operands = [query_rows, keys, values]
    aliases = {}
    if state is not None:
        in_specs += [pl.BlockSpec(memory_space=pl.ANY)] * 2
        operands += list(state)
        aliases = {3: 0, 4: 1}
    pieces = [piece for terms in sums for piece in terms]
    sum_shapes = [terms[0][1].block_shape[-2:] for terms in sums]
    in_specs += [spec for _, spec in pieces]
    operands += [array for array, _ in pieces]
    out_specs += [pl.BlockSpec(shape, lambda i: (0, 0)) for shape in sum_shapes]
    acc, stat, *made = pl.pallas_call(
        functools.partial(
            prefix_kernel, scale, heads, [len(terms) for terms in sums], len(aliases)
        ),
        grid=(steps,),
        in_specs=in_specs,
        out_specs=out_specs,
        out_shape=[
            jax.ShapeDtypeStruct((width, row_total), jnp.float32),
            jax.ShapeDtypeStruct((8, row_total), jnp.float32),
        ]
        + [jax.ShapeDtypeStruct(shape, jnp.bfloat16) for shape in sum_shapes],
        input_output_aliases=aliases,
        scratch_shapes=[pltpu.VMEM((rows, width), jnp.float32)],
        compiler_params=params(),
        cost_estimate=cost("prefix_attend"),
        name="prefix_attend",
    )(*operands)
    return ([acc, stat], made) if sums else [acc, stat]


def fresh_kernel(
    scale, heads, per_token, first_row, counts, length_ref, query_ref, acc_ref, stat_ref, *rest
):
    early_count, term_count = counts
    earlier, terms = rest[:early_count], rest[early_count : early_count + term_count]
    out_ref, fresh_ref, keys, values, flat, mixed_rows = rest[-6:]
    rows, width = query_ref.shape
    wide, tall = heads * width, width + ONES
    step = pl.program_id(0)

    @pl.when(step == 0)
    def _():
        values[...] = jnp.ones_like(values)
        fresh_ref[...] = total_of(terms).astype(fresh_ref.dtype)
        for index, ref in enumerate([*earlier, fresh_ref]):
            here = slice(index * ref.shape[0], (index + 1) * ref.shape[0])
            fresh = ref[...]
            keys[here, :] = fresh[:, :wide]
            put_values(values, here, fresh[:, wide:], heads)

    half = stat_ref.shape[0] // 2
    flat[...] = query_ref[...].astype(jnp.float32)
    for head, taken, here in each_part(rows, heads):
        query_block = flat[taken, :].astype(jnp.bfloat16)
        scores = dot_queries(keys[:, head * width : (head + 1) * width], query_block) * scale
        row = taken.start + heads * lax.broadcasted_iota(jnp.int32, (1, taken.size), 1)
        token = first_row + step * (rows // per_token) + (
            row // per_token if per_token & (per_token - 1) else row >> (per_token.bit_length() - 1)
        )
        key_at = lax.broadcasted_iota(jnp.int32, scores.shape, 0)
        scores = jnp.where(key_at <= token, scores, -jnp.inf)
        old_max, old_total = stat_ref[:1, here], stat_ref[half : half + 1, here]
        row_max, weights = softmax_parts(scores, old_max)
        fade = jnp.exp2(old_max - row_max)
        mixed = jnp.dot(
            values[head * tall : (head + 1) * tall, :], weights, preferred_element_type=jnp.float32
        )
        row_total = old_total * fade + mixed[width : width + 1]
        share = jnp.where(token < length_ref[0], 1.0 / row_total, 0.0)
        result = acc_ref[:, here] * (fade * share) + mixed[:width] * share
        mixed_rows[taken, :] = result.T
    out_ref[...] = mixed_rows[...].astype(out_ref.dtype)


def fresh_attend(
    length, query_rows, acc, stat, earlier, pieces, result, chunk, scale, heads, per_token
):
    row_total, width = query_rows.shape
    chunk_rows = row_total // CHUNKS
    rows = min(2048, chunk_rows)
    steps = chunk_rows // rows
    block = pl.BlockSpec((rows, width), lambda i, length: (chunk * steps + i, 0))
    fresh_shape = pieces[0][1].block_shape[-2:]
    key_count = (len(earlier) + 1) * fresh_shape[0]
    whole = pl.BlockSpec(fresh_shape, lambda i, length: (0, 0))
    in_specs = [
        block,
        pl.BlockSpec((width, rows), lambda i, length: (0, i)),
        pl.BlockSpec((stat.shape[0], rows), lambda i, length: (0, i)),
        *(whole for _ in earlier),
        *(spec for _, spec in pieces),
    ]
    operands = [length, query_rows, acc, stat, *earlier, *(array for array, _ in pieces)]
    aliases = {}
    if result is not None:
        in_specs.append(pl.BlockSpec(memory_space=pl.ANY))
        aliases = {len(operands): 0}
        operands.append(result)
    return pl.pallas_call(
        functools.partial(
            fresh_kernel,
            scale,
            heads,
            per_token,
            chunk * (chunk_rows // per_token),
            (len(earlier), len(pieces)),
        ),
        grid_spec=pltpu.PrefetchScalarGridSpec(
            num_scalar_prefetch=1,
            grid=(steps,),
            in_specs=in_specs,
            out_specs=[block, whole],
            scratch_shapes=[
                pltpu.VMEM((key_count, heads * width), jnp.bfloat16),
                pltpu.VMEM((heads * (width + ONES), key_count), jnp.bfloat16),
                pltpu.VMEM((rows, width), jnp.float32),
                pltpu.VMEM((rows, width), jnp.float32),
            ],
        ),
        out_shape=[
            jax.ShapeDtypeStruct((row_total, width), jnp.bfloat16),
            jax.ShapeDtypeStruct(fresh_shape, jnp.bfloat16),
        ],
        input_output_aliases=aliases,
        compiler_params=params(),
        cost_estimate=cost("fresh_attend"),
        name="fresh_attend",
    )(*operands)


def reduced_shards(tokens, key_weight, value_weight, queries, prefix_pool, block_table, lengths):
    batch_count = lax.axis_size("batch")
    ctx_count = lax.axis_size("ctx")
    head_count = lax.axis_size("head")
    batch_at, ctx_at, head_at = (lax.axis_index(a) for a in ("batch", "ctx", "head"))
    place = jnp.stack([batch_at, ctx_at, head_at]).astype(jnp.int32)
    token_count = tokens.shape[0]
    heads = queries.shape[1]
    width = prefix_pool.shape[4] // 2
    group = queries.shape[3] // width
    per_token = heads * group
    depth = key_weight.shape[2]
    rows = token_count // CHUNKS
    scale = math.log2(math.e) / math.sqrt(width)

    top = batch_count // 2
    steps = list(range(batch_count - 1, top, -1)) + list(range(1, top))
    pieces = cut_tokens(place, tokens, depth, [*steps, top])
    pieces, prefix_pool = after(pieces, prefix_pool)
    arrived = [trade(piece, "batch", bits) for piece, bits in zip(pieces, steps)]
    pools = arrange_pool(place, prefix_pool, ctx_count, heads)
    pools, (key_weight, value_weight) = after(pools, (key_weight, value_weight))
    pools = [shift(part, "ctx", step) if step else part for step, part in enumerate(pools)]

    weights = arrange_weights(key_weight, value_weight, ctx_count, heads, head_count)
    weights, last = after(weights, pieces[-1])
    last = trade(last, "batch", top)

    query_rows = queries.reshape(token_count, heads, group, width)
    query_rows = query_rows.transpose(0, 2, 1, 3).reshape(-1, width)
    def projected(blocks, name):
        terms = [
            shift(project(place, blocks, weights, step, jnp.bfloat16, name + "_away"), "head", step)
            for step in range(1, head_count)
        ]
        return [project(place, blocks, weights, 0, jnp.float32, name + "_kept"), *terms]

    def added(terms, step, here):
        return sum(term[step, here].astype(jnp.float32) for term in terms)

    def others(terms, here):
        return [added(terms, step, here).astype(jnp.bfloat16) for step in range(1, ctx_count)]

    def spread(parts):
        return [shift(part, "ctx", step + 1) for step, part in enumerate(parts)]

    every = slice(None)
    parts_of = [slice(i * rows, (i + 1) * rows) for i in range(CHUNKS)]

    sums = [[], []]
    if steps:
        early = projected(arrived, "early")
        cuts = [slice(i * token_count, (i + 1) * token_count) for i in range(len(steps))]
        leaving = [others(early, cut) for cut in cuts]
        leaving, pools = after(leaving, pools)
        sums = [
            [
                [piece_of(t, token_count, i, 0) for t in early]
                + [piece_of(p, token_count, 0) for p in spread(parts)]
            ]
            for i, parts in enumerate(leaving)
        ]
    keys, values = pick_blocks(place, block_table[0], pools, heads)
    states = [prefix_attend(query_rows, keys, values, 0, scale, heads)]
    state, far = prefix_attend(
        query_rows, keys, values, 1, scale, heads, (0, 2), None, sums[0]
    )
    far = [trade(part, "batch", 1) for part in far]
    (states[0], state), last = after((states[0], state), last)

    def late_project(step, dtype, name, sums):
        result = project(place, [last, tokens], weights, step, dtype, name, sums)
        return result if sums else (result,)

    terms, near = [], []
    for step in range(1, head_count):
        term, *made = late_project(step, jnp.bfloat16, "late_away", sums[1] if step == 1 else [])
        near += made
        terms.append(shift(term, "head", step))
    kept, *_ = late_project(0, jnp.float32, "late_kept", [])
    late = [kept, *terms]
    own_at = slice(token_count, 2 * token_count)
    *late_others, own_others = [others(late, here) for here in [*parts_of, own_at]]
    late_others[0] = spread(late_others[0])
    late_others[1], (keys, values) = after(late_others[1], (keys, values))
    state = prefix_attend(query_rows, keys, values, 1, scale, heads, (2, 4), state)
    state, (late_others[1], own_others) = after(state, (late_others[1], own_others))
    late_others[1], own_others = spread(late_others[1]), spread(own_others)

    away = []
    for chunk, here in enumerate(parts_of):
        part = added(late, 0, here) + sum(p.astype(jnp.float32) for p in late_others[chunk])
        part = part + sum(p[here].astype(jnp.float32) for p in far)
        part = part.astype(jnp.bfloat16)
        if chunk == 0:
            (far, late), late_others[1] = after((far, late), late_others[1])
            part, (state, near) = after(part, (state, near))
            near = [trade(piece, "batch", 1) for piece in near]
        else:
            away[-1], part = after(away[-1], part)
        away.append(trade(part, "batch", top))
    states.append(prefix_attend(query_rows, keys, values, 1, scale, heads, (3, 4), state))

    result = None
    fresh = []
    for chunk in range(CHUNKS):
        pieces = [piece_of(t, rows, CHUNKS + chunk, 0) for t in late]
        pieces += [piece_of(part, rows, chunk) for part in (*own_others, *near)]
        pieces.append(piece_of(away[chunk], rows, 0))
        result, new = fresh_attend(
            lengths,
            query_rows,
            *states[chunk],
            fresh,
            pieces,
            result,
            chunk,
            scale,
            heads,
            per_token,
        )
        fresh.append(new)
    result = result.reshape(token_count, group, heads, width).transpose(0, 2, 1, 3)
    return result.reshape(token_count, heads, 1, group * width)


def solution(mesh):
    def shards(tokens, key_weight, value_weight, *rest):
        prompts = mesh.shape["batch"]
        columns = 2 * math.prod(key_weight.shape[3:])
        few_tokens = prompts * tokens.shape[0] <= columns and prompts in (2, 4)
        form = reduced_shards if few_tokens else gathered_shards
        return form(tokens, key_weight, value_weight, *rest)

    return jax.shard_map(
        shards,
        mesh=mesh,
        in_specs=(
            P(("groups", "batch"), ("ctx", "head")),
            P("ctx", "head", "batch", None, None, None),
            P("ctx", "head", "batch", None, None, None),
            P(("groups", "batch"), "ctx", "head", None),
            P(("groups", "ctx"), None, None, "head", None),
            P(("groups", "batch"), None),
            P(("groups", "batch")),
        ),
        out_specs=P(("groups", "batch"), "ctx", "head", None),
        check_vma=False,
    )
```

```python
import functools
import math

import jax
import jax.numpy as jnp
from jax import lax
from jax.experimental import pallas as pl
from jax.experimental.pallas import tpu as pltpu
from jax.sharding import PartitionSpec as P

CHUNKS = 2
PART = 1024
ONES = 16
VMEM_BYTES = 16 * 1024 * 1024
MOST_VMEM_BYTES = 60 * 1024 * 1024
LONG = pl.CostEstimate(flops=2 * 10**10, bytes_accessed=1, transcendentals=0)
COSTS = {}


def cost(name):
    return COSTS.get(name, LONG)


def attend_head(query_rows, prefix, fresh_rows, length):
    token_count = query_rows.shape[0]
    head_width = prefix.shape[1] // 2
    group_size = query_rows.shape[1] // head_width
    prefix_len = prefix.shape[0]
    key_rows = jnp.concatenate([prefix[:, :head_width], fresh_rows[:, :head_width]], 0)
    value_rows = jnp.concatenate([prefix[:, head_width:], fresh_rows[:, head_width:]], 0)
    block_len = min(token_count, 64)
    pieces = []
    for first_row in range(0, token_count, block_len):
        block_rows = query_rows[first_row : first_row + block_len].reshape(
            block_len * group_size, head_width
        )
        scores = jnp.dot(
            block_rows, key_rows.T, preferred_element_type=jnp.float32
        ) * head_width ** (-0.5)
        position = first_row + jnp.arange(block_len * group_size) // group_size
        column = jnp.arange(prefix_len + token_count) - prefix_len
        allowed = column[None, :] <= position[:, None]
        scores = jnp.where(allowed, scores, -jnp.inf)
        row_max = jnp.max(scores, axis=1, keepdims=True)
        weights = jnp.exp(scores - row_max)
        row_total = jnp.sum(weights, axis=1, keepdims=True)
        probs_bf = (weights / row_total).astype(jnp.bfloat16)
        mixed_rows = jnp.dot(probs_bf, value_rows, preferred_element_type=jnp.float32)
        is_live = position < length
        mixed_rows = jnp.where(is_live[:, None], mixed_rows, 0.0)
        pieces.append(mixed_rows.astype(jnp.bfloat16).reshape(block_len, group_size * head_width))
    return jnp.concatenate(pieces, 0)


def gathered_shards(tokens, key_weight, value_weight, queries, prefix_pool, block_table, lengths):
    token_count = tokens.shape[0]
    local_heads = queries.shape[1]
    head_width = prefix_pool.shape[4] // 2
    ctx_count = lax.axis_size("ctx")
    head_count = lax.axis_size("head")
    features = lax.all_gather(tokens, ("ctx", "head"), axis=1, tiled=True)
    key_cols, value_cols = (
        lax.all_to_all(
            lax.all_to_all(weight, "ctx", split_axis=3, concat_axis=0, tiled=True),
            "head",
            split_axis=4,
            concat_axis=1,
            tiled=True,
        )
        for weight in (key_weight, value_weight)
    )
    span_len = features.shape[1] // (ctx_count * head_count)
    feature_view = features.reshape(token_count, ctx_count, head_count, span_len)
    pieces = (
        lax.all_gather(key_cols, "batch", axis=2, tiled=True),
        lax.all_gather(value_cols, "batch", axis=2, tiled=True),
    )
    row_count = pieces[0].shape[2]

    def one_term(weight_piece):
        shaped = weight_piece.reshape(ctx_count, head_count, row_count, local_heads * head_width)
        return jnp.einsum("tchr,chrk->tk", feature_view, shaped, preferred_element_type=jnp.float32)

    new_keys = one_term(pieces[0]).astype(jnp.bfloat16).reshape(token_count, local_heads, head_width)
    new_values = one_term(pieces[1]).astype(jnp.bfloat16).reshape(token_count, local_heads, head_width)
    fresh_all = jnp.concatenate([new_keys, new_values], 2)
    pool_heads = lax.all_to_all(prefix_pool, "ctx", split_axis=2, concat_axis=0, tiled=True)
    chosen = jnp.take(pool_heads, block_table[0], axis=0)
    chosen = chosen.reshape(-1, local_heads, 2 * head_width)
    outputs = [
        attend_head(
            queries[:, head_idx, 0], chosen[:, head_idx], fresh_all[:, head_idx], lengths[0]
        )
        for head_idx in range(local_heads)
    ]
    return jnp.stack(outputs, 1)[:, :, None, :]


def shift(array, axis, step):
    count = lax.axis_size(axis)
    return lax.ppermute(array, axis, [(i, (i + step) % count) for i in range(count)])


def trade(array, axis, bits):
    return lax.ppermute(array, axis, [(i, i ^ bits) for i in range(lax.axis_size(axis))])


def after(first, second):
    return lax.optimization_barrier((first, second))


def softmax_parts(scores, old_max=None):
    row_max = jnp.max(scores, axis=0, keepdims=True)
    if old_max is not None:
        row_max = jnp.maximum(row_max, old_max)
    return row_max, jnp.exp2(scores - row_max).astype(jnp.bfloat16)


def dot_queries(keys, query_block):
    return lax.dot_general(
        keys, query_block, (((1,), (1,)), ((), ())), preferred_element_type=jnp.float32
    )


def params(limit=None):
    return pltpu.CompilerParams(vmem_limit_bytes=limit or VMEM_BYTES)


def weight_kernel(ctx_count, heads, head_count, key_ref, value_ref, out_ref, flat):
    depth, slots, width = key_ref.shape
    for kind, ref in enumerate((key_ref, value_ref)):
        flat[...] = ref[...].astype(jnp.float32).reshape(depth * slots, width)
        for ctx in range(ctx_count):
            for head in range(heads):
                for core in range(head_count):
                    slot = (ctx * heads + head) * head_count + core
                    at = (kind * heads + head) * width
                    out_ref[core, ctx, :, at : at + width] = flat[
                        pl.ds(slot, depth, stride=slots), :
                    ].astype(out_ref.dtype)


def arrange_weights(key_weight, value_weight, ctx_count, heads, head_count):
    depth, width = key_weight.shape[2], key_weight.shape[5]
    slots = ctx_count * heads * head_count
    rows = min(128, depth)
    views = [w.reshape(depth, slots, width) for w in (key_weight, value_weight)]
    block = pl.BlockSpec((rows, slots, width), lambda i: (i, 0, 0))
    columns = 2 * heads * width
    return pl.pallas_call(
        functools.partial(weight_kernel, ctx_count, heads, head_count),
        grid=(depth // rows,),
        in_specs=[block, block],
        out_specs=pl.BlockSpec((head_count, ctx_count, rows, columns), lambda i: (0, 0, i, 0)),
        out_shape=jax.ShapeDtypeStruct((head_count, ctx_count, depth, columns), jnp.bfloat16),
        scratch_shapes=[pltpu.VMEM((rows * slots, width), jnp.float32)],
        compiler_params=params(),
        cost_estimate=cost("arrange_weights"),
        name="arrange_weights",
    )(*views)


def cut_kernel(bits, place_ref, tokens_ref, *refs):
    pieces, sems = refs[:-1], refs[-1]
    depth = pieces[0].shape[1]
    copies = []
    for index, piece in enumerate(pieces):
        start = pl.multiple_of((place_ref[0] ^ bits[index]) * depth, depth)
        source = tokens_ref.at[:, pl.ds(start, depth)]
        copies.append(pltpu.make_async_copy(source, piece, sems.at[index]))
    for copy in copies:
        copy.start()
    for copy in copies:
        copy.wait()


def cut_tokens(place, tokens, depth, bits):
    far = pl.BlockSpec(memory_space=pltpu.HBM)
    piece = jax.ShapeDtypeStruct((tokens.shape[0], depth), tokens.dtype)
    return pl.pallas_call(
        functools.partial(cut_kernel, bits),
        grid_spec=pltpu.PrefetchScalarGridSpec(
            num_scalar_prefetch=1,
            grid=(1,),
            in_specs=[far],
            out_specs=[pl.BlockSpec(piece.shape, lambda i, place: (0, 0))] * len(bits),
            scratch_shapes=[pltpu.SemaphoreType.DMA((len(bits),))],
        ),
        out_shape=[piece] * len(bits),
        compiler_params=params(),
        cost_estimate=cost("cut_tokens"),
        name="cut_tokens",
    )(place, tokens)


def pool_kernel(ctx_count, heads, place_ref, pool_ref, *refs):
    outs, flat = refs[:-1], refs[-1]
    some, length, slots, width = pool_ref.shape
    length *= some
    flat[...] = pool_ref[...].astype(jnp.float32).reshape(length * slots, width)
    for kind in range(2):
        for head in range(heads):
            at = (kind * heads + head) * width
            held = []
            for ctx in range(ctx_count):
                slot = (kind * ctx_count + ctx) * heads + head
                held.append(flat[pl.ds(slot, length, stride=slots), :])
            for step, out_ref in enumerate(outs):
                target = lax.rem(place_ref[1] + step, ctx_count)
                value = held[0]
                for ctx in range(1, ctx_count):
                    value = jnp.where(target == ctx, held[ctx], value)
                out_ref[:, :, at : at + width] = value.astype(out_ref.dtype).reshape(
                    some, length // some, width
                )


def arrange_pool(place, prefix_pool, ctx_count, heads):
    blocks, length, all_heads, _, double = prefix_pool.shape
    width = double // 2
    slots = 2 * all_heads
    view = prefix_pool.reshape(blocks, length, all_heads, 2, width)
    view = view.transpose(0, 1, 3, 2, 4).reshape(blocks, length, slots, width)
    columns = 2 * heads * width
    some = 2 if blocks % 2 == 0 else 1
    out = pl.BlockSpec((some, length, columns), lambda i, place: (i, 0, 0))
    return pl.pallas_call(
        functools.partial(pool_kernel, ctx_count, heads),
        grid_spec=pltpu.PrefetchScalarGridSpec(
            num_scalar_prefetch=1,
            grid=(blocks // some,),
            in_specs=[pl.BlockSpec((some, length, slots, width), lambda i, place: (i, 0, 0, 0))],
            out_specs=[out] * ctx_count,
            scratch_shapes=[pltpu.VMEM((some * length * slots, width), jnp.float32)],
        ),
        out_shape=[jax.ShapeDtypeStruct((blocks, length, columns), jnp.bfloat16)] * ctx_count,
        compiler_params=params(),
        cost_estimate=cost("arrange_pool"),
        name="arrange_pool",
    )(place, view)


def total_of(refs):
    return sum(ref[...].astype(jnp.float32).reshape(ref.shape[-2:]) for ref in refs)


def put_sums(terms, counts, sum_refs):
    at = 0
    for count, sum_ref in zip(counts, sum_refs):
        sum_ref[...] = total_of(terms[at : at + count]).astype(sum_ref.dtype)
        at += count


def project_kernel(block_count, term_counts, place_ref, *refs):
    token_refs, weight_ref = refs[:block_count], refs[block_count]
    terms = refs[block_count + 1 : block_count + 1 + sum(term_counts)]
    out_ref, *sum_refs = refs[block_count + 1 + sum(term_counts) : -1]
    stacked = refs[-1]

    @pl.when(pl.program_id(0) == 0)
    def _():
        at = 0
        for token_ref in token_refs:
            rows = token_ref.shape[0]
            stacked[at : at + rows, :] = token_ref[...]
            at += rows
        put_sums(terms, term_counts, sum_refs)

    out_ref[0] = jnp.dot(
        stacked[...], weight_ref[0, 0], preferred_element_type=jnp.float32
    ).astype(out_ref.dtype)


def piece_of(array, *index):
    rows, block, *leading = index
    shape = (1,) * len(leading) + (rows, array.shape[-1])
    return array, pl.BlockSpec(shape, lambda j, *_: (*leading, block, 0))


def project(place, blocks, weights, head_step, out_dtype, name, sums=()):
    head_count, ctx_count, depth, width = weights.shape
    row_total = sum(block.shape[0] for block in blocks)

    def block_spec(block):
        if block.shape[1] == depth:
            return pl.BlockSpec(block.shape, lambda j, place: (0, 0))
        return pl.BlockSpec((block.shape[0], depth), lambda j, place: (0, place[0]))

    pieces = [piece for terms in sums for piece in terms]
    sum_shapes = [terms[0][1].block_shape[-2:] for terms in sums]
    result = pl.pallas_call(
        functools.partial(project_kernel, len(blocks), [len(terms) for terms in sums]),
        grid_spec=pltpu.PrefetchScalarGridSpec(
            num_scalar_prefetch=1,
            grid=(ctx_count,),
            in_specs=[block_spec(block) for block in blocks]
            + [
                pl.BlockSpec(
                    (1, 1, depth, width),
                    lambda j, place: (
                        lax.rem(place[2] + head_step, head_count),
                        lax.rem(place[1] + j, ctx_count),
                        0,
                        0,
                    ),
                )
            ]
            + [spec for _, spec in pieces],
            out_specs=[pl.BlockSpec((1, row_total, width), lambda j, place: (j, 0, 0))]
            + [pl.BlockSpec(shape, lambda j, place: (0, 0)) for shape in sum_shapes],
            scratch_shapes=[pltpu.VMEM((row_total, depth), weights.dtype)],
        ),
        out_shape=[jax.ShapeDtypeStruct((ctx_count, row_total, width), out_dtype)]
        + [jax.ShapeDtypeStruct(shape, jnp.bfloat16) for shape in sum_shapes],
        compiler_params=params(),
        cost_estimate=cost(name),
        name=name,
    )(place, *blocks, weights, *(array for array, _ in pieces))
    return result if sums else result[0]


def pick_kernel(heads, ctx_count, place_ref, table_ref, *refs):
    pool_refs, (keys, values) = refs[:ctx_count], refs[ctx_count:]
    blocks, length, columns = pool_refs[0].shape
    wide = columns // 2
    width = wide // heads
    values[...] = jnp.ones_like(values)
    for at in range(table_ref.shape[0]):
        entry = table_ref[at]
        here = slice(at * length, (at + 1) * length)
        step = lax.rem(place_ref[1] - entry // blocks + ctx_count, ctx_count)
        for ctx_step, pool_ref in enumerate(pool_refs):

            @pl.when(step == ctx_step)
            def _():
                block = pool_ref[entry % blocks]
                keys[here, :] = block[:, :wide]
                put_values(values, here, block[:, wide:], heads)


def put_values(values, here, block, heads):
    width = block.shape[1] // heads
    for head in range(heads):
        low = head * (width + ONES)
        values[low : low + width, here] = (
            block[:, head * width : (head + 1) * width].astype(jnp.float32).T.astype(jnp.bfloat16)
        )


def pick_blocks(place, table, pools, heads):
    length, columns = pools[0].shape[1:]
    count = table.shape[0] * length
    wide = columns // 2
    tall = wide + heads * ONES
    return pl.pallas_call(
        functools.partial(pick_kernel, heads, len(pools)),
        grid_spec=pltpu.PrefetchScalarGridSpec(
            num_scalar_prefetch=2,
            grid=(1,),
            in_specs=[pl.BlockSpec(p.shape, lambda i, *_: (0, 0, 0)) for p in pools],
            out_specs=[
                pl.BlockSpec((count, wide), lambda i, *_: (0, 0)),
                pl.BlockSpec((tall, count), lambda i, *_: (0, 0)),
            ],
        ),
        out_shape=[
            jax.ShapeDtypeStruct((count, wide), jnp.bfloat16),
            jax.ShapeDtypeStruct((tall, count), jnp.bfloat16),
        ],
        compiler_params=params(),
        cost_estimate=cost("pick_blocks"),
        name="pick_blocks",
    )(place, table, *pools)


def each_part(rows, heads):
    part_rows = min(PART, rows)
    each = part_rows // heads
    for low in range(0, rows, part_rows):
        for head in range(heads):
            at = low + head * each
            yield head, pl.ds(low + head, each, stride=heads), slice(at, at + each)


def prefix_kernel(scale, heads, term_counts, held, query_ref, keys, values, *refs):
    terms = refs[held : held + sum(term_counts)]
    acc_ref, stat_ref, *sum_refs, flat = refs[held + sum(term_counts) :]
    rows, width = query_ref.shape
    tall = width + ONES
    half = stat_ref.shape[0] // 2

    @pl.when(pl.program_id(0) == 0)
    def _():
        put_sums(terms, term_counts, sum_refs)

    flat[...] = query_ref[...].astype(jnp.float32)
    for head, taken, here in each_part(rows, heads):
        query_block = flat[taken, :].astype(jnp.bfloat16)
        scores = dot_queries(keys[:, head * width : (head + 1) * width], query_block) * scale
        row_max, weights = softmax_parts(scores)
        mixed = jnp.dot(
            values[head * tall : (head + 1) * tall, :], weights, preferred_element_type=jnp.float32
        )
        acc_ref[:, here] = mixed[:width]
        stat_ref[:half, here] = jnp.broadcast_to(row_max, (half, row_max.shape[1]))
        stat_ref[half:, here] = jnp.broadcast_to(mixed[width : width + 1], (half, row_max.shape[1]))


def prefix_attend(
    query_rows, keys, values, chunk, scale, heads, part=(0, 1), state=None, sums=()
):
    all_rows, width = query_rows.shape
    row_total = all_rows // CHUNKS
    at, count = part
    rows = min(2048, row_total // count)
    steps = row_total // rows // count
    first = chunk * count * steps + at * steps
    out_specs = [
        pl.BlockSpec((width, rows), lambda i: (0, at * steps + i)),
        pl.BlockSpec((8, rows), lambda i: (0, at * steps + i)),
    ]
    in_specs = [
        pl.BlockSpec((rows, width), lambda i: (first + i, 0)),
        pl.BlockSpec(keys.shape, lambda i: (0, 0)),
        pl.BlockSpec(values.shape, lambda i: (0, 0)),
    ]
    operands = [query_rows, keys, values]
    aliases = {}
    if state is not None:
        in_specs += [pl.BlockSpec(memory_space=pl.ANY)] * 2
        operands += list(state)
        aliases = {3: 0, 4: 1}
    pieces = [piece for terms in sums for piece in terms]
    sum_shapes = [terms[0][1].block_shape[-2:] for terms in sums]
    in_specs += [spec for _, spec in pieces]
    operands += [array for array, _ in pieces]
    out_specs += [pl.BlockSpec(shape, lambda i: (0, 0)) for shape in sum_shapes]
    acc, stat, *made = pl.pallas_call(
        functools.partial(
            prefix_kernel, scale, heads, [len(terms) for terms in sums], len(aliases)
        ),
        grid=(steps,),
        in_specs=in_specs,
        out_specs=out_specs,
        out_shape=[
            jax.ShapeDtypeStruct((width, row_total), jnp.float32),
            jax.ShapeDtypeStruct((8, row_total), jnp.float32),
        ]
        + [jax.ShapeDtypeStruct(shape, jnp.bfloat16) for shape in sum_shapes],
        input_output_aliases=aliases,
        scratch_shapes=[pltpu.VMEM((rows, width), jnp.float32)],
        compiler_params=params(),
        cost_estimate=cost("prefix_attend"),
        name="prefix_attend",
    )(*operands)
    return ([acc, stat], made) if sums else [acc, stat]


def fresh_kernel(
    scale, heads, per_token, first_row, counts, length_ref, query_ref, acc_ref, stat_ref, *rest
):
    early_count, term_count = counts
    earlier, terms = rest[:early_count], rest[early_count : early_count + term_count]
    out_ref, fresh_ref, keys, values, flat, mixed_rows = rest[-6:]
    rows, width = query_ref.shape
    wide, tall = heads * width, width + ONES
    step = pl.program_id(0)

    @pl.when(step == 0)
    def _():
        values[...] = jnp.ones_like(values)
        fresh_ref[...] = total_of(terms).astype(fresh_ref.dtype)
        for index, ref in enumerate([*earlier, fresh_ref]):
            here = slice(index * ref.shape[0], (index + 1) * ref.shape[0])
            fresh = ref[...]
            keys[here, :] = fresh[:, :wide]
            put_values(values, here, fresh[:, wide:], heads)

    half = stat_ref.shape[0] // 2
    flat[...] = query_ref[...].astype(jnp.float32)
    for head, taken, here in each_part(rows, heads):
        query_block = flat[taken, :].astype(jnp.bfloat16)
        scores = dot_queries(keys[:, head * width : (head + 1) * width], query_block) * scale
        row = taken.start + heads * lax.broadcasted_iota(jnp.int32, (1, taken.size), 1)
        token = first_row + step * (rows // per_token) + (
            row // per_token if per_token & (per_token - 1) else row >> (per_token.bit_length() - 1)
        )
        key_at = lax.broadcasted_iota(jnp.int32, scores.shape, 0)
        scores = jnp.where(key_at <= token, scores, -jnp.inf)
        old_max, old_total = stat_ref[:1, here], stat_ref[half : half + 1, here]
        row_max, weights = softmax_parts(scores, old_max)
        fade = jnp.exp2(old_max - row_max)
        mixed = jnp.dot(
            values[head * tall : (head + 1) * tall, :], weights, preferred_element_type=jnp.float32
        )
        row_total = old_total * fade + mixed[width : width + 1]
        share = jnp.where(token < length_ref[0], 1.0 / row_total, 0.0)
        result = acc_ref[:, here] * (fade * share) + mixed[:width] * share
        mixed_rows[taken, :] = result.T
    out_ref[...] = mixed_rows[...].astype(out_ref.dtype)


def fresh_attend(
    length, query_rows, acc, stat, earlier, pieces, result, chunk, scale, heads, per_token
):
    row_total, width = query_rows.shape
    chunk_rows = row_total // CHUNKS
    rows = min(2048, chunk_rows)
    steps = chunk_rows // rows
    block = pl.BlockSpec((rows, width), lambda i, length: (chunk * steps + i, 0))
    fresh_shape = pieces[0][1].block_shape[-2:]
    key_count = (len(earlier) + 1) * fresh_shape[0]
    whole = pl.BlockSpec(fresh_shape, lambda i, length: (0, 0))
    in_specs = [
        block,
        pl.BlockSpec((width, rows), lambda i, length: (0, i)),
        pl.BlockSpec((stat.shape[0], rows), lambda i, length: (0, i)),
        *(whole for _ in earlier),
        *(spec for _, spec in pieces),
    ]
    operands = [length, query_rows, acc, stat, *earlier, *(array for array, _ in pieces)]
    aliases = {}
    if result is not None:
        in_specs.append(pl.BlockSpec(memory_space=pl.ANY))
        aliases = {len(operands): 0}
        operands.append(result)
    return pl.pallas_call(
        functools.partial(
            fresh_kernel,
            scale,
            heads,
            per_token,
            chunk * (chunk_rows // per_token),
            (len(earlier), len(pieces)),
        ),
        grid_spec=pltpu.PrefetchScalarGridSpec(
            num_scalar_prefetch=1,
            grid=(steps,),
            in_specs=in_specs,
            out_specs=[block, whole],
            scratch_shapes=[
                pltpu.VMEM((key_count, heads * width), jnp.bfloat16),
                pltpu.VMEM((heads * (width + ONES), key_count), jnp.bfloat16),
                pltpu.VMEM((rows, width), jnp.float32),
                pltpu.VMEM((rows, width), jnp.float32),
            ],
        ),
        out_shape=[
            jax.ShapeDtypeStruct((row_total, width), jnp.bfloat16),
            jax.ShapeDtypeStruct(fresh_shape, jnp.bfloat16),
        ],
        input_output_aliases=aliases,
        compiler_params=params(),
        cost_estimate=cost("fresh_attend"),
        name="fresh_attend",
    )(*operands)


def reduced_shards(tokens, key_weight, value_weight, queries, prefix_pool, block_table, lengths):
    batch_count = lax.axis_size("batch")
    ctx_count = lax.axis_size("ctx")
    head_count = lax.axis_size("head")
    batch_at, ctx_at, head_at = (lax.axis_index(a) for a in ("batch", "ctx", "head"))
    place = jnp.stack([batch_at, ctx_at, head_at]).astype(jnp.int32)
    token_count = tokens.shape[0]
    heads = queries.shape[1]
    width = prefix_pool.shape[4] // 2
    group = queries.shape[3] // width
    per_token = heads * group
    depth = key_weight.shape[2]
    rows = token_count // CHUNKS
    scale = math.log2(math.e) / math.sqrt(width)

    top = batch_count // 2
    steps = list(range(batch_count - 1, top, -1)) + list(range(1, top))
    pieces = cut_tokens(place, tokens, depth, [*steps, top])
    pieces, prefix_pool = after(pieces, prefix_pool)
    arrived = [trade(piece, "batch", bits) for piece, bits in zip(pieces, steps)]
    pools = arrange_pool(place, prefix_pool, ctx_count, heads)
    pools, (key_weight, value_weight) = after(pools, (key_weight, value_weight))
    pools = [shift(part, "ctx", step) if step else part for step, part in enumerate(pools)]

    weights = arrange_weights(key_weight, value_weight, ctx_count, heads, head_count)
    weights, last = after(weights, pieces[-1])
    last = trade(last, "batch", top)

    query_rows = queries.reshape(token_count, heads, group, width)
    query_rows = query_rows.transpose(0, 2, 1, 3).reshape(-1, width)
    def projected(blocks, name):
        terms = [
            shift(project(place, blocks, weights, step, jnp.bfloat16, name + "_away"), "head", step)
            for step in range(1, head_count)
        ]
        return [project(place, blocks, weights, 0, jnp.float32, name + "_kept"), *terms]

    def added(terms, step, here):
        return sum(term[step, here].astype(jnp.float32) for term in terms)

    def others(terms, here):
        return [added(terms, step, here).astype(jnp.bfloat16) for step in range(1, ctx_count)]

    def spread(parts):
        return [shift(part, "ctx", step + 1) for step, part in enumerate(parts)]

    every = slice(None)
    parts_of = [slice(i * rows, (i + 1) * rows) for i in range(CHUNKS)]

    sums = [[], []]
    if steps:
        early = projected(arrived, "early")
        cuts = [slice(i * token_count, (i + 1) * token_count) for i in range(len(steps))]
        leaving = [others(early, cut) for cut in cuts]
        leaving, pools = after(leaving, pools)
        sums = [
            [
                [piece_of(t, token_count, i, 0) for t in early]
                + [piece_of(p, token_count, 0) for p in spread(parts)]
            ]
            for i, parts in enumerate(leaving)
        ]
    keys, values = pick_blocks(place, block_table[0], pools, heads)
    states = [prefix_attend(query_rows, keys, values, 0, scale, heads)]
    state, far = prefix_attend(
        query_rows, keys, values, 1, scale, heads, (0, 2), None, sums[0]
    )
    far = [trade(part, "batch", 1) for part in far]
    (states[0], state), last = after((states[0], state), last)

    def late_project(step, dtype, name, sums):
        result = project(place, [last, tokens], weights, step, dtype, name, sums)
        return result if sums else (result,)

    terms, near = [], []
    for step in range(1, head_count):
        term, *made = late_project(step, jnp.bfloat16, "late_away", sums[1] if step == 1 else [])
        near += [trade(part, "batch", 1) for part in made]
        terms.append(shift(term, "head", step))
    kept, *_ = late_project(0, jnp.float32, "late_kept", [])
    late = [kept, *terms]
    own_at = slice(token_count, 2 * token_count)
    *late_others, own_others = [others(late, here) for here in [*parts_of, own_at]]
    late_others[0] = spread(late_others[0])
    late_others[1], (keys, values) = after(late_others[1], (keys, values))
    state = prefix_attend(query_rows, keys, values, 1, scale, heads, (2, 4), state)
    state, (late_others[1], own_others) = after(state, (late_others[1], own_others))
    late_others[1], own_others = spread(late_others[1]), spread(own_others)

    away = []
    for chunk, here in enumerate(parts_of):
        part = added(late, 0, here) + sum(p.astype(jnp.float32) for p in late_others[chunk])
        part = part + sum(p[here].astype(jnp.float32) for p in far)
        part = part.astype(jnp.bfloat16)
        if chunk == 0:
            (far, late), late_others[1] = after((far, late), late_others[1])
            part, state = after(part, state)
        else:
            away[-1], part = after(away[-1], part)
        away.append(trade(part, "batch", top))
    states.append(prefix_attend(query_rows, keys, values, 1, scale, heads, (3, 4), state))

    result = None
    fresh = []
    for chunk in range(CHUNKS):
        pieces = [piece_of(t, rows, CHUNKS + chunk, 0) for t in late]
        pieces += [piece_of(part, rows, chunk) for part in (*own_others, *near)]
        pieces.append(piece_of(away[chunk], rows, 0))
        result, new = fresh_attend(
            lengths,
            query_rows,
            *states[chunk],
            fresh,
            pieces,
            result,
            chunk,
            scale,
            heads,
            per_token,
        )
        fresh.append(new)
    result = result.reshape(token_count, group, heads, width).transpose(0, 2, 1, 3)
    return result.reshape(token_count, heads, 1, group * width)


def solution(mesh):
    def shards(tokens, key_weight, value_weight, *rest):
        prompts = mesh.shape["batch"]
        columns = 2 * math.prod(key_weight.shape[3:])
        few_tokens = prompts * tokens.shape[0] <= columns and prompts in (2, 4)
        form = reduced_shards if few_tokens else gathered_shards
        return form(tokens, key_weight, value_weight, *rest)

    return jax.shard_map(
        shards,
        mesh=mesh,
        in_specs=(
            P(("groups", "batch"), ("ctx", "head")),
            P("ctx", "head", "batch", None, None, None),
            P("ctx", "head", "batch", None, None, None),
            P(("groups", "batch"), "ctx", "head", None),
            P(("groups", "ctx"), None, None, "head", None),
            P(("groups", "batch"), None),
            P(("groups", "batch")),
        ),
        out_specs=P(("groups", "batch"), "ctx", "head", None),
        check_vma=False,
    )
```

```python
import functools
import math

import jax
import jax.numpy as jnp
from jax import lax
from jax.experimental import pallas as pl
from jax.experimental.pallas import tpu as pltpu
from jax.sharding import PartitionSpec as P

CHUNKS = 2
PART = 1024
ONES = 16
VMEM_BYTES = 16 * 1024 * 1024
MOST_VMEM_BYTES = 52 * 1024 * 1024
LONG = pl.CostEstimate(flops=2 * 10**10, bytes_accessed=1, transcendentals=0)
COSTS = {}


def cost(name):
    return COSTS.get(name, LONG)


def attend_head(query_rows, prefix, fresh_rows, length):
    token_count = query_rows.shape[0]
    head_width = prefix.shape[1] // 2
    group_size = query_rows.shape[1] // head_width
    prefix_len = prefix.shape[0]
    key_rows = jnp.concatenate([prefix[:, :head_width], fresh_rows[:, :head_width]], 0)
    value_rows = jnp.concatenate([prefix[:, head_width:], fresh_rows[:, head_width:]], 0)
    block_len = min(token_count, 64)
    pieces = []
    for first_row in range(0, token_count, block_len):
        block_rows = query_rows[first_row : first_row + block_len].reshape(
            block_len * group_size, head_width
        )
        scores = jnp.dot(
            block_rows, key_rows.T, preferred_element_type=jnp.float32
        ) * head_width ** (-0.5)
        position = first_row + jnp.arange(block_len * group_size) // group_size
        column = jnp.arange(prefix_len + token_count) - prefix_len
        allowed = column[None, :] <= position[:, None]
        scores = jnp.where(allowed, scores, -jnp.inf)
        row_max = jnp.max(scores, axis=1, keepdims=True)
        weights = jnp.exp(scores - row_max)
        row_total = jnp.sum(weights, axis=1, keepdims=True)
        probs_bf = (weights / row_total).astype(jnp.bfloat16)
        mixed_rows = jnp.dot(probs_bf, value_rows, preferred_element_type=jnp.float32)
        is_live = position < length
        mixed_rows = jnp.where(is_live[:, None], mixed_rows, 0.0)
        pieces.append(mixed_rows.astype(jnp.bfloat16).reshape(block_len, group_size * head_width))
    return jnp.concatenate(pieces, 0)


def gathered_shards(tokens, key_weight, value_weight, queries, prefix_pool, block_table, lengths):
    token_count = tokens.shape[0]
    local_heads = queries.shape[1]
    head_width = prefix_pool.shape[4] // 2
    ctx_count = lax.axis_size("ctx")
    head_count = lax.axis_size("head")
    features = lax.all_gather(tokens, ("ctx", "head"), axis=1, tiled=True)
    key_cols, value_cols = (
        lax.all_to_all(
            lax.all_to_all(weight, "ctx", split_axis=3, concat_axis=0, tiled=True),
            "head",
            split_axis=4,
            concat_axis=1,
            tiled=True,
        )
        for weight in (key_weight, value_weight)
    )
    span_len = features.shape[1] // (ctx_count * head_count)
    feature_view = features.reshape(token_count, ctx_count, head_count, span_len)
    pieces = (
        lax.all_gather(key_cols, "batch", axis=2, tiled=True),
        lax.all_gather(value_cols, "batch", axis=2, tiled=True),
    )
    row_count = pieces[0].shape[2]

    def one_term(weight_piece):
        shaped = weight_piece.reshape(ctx_count, head_count, row_count, local_heads * head_width)
        return jnp.einsum("tchr,chrk->tk", feature_view, shaped, preferred_element_type=jnp.float32)

    new_keys = one_term(pieces[0]).astype(jnp.bfloat16).reshape(token_count, local_heads, head_width)
    new_values = one_term(pieces[1]).astype(jnp.bfloat16).reshape(token_count, local_heads, head_width)
    fresh_all = jnp.concatenate([new_keys, new_values], 2)
    pool_heads = lax.all_to_all(prefix_pool, "ctx", split_axis=2, concat_axis=0, tiled=True)
    chosen = jnp.take(pool_heads, block_table[0], axis=0)
    chosen = chosen.reshape(-1, local_heads, 2 * head_width)
    outputs = [
        attend_head(
            queries[:, head_idx, 0], chosen[:, head_idx], fresh_all[:, head_idx], lengths[0]
        )
        for head_idx in range(local_heads)
    ]
    return jnp.stack(outputs, 1)[:, :, None, :]


def shift(array, axis, step):
    count = lax.axis_size(axis)
    return lax.ppermute(array, axis, [(i, (i + step) % count) for i in range(count)])


def trade(array, axis, bits):
    return lax.ppermute(array, axis, [(i, i ^ bits) for i in range(lax.axis_size(axis))])


def after(first, second):
    return lax.optimization_barrier((first, second))


def softmax_parts(scores, old_max=None):
    row_max = jnp.max(scores, axis=0, keepdims=True)
    if old_max is not None:
        row_max = jnp.maximum(row_max, old_max)
    return row_max, jnp.exp2(scores - row_max).astype(jnp.bfloat16)


def dot_queries(keys, query_block):
    return lax.dot_general(
        keys, query_block, (((1,), (1,)), ((), ())), preferred_element_type=jnp.float32
    )


def params(limit=None):
    return pltpu.CompilerParams(vmem_limit_bytes=limit or VMEM_BYTES)


def weight_kernel(ctx_count, heads, head_count, key_ref, value_ref, out_ref, flat):
    depth, slots, width = key_ref.shape
    for kind, ref in enumerate((key_ref, value_ref)):
        flat[...] = ref[...].astype(jnp.float32).reshape(depth * slots, width)
        for ctx in range(ctx_count):
            for head in range(heads):
                for core in range(head_count):
                    slot = (ctx * heads + head) * head_count + core
                    at = (kind * heads + head) * width
                    out_ref[core, ctx, :, at : at + width] = flat[
                        pl.ds(slot, depth, stride=slots), :
                    ].astype(out_ref.dtype)


def arrange_weights(key_weight, value_weight, ctx_count, heads, head_count):
    depth, width = key_weight.shape[2], key_weight.shape[5]
    slots = ctx_count * heads * head_count
    rows = min(128, depth)
    views = [w.reshape(depth, slots, width) for w in (key_weight, value_weight)]
    block = pl.BlockSpec((rows, slots, width), lambda i: (i, 0, 0))
    columns = 2 * heads * width
    return pl.pallas_call(
        functools.partial(weight_kernel, ctx_count, heads, head_count),
        grid=(depth // rows,),
        in_specs=[block, block],
        out_specs=pl.BlockSpec((head_count, ctx_count, rows, columns), lambda i: (0, 0, i, 0)),
        out_shape=jax.ShapeDtypeStruct((head_count, ctx_count, depth, columns), jnp.bfloat16),
        scratch_shapes=[pltpu.VMEM((rows * slots, width), jnp.float32)],
        compiler_params=params(),
        cost_estimate=cost("arrange_weights"),
        name="arrange_weights",
    )(*views)


def cut_kernel(bits, place_ref, tokens_ref, *refs):
    pieces, sems = refs[:-1], refs[-1]
    depth = pieces[0].shape[1]
    copies = []
    for index, piece in enumerate(pieces):
        start = pl.multiple_of((place_ref[0] ^ bits[index]) * depth, depth)
        source = tokens_ref.at[:, pl.ds(start, depth)]
        copies.append(pltpu.make_async_copy(source, piece, sems.at[index]))
    for copy in copies:
        copy.start()
    for copy in copies:
        copy.wait()


def cut_tokens(place, tokens, depth, bits):
    far = pl.BlockSpec(memory_space=pltpu.HBM)
    piece = jax.ShapeDtypeStruct((tokens.shape[0], depth), tokens.dtype)
    return pl.pallas_call(
        functools.partial(cut_kernel, bits),
        grid_spec=pltpu.PrefetchScalarGridSpec(
            num_scalar_prefetch=1,
            grid=(1,),
            in_specs=[far],
            out_specs=[pl.BlockSpec(piece.shape, lambda i, place: (0, 0))] * len(bits),
            scratch_shapes=[pltpu.SemaphoreType.DMA((len(bits),))],
        ),
        out_shape=[piece] * len(bits),
        compiler_params=params(MOST_VMEM_BYTES),
        cost_estimate=cost("cut_tokens"),
        name="cut_tokens",
    )(place, tokens)


def pool_kernel(ctx_count, heads, place_ref, pool_ref, *refs):
    outs, flat = refs[:-1], refs[-1]
    some, length, slots, width = pool_ref.shape
    length *= some
    flat[...] = pool_ref[...].astype(jnp.float32).reshape(length * slots, width)
    for kind in range(2):
        for head in range(heads):
            at = (kind * heads + head) * width
            held = []
            for ctx in range(ctx_count):
                slot = (kind * ctx_count + ctx) * heads + head
                held.append(flat[pl.ds(slot, length, stride=slots), :])
            for step, out_ref in enumerate(outs):
                target = lax.rem(place_ref[1] + step, ctx_count)
                value = held[0]
                for ctx in range(1, ctx_count):
                    value = jnp.where(target == ctx, held[ctx], value)
                out_ref[:, :, at : at + width] = value.astype(out_ref.dtype).reshape(
                    some, length // some, width
                )


def arrange_pool(place, prefix_pool, ctx_count, heads):
    blocks, length, all_heads, _, double = prefix_pool.shape
    width = double // 2
    slots = 2 * all_heads
    view = prefix_pool.reshape(blocks, length, all_heads, 2, width)
    view = view.transpose(0, 1, 3, 2, 4).reshape(blocks, length, slots, width)
    columns = 2 * heads * width
    some = 2 if blocks % 2 == 0 else 1
    out = pl.BlockSpec((some, length, columns), lambda i, place: (i, 0, 0))
    return pl.pallas_call(
        functools.partial(pool_kernel, ctx_count, heads),
        grid_spec=pltpu.PrefetchScalarGridSpec(
            num_scalar_prefetch=1,
            grid=(blocks // some,),
            in_specs=[pl.BlockSpec((some, length, slots, width), lambda i, place: (i, 0, 0, 0))],
            out_specs=[out] * ctx_count,
            scratch_shapes=[pltpu.VMEM((some * length * slots, width), jnp.float32)],
        ),
        out_shape=[jax.ShapeDtypeStruct((blocks, length, columns), jnp.bfloat16)] * ctx_count,
        compiler_params=params(),
        cost_estimate=cost("arrange_pool"),
        name="arrange_pool",
    )(place, view)


def total_of(refs):
    return sum(ref[...].astype(jnp.float32).reshape(ref.shape[-2:]) for ref in refs)


def put_sums(terms, counts, sum_refs):
    at = 0
    for count, sum_ref in zip(counts, sum_refs):
        sum_ref[...] = total_of(terms[at : at + count]).astype(sum_ref.dtype)
        at += count


def project_kernel(block_count, term_counts, place_ref, *refs):
    token_refs, weight_ref = refs[:block_count], refs[block_count]
    terms = refs[block_count + 1 : block_count + 1 + sum(term_counts)]
    out_ref, *sum_refs = refs[block_count + 1 + sum(term_counts) : -1]
    stacked = refs[-1]

    @pl.when(pl.program_id(0) == 0)
    def _():
        at = 0
        for token_ref in token_refs:
            rows = token_ref.shape[0]
            stacked[at : at + rows, :] = token_ref[...]
            at += rows
        put_sums(terms, term_counts, sum_refs)

    out_ref[0] = jnp.dot(
        stacked[...], weight_ref[0, 0], preferred_element_type=jnp.float32
    ).astype(out_ref.dtype)


def piece_of(array, *index):
    rows, block, *leading = index
    shape = (1,) * len(leading) + (rows, array.shape[-1])
    return array, pl.BlockSpec(shape, lambda j, *_: (*leading, block, 0))


def project(place, blocks, weights, head_step, out_dtype, name, sums=()):
    head_count, ctx_count, depth, width = weights.shape
    row_total = sum(block.shape[0] for block in blocks)

    def block_spec(block):
        if block.shape[1] == depth:
            return pl.BlockSpec(block.shape, lambda j, place: (0, 0))
        return pl.BlockSpec((block.shape[0], depth), lambda j, place: (0, place[0]))

    pieces = [piece for terms in sums for piece in terms]
    sum_shapes = [terms[0][1].block_shape[-2:] for terms in sums]
    result = pl.pallas_call(
        functools.partial(project_kernel, len(blocks), [len(terms) for terms in sums]),
        grid_spec=pltpu.PrefetchScalarGridSpec(
            num_scalar_prefetch=1,
            grid=(ctx_count,),
            in_specs=[block_spec(block) for block in blocks]
            + [
                pl.BlockSpec(
                    (1, 1, depth, width),
                    lambda j, place: (
                        lax.rem(place[2] + head_step, head_count),
                        lax.rem(place[1] + j, ctx_count),
                        0,
                        0,
                    ),
                )
            ]
            + [spec for _, spec in pieces],
            out_specs=[pl.BlockSpec((1, row_total, width), lambda j, place: (j, 0, 0))]
            + [pl.BlockSpec(shape, lambda j, place: (0, 0)) for shape in sum_shapes],
            scratch_shapes=[pltpu.VMEM((row_total, depth), weights.dtype)],
        ),
        out_shape=[jax.ShapeDtypeStruct((ctx_count, row_total, width), out_dtype)]
        + [jax.ShapeDtypeStruct(shape, jnp.bfloat16) for shape in sum_shapes],
        compiler_params=params(),
        cost_estimate=cost(name),
        name=name,
    )(place, *blocks, weights, *(array for array, _ in pieces))
    return result if sums else result[0]


def pick_kernel(heads, ctx_count, place_ref, table_ref, *refs):
    pool_refs, (keys, values) = refs[:ctx_count], refs[ctx_count:]
    blocks, length, columns = pool_refs[0].shape
    wide = columns // 2
    width = wide // heads
    values[...] = jnp.ones_like(values)
    for at in range(table_ref.shape[0]):
        entry = table_ref[at]
        here = slice(at * length, (at + 1) * length)
        step = lax.rem(place_ref[1] - entry // blocks + ctx_count, ctx_count)
        for ctx_step, pool_ref in enumerate(pool_refs):

            @pl.when(step == ctx_step)
            def _():
                block = pool_ref[entry % blocks]
                keys[here, :] = block[:, :wide]
                put_values(values, here, block[:, wide:], heads)


def put_values(values, here, block, heads):
    width = block.shape[1] // heads
    for head in range(heads):
        low = head * (width + ONES)
        values[low : low + width, here] = (
            block[:, head * width : (head + 1) * width].astype(jnp.float32).T.astype(jnp.bfloat16)
        )


def pick_blocks(place, table, pools, heads):
    length, columns = pools[0].shape[1:]
    count = table.shape[0] * length
    wide = columns // 2
    tall = wide + heads * ONES
    return pl.pallas_call(
        functools.partial(pick_kernel, heads, len(pools)),
        grid_spec=pltpu.PrefetchScalarGridSpec(
            num_scalar_prefetch=2,
            grid=(1,),
            in_specs=[pl.BlockSpec(p.shape, lambda i, *_: (0, 0, 0)) for p in pools],
            out_specs=[
                pl.BlockSpec((count, wide), lambda i, *_: (0, 0)),
                pl.BlockSpec((tall, count), lambda i, *_: (0, 0)),
            ],
        ),
        out_shape=[
            jax.ShapeDtypeStruct((count, wide), jnp.bfloat16),
            jax.ShapeDtypeStruct((tall, count), jnp.bfloat16),
        ],
        compiler_params=params(),
        cost_estimate=cost("pick_blocks"),
        name="pick_blocks",
    )(place, table, *pools)


def each_part(rows, heads):
    part_rows = min(PART, rows)
    each = part_rows // heads
    for low in range(0, rows, part_rows):
        for head in range(heads):
            at = low + head * each
            yield head, pl.ds(low + head, each, stride=heads), slice(at, at + each)


def prefix_kernel(scale, heads, term_counts, held, query_ref, keys, values, *refs):
    terms = refs[held : held + sum(term_counts)]
    acc_ref, stat_ref, *sum_refs, flat = refs[held + sum(term_counts) :]
    rows, width = query_ref.shape
    tall = width + ONES
    half = stat_ref.shape[0] // 2

    @pl.when(pl.program_id(0) == 0)
    def _():
        put_sums(terms, term_counts, sum_refs)

    flat[...] = query_ref[...].astype(jnp.float32)
    for head, taken, here in each_part(rows, heads):
        query_block = flat[taken, :].astype(jnp.bfloat16)
        scores = dot_queries(keys[:, head * width : (head + 1) * width], query_block) * scale
        row_max, weights = softmax_parts(scores)
        mixed = jnp.dot(
            values[head * tall : (head + 1) * tall, :], weights, preferred_element_type=jnp.float32
        )
        acc_ref[:, here] = mixed[:width]
        stat_ref[:half, here] = jnp.broadcast_to(row_max, (half, row_max.shape[1]))
        stat_ref[half:, here] = jnp.broadcast_to(mixed[width : width + 1], (half, row_max.shape[1]))


def prefix_attend(
    query_rows, keys, values, chunk, scale, heads, part=(0, 1), state=None, sums=()
):
    all_rows, width = query_rows.shape
    row_total = all_rows // CHUNKS
    at, count = part
    rows = min(2048, row_total // count)
    steps = row_total // rows // count
    first = chunk * count * steps + at * steps
    out_specs = [
        pl.BlockSpec((width, rows), lambda i: (0, at * steps + i)),
        pl.BlockSpec((8, rows), lambda i: (0, at * steps + i)),
    ]
    in_specs = [
        pl.BlockSpec((rows, width), lambda i: (first + i, 0)),
        pl.BlockSpec(keys.shape, lambda i: (0, 0)),
        pl.BlockSpec(values.shape, lambda i: (0, 0)),
    ]
    operands = [query_rows, keys, values]
    aliases = {}
    if state is not None:
        in_specs += [pl.BlockSpec(memory_space=pl.ANY)] * 2
        operands += list(state)
        aliases = {3: 0, 4: 1}
    pieces = [piece for terms in sums for piece in terms]
    sum_shapes = [terms[0][1].block_shape[-2:] for terms in sums]
    in_specs += [spec for _, spec in pieces]
    operands += [array for array, _ in pieces]
    out_specs += [pl.BlockSpec(shape, lambda i: (0, 0)) for shape in sum_shapes]
    acc, stat, *made = pl.pallas_call(
        functools.partial(
            prefix_kernel, scale, heads, [len(terms) for terms in sums], len(aliases)
        ),
        grid=(steps,),
        in_specs=in_specs,
        out_specs=out_specs,
        out_shape=[
            jax.ShapeDtypeStruct((width, row_total), jnp.float32),
            jax.ShapeDtypeStruct((8, row_total), jnp.float32),
        ]
        + [jax.ShapeDtypeStruct(shape, jnp.bfloat16) for shape in sum_shapes],
        input_output_aliases=aliases,
        scratch_shapes=[pltpu.VMEM((rows, width), jnp.float32)],
        compiler_params=params(),
        cost_estimate=cost("prefix_attend"),
        name="prefix_attend",
    )(*operands)
    return ([acc, stat], made) if sums else [acc, stat]


def fresh_kernel(
    scale, heads, per_token, first_row, counts, length_ref, query_ref, acc_ref, stat_ref, *rest
):
    early_count, term_count = counts
    earlier, terms = rest[:early_count], rest[early_count : early_count + term_count]
    out_ref, fresh_ref, keys, values, flat, mixed_rows = rest[-6:]
    rows, width = query_ref.shape
    wide, tall = heads * width, width + ONES
    step = pl.program_id(0)

    @pl.when(step == 0)
    def _():
        values[...] = jnp.ones_like(values)
        fresh_ref[...] = total_of(terms).astype(fresh_ref.dtype)
        for index, ref in enumerate([*earlier, fresh_ref]):
            here = slice(index * ref.shape[0], (index + 1) * ref.shape[0])
            fresh = ref[...]
            keys[here, :] = fresh[:, :wide]
            put_values(values, here, fresh[:, wide:], heads)

    half = stat_ref.shape[0] // 2
    flat[...] = query_ref[...].astype(jnp.float32)
    for head, taken, here in each_part(rows, heads):
        query_block = flat[taken, :].astype(jnp.bfloat16)
        scores = dot_queries(keys[:, head * width : (head + 1) * width], query_block) * scale
        row = taken.start + heads * lax.broadcasted_iota(jnp.int32, (1, taken.size), 1)
        token = first_row + step * (rows // per_token) + (
            row // per_token if per_token & (per_token - 1) else row >> (per_token.bit_length() - 1)
        )
        key_at = lax.broadcasted_iota(jnp.int32, scores.shape, 0)
        scores = jnp.where(key_at <= token, scores, -jnp.inf)
        old_max, old_total = stat_ref[:1, here], stat_ref[half : half + 1, here]
        row_max, weights = softmax_parts(scores, old_max)
        fade = jnp.exp2(old_max - row_max)
        mixed = jnp.dot(
            values[head * tall : (head + 1) * tall, :], weights, preferred_element_type=jnp.float32
        )
        row_total = old_total * fade + mixed[width : width + 1]
        share = jnp.where(token < length_ref[0], 1.0 / row_total, 0.0)
        result = acc_ref[:, here] * (fade * share) + mixed[:width] * share
        mixed_rows[taken, :] = result.T
    out_ref[...] = mixed_rows[...].astype(out_ref.dtype)


def fresh_attend(
    length, query_rows, acc, stat, earlier, pieces, result, chunk, scale, heads, per_token
):
    row_total, width = query_rows.shape
    chunk_rows = row_total // CHUNKS
    rows = min(2048, chunk_rows)
    steps = chunk_rows // rows
    block = pl.BlockSpec((rows, width), lambda i, length: (chunk * steps + i, 0))
    fresh_shape = pieces[0][1].block_shape[-2:]
    key_count = (len(earlier) + 1) * fresh_shape[0]
    whole = pl.BlockSpec(fresh_shape, lambda i, length: (0, 0))
    in_specs = [
        block,
        pl.BlockSpec((width, rows), lambda i, length: (0, i)),
        pl.BlockSpec((stat.shape[0], rows), lambda i, length: (0, i)),
        *(whole for _ in earlier),
        *(spec for _, spec in pieces),
    ]
    operands = [length, query_rows, acc, stat, *earlier, *(array for array, _ in pieces)]
    aliases = {}
    if result is not None:
        in_specs.append(pl.BlockSpec(memory_space=pl.ANY))
        aliases = {len(operands): 0}
        operands.append(result)
    return pl.pallas_call(
        functools.partial(
            fresh_kernel,
            scale,
            heads,
            per_token,
            chunk * (chunk_rows // per_token),
            (len(earlier), len(pieces)),
        ),
        grid_spec=pltpu.PrefetchScalarGridSpec(
            num_scalar_prefetch=1,
            grid=(steps,),
            in_specs=in_specs,
            out_specs=[block, whole],
            scratch_shapes=[
                pltpu.VMEM((key_count, heads * width), jnp.bfloat16),
                pltpu.VMEM((heads * (width + ONES), key_count), jnp.bfloat16),
                pltpu.VMEM((rows, width), jnp.float32),
                pltpu.VMEM((rows, width), jnp.float32),
            ],
        ),
        out_shape=[
            jax.ShapeDtypeStruct((row_total, width), jnp.bfloat16),
            jax.ShapeDtypeStruct(fresh_shape, jnp.bfloat16),
        ],
        input_output_aliases=aliases,
        compiler_params=params(),
        cost_estimate=cost("fresh_attend"),
        name="fresh_attend",
    )(*operands)


def reduced_shards(tokens, key_weight, value_weight, queries, prefix_pool, block_table, lengths):
    batch_count = lax.axis_size("batch")
    ctx_count = lax.axis_size("ctx")
    head_count = lax.axis_size("head")
    batch_at, ctx_at, head_at = (lax.axis_index(a) for a in ("batch", "ctx", "head"))
    place = jnp.stack([batch_at, ctx_at, head_at]).astype(jnp.int32)
    token_count = tokens.shape[0]
    heads = queries.shape[1]
    width = prefix_pool.shape[4] // 2
    group = queries.shape[3] // width
    per_token = heads * group
    depth = key_weight.shape[2]
    rows = token_count // CHUNKS
    scale = math.log2(math.e) / math.sqrt(width)

    top = batch_count // 2
    steps = list(range(batch_count - 1, top, -1)) + list(range(1, top))
    pieces = cut_tokens(place, tokens, depth, [*steps, top])
    pieces, prefix_pool = after(pieces, prefix_pool)
    arrived = [trade(piece, "batch", bits) for piece, bits in zip(pieces, steps)]
    pools = arrange_pool(place, prefix_pool, ctx_count, heads)
    pools, (key_weight, value_weight) = after(pools, (key_weight, value_weight))
    pools = [shift(part, "ctx", step) if step else part for step, part in enumerate(pools)]

    weights = arrange_weights(key_weight, value_weight, ctx_count, heads, head_count)
    weights, last = after(weights, pieces[-1])
    last = trade(last, "batch", top)

    query_rows = queries.reshape(token_count, heads, group, width)
    query_rows = query_rows.transpose(0, 2, 1, 3).reshape(-1, width)
    def projected(blocks, name):
        terms = [
            shift(project(place, blocks, weights, step, jnp.bfloat16, name + "_away"), "head", step)
            for step in range(1, head_count)
        ]
        return [project(place, blocks, weights, 0, jnp.float32, name + "_kept"), *terms]

    def added(terms, step, here):
        return sum(term[step, here].astype(jnp.float32) for term in terms)

    def others(terms, here):
        return [added(terms, step, here).astype(jnp.bfloat16) for step in range(1, ctx_count)]

    def spread(parts):
        return [shift(part, "ctx", step + 1) for step, part in enumerate(parts)]

    every = slice(None)
    parts_of = [slice(i * rows, (i + 1) * rows) for i in range(CHUNKS)]

    sums = [[], []]
    if steps:
        early = projected(arrived, "early")
        cuts = [slice(i * token_count, (i + 1) * token_count) for i in range(len(steps))]
        leaving = [others(early, cut) for cut in cuts]
        leaving, pools = after(leaving, pools)
        sums = [
            [
                [piece_of(t, token_count, i, 0) for t in early]
                + [piece_of(p, token_count, 0) for p in spread(parts)]
            ]
            for i, parts in enumerate(leaving)
        ]
    keys, values = pick_blocks(place, block_table[0], pools, heads)
    states = [prefix_attend(query_rows, keys, values, 0, scale, heads)]
    state, far = prefix_attend(
        query_rows, keys, values, 1, scale, heads, (0, 2), None, sums[0]
    )
    far = [trade(part, "batch", 1) for part in far]
    (states[0], state), last = after((states[0], state), last)

    def late_project(step, dtype, name, sums):
        result = project(place, [last, tokens], weights, step, dtype, name, sums)
        return result if sums else (result,)

    terms, near = [], []
    for step in range(1, head_count):
        term, *made = late_project(step, jnp.bfloat16, "late_away", sums[1] if step == 1 else [])
        near += [trade(part, "batch", 1) for part in made]
        terms.append(shift(term, "head", step))
    kept, *_ = late_project(0, jnp.float32, "late_kept", [])
    late = [kept, *terms]
    own_at = slice(token_count, 2 * token_count)
    *late_others, own_others = [others(late, here) for here in [*parts_of, own_at]]
    late_others[0] = spread(late_others[0])
    late_others[1], (keys, values) = after(late_others[1], (keys, values))
    state = prefix_attend(query_rows, keys, values, 1, scale, heads, (2, 4), state)
    state, (late_others[1], own_others) = after(state, (late_others[1], own_others))
    late_others[1], own_others = spread(late_others[1]), spread(own_others)

    away = []
    for chunk, here in enumerate(parts_of):
        part = added(late, 0, here) + sum(p.astype(jnp.float32) for p in late_others[chunk])
        part = part + sum(p[here].astype(jnp.float32) for p in far)
        part = part.astype(jnp.bfloat16)
        if chunk == 0:
            (far, late), late_others[1] = after((far, late), late_others[1])
            part, state = after(part, state)
        else:
            away[-1], part = after(away[-1], part)
        away.append(trade(part, "batch", top))
    states.append(prefix_attend(query_rows, keys, values, 1, scale, heads, (3, 4), state))

    result = None
    fresh = []
    for chunk in range(CHUNKS):
        pieces = [piece_of(t, rows, CHUNKS + chunk, 0) for t in late]
        pieces += [piece_of(part, rows, chunk) for part in (*own_others, *near)]
        pieces.append(piece_of(away[chunk], rows, 0))
        result, new = fresh_attend(
            lengths,
            query_rows,
            *states[chunk],
            fresh,
            pieces,
            result,
            chunk,
            scale,
            heads,
            per_token,
        )
        fresh.append(new)
    result = result.reshape(token_count, group, heads, width).transpose(0, 2, 1, 3)
    return result.reshape(token_count, heads, 1, group * width)


def solution(mesh):
    def shards(tokens, key_weight, value_weight, *rest):
        prompts = mesh.shape["batch"]
        columns = 2 * math.prod(key_weight.shape[3:])
        few_tokens = prompts * tokens.shape[0] <= columns and prompts in (2, 4)
        form = reduced_shards if few_tokens else gathered_shards
        return form(tokens, key_weight, value_weight, *rest)

    return jax.shard_map(
        shards,
        mesh=mesh,
        in_specs=(
            P(("groups", "batch"), ("ctx", "head")),
            P("ctx", "head", "batch", None, None, None),
            P("ctx", "head", "batch", None, None, None),
            P(("groups", "batch"), "ctx", "head", None),
            P(("groups", "ctx"), None, None, "head", None),
            P(("groups", "batch"), None),
            P(("groups", "batch")),
        ),
        out_specs=P(("groups", "batch"), "ctx", "head", None),
        check_vma=False,
    )
```

```python
import functools
import math

import jax
import jax.numpy as jnp
from jax import lax
from jax.experimental import pallas as pl
from jax.experimental.pallas import tpu as pltpu
from jax.sharding import PartitionSpec as P

CHUNKS = 2
PART = 1024
ONES = 16
VMEM_BYTES = 16 * 1024 * 1024
MOST_VMEM_BYTES = 52 * 1024 * 1024
LONG = pl.CostEstimate(flops=2 * 10**10, bytes_accessed=1, transcendentals=0)
COSTS = {}


def cost(name):
    return COSTS.get(name, LONG)


def attend_head(query_rows, prefix, fresh_rows, length):
    token_count = query_rows.shape[0]
    head_width = prefix.shape[1] // 2
    group_size = query_rows.shape[1] // head_width
    prefix_len = prefix.shape[0]
    key_rows = jnp.concatenate([prefix[:, :head_width], fresh_rows[:, :head_width]], 0)
    value_rows = jnp.concatenate([prefix[:, head_width:], fresh_rows[:, head_width:]], 0)
    block_len = min(token_count, 64)
    pieces = []
    for first_row in range(0, token_count, block_len):
        block_rows = query_rows[first_row : first_row + block_len].reshape(
            block_len * group_size, head_width
        )
        scores = jnp.dot(
            block_rows, key_rows.T, preferred_element_type=jnp.float32
        ) * head_width ** (-0.5)
        position = first_row + jnp.arange(block_len * group_size) // group_size
        column = jnp.arange(prefix_len + token_count) - prefix_len
        allowed = column[None, :] <= position[:, None]
        scores = jnp.where(allowed, scores, -jnp.inf)
        row_max = jnp.max(scores, axis=1, keepdims=True)
        weights = jnp.exp(scores - row_max)
        row_total = jnp.sum(weights, axis=1, keepdims=True)
        probs_bf = (weights / row_total).astype(jnp.bfloat16)
        mixed_rows = jnp.dot(probs_bf, value_rows, preferred_element_type=jnp.float32)
        is_live = position < length
        mixed_rows = jnp.where(is_live[:, None], mixed_rows, 0.0)
        pieces.append(mixed_rows.astype(jnp.bfloat16).reshape(block_len, group_size * head_width))
    return jnp.concatenate(pieces, 0)


def gathered_shards(tokens, key_weight, value_weight, queries, prefix_pool, block_table, lengths):
    token_count = tokens.shape[0]
    local_heads = queries.shape[1]
    head_width = prefix_pool.shape[4] // 2
    ctx_count = lax.axis_size("ctx")
    head_count = lax.axis_size("head")
    features = lax.all_gather(tokens, ("ctx", "head"), axis=1, tiled=True)
    key_cols, value_cols = (
        lax.all_to_all(
            lax.all_to_all(weight, "ctx", split_axis=3, concat_axis=0, tiled=True),
            "head",
            split_axis=4,
            concat_axis=1,
            tiled=True,
        )
        for weight in (key_weight, value_weight)
    )
    span_len = features.shape[1] // (ctx_count * head_count)
    feature_view = features.reshape(token_count, ctx_count, head_count, span_len)
    pieces = (
        lax.all_gather(key_cols, "batch", axis=2, tiled=True),
        lax.all_gather(value_cols, "batch", axis=2, tiled=True),
    )
    row_count = pieces[0].shape[2]

    def one_term(weight_piece):
        shaped = weight_piece.reshape(ctx_count, head_count, row_count, local_heads * head_width)
        return jnp.einsum("tchr,chrk->tk", feature_view, shaped, preferred_element_type=jnp.float32)

    new_keys = one_term(pieces[0]).astype(jnp.bfloat16).reshape(token_count, local_heads, head_width)
    new_values = one_term(pieces[1]).astype(jnp.bfloat16).reshape(token_count, local_heads, head_width)
    fresh_all = jnp.concatenate([new_keys, new_values], 2)
    pool_heads = lax.all_to_all(prefix_pool, "ctx", split_axis=2, concat_axis=0, tiled=True)
    chosen = jnp.take(pool_heads, block_table[0], axis=0)
    chosen = chosen.reshape(-1, local_heads, 2 * head_width)
    outputs = [
        attend_head(
            queries[:, head_idx, 0], chosen[:, head_idx], fresh_all[:, head_idx], lengths[0]
        )
        for head_idx in range(local_heads)
    ]
    return jnp.stack(outputs, 1)[:, :, None, :]


def shift(array, axis, step):
    count = lax.axis_size(axis)
    return lax.ppermute(array, axis, [(i, (i + step) % count) for i in range(count)])


def trade(array, axis, bits):
    return lax.ppermute(array, axis, [(i, i ^ bits) for i in range(lax.axis_size(axis))])


def after(first, second):
    return lax.optimization_barrier((first, second))


def softmax_parts(scores, old_max=None):
    row_max = jnp.max(scores, axis=0, keepdims=True)
    if old_max is not None:
        row_max = jnp.maximum(row_max, old_max)
    return row_max, jnp.exp2(scores - row_max).astype(jnp.bfloat16)


def dot_queries(keys, query_block):
    return lax.dot_general(
        keys, query_block, (((1,), (1,)), ((), ())), preferred_element_type=jnp.float32
    )


def params(limit=None):
    return pltpu.CompilerParams(vmem_limit_bytes=limit or VMEM_BYTES)


def weight_kernel(ctx_count, heads, head_count, key_ref, value_ref, out_ref, flat):
    depth, slots, width = key_ref.shape
    for kind, ref in enumerate((key_ref, value_ref)):
        flat[...] = ref[...].astype(jnp.float32).reshape(depth * slots, width)
        for ctx in range(ctx_count):
            for head in range(heads):
                for core in range(head_count):
                    slot = (ctx * heads + head) * head_count + core
                    at = (kind * heads + head) * width
                    out_ref[core, ctx, :, at : at + width] = flat[
                        pl.ds(slot, depth, stride=slots), :
                    ].astype(out_ref.dtype)


def arrange_weights(key_weight, value_weight, ctx_count, heads, head_count):
    depth, width = key_weight.shape[2], key_weight.shape[5]
    slots = ctx_count * heads * head_count
    rows = min(128, depth)
    views = [w.reshape(depth, slots, width) for w in (key_weight, value_weight)]
    block = pl.BlockSpec((rows, slots, width), lambda i: (i, 0, 0))
    columns = 2 * heads * width
    return pl.pallas_call(
        functools.partial(weight_kernel, ctx_count, heads, head_count),
        grid=(depth // rows,),
        in_specs=[block, block],
        out_specs=pl.BlockSpec((head_count, ctx_count, rows, columns), lambda i: (0, 0, i, 0)),
        out_shape=jax.ShapeDtypeStruct((head_count, ctx_count, depth, columns), jnp.bfloat16),
        scratch_shapes=[pltpu.VMEM((rows * slots, width), jnp.float32)],
        compiler_params=params(),
        cost_estimate=cost("arrange_weights"),
        name="arrange_weights",
    )(*views)


def cut_kernel(bits, place_ref, tokens_ref, *refs):
    pieces, sems = refs[:-1], refs[-1]
    depth = pieces[0].shape[1]
    copies = []
    for index, piece in enumerate(pieces):
        start = pl.multiple_of((place_ref[0] ^ bits[index]) * depth, depth)
        source = tokens_ref.at[:, pl.ds(start, depth)]
        copies.append(pltpu.make_async_copy(source, piece, sems.at[index]))
    for copy in copies:
        copy.start()
    for copy in copies:
        copy.wait()


def cut_tokens(place, tokens, depth, bits):
    far = pl.BlockSpec(memory_space=pltpu.HBM)
    piece = jax.ShapeDtypeStruct((tokens.shape[0], depth), tokens.dtype)
    return pl.pallas_call(
        functools.partial(cut_kernel, bits),
        grid_spec=pltpu.PrefetchScalarGridSpec(
            num_scalar_prefetch=1,
            grid=(1,),
            in_specs=[far],
            out_specs=[pl.BlockSpec(piece.shape, lambda i, place: (0, 0))] * len(bits),
            scratch_shapes=[pltpu.SemaphoreType.DMA((len(bits),))],
        ),
        out_shape=[piece] * len(bits),
        compiler_params=params(MOST_VMEM_BYTES),
        cost_estimate=cost("cut_tokens"),
        name="cut_tokens",
    )(place, tokens)


def pool_kernel(ctx_count, heads, place_ref, pool_ref, *refs):
    outs, flat = refs[:-1], refs[-1]
    some, length, slots, width = pool_ref.shape
    length *= some
    flat[...] = pool_ref[...].astype(jnp.float32).reshape(length * slots, width)
    for kind in range(2):
        for head in range(heads):
            at = (kind * heads + head) * width
            held = []
            for ctx in range(ctx_count):
                slot = (kind * ctx_count + ctx) * heads + head
                held.append(flat[pl.ds(slot, length, stride=slots), :])
            for step, out_ref in enumerate(outs):
                target = lax.rem(place_ref[1] + step, ctx_count)
                value = held[0]
                for ctx in range(1, ctx_count):
                    value = jnp.where(target == ctx, held[ctx], value)
                out_ref[:, :, at : at + width] = value.astype(out_ref.dtype).reshape(
                    some, length // some, width
                )


def arrange_pool(place, prefix_pool, ctx_count, heads):
    blocks, length, all_heads, _, double = prefix_pool.shape
    width = double // 2
    slots = 2 * all_heads
    view = prefix_pool.reshape(blocks, length, all_heads, 2, width)
    view = view.transpose(0, 1, 3, 2, 4).reshape(blocks, length, slots, width)
    columns = 2 * heads * width
    some = 2 if blocks % 2 == 0 else 1
    out = pl.BlockSpec((some, length, columns), lambda i, place: (i, 0, 0))
    return pl.pallas_call(
        functools.partial(pool_kernel, ctx_count, heads),
        grid_spec=pltpu.PrefetchScalarGridSpec(
            num_scalar_prefetch=1,
            grid=(blocks // some,),
            in_specs=[pl.BlockSpec((some, length, slots, width), lambda i, place: (i, 0, 0, 0))],
            out_specs=[out] * ctx_count,
            scratch_shapes=[pltpu.VMEM((some * length * slots, width), jnp.float32)],
        ),
        out_shape=[jax.ShapeDtypeStruct((blocks, length, columns), jnp.bfloat16)] * ctx_count,
        compiler_params=params(),
        cost_estimate=cost("arrange_pool"),
        name="arrange_pool",
    )(place, view)


def total_of(refs):
    return sum(ref[...].astype(jnp.float32).reshape(ref.shape[-2:]) for ref in refs)


def put_sums(terms, counts, sum_refs):
    at = 0
    for count, sum_ref in zip(counts, sum_refs):
        sum_ref[...] = total_of(terms[at : at + count]).astype(sum_ref.dtype)
        at += count


def project_kernel(block_count, term_counts, place_ref, *refs):
    token_refs, weight_ref = refs[:block_count], refs[block_count]
    terms = refs[block_count + 1 : block_count + 1 + sum(term_counts)]
    out_ref, *sum_refs = refs[block_count + 1 + sum(term_counts) : -1]
    stacked = refs[-1]

    @pl.when(pl.program_id(0) == 0)
    def _():
        at = 0
        for token_ref in token_refs:
            rows = token_ref.shape[0]
            stacked[at : at + rows, :] = token_ref[...]
            at += rows
        put_sums(terms, term_counts, sum_refs)

    out_ref[0] = jnp.dot(
        stacked[...], weight_ref[0, 0], preferred_element_type=jnp.float32
    ).astype(out_ref.dtype)


def piece_of(array, *index):
    rows, block, *leading = index
    shape = (1,) * len(leading) + (rows, array.shape[-1])
    return array, pl.BlockSpec(shape, lambda j, *_: (*leading, block, 0))


def project(place, blocks, weights, head_step, out_dtype, name, sums=()):
    head_count, ctx_count, depth, width = weights.shape
    row_total = sum(block.shape[0] for block in blocks)

    def block_spec(block):
        if block.shape[1] == depth:
            return pl.BlockSpec(block.shape, lambda j, place: (0, 0))
        return pl.BlockSpec((block.shape[0], depth), lambda j, place: (0, place[0]))

    pieces = [piece for terms in sums for piece in terms]
    sum_shapes = [terms[0][1].block_shape[-2:] for terms in sums]
    result = pl.pallas_call(
        functools.partial(project_kernel, len(blocks), [len(terms) for terms in sums]),
        grid_spec=pltpu.PrefetchScalarGridSpec(
            num_scalar_prefetch=1,
            grid=(ctx_count,),
            in_specs=[block_spec(block) for block in blocks]
            + [
                pl.BlockSpec(
                    (1, 1, depth, width),
                    lambda j, place: (
                        lax.rem(place[2] + head_step, head_count),
                        lax.rem(place[1] + j, ctx_count),
                        0,
                        0,
                    ),
                )
            ]
            + [spec for _, spec in pieces],
            out_specs=[pl.BlockSpec((1, row_total, width), lambda j, place: (j, 0, 0))]
            + [pl.BlockSpec(shape, lambda j, place: (0, 0)) for shape in sum_shapes],
            scratch_shapes=[pltpu.VMEM((row_total, depth), weights.dtype)],
        ),
        out_shape=[jax.ShapeDtypeStruct((ctx_count, row_total, width), out_dtype)]
        + [jax.ShapeDtypeStruct(shape, jnp.bfloat16) for shape in sum_shapes],
        compiler_params=params(),
        cost_estimate=cost(name),
        name=name,
    )(place, *blocks, weights, *(array for array, _ in pieces))
    return result if sums else result[0]


def pick_kernel(heads, ctx_count, place_ref, table_ref, *refs):
    pool_refs, (keys, values) = refs[:ctx_count], refs[ctx_count:]
    blocks, length, columns = pool_refs[0].shape
    wide = columns // 2
    width = wide // heads
    values[...] = jnp.ones_like(values)
    for at in range(table_ref.shape[0]):
        entry = table_ref[at]
        here = slice(at * length, (at + 1) * length)
        step = lax.rem(place_ref[1] - entry // blocks + ctx_count, ctx_count)
        for ctx_step, pool_ref in enumerate(pool_refs):

            @pl.when(step == ctx_step)
            def _():
                block = pool_ref[entry % blocks]
                keys[here, :] = block[:, :wide]
                put_values(values, here, block[:, wide:], heads)


def put_values(values, here, block, heads):
    width = block.shape[1] // heads
    for head in range(heads):
        low = head * (width + ONES)
        values[low : low + width, here] = (
            block[:, head * width : (head + 1) * width].astype(jnp.float32).T.astype(jnp.bfloat16)
        )


def pick_blocks(place, table, pools, heads):
    length, columns = pools[0].shape[1:]
    count = table.shape[0] * length
    wide = columns // 2
    tall = wide + heads * ONES
    return pl.pallas_call(
        functools.partial(pick_kernel, heads, len(pools)),
        grid_spec=pltpu.PrefetchScalarGridSpec(
            num_scalar_prefetch=2,
            grid=(1,),
            in_specs=[pl.BlockSpec(p.shape, lambda i, *_: (0, 0, 0)) for p in pools],
            out_specs=[
                pl.BlockSpec((count, wide), lambda i, *_: (0, 0)),
                pl.BlockSpec((tall, count), lambda i, *_: (0, 0)),
            ],
        ),
        out_shape=[
            jax.ShapeDtypeStruct((count, wide), jnp.bfloat16),
            jax.ShapeDtypeStruct((tall, count), jnp.bfloat16),
        ],
        compiler_params=params(),
        cost_estimate=cost("pick_blocks"),
        name="pick_blocks",
    )(place, table, *pools)


def each_part(rows, heads):
    part_rows = min(PART, rows)
    each = part_rows // heads
    for low in range(0, rows, part_rows):
        for head in range(heads):
            at = low + head * each
            yield head, pl.ds(low + head, each, stride=heads), slice(at, at + each)


def prefix_kernel(scale, heads, term_counts, held, query_ref, keys, values, *refs):
    terms = refs[held : held + sum(term_counts)]
    acc_ref, stat_ref, *sum_refs, flat = refs[held + sum(term_counts) :]
    rows, width = query_ref.shape
    tall = width + ONES
    half = stat_ref.shape[0] // 2

    @pl.when(pl.program_id(0) == 0)
    def _():
        put_sums(terms, term_counts, sum_refs)

    flat[...] = query_ref[...].astype(jnp.float32)
    for head, taken, here in each_part(rows, heads):
        query_block = flat[taken, :].astype(jnp.bfloat16)
        scores = dot_queries(keys[:, head * width : (head + 1) * width], query_block) * scale
        row_max, weights = softmax_parts(scores)
        mixed = jnp.dot(
            values[head * tall : (head + 1) * tall, :], weights, preferred_element_type=jnp.float32
        )
        acc_ref[:, here] = mixed[:width]
        stat_ref[:half, here] = jnp.broadcast_to(row_max, (half, row_max.shape[1]))
        stat_ref[half:, here] = jnp.broadcast_to(mixed[width : width + 1], (half, row_max.shape[1]))


def prefix_attend(
    query_rows, keys, values, chunk, scale, heads, part=(0, 1), state=None, sums=()
):
    all_rows, width = query_rows.shape
    row_total = all_rows // CHUNKS
    at, count = part
    rows = min(2048, row_total // count)
    steps = row_total // rows // count
    first = chunk * count * steps + at * steps
    out_specs = [
        pl.BlockSpec((width, rows), lambda i: (0, at * steps + i)),
        pl.BlockSpec((8, rows), lambda i: (0, at * steps + i)),
    ]
    in_specs = [
        pl.BlockSpec((rows, width), lambda i: (first + i, 0)),
        pl.BlockSpec(keys.shape, lambda i: (0, 0)),
        pl.BlockSpec(values.shape, lambda i: (0, 0)),
    ]
    operands = [query_rows, keys, values]
    aliases = {}
    if state is not None:
        in_specs += [pl.BlockSpec(memory_space=pl.ANY)] * 2
        operands += list(state)
        aliases = {3: 0, 4: 1}
    pieces = [piece for terms in sums for piece in terms]
    sum_shapes = [terms[0][1].block_shape[-2:] for terms in sums]
    in_specs += [spec for _, spec in pieces]
    operands += [array for array, _ in pieces]
    out_specs += [pl.BlockSpec(shape, lambda i: (0, 0)) for shape in sum_shapes]
    acc, stat, *made = pl.pallas_call(
        functools.partial(
            prefix_kernel, scale, heads, [len(terms) for terms in sums], len(aliases)
        ),
        grid=(steps,),
        in_specs=in_specs,
        out_specs=out_specs,
        out_shape=[
            jax.ShapeDtypeStruct((width, row_total), jnp.float32),
            jax.ShapeDtypeStruct((8, row_total), jnp.float32),
        ]
        + [jax.ShapeDtypeStruct(shape, jnp.bfloat16) for shape in sum_shapes],
        input_output_aliases=aliases,
        scratch_shapes=[pltpu.VMEM((rows, width), jnp.float32)],
        compiler_params=params(),
        cost_estimate=cost("prefix_attend"),
        name="prefix_attend",
    )(*operands)
    return ([acc, stat], made) if sums else [acc, stat]


def fresh_kernel(
    scale, heads, per_token, first_row, counts, length_ref, query_ref, acc_ref, stat_ref, *rest
):
    early_count, term_count = counts
    earlier, terms = rest[:early_count], rest[early_count : early_count + term_count]
    out_ref, fresh_ref, keys, values, flat, mixed_rows = rest[-6:]
    rows, width = query_ref.shape
    wide, tall = heads * width, width + ONES
    step = pl.program_id(0)

    @pl.when(step == 0)
    def _():
        values[...] = jnp.ones_like(values)
        fresh_ref[...] = total_of(terms).astype(fresh_ref.dtype)
        for index, ref in enumerate([*earlier, fresh_ref]):
            here = slice(index * ref.shape[0], (index + 1) * ref.shape[0])
            fresh = ref[...]
            keys[here, :] = fresh[:, :wide]
            put_values(values, here, fresh[:, wide:], heads)

    half = stat_ref.shape[0] // 2
    flat[...] = query_ref[...].astype(jnp.float32)
    for head, taken, here in each_part(rows, heads):
        query_block = flat[taken, :].astype(jnp.bfloat16)
        scores = dot_queries(keys[:, head * width : (head + 1) * width], query_block) * scale
        row = taken.start + heads * lax.broadcasted_iota(jnp.int32, (1, taken.size), 1)
        token = first_row + step * (rows // per_token) + (
            row // per_token if per_token & (per_token - 1) else row >> (per_token.bit_length() - 1)
        )
        key_at = lax.broadcasted_iota(jnp.int32, scores.shape, 0)
        scores = jnp.where(key_at <= token, scores, -jnp.inf)
        old_max, old_total = stat_ref[:1, here], stat_ref[half : half + 1, here]
        row_max, weights = softmax_parts(scores, old_max)
        fade = jnp.exp2(old_max - row_max)
        mixed = jnp.dot(
            values[head * tall : (head + 1) * tall, :], weights, preferred_element_type=jnp.float32
        )
        row_total = old_total * fade + mixed[width : width + 1]
        share = jnp.where(token < length_ref[0], 1.0 / row_total, 0.0)
        result = acc_ref[:, here] * (fade * share) + mixed[:width] * share
        mixed_rows[taken, :] = result.T
    out_ref[...] = mixed_rows[...].astype(out_ref.dtype)


def fresh_attend(
    length, query_rows, acc, stat, earlier, pieces, result, chunk, scale, heads, per_token
):
    row_total, width = query_rows.shape
    chunk_rows = row_total // CHUNKS
    rows = min(2048, chunk_rows)
    steps = chunk_rows // rows
    block = pl.BlockSpec((rows, width), lambda i, length: (chunk * steps + i, 0))
    fresh_shape = pieces[0][1].block_shape[-2:]
    key_count = (len(earlier) + 1) * fresh_shape[0]
    whole = pl.BlockSpec(fresh_shape, lambda i, length: (0, 0))
    in_specs = [
        block,
        pl.BlockSpec((width, rows), lambda i, length: (0, i)),
        pl.BlockSpec((stat.shape[0], rows), lambda i, length: (0, i)),
        *(whole for _ in earlier),
        *(spec for _, spec in pieces),
    ]
    operands = [length, query_rows, acc, stat, *earlier, *(array for array, _ in pieces)]
    aliases = {}
    if result is not None:
        in_specs.append(pl.BlockSpec(memory_space=pl.ANY))
        aliases = {len(operands): 0}
        operands.append(result)
    return pl.pallas_call(
        functools.partial(
            fresh_kernel,
            scale,
            heads,
            per_token,
            chunk * (chunk_rows // per_token),
            (len(earlier), len(pieces)),
        ),
        grid_spec=pltpu.PrefetchScalarGridSpec(
            num_scalar_prefetch=1,
            grid=(steps,),
            in_specs=in_specs,
            out_specs=[block, whole],
            scratch_shapes=[
                pltpu.VMEM((key_count, heads * width), jnp.bfloat16),
                pltpu.VMEM((heads * (width + ONES), key_count), jnp.bfloat16),
                pltpu.VMEM((rows, width), jnp.float32),
                pltpu.VMEM((rows, width), jnp.float32),
            ],
        ),
        out_shape=[
            jax.ShapeDtypeStruct((row_total, width), jnp.bfloat16),
            jax.ShapeDtypeStruct(fresh_shape, jnp.bfloat16),
        ],
        input_output_aliases=aliases,
        compiler_params=params(),
        cost_estimate=cost("fresh_attend"),
        name="fresh_attend",
    )(*operands)


def reduced_shards(tokens, key_weight, value_weight, queries, prefix_pool, block_table, lengths):
    batch_count = lax.axis_size("batch")
    ctx_count = lax.axis_size("ctx")
    head_count = lax.axis_size("head")
    batch_at, ctx_at, head_at = (lax.axis_index(a) for a in ("batch", "ctx", "head"))
    place = jnp.stack([batch_at, ctx_at, head_at]).astype(jnp.int32)
    token_count = tokens.shape[0]
    heads = queries.shape[1]
    width = prefix_pool.shape[4] // 2
    group = queries.shape[3] // width
    per_token = heads * group
    depth = key_weight.shape[2]
    rows = token_count // CHUNKS
    scale = math.log2(math.e) / math.sqrt(width)

    top = batch_count // 2
    steps = list(range(batch_count - 1, top, -1)) + list(range(1, top))
    pieces = cut_tokens(place, tokens, depth, [*steps, top])
    pieces, prefix_pool = after(pieces, prefix_pool)
    arrived = [trade(piece, "batch", bits) for piece, bits in zip(pieces, steps)]
    pools = arrange_pool(place, prefix_pool, ctx_count, heads)
    pools, (key_weight, value_weight) = after(pools, (key_weight, value_weight))
    pools = [shift(part, "ctx", step) if step else part for step, part in enumerate(pools)]

    weights = arrange_weights(key_weight, value_weight, ctx_count, heads, head_count)
    weights, last = after(weights, pieces[-1])
    last = trade(last, "batch", top)

    query_rows = queries.reshape(token_count, heads, group, width)
    query_rows = query_rows.transpose(0, 2, 1, 3).reshape(-1, width)
    def projected(blocks, name):
        terms = [
            shift(project(place, blocks, weights, step, jnp.bfloat16, name + "_away"), "head", step)
            for step in range(1, head_count)
        ]
        return [project(place, blocks, weights, 0, jnp.float32, name + "_kept"), *terms]

    def added(terms, step, here):
        return sum(term[step, here].astype(jnp.float32) for term in terms)

    def others(terms, here):
        return [added(terms, step, here).astype(jnp.bfloat16) for step in range(1, ctx_count)]

    def spread(parts):
        return [shift(part, "ctx", step + 1) for step, part in enumerate(parts)]

    every = slice(None)
    parts_of = [slice(i * rows, (i + 1) * rows) for i in range(CHUNKS)]

    sums = [[], []]
    if steps:
        early = projected(arrived, "early")
        cuts = [slice(i * token_count, (i + 1) * token_count) for i in range(len(steps))]
        leaving = [others(early, cut) for cut in cuts]
        leaving, pools = after(leaving, pools)
        sums = [
            [
                [piece_of(t, token_count, i, 0) for t in early]
                + [piece_of(p, token_count, 0) for p in spread(parts)]
            ]
            for i, parts in enumerate(leaving)
        ]
    keys, values = pick_blocks(place, block_table[0], pools, heads)
    states = [prefix_attend(query_rows, keys, values, 0, scale, heads)]
    state, far = prefix_attend(
        query_rows, keys, values, 1, scale, heads, (0, 2), None, sums[0]
    )
    far = [trade(part, "batch", 1) for part in far]
    (states[0], state), last = after((states[0], state), last)

    def late_project(step, dtype, name, sums):
        result = project(place, [last, tokens], weights, step, dtype, name, sums)
        return result if sums else (result,)

    terms, near = [], []
    for step in range(1, head_count):
        term, *made = late_project(step, jnp.bfloat16, "late_away", sums[1] if step == 1 else [])
        near += [trade(part, "batch", 1) for part in made]
        terms.append(shift(term, "head", step))
    kept, *_ = late_project(0, jnp.float32, "late_kept", [])
    late = [kept, *terms]
    own_at = slice(token_count, 2 * token_count)
    *late_others, own_others = [others(late, here) for here in [*parts_of, own_at]]
    late_others[0] = spread(late_others[0])
    late_others[1], (keys, values) = after(late_others[1], (keys, values))
    state = prefix_attend(query_rows, keys, values, 1, scale, heads, (2, 4), state)
    state, (late_others[1], own_others) = after(state, (late_others[1], own_others))
    late_others[1] = spread(late_others[1])

    away = []
    for chunk, here in enumerate(parts_of):
        part = added(late, 0, here) + sum(p.astype(jnp.float32) for p in late_others[chunk])
        part = part + sum(p[here].astype(jnp.float32) for p in far)
        part = part.astype(jnp.bfloat16)
        if chunk == 0:
            (far, late), late_others[1] = after((far, late), late_others[1])
            part, (state, own_others) = after(part, (state, own_others))
            own_others = spread(own_others)
        else:
            away[-1], part = after(away[-1], part)
        away.append(trade(part, "batch", top))
    states.append(prefix_attend(query_rows, keys, values, 1, scale, heads, (3, 4), state))

    result = None
    fresh = []
    for chunk in range(CHUNKS):
        pieces = [piece_of(t, rows, CHUNKS + chunk, 0) for t in late]
        pieces += [piece_of(part, rows, chunk) for part in (*own_others, *near)]
        pieces.append(piece_of(away[chunk], rows, 0))
        result, new = fresh_attend(
            lengths,
            query_rows,
            *states[chunk],
            fresh,
            pieces,
            result,
            chunk,
            scale,
            heads,
            per_token,
        )
        fresh.append(new)
    result = result.reshape(token_count, group, heads, width).transpose(0, 2, 1, 3)
    return result.reshape(token_count, heads, 1, group * width)


def solution(mesh):
    def shards(tokens, key_weight, value_weight, *rest):
        prompts = mesh.shape["batch"]
        columns = 2 * math.prod(key_weight.shape[3:])
        few_tokens = prompts * tokens.shape[0] <= columns and prompts in (2, 4)
        form = reduced_shards if few_tokens else gathered_shards
        return form(tokens, key_weight, value_weight, *rest)

    return jax.shard_map(
        shards,
        mesh=mesh,
        in_specs=(
            P(("groups", "batch"), ("ctx", "head")),
            P("ctx", "head", "batch", None, None, None),
            P("ctx", "head", "batch", None, None, None),
            P(("groups", "batch"), "ctx", "head", None),
            P(("groups", "ctx"), None, None, "head", None),
            P(("groups", "batch"), None),
            P(("groups", "batch")),
        ),
        out_specs=P(("groups", "batch"), "ctx", "head", None),
        check_vma=False,
    )
```

```python
import functools
import math

import jax
import jax.numpy as jnp
from jax import lax
from jax.experimental import pallas as pl
from jax.experimental.pallas import tpu as pltpu
from jax.sharding import PartitionSpec as P

CHUNKS = 2
PART = 1024
VMEM_BYTES = 16 * 1024 * 1024
MOST_VMEM_BYTES = 52 * 1024 * 1024
LONG = pl.CostEstimate(flops=2 * 10**10, bytes_accessed=1, transcendentals=0)
COSTS = {}


def cost(name):
    return COSTS.get(name, LONG)


def attend_head(query_rows, prefix, fresh_rows, length):
    token_count = query_rows.shape[0]
    head_width = prefix.shape[1] // 2
    group_size = query_rows.shape[1] // head_width
    prefix_len = prefix.shape[0]
    key_rows = jnp.concatenate([prefix[:, :head_width], fresh_rows[:, :head_width]], 0)
    value_rows = jnp.concatenate([prefix[:, head_width:], fresh_rows[:, head_width:]], 0)
    block_len = min(token_count, 64)
    pieces = []
    for first_row in range(0, token_count, block_len):
        block_rows = query_rows[first_row : first_row + block_len].reshape(
            block_len * group_size, head_width
        )
        scores = jnp.dot(
            block_rows, key_rows.T, preferred_element_type=jnp.float32
        ) * head_width ** (-0.5)
        position = first_row + jnp.arange(block_len * group_size) // group_size
        column = jnp.arange(prefix_len + token_count) - prefix_len
        allowed = column[None, :] <= position[:, None]
        scores = jnp.where(allowed, scores, -jnp.inf)
        row_max = jnp.max(scores, axis=1, keepdims=True)
        weights = jnp.exp(scores - row_max)
        row_total = jnp.sum(weights, axis=1, keepdims=True)
        probs_bf = (weights / row_total).astype(jnp.bfloat16)
        mixed_rows = jnp.dot(probs_bf, value_rows, preferred_element_type=jnp.float32)
        is_live = position < length
        mixed_rows = jnp.where(is_live[:, None], mixed_rows, 0.0)
        pieces.append(mixed_rows.astype(jnp.bfloat16).reshape(block_len, group_size * head_width))
    return jnp.concatenate(pieces, 0)


def gathered_shards(tokens, key_weight, value_weight, queries, prefix_pool, block_table, lengths):
    token_count = tokens.shape[0]
    local_heads = queries.shape[1]
    head_width = prefix_pool.shape[4] // 2
    ctx_count = lax.axis_size("ctx")
    head_count = lax.axis_size("head")
    features = lax.all_gather(tokens, ("ctx", "head"), axis=1, tiled=True)
    key_cols, value_cols = (
        lax.all_to_all(
            lax.all_to_all(weight, "ctx", split_axis=3, concat_axis=0, tiled=True),
            "head",
            split_axis=4,
            concat_axis=1,
            tiled=True,
        )
        for weight in (key_weight, value_weight)
    )
    span_len = features.shape[1] // (ctx_count * head_count)
    feature_view = features.reshape(token_count, ctx_count, head_count, span_len)
    pieces = (
        lax.all_gather(key_cols, "batch", axis=2, tiled=True),
        lax.all_gather(value_cols, "batch", axis=2, tiled=True),
    )
    row_count = pieces[0].shape[2]

    def one_term(weight_piece):
        shaped = weight_piece.reshape(ctx_count, head_count, row_count, local_heads * head_width)
        return jnp.einsum("tchr,chrk->tk", feature_view, shaped, preferred_element_type=jnp.float32)

    new_keys = one_term(pieces[0]).astype(jnp.bfloat16).reshape(token_count, local_heads, head_width)
    new_values = one_term(pieces[1]).astype(jnp.bfloat16).reshape(token_count, local_heads, head_width)
    fresh_all = jnp.concatenate([new_keys, new_values], 2)
    pool_heads = lax.all_to_all(prefix_pool, "ctx", split_axis=2, concat_axis=0, tiled=True)
    chosen = jnp.take(pool_heads, block_table[0], axis=0)
    chosen = chosen.reshape(-1, local_heads, 2 * head_width)
    outputs = [
        attend_head(
            queries[:, head_idx, 0], chosen[:, head_idx], fresh_all[:, head_idx], lengths[0]
        )
        for head_idx in range(local_heads)
    ]
    return jnp.stack(outputs, 1)[:, :, None, :]


def shift(array, axis, step):
    count = lax.axis_size(axis)
    return lax.ppermute(array, axis, [(i, (i + step) % count) for i in range(count)])


def trade(array, axis, bits):
    return lax.ppermute(array, axis, [(i, i ^ bits) for i in range(lax.axis_size(axis))])


def after(first, second):
    return lax.optimization_barrier((first, second))


def softmax_parts(scores, old_max=None):
    row_max = jnp.max(scores, axis=0, keepdims=True)
    if old_max is not None:
        row_max = jnp.maximum(row_max, old_max)
    weights = jnp.exp2(scores - row_max)
    return row_max, weights.astype(jnp.bfloat16), jnp.sum(weights, axis=0, keepdims=True)


def dot_queries(keys, query_block):
    return lax.dot_general(
        keys, query_block, (((1,), (1,)), ((), ())), preferred_element_type=jnp.float32
    )


def params(limit=None):
    return pltpu.CompilerParams(vmem_limit_bytes=limit or VMEM_BYTES)


def weight_kernel(ctx_count, heads, head_count, key_ref, value_ref, out_ref, flat):
    depth, slots, width = key_ref.shape
    for kind, ref in enumerate((key_ref, value_ref)):
        flat[...] = ref[...].astype(jnp.float32).reshape(depth * slots, width)
        for ctx in range(ctx_count):
            for head in range(heads):
                for core in range(head_count):
                    slot = (ctx * heads + head) * head_count + core
                    at = (kind * heads + head) * width
                    out_ref[core, ctx, :, at : at + width] = flat[
                        pl.ds(slot, depth, stride=slots), :
                    ].astype(out_ref.dtype)


def arrange_weights(key_weight, value_weight, ctx_count, heads, head_count):
    depth, width = key_weight.shape[2], key_weight.shape[5]
    slots = ctx_count * heads * head_count
    rows = min(128, depth)
    views = [w.reshape(depth, slots, width) for w in (key_weight, value_weight)]
    block = pl.BlockSpec((rows, slots, width), lambda i: (i, 0, 0))
    columns = 2 * heads * width
    return pl.pallas_call(
        functools.partial(weight_kernel, ctx_count, heads, head_count),
        grid=(depth // rows,),
        in_specs=[block, block],
        out_specs=pl.BlockSpec((head_count, ctx_count, rows, columns), lambda i: (0, 0, i, 0)),
        out_shape=jax.ShapeDtypeStruct((head_count, ctx_count, depth, columns), jnp.bfloat16),
        scratch_shapes=[pltpu.VMEM((rows * slots, width), jnp.float32)],
        compiler_params=params(),
        cost_estimate=cost("arrange_weights"),
        name="arrange_weights",
    )(*views)


def cut_kernel(bits, place_ref, tokens_ref, *refs):
    pieces, sems = refs[:-1], refs[-1]
    depth = pieces[0].shape[1]
    copies = []
    for index, piece in enumerate(pieces):
        start = pl.multiple_of((place_ref[0] ^ bits[index]) * depth, depth)
        source = tokens_ref.at[:, pl.ds(start, depth)]
        copies.append(pltpu.make_async_copy(source, piece, sems.at[index]))
    for copy in copies:
        copy.start()
    for copy in copies:
        copy.wait()


def cut_tokens(place, tokens, depth, bits):
    far = pl.BlockSpec(memory_space=pltpu.HBM)
    piece = jax.ShapeDtypeStruct((tokens.shape[0], depth), tokens.dtype)
    return pl.pallas_call(
        functools.partial(cut_kernel, bits),
        grid_spec=pltpu.PrefetchScalarGridSpec(
            num_scalar_prefetch=1,
            grid=(1,),
            in_specs=[far],
            out_specs=[pl.BlockSpec(piece.shape, lambda i, place: (0, 0))] * len(bits),
            scratch_shapes=[pltpu.SemaphoreType.DMA((len(bits),))],
        ),
        out_shape=[piece] * len(bits),
        compiler_params=params(MOST_VMEM_BYTES),
        cost_estimate=cost("cut_tokens"),
        name="cut_tokens",
    )(place, tokens)


def pool_kernel(ctx_count, heads, place_ref, pool_ref, *refs):
    outs, flat = refs[:-1], refs[-1]
    some, length, slots, width = pool_ref.shape
    length *= some
    flat[...] = pool_ref[...].astype(jnp.float32).reshape(length * slots, width)
    for kind in range(2):
        for head in range(heads):
            at = (kind * heads + head) * width
            held = []
            for ctx in range(ctx_count):
                slot = (kind * ctx_count + ctx) * heads + head
                held.append(flat[pl.ds(slot, length, stride=slots), :])
            for step, out_ref in enumerate(outs):
                target = lax.rem(place_ref[1] + step, ctx_count)
                value = held[0]
                for ctx in range(1, ctx_count):
                    value = jnp.where(target == ctx, held[ctx], value)
                out_ref[:, :, at : at + width] = value.astype(out_ref.dtype).reshape(
                    some, length // some, width
                )


def arrange_pool(place, prefix_pool, ctx_count, heads):
    blocks, length, all_heads, _, double = prefix_pool.shape
    width = double // 2
    slots = 2 * all_heads
    view = prefix_pool.reshape(blocks, length, all_heads, 2, width)
    view = view.transpose(0, 1, 3, 2, 4).reshape(blocks, length, slots, width)
    columns = 2 * heads * width
    some = 2 if blocks % 2 == 0 else 1
    out = pl.BlockSpec((some, length, columns), lambda i, place: (i, 0, 0))
    return pl.pallas_call(
        functools.partial(pool_kernel, ctx_count, heads),
        grid_spec=pltpu.PrefetchScalarGridSpec(
            num_scalar_prefetch=1,
            grid=(blocks // some,),
            in_specs=[pl.BlockSpec((some, length, slots, width), lambda i, place: (i, 0, 0, 0))],
            out_specs=[out] * ctx_count,
            scratch_shapes=[pltpu.VMEM((some * length * slots, width), jnp.float32)],
        ),
        out_shape=[jax.ShapeDtypeStruct((blocks, length, columns), jnp.bfloat16)] * ctx_count,
        compiler_params=params(),
        cost_estimate=cost("arrange_pool"),
        name="arrange_pool",
    )(place, view)


def total_of(refs):
    return sum(ref[...].astype(jnp.float32).reshape(ref.shape[-2:]) for ref in refs)


def put_sums(terms, counts, sum_refs):
    at = 0
    for count, sum_ref in zip(counts, sum_refs):
        sum_ref[...] = total_of(terms[at : at + count]).astype(sum_ref.dtype)
        at += count


def project_kernel(block_count, term_counts, place_ref, *refs):
    token_refs, weight_ref = refs[:block_count], refs[block_count]
    terms = refs[block_count + 1 : block_count + 1 + sum(term_counts)]
    out_ref, *sum_refs = refs[block_count + 1 + sum(term_counts) : -1]
    stacked = refs[-1]

    @pl.when(pl.program_id(0) == 0)
    def _():
        at = 0
        for token_ref in token_refs:
            rows = token_ref.shape[0]
            stacked[at : at + rows, :] = token_ref[...]
            at += rows
        put_sums(terms, term_counts, sum_refs)

    out_ref[0] = jnp.dot(
        stacked[...], weight_ref[0, 0], preferred_element_type=jnp.float32
    ).astype(out_ref.dtype)


def piece_of(array, *index):
    rows, block, *leading = index
    shape = (1,) * len(leading) + (rows, array.shape[-1])
    return array, pl.BlockSpec(shape, lambda j, *_: (*leading, block, 0))


def project(place, blocks, weights, head_step, out_dtype, name, sums=()):
    head_count, ctx_count, depth, width = weights.shape
    row_total = sum(block.shape[0] for block in blocks)

    def block_spec(block):
        if block.shape[1] == depth:
            return pl.BlockSpec(block.shape, lambda j, place: (0, 0))
        return pl.BlockSpec((block.shape[0], depth), lambda j, place: (0, place[0]))

    pieces = [piece for terms in sums for piece in terms]
    sum_shapes = [terms[0][1].block_shape[-2:] for terms in sums]
    result = pl.pallas_call(
        functools.partial(project_kernel, len(blocks), [len(terms) for terms in sums]),
        grid_spec=pltpu.PrefetchScalarGridSpec(
            num_scalar_prefetch=1,
            grid=(ctx_count,),
            in_specs=[block_spec(block) for block in blocks]
            + [
                pl.BlockSpec(
                    (1, 1, depth, width),
                    lambda j, place: (
                        lax.rem(place[2] + head_step, head_count),
                        lax.rem(place[1] + j, ctx_count),
                        0,
                        0,
                    ),
                )
            ]
            + [spec for _, spec in pieces],
            out_specs=[pl.BlockSpec((1, row_total, width), lambda j, place: (j, 0, 0))]
            + [pl.BlockSpec(shape, lambda j, place: (0, 0)) for shape in sum_shapes],
            scratch_shapes=[pltpu.VMEM((row_total, depth), weights.dtype)],
        ),
        out_shape=[jax.ShapeDtypeStruct((ctx_count, row_total, width), out_dtype)]
        + [jax.ShapeDtypeStruct(shape, jnp.bfloat16) for shape in sum_shapes],
        compiler_params=params(),
        cost_estimate=cost(name),
        name=name,
    )(place, *blocks, weights, *(array for array, _ in pieces))
    return result if sums else result[0]


def pick_kernel(heads, ctx_count, place_ref, table_ref, *refs):
    pool_refs, (keys, values) = refs[:ctx_count], refs[ctx_count:]
    blocks, length, columns = pool_refs[0].shape
    wide = columns // 2
    width = wide // heads
    for at in range(table_ref.shape[0]):
        entry = table_ref[at]
        here = slice(at * length, (at + 1) * length)
        step = lax.rem(place_ref[1] - entry // blocks + ctx_count, ctx_count)
        for ctx_step, pool_ref in enumerate(pool_refs):

            @pl.when(step == ctx_step)
            def _():
                block = pool_ref[entry % blocks]
                keys[here, :] = block[:, :wide]
                put_values(values, here, block[:, wide:], heads)


def put_values(values, here, block, heads):
    width = block.shape[1] // heads
    for head in range(heads):
        low = head * width
        values[low : low + width, here] = (
            block[:, head * width : (head + 1) * width].astype(jnp.float32).T.astype(jnp.bfloat16)
        )


def pick_blocks(place, table, pools, heads):
    length, columns = pools[0].shape[1:]
    count = table.shape[0] * length
    wide = columns // 2
    tall = wide
    return pl.pallas_call(
        functools.partial(pick_kernel, heads, len(pools)),
        grid_spec=pltpu.PrefetchScalarGridSpec(
            num_scalar_prefetch=2,
            grid=(1,),
            in_specs=[pl.BlockSpec(p.shape, lambda i, *_: (0, 0, 0)) for p in pools],
            out_specs=[
                pl.BlockSpec((count, wide), lambda i, *_: (0, 0)),
                pl.BlockSpec((tall, count), lambda i, *_: (0, 0)),
            ],
        ),
        out_shape=[
            jax.ShapeDtypeStruct((count, wide), jnp.bfloat16),
            jax.ShapeDtypeStruct((tall, count), jnp.bfloat16),
        ],
        compiler_params=params(),
        cost_estimate=cost("pick_blocks"),
        name="pick_blocks",
    )(place, table, *pools)


def each_part(rows, heads):
    part_rows = min(PART, rows)
    each = part_rows // heads
    for low in range(0, rows, part_rows):
        for head in range(heads):
            at = low + head * each
            yield head, pl.ds(low + head, each, stride=heads), slice(at, at + each)


def prefix_kernel(scale, heads, term_counts, held, query_ref, keys, values, *refs):
    terms = refs[held : held + sum(term_counts)]
    acc_ref, stat_ref, *sum_refs, flat = refs[held + sum(term_counts) :]
    rows, width = query_ref.shape
    tall = width
    half = stat_ref.shape[0] // 2

    @pl.when(pl.program_id(0) == 0)
    def _():
        put_sums(terms, term_counts, sum_refs)

    flat[...] = query_ref[...].astype(jnp.float32)
    for head, taken, here in each_part(rows, heads):
        query_block = flat[taken, :].astype(jnp.bfloat16)
        scores = dot_queries(keys[:, head * width : (head + 1) * width], query_block) * scale
        row_max, weights, total = softmax_parts(scores)
        mixed = jnp.dot(
            values[head * tall : (head + 1) * tall, :], weights, preferred_element_type=jnp.float32
        )
        acc_ref[:, here] = mixed[:width]
        stat_ref[:half, here] = jnp.broadcast_to(row_max, (half, row_max.shape[1]))
        stat_ref[half:, here] = jnp.broadcast_to(total, (half, row_max.shape[1]))


def prefix_attend(
    query_rows, keys, values, chunk, scale, heads, part=(0, 1), state=None, sums=()
):
    all_rows, width = query_rows.shape
    row_total = all_rows // CHUNKS
    at, count = part
    rows = min(2048, row_total // count)
    steps = row_total // rows // count
    first = chunk * count * steps + at * steps
    out_specs = [
        pl.BlockSpec((width, rows), lambda i: (0, at * steps + i)),
        pl.BlockSpec((8, rows), lambda i: (0, at * steps + i)),
    ]
    in_specs = [
        pl.BlockSpec((rows, width), lambda i: (first + i, 0)),
        pl.BlockSpec(keys.shape, lambda i: (0, 0)),
        pl.BlockSpec(values.shape, lambda i: (0, 0)),
    ]
    operands = [query_rows, keys, values]
    aliases = {}
    if state is not None:
        in_specs += [pl.BlockSpec(memory_space=pl.ANY)] * 2
        operands += list(state)
        aliases = {3: 0, 4: 1}
    pieces = [piece for terms in sums for piece in terms]
    sum_shapes = [terms[0][1].block_shape[-2:] for terms in sums]
    in_specs += [spec for _, spec in pieces]
    operands += [array for array, _ in pieces]
    out_specs += [pl.BlockSpec(shape, lambda i: (0, 0)) for shape in sum_shapes]
    acc, stat, *made = pl.pallas_call(
        functools.partial(
            prefix_kernel, scale, heads, [len(terms) for terms in sums], len(aliases)
        ),
        grid=(steps,),
        in_specs=in_specs,
        out_specs=out_specs,
        out_shape=[
            jax.ShapeDtypeStruct((width, row_total), jnp.float32),
            jax.ShapeDtypeStruct((8, row_total), jnp.float32),
        ]
        + [jax.ShapeDtypeStruct(shape, jnp.bfloat16) for shape in sum_shapes],
        input_output_aliases=aliases,
        scratch_shapes=[pltpu.VMEM((rows, width), jnp.float32)],
        compiler_params=params(),
        cost_estimate=cost("prefix_attend"),
        name="prefix_attend",
    )(*operands)
    return ([acc, stat], made) if sums else [acc, stat]


def fresh_kernel(
    scale, heads, per_token, first_row, counts, length_ref, query_ref, acc_ref, stat_ref, *rest
):
    early_count, term_count = counts
    earlier, terms = rest[:early_count], rest[early_count : early_count + term_count]
    out_ref, fresh_ref, keys, values, flat, mixed_rows = rest[-6:]
    rows, width = query_ref.shape
    wide, tall = heads * width, width
    step = pl.program_id(0)

    @pl.when(step == 0)
    def _():
        fresh_ref[...] = total_of(terms).astype(fresh_ref.dtype)
        for index, ref in enumerate([*earlier, fresh_ref]):
            here = slice(index * ref.shape[0], (index + 1) * ref.shape[0])
            fresh = ref[...]
            keys[here, :] = fresh[:, :wide]
            put_values(values, here, fresh[:, wide:], heads)

    half = stat_ref.shape[0] // 2
    flat[...] = query_ref[...].astype(jnp.float32)
    for head, taken, here in each_part(rows, heads):
        query_block = flat[taken, :].astype(jnp.bfloat16)
        scores = dot_queries(keys[:, head * width : (head + 1) * width], query_block) * scale
        row = taken.start + heads * lax.broadcasted_iota(jnp.int32, (1, taken.size), 1)
        token = first_row + step * (rows // per_token) + (
            row // per_token if per_token & (per_token - 1) else row >> (per_token.bit_length() - 1)
        )
        key_at = lax.broadcasted_iota(jnp.int32, scores.shape, 0)
        scores = jnp.where(key_at <= token, scores, -jnp.inf)
        old_max, old_total = stat_ref[:1, here], stat_ref[half : half + 1, here]
        row_max, weights, total = softmax_parts(scores, old_max)
        fade = jnp.exp2(old_max - row_max)
        mixed = jnp.dot(
            values[head * tall : (head + 1) * tall, :], weights, preferred_element_type=jnp.float32
        )
        row_total = old_total * fade + total
        share = jnp.where(token < length_ref[0], 1.0 / row_total, 0.0)
        result = acc_ref[:, here] * (fade * share) + mixed[:width] * share
        mixed_rows[taken, :] = result.T
    out_ref[...] = mixed_rows[...].astype(out_ref.dtype)


def fresh_attend(
    length, query_rows, acc, stat, earlier, pieces, result, chunk, scale, heads, per_token
):
    row_total, width = query_rows.shape
    chunk_rows = row_total // CHUNKS
    rows = min(2048, chunk_rows)
    steps = chunk_rows // rows
    block = pl.BlockSpec((rows, width), lambda i, length: (chunk * steps + i, 0))
    fresh_shape = pieces[0][1].block_shape[-2:]
    key_count = (len(earlier) + 1) * fresh_shape[0]
    whole = pl.BlockSpec(fresh_shape, lambda i, length: (0, 0))
    in_specs = [
        block,
        pl.BlockSpec((width, rows), lambda i, length: (0, i)),
        pl.BlockSpec((stat.shape[0], rows), lambda i, length: (0, i)),
        *(whole for _ in earlier),
        *(spec for _, spec in pieces),
    ]
    operands = [length, query_rows, acc, stat, *earlier, *(array for array, _ in pieces)]
    aliases = {}
    if result is not None:
        in_specs.append(pl.BlockSpec(memory_space=pl.ANY))
        aliases = {len(operands): 0}
        operands.append(result)
    return pl.pallas_call(
        functools.partial(
            fresh_kernel,
            scale,
            heads,
            per_token,
            chunk * (chunk_rows // per_token),
            (len(earlier), len(pieces)),
        ),
        grid_spec=pltpu.PrefetchScalarGridSpec(
            num_scalar_prefetch=1,
            grid=(steps,),
            in_specs=in_specs,
            out_specs=[block, whole],
            scratch_shapes=[
                pltpu.VMEM((key_count, heads * width), jnp.bfloat16),
                pltpu.VMEM((heads * width, key_count), jnp.bfloat16),
                pltpu.VMEM((rows, width), jnp.float32),
                pltpu.VMEM((rows, width), jnp.float32),
            ],
        ),
        out_shape=[
            jax.ShapeDtypeStruct((row_total, width), jnp.bfloat16),
            jax.ShapeDtypeStruct(fresh_shape, jnp.bfloat16),
        ],
        input_output_aliases=aliases,
        compiler_params=params(),
        cost_estimate=cost("fresh_attend"),
        name="fresh_attend",
    )(*operands)


def reduced_shards(tokens, key_weight, value_weight, queries, prefix_pool, block_table, lengths):
    batch_count = lax.axis_size("batch")
    ctx_count = lax.axis_size("ctx")
    head_count = lax.axis_size("head")
    batch_at, ctx_at, head_at = (lax.axis_index(a) for a in ("batch", "ctx", "head"))
    place = jnp.stack([batch_at, ctx_at, head_at]).astype(jnp.int32)
    token_count = tokens.shape[0]
    heads = queries.shape[1]
    width = prefix_pool.shape[4] // 2
    group = queries.shape[3] // width
    per_token = heads * group
    depth = key_weight.shape[2]
    rows = token_count // CHUNKS
    scale = math.log2(math.e) / math.sqrt(width)

    top = batch_count // 2
    steps = list(range(batch_count - 1, top, -1)) + list(range(1, top))
    pieces = cut_tokens(place, tokens, depth, [*steps, top])
    pieces, prefix_pool = after(pieces, prefix_pool)
    arrived = [trade(piece, "batch", bits) for piece, bits in zip(pieces, steps)]
    pools = arrange_pool(place, prefix_pool, ctx_count, heads)
    pools, (key_weight, value_weight) = after(pools, (key_weight, value_weight))
    pools = [shift(part, "ctx", step) if step else part for step, part in enumerate(pools)]

    weights = arrange_weights(key_weight, value_weight, ctx_count, heads, head_count)
    weights, last = after(weights, pieces[-1])
    last = trade(last, "batch", top)

    query_rows = queries.reshape(token_count, heads, group, width)
    query_rows = query_rows.transpose(0, 2, 1, 3).reshape(-1, width)
    def projected(blocks, name):
        terms = [
            shift(project(place, blocks, weights, step, jnp.bfloat16, name + "_away"), "head", step)
            for step in range(1, head_count)
        ]
        return [project(place, blocks, weights, 0, jnp.float32, name + "_kept"), *terms]

    def added(terms, step, here):
        return sum(term[step, here].astype(jnp.float32) for term in terms)

    def others(terms, here):
        return [added(terms, step, here).astype(jnp.bfloat16) for step in range(1, ctx_count)]

    def spread(parts):
        return [shift(part, "ctx", step + 1) for step, part in enumerate(parts)]

    every = slice(None)
    parts_of = [slice(i * rows, (i + 1) * rows) for i in range(CHUNKS)]

    sums = [[], []]
    if steps:
        early = projected(arrived, "early")
        cuts = [slice(i * token_count, (i + 1) * token_count) for i in range(len(steps))]
        leaving = [others(early, cut) for cut in cuts]
        leaving, pools = after(leaving, pools)
        sums = [
            [
                [piece_of(t, token_count, i, 0) for t in early]
                + [piece_of(p, token_count, 0) for p in spread(parts)]
            ]
            for i, parts in enumerate(leaving)
        ]
    keys, values = pick_blocks(place, block_table[0], pools, heads)
    states = [prefix_attend(query_rows, keys, values, 0, scale, heads)]
    state, far = prefix_attend(
        query_rows, keys, values, 1, scale, heads, (0, 2), None, sums[0]
    )
    far = [trade(part, "batch", 1) for part in far]
    (states[0], state), last = after((states[0], state), last)

    def late_project(step, dtype, name, sums):
        result = project(place, [last, tokens], weights, step, dtype, name, sums)
        return result if sums else (result,)

    terms, near = [], []
    for step in range(1, head_count):
        term, *made = late_project(step, jnp.bfloat16, "late_away", sums[1] if step == 1 else [])
        near += [trade(part, "batch", 1) for part in made]
        terms.append(shift(term, "head", step))
    kept, *_ = late_project(0, jnp.float32, "late_kept", [])
    late = [kept, *terms]
    own_at = slice(token_count, 2 * token_count)
    *late_others, own_others = [others(late, here) for here in [*parts_of, own_at]]
    late_others[0] = spread(late_others[0])
    late_others[1], (keys, values) = after(late_others[1], (keys, values))
    state = prefix_attend(query_rows, keys, values, 1, scale, heads, (2, 4), state)
    state, (late_others[1], own_others) = after(state, (late_others[1], own_others))
    late_others[1] = spread(late_others[1])

    away = []
    for chunk, here in enumerate(parts_of):
        part = added(late, 0, here) + sum(p.astype(jnp.float32) for p in late_others[chunk])
        part = part + sum(p[here].astype(jnp.float32) for p in far)
        part = part.astype(jnp.bfloat16)
        if chunk == 0:
            (far, late), late_others[1] = after((far, late), late_others[1])
            part, (state, own_others) = after(part, (state, own_others))
            own_others = spread(own_others)
        else:
            away[-1], part = after(away[-1], part)
        away.append(trade(part, "batch", top))
    states.append(prefix_attend(query_rows, keys, values, 1, scale, heads, (3, 4), state))

    result = None
    fresh = []
    for chunk in range(CHUNKS):
        pieces = [piece_of(t, rows, CHUNKS + chunk, 0) for t in late]
        pieces += [piece_of(part, rows, chunk) for part in (*own_others, *near)]
        pieces.append(piece_of(away[chunk], rows, 0))
        result, new = fresh_attend(
            lengths,
            query_rows,
            *states[chunk],
            fresh,
            pieces,
            result,
            chunk,
            scale,
            heads,
            per_token,
        )
        fresh.append(new)
    result = result.reshape(token_count, group, heads, width).transpose(0, 2, 1, 3)
    return result.reshape(token_count, heads, 1, group * width)


def solution(mesh):
    def shards(tokens, key_weight, value_weight, *rest):
        prompts = mesh.shape["batch"]
        columns = 2 * math.prod(key_weight.shape[3:])
        few_tokens = prompts * tokens.shape[0] <= columns and prompts in (2, 4)
        form = reduced_shards if few_tokens else gathered_shards
        return form(tokens, key_weight, value_weight, *rest)

    return jax.shard_map(
        shards,
        mesh=mesh,
        in_specs=(
            P(("groups", "batch"), ("ctx", "head")),
            P("ctx", "head", "batch", None, None, None),
            P("ctx", "head", "batch", None, None, None),
            P(("groups", "batch"), "ctx", "head", None),
            P(("groups", "ctx"), None, None, "head", None),
            P(("groups", "batch"), None),
            P(("groups", "batch")),
        ),
        out_specs=P(("groups", "batch"), "ctx", "head", None),
        check_vma=False,
    )
```
